32 devices in a mesh: seq: 16 (over z, x, core), tp: 2 (over y).
Axes of the slice: x: 2, y: 2, z: 4, core: 2. Of those that a mesh axis runs over, the one named last changes fastest.
Arguments:
- block_in: bfloat16 [2048, 2048], P(('seq', 'tp')), may hold values from -6 to 6
- cotangent: bfloat16 [2048, 2048], P('seq'), may hold values from -6 to 6
- segment_ids: int32 [2048], replicated, may hold values from 0 to 7, never falling along the last dimension, each value on 1 to 1024 neighbouring positions
- norm_gain: float32 [2048], replicated, may hold values from 0.5 to 1.5
- in_weight: float32 [2048, 2, 4096], P('seq', None, 'tp'), may hold values from -0.125 to 0.125
- out_weight: float32 [2048, 4096], P('seq', 'tp'), may hold values from -0.1875 to 0.1875
- conv_weight: float32 [4, 4096], P(None, 'tp'), may hold values from -3 to 3
- conv_bias: float32 [4096], P('tp'), may hold values from -0.5 to 0.5
- select_weight: float32 [160, 4096], P(None, 'tp'), may hold values from -0.09375 to 0.09375
- step_weight: float32 [128, 4096], P(None, 'tp'), may hold values from -0.5 to 0.5
- step_bias: float32 [4096], P('tp'), may hold values from -6 to -2
- decay_log: float32 [16, 4096], P(None, 'tp'), may hold values from -5 to 2
- skip_gain: float32 [4096], P('tp'), may hold values from 0.5 to 1.5
- norm_moment: float32 [2048], replicated, may hold values from 1000 to 30000
- in_rows: float32 [2048], P('seq'), may hold values from 3000 to 30000
- in_cols: float32 [2, 4096], P(None, 'tp'), may hold values from 3000 to 30000
- out_rows: float32 [2048], P('seq'), may hold values from 3000 to 30000
- out_cols: float32 [4096], P('tp'), may hold values from 3000 to 30000
- conv_rows: float32 [4], replicated, may hold values from 1000 to 30000
- conv_cols: float32 [4096], P('tp'), may hold values from 1000 to 30000
- bias_moment: float32 [4096], P('tp'), may hold values from 100 to 10000
- select_rows: float32 [160], replicated, may hold values from 10 to 10000
- select_cols: float32 [4096], P('tp'), may hold values from 30000 to 30000000
- step_rows: float32 [128], replicated, may hold values from 10 to 10000
- step_cols: float32 [4096], P('tp'), may hold values from 10 to 10000
- step_moment: float32 [4096], P('tp'), may hold values from 10 to 10000
- decay_rows: float32 [16], replicated, may hold values from 10 to 10000
- decay_cols: float32 [4096], P('tp'), may hold values from 10 to 10000
- skip_moment: float32 [4096], P('tp'), may hold values from 100 to 10000
Outputs:
- block_out: float32 [2048, 2048], P(('seq', 'tp'))
- input_grad: float32 [2048, 2048], P(('seq', 'tp'))
- norm_gain_grad: float32 [2048], replicated
- norm_gain_new: float32 [2048], replicated
- norm_gain_copy: bfloat16 [2048], replicated
- norm_moment_new: float32 [2048], replicated
- in_weight_grad: float32 [2048, 2, 4096], P('seq', None, 'tp')
- in_weight_new: float32 [2048, 2, 4096], P('seq', None, 'tp')
- in_weight_copy: bfloat16 [2048, 2, 4096], P('seq', None, 'tp')
- in_rows_new: float32 [2048], P('seq')
- in_cols_new: float32 [2, 4096], P(None, 'tp')
- out_weight_grad: float32 [2048, 4096], P('seq', 'tp')
- out_weight_new: float32 [2048, 4096], P('seq', 'tp')
- out_weight_copy: bfloat16 [2048, 4096], P('seq', 'tp')
- out_rows_new: float32 [2048], P('seq')
- out_cols_new: float32 [4096], P('tp')
- conv_weight_grad: float32 [4, 4096], P(None, 'tp')
- conv_weight_new: float32 [4, 4096], P(None, 'tp')
- conv_weight_copy: bfloat16 [4, 4096], P(None, 'tp')
- conv_rows_new: float32 [4], replicated
- conv_cols_new: float32 [4096], P('tp')
- conv_bias_grad: float32 [4096], P('tp')
- conv_bias_new: float32 [4096], P('tp')
- conv_bias_copy: bfloat16 [4096], P('tp')
- bias_moment_new: float32 [4096], P('tp')
- select_weight_grad: float32 [160, 4096], P(None, 'tp')
- select_weight_new: float32 [160, 4096], P(None, 'tp')
- select_weight_copy: bfloat16 [160, 4096], P(None, 'tp')
- select_rows_new: float32 [160], replicated
- select_cols_new: float32 [4096], P('tp')
- step_weight_grad: float32 [128, 4096], P(None, 'tp')
- step_weight_new: float32 [128, 4096], P(None, 'tp')
- step_weight_copy: bfloat16 [128, 4096], P(None, 'tp')
- step_rows_new: float32 [128], replicated
- step_cols_new: float32 [4096], P('tp')
- step_bias_grad: float32 [4096], P('tp')
- step_bias_new: float32 [4096], P('tp')
- step_bias_copy: bfloat16 [4096], P('tp')
- step_moment_new: float32 [4096], P('tp')
- decay_log_grad: float32 [16, 4096], P(None, 'tp')
- decay_log_new: float32 [16, 4096], P(None, 'tp')
- decay_log_copy: bfloat16 [16, 4096], P(None, 'tp')
- decay_rows_new: float32 [16], replicated
- decay_cols_new: float32 [4096], P('tp')
- skip_gain_grad: float32 [4096], P('tp')
- skip_gain_new: float32 [4096], P('tp')
- skip_gain_copy: bfloat16 [4096], P('tp')
- skip_moment_new: float32 [4096], P('tp')
The draws below stay inside these ranges and needn't reach their ends.
Inputs may be any that keep to these rules, and one draw needn't show every extreme that they name: `segment_ids`: never falling along the stream; each document has 1 to 1024 tokens and one has exactly 1024.
All inputs are finite; a program needn't handle non-finite values.
Results may differ from the reference program's by a relative error of at most 0.0075.
The reference program's roundings to bfloat16 on the way count: a program that leaves them out, or rounds other values in their place, can miss the bound.
Values may be sent and summed in bfloat16 or wider, within the bound.
A program may use at most 112 MiB of HBM per device.

```python
import math
import jax
import jax.numpy as jnp
import numpy as np
from jax import lax

D = 2048
E = 4096
N = 16
R = 128
K = 4
TOKENS = 2048
DOC_MOST = 1024
DOCS = 8


def levels(own_key, dims, split, low, largest):
    factor_of = 1.0
    for dim, blocks in split:
        steps = jax.random.uniform(jax.random.fold_in(jax.random.fold_in(own_key, 6), dim), (blocks,), jnp.float32, low / len(split), largest / len(split))
        factor_of = factor_of * jnp.repeat(jnp.exp(steps), dims[dim] // blocks).reshape((-1,) + (1,) * (len(dims) - 1 - dim))
    return factor_of


def profile(count, total, reach, skew):
    portions = [(1 << 20) // math.isqrt(grade ** skew) + 1 for grade in range(2, count + 1)]
    spare, counts = total - reach - (count - 1), [1] * (count - 1)
    while spare > 0:
        movable = [i for i in range(count - 1) if counts[i] < reach]
        pool, left = sum([portions[i] for i in movable]), spare
        for i in movable:
            extra = min(reach - counts[i], max(1, left * portions[i] // pool), spare)
            counts[i] = counts[i] + extra
            spare = spare - extra
    return np.array([reach] + counts)


def ragged(key, count, total, bound, slope):
    if count == 2:
        one = jax.random.randint(key, (), max(1, total - bound), min(bound, total - 1) + 1)
        return jnp.stack([one, total - one])
    tallies = jnp.asarray(profile(count, total, bound, slope), jnp.int32)
    twos = (count - 1) // 2
    donor, receiver = tallies[1:1 + 2 * twos:2], tallies[2:2 + 2 * twos:2]
    slack = jnp.minimum(donor - 1, bound - receiver)
    shifted = jax.random.randint(jax.random.fold_in(key, 1), (twos,), 0, 1 << 20) % (slack + 1)
    tallies = tallies.at[1:1 + 2 * twos:2].set(donor - shifted).at[2:2 + 2 * twos:2].set(receiver + shifted)
    return tallies[jax.random.permutation(jax.random.fold_in(key, 2), count)]


def noise(stream_key, extent, width, limit, cuts=(), dtype=jnp.bfloat16):
    array = width * jax.random.normal(stream_key, extent, jnp.float32)
    if cuts:
        array = array * levels(stream_key, extent, cuts, -0.22, 0.18)
    return jnp.clip(array, -limit, limit).astype(dtype)


def setup_inputs(seed: int = 0) -> dict:
    splits = jax.random.split(jax.random.key(seed), 30)
    block_in = noise(splits[0], (TOKENS, D), 1.0, 6.0, ((0, 32),))
    cotangent = noise(splits[1], (TOKENS, D), 1.0, 6.0, ((0, 16),))
    segment_ids = jnp.searchsorted(jnp.cumsum(ragged(splits[2], DOCS, TOKENS, DOC_MOST, 2)), jnp.arange(TOKENS), side="right").astype(jnp.int32)
    norm_gain = jnp.clip(1.0 + 0.1 * jax.random.normal(splits[3], (D,), jnp.float32), 0.5, 1.5)
    in_weight = noise(splits[4], (D, 2, E), D ** -0.5, 0.125, ((0, 16), (2, 2)), jnp.float32)
    out_weight = noise(splits[5], (D, E), (E // 4) ** -0.5, 0.1875, ((0, 16), (1, 2)), jnp.float32)
    conv_weight = noise(splits[6], (K, E), K ** -0.5, 3.0, ((1, 2),), jnp.float32)
    conv_bias = jnp.clip(jax.random.uniform(splits[7], (E,), jnp.float32, -0.5, 0.5) * levels(splits[7], (E,), ((0, 2),), -0.4, 0.0), -0.5, 0.5)
    select_weight = noise(splits[8], (R + 2 * N, E), E ** -0.5, 0.09375, ((1, 2),), jnp.float32)
    step_weight = noise(splits[9], (R, E), R ** -0.5, 0.5, ((1, 2),), jnp.float32)
    step_bias = jnp.clip(-6.0 + 4.0 * jax.random.uniform(splits[10], (E,), jnp.float32) ** levels(splits[10], (E,), ((0, 2),), -0.2, 0.2), -6.0, -2.0)
    decay_log = jnp.clip(-5.0 + 7.0 * jax.random.uniform(splits[11], (N, E), jnp.float32) ** levels(splits[11], (N, E), ((1, 2),), -0.2, 0.2), -5.0, 2.0)
    skip_gain = jnp.clip(0.5 + 1.0 * jax.random.uniform(splits[12], (E,), jnp.float32) ** levels(splits[12], (E,), ((0, 2),), -0.2, 0.2), 0.5, 1.5)
    norm_moment = jnp.clip(jnp.exp(jax.random.uniform(splits[13], (D,), jnp.float32, math.log(1000.0), math.log(30000.0))), 1000.0, 30000.0)
    in_rows = jnp.clip(jnp.exp(math.log(30000.0) - 2.3025851 * jax.random.uniform(splits[14], (D,), jnp.float32) ** levels(splits[14], (D,), ((0, 16),), -0.2, 0.2)), 3000.0, 30000.0)
    in_cols = jnp.clip(jnp.exp(math.log(30000.0) - 2.3025851 * jax.random.uniform(splits[15], (2, E), jnp.float32) ** levels(splits[15], (2, E), ((1, 2),), -0.2, 0.2)), 3000.0, 30000.0)
    out_rows = jnp.clip(jnp.exp(math.log(30000.0) - 2.3025851 * jax.random.uniform(splits[16], (D,), jnp.float32) ** levels(splits[16], (D,), ((0, 16),), -0.2, 0.2)), 3000.0, 30000.0)
    out_cols = jnp.clip(jnp.exp(math.log(30000.0) - 2.3025851 * jax.random.uniform(splits[17], (E,), jnp.float32) ** levels(splits[17], (E,), ((0, 2),), -0.2, 0.2)), 3000.0, 30000.0)
    conv_rows = jnp.clip(jnp.exp(jax.random.uniform(splits[18], (K,), jnp.float32, math.log(1000.0), math.log(30000.0))), 1000.0, 30000.0)
    conv_cols = jnp.clip(jnp.exp(math.log(30000.0) - 3.4011974 * jax.random.uniform(splits[19], (E,), jnp.float32) ** levels(splits[19], (E,), ((0, 2),), -0.2, 0.2)), 1000.0, 30000.0)
    bias_moment = jnp.clip(jnp.exp(math.log(10000.0) - 4.6051702 * jax.random.uniform(splits[20], (E,), jnp.float32) ** levels(splits[20], (E,), ((0, 2),), -0.2, 0.2)), 100.0, 10000.0)
    select_rows = jnp.clip(jnp.exp(jax.random.uniform(splits[21], (R + 2 * N,), jnp.float32, math.log(10.0), math.log(10000.0))), 10.0, 10000.0)
    select_cols = jnp.clip(jnp.exp(math.log(30000000) - 6.9077553 * jax.random.uniform(splits[22], (E,), jnp.float32) ** levels(splits[22], (E,), ((0, 2),), -0.2, 0.2)), 30000.0, 30000000)
    step_rows = jnp.clip(jnp.exp(jax.random.uniform(splits[23], (R,), jnp.float32, math.log(10.0), math.log(10000.0))), 10.0, 10000.0)
    step_cols = jnp.clip(jnp.exp(math.log(10000.0) - 6.9077553 * jax.random.uniform(splits[24], (E,), jnp.float32) ** levels(splits[24], (E,), ((0, 2),), -0.2, 0.2)), 10.0, 10000.0)
    step_moment = jnp.clip(jnp.exp(math.log(10000.0) - 6.9077553 * jax.random.uniform(splits[25], (E,), jnp.float32) ** levels(splits[25], (E,), ((0, 2),), -0.2, 0.2)), 10.0, 10000.0)
    decay_rows = jnp.clip(jnp.exp(jax.random.uniform(splits[26], (N,), jnp.float32, math.log(10.0), math.log(10000.0))), 10.0, 10000.0)
    decay_cols = jnp.clip(jnp.exp(math.log(10000.0) - 6.9077553 * jax.random.uniform(splits[27], (E,), jnp.float32) ** levels(splits[27], (E,), ((0, 2),), -0.2, 0.2)), 10.0, 10000.0)
    skip_moment = jnp.clip(jnp.exp(math.log(10000.0) - 4.6051702 * jax.random.uniform(splits[28], (E,), jnp.float32) ** levels(splits[28], (E,), ((0, 2),), -0.2, 0.2)), 100.0, 10000.0)
    return dict(block_in=block_in, cotangent=cotangent, segment_ids=segment_ids, norm_gain=norm_gain, in_weight=in_weight, out_weight=out_weight, conv_weight=conv_weight, conv_bias=conv_bias, select_weight=select_weight, step_weight=step_weight, step_bias=step_bias, decay_log=decay_log, skip_gain=skip_gain, norm_moment=norm_moment, in_rows=in_rows, in_cols=in_cols, out_rows=out_rows, out_cols=out_cols, conv_rows=conv_rows, conv_cols=conv_cols, bias_moment=bias_moment, select_rows=select_rows, select_cols=select_cols, step_rows=step_rows, step_cols=step_cols, step_moment=step_moment, decay_rows=decay_rows, decay_cols=decay_cols, skip_moment=skip_moment)


EPS_NORM = 1e-05
EPS_FACTOR = 1e-30
DECAY = 0.5
CLIP = 0.5
RATES = (0.45, 0.02, 0.03, 0.1, 0.05, 0.016, 0.09, 1.8, 0.3, 0.45)
highest = lax.Precision.HIGHEST

@jax.custom_vjp
def low(v):
    return lax.optimization_barrier(v.astype(jnp.bfloat16)).astype(jnp.float32)

@jax.custom_vjp
def low_back(v):
    return v

def low_keep(v):
    return (low(v), None)

def low_pass(kept, grad):
    return (grad,)

def back_keep(v):
    return (v, None)

def back_low(kept, grad):
    return (low(grad),)
low.defvjp(low_keep, low_pass)
low_back.defvjp(back_keep, back_low)

def forward(block_in, norm_gain, in_weight, out_weight, conv_weight, conv_bias, select_weight, step_weight, step_bias, decay_log, skip_gain, segment_ids):
    in_low = low(in_weight)
    out_low = low(out_weight)
    select_low = low(select_weight)
    step_low = low(step_weight)
    decay_rate = -jnp.exp(decay_log)
    conv_taps = conv_weight.shape[0]
    step_rank = step_weight.shape[0]
    states = decay_log.shape[0]
    channels = conv_weight.shape[1]
    total_rows = block_in.shape[0]
    block_len = min(4096, total_rows)
    part_len = min(256, block_len)
    block_count = total_rows // block_len

    def token_step(state_now, inputs):
        step_t, drive_t, enter_t, leave_t, keep_t = inputs
        state_now = jnp.exp(decay_rate * step_t[None, :]) * keep_t * state_now + drive_t[None, :] * enter_t[:, None]
        return (state_now, lax.optimization_barrier(jnp.sum(leave_t[:, None] * state_now, axis=0)))

    def part_scan(state_now, inputs):
        return lax.scan(token_step, state_now, inputs)

    def block_step(carry_in, inputs):
        state_now, tail_rows, tail_ids = carry_in
        rows_in, block_ids = inputs
        row_count = block_ids.shape[0]
        mean_sq = lax.optimization_barrier(jnp.mean(rows_in * rows_in, axis=1, keepdims=True))
        normed = rows_in * lax.rsqrt(mean_sq + EPS_NORM)
        hidden = low(normed * norm_gain[None, :])
        projected = jnp.einsum('td,dke->tke', hidden, in_low, precision=highest)
        conv_in = low(low_back(projected[:, 0]))
        gate_pre = low_back(projected[:, 1])
        ext_rows = jnp.concatenate([tail_rows, conv_in], axis=0)
        ext_ids = jnp.concatenate([tail_ids, block_ids])
        conv_pre = jnp.zeros_like(gate_pre) + conv_bias[None, :]
        for shift_lag in range(conv_taps):
            first_row = conv_taps - 1 - shift_lag
            same_doc = (ext_ids[first_row:first_row + row_count] == block_ids).astype(jnp.float32)
            conv_pre = conv_pre + conv_weight[shift_lag][None, :] * ext_rows[first_row:first_row + row_count] * same_doc[:, None]
        conv_out = low(jax.nn.silu(conv_pre))
        select_out = low_back(jnp.einsum('te,ke->tk', conv_out, select_low, precision=highest))
        step_in = low(select_out[:, :step_rank])
        state_in = select_out[:, step_rank:step_rank + states]
        state_out = select_out[:, step_rank + states:]
        step_pre = low_back(jnp.dot(step_in, step_low, precision=highest) + step_bias[None, :])
        step_size = jax.nn.softplus(step_pre)
        keep_mask = (block_ids == jnp.concatenate([tail_ids[-1:], block_ids[:-1]])).astype(jnp.float32)
        part_count = row_count // part_len
        state_now, scanned = lax.scan(jax.checkpoint(part_scan), state_now, (step_size.reshape(part_count, part_len, channels), (step_size * conv_out).reshape(part_count, part_len, channels), state_in.reshape(part_count, part_len, states), state_out.reshape(part_count, part_len, states), keep_mask.reshape(part_count, part_len)))
        mixed = scanned.reshape(row_count, channels) + skip_gain[None, :] * conv_out
        gated = low(mixed * jax.nn.silu(gate_pre))
        branch = jnp.einsum('te,de->td', gated, out_low, precision=highest)
        new_carry = (state_now, conv_in[row_count - (conv_taps - 1):], block_ids[row_count - (conv_taps - 1):])
        return (new_carry, rows_in + branch)
    start_carry = (jnp.zeros(decay_log.shape, jnp.float32), jnp.zeros((conv_taps - 1, channels), jnp.float32), jnp.full((conv_taps - 1,), -1, jnp.int32))
    _, outputs = lax.scan(jax.checkpoint(block_step), start_carry, (block_in.reshape(block_count, block_len, -1), segment_ids.reshape(block_count, block_len)))
    return outputs.reshape(block_in.shape)

def factor_step(grad_in, weight, rows_old, cols_old, step_rate):
    square = grad_in * grad_in
    rows_new = DECAY * rows_old + (1.0 - DECAY) * (lax.optimization_barrier(jnp.mean(square, axis=tuple(range(1, grad_in.ndim)))) + EPS_FACTOR)
    cols_new = DECAY * cols_old + (1.0 - DECAY) * (lax.optimization_barrier(jnp.mean(square, axis=0)) + EPS_FACTOR)
    row_shape = (grad_in.shape[0],) + (1,) * (grad_in.ndim - 1)
    scale_sq = rows_new.reshape(row_shape) * cols_new[None] / jnp.mean(rows_new)
    update = grad_in * lax.rsqrt(scale_sq)
    root_mean = jnp.sqrt(jnp.mean(update * update))
    fresh = weight - step_rate * update / jnp.maximum(1.0, root_mean / CLIP)
    return (fresh, rows_new, cols_new)

def vector_step(grad_in, weight, moment_old, step_rate):
    moment_new = DECAY * moment_old + (1.0 - DECAY) * (grad_in * grad_in + EPS_FACTOR)
    update = grad_in * lax.rsqrt(moment_new)
    root_mean = jnp.sqrt(jnp.mean(update * update))
    fresh = weight - step_rate * update / jnp.maximum(1.0, root_mean / CLIP)
    return (fresh, moment_new)

def reference(block_in, cotangent, segment_ids, norm_gain, in_weight, out_weight, conv_weight, conv_bias, select_weight, step_weight, step_bias, decay_log, skip_gain, norm_moment, in_rows, in_cols, out_rows, out_cols, conv_rows, conv_cols, bias_moment, select_rows, select_cols, step_rows, step_cols, step_moment, decay_rows, decay_cols, skip_moment):
    weights = (norm_gain, in_weight, out_weight, conv_weight, conv_bias, select_weight, step_weight, step_bias, decay_log, skip_gain)

    def run_block(residual, *params):
        return forward(residual, *params, segment_ids)
    block_out, pullback = jax.vjp(run_block, block_in.astype(jnp.float32), *weights)
    grads = pullback(cotangent.astype(jnp.float32))
    input_grad = grads[0]
    gain_grad, in_grad, out_grad, convw_grad, convb_grad, select_grad, stepw_grad, stepb_grad, decay_grad, skip_grad = grads[1:]
    gain_new, gain_moment = vector_step(gain_grad, norm_gain, norm_moment, RATES[0])
    in_new, in_rows_new, in_cols_new = factor_step(in_grad, in_weight, in_rows, in_cols, RATES[1])
    out_new, out_rows_new, out_cols_new = factor_step(out_grad, out_weight, out_rows, out_cols, RATES[2])
    convw_new, conv_rows_new, conv_cols_new = factor_step(convw_grad, conv_weight, conv_rows, conv_cols, RATES[3])
    convb_new, bias_moment_new = vector_step(convb_grad, conv_bias, bias_moment, RATES[4])
    select_new, select_rows_new, select_cols_new = factor_step(select_grad, select_weight, select_rows, select_cols, RATES[5])
    stepw_new, step_rows_new, step_cols_new = factor_step(stepw_grad, step_weight, step_rows, step_cols, RATES[6])
    stepb_new, step_moment_new = vector_step(stepb_grad, step_bias, step_moment, RATES[7])
    decay_new, decay_rows_new, decay_cols_new = factor_step(decay_grad, decay_log, decay_rows, decay_cols, RATES[8])
    skip_new, skip_moment_new = vector_step(skip_grad, skip_gain, skip_moment, RATES[9])
    bf = jnp.bfloat16
    return (block_out, input_grad, gain_grad, gain_new, gain_new.astype(bf), gain_moment, in_grad, in_new, in_new.astype(bf), in_rows_new, in_cols_new, out_grad, out_new, out_new.astype(bf), out_rows_new, out_cols_new, convw_grad, convw_new, convw_new.astype(bf), conv_rows_new, conv_cols_new, convb_grad, convb_new, convb_new.astype(bf), bias_moment_new, select_grad, select_new, select_new.astype(bf), select_rows_new, select_cols_new, stepw_grad, stepw_new, stepw_new.astype(bf), step_rows_new, step_cols_new, stepb_grad, stepb_new, stepb_new.astype(bf), step_moment_new, decay_grad, decay_new, decay_new.astype(bf), decay_rows_new, decay_cols_new, skip_grad, skip_new, skip_new.astype(bf), skip_moment_new)
```

```python
import functools

import jax
import jax.numpy as jnp
from jax import lax
from jax.experimental import pallas as pl
from jax.experimental.pallas import tpu as pltpu
from jax.sharding import PartitionSpec as P

EPS_NORM = 1e-05
EPS_FACTOR = 1e-30
DECAY = 0.5
CLIP = 0.5
RATES = (0.45, 0.02, 0.03, 0.1, 0.05, 0.016, 0.09, 1.8, 0.3, 0.45)
LOG2E = 1.4426950408889634
RESET = 1e9
TILE = 512
VMEM_LIMIT = 48 * 1024 * 1024


def passed_along(value, axis, steps):
    count = lax.axis_size(axis)
    initial, last = (max(0, -steps), min(count, count - steps))
    return lax.ppermute(value, axis, [(source, source + steps) for source in range(initial, last)])


def silu_slope(values):
    sigmoid_v = jax.nn.sigmoid(values)
    return sigmoid_v * (1.0 + values * (1.0 - sigmoid_v))


def widen_last(piece_in, index_of, total_len):
    zero_block = jnp.zeros(piece_in.shape[:-1] + (total_len,), jnp.float32)
    return lax.dynamic_update_slice_in_dim(
        zero_block, piece_in, index_of * piece_in.shape[-1], piece_in.ndim - 1
    )


def narrow(full_array, index_of, size_of):
    return lax.dynamic_slice_in_dim(full_array, index_of * size_of, size_of, full_array.ndim - 1)


def factor_update(full_grad, local_grad, rows_old, cols_old):
    rows_new = DECAY * rows_old + (1.0 - DECAY) * (
        jnp.mean(full_grad * full_grad, axis=1) + EPS_FACTOR
    )
    cols_new = DECAY * cols_old + (1.0 - DECAY) * (
        jnp.mean(local_grad * local_grad, axis=0) + EPS_FACTOR
    )
    scale_sq = rows_new[:, None] * cols_new[None, :] / jnp.mean(rows_new)
    return (rows_new, cols_new, local_grad * lax.rsqrt(scale_sq))


def moment_update(grad_in, moment_old):
    moment_new = DECAY * moment_old + (1.0 - DECAY) * (grad_in * grad_in + EPS_FACTOR)
    return (moment_new, grad_in * lax.rsqrt(moment_new))


def sum_squares(update):
    return jnp.sum(update * update)


def apply_step(weight, update, total_sum, count_all, step_rate):
    root_mean = jnp.sqrt(total_sum / count_all)
    return weight - step_rate * update / jnp.maximum(1.0, root_mean / CLIP)


def wide(tile, width):
    return jnp.concatenate([tile] * (width // tile.shape[1]), axis=1)


def fold_lanes(value):
    pieces = [value[:, at : at + 128] for at in range(0, value.shape[1], 128)]
    while len(pieces) > 1:
        pieces = [first + second for first, second in zip(pieces[::2], pieces[1::2])]
    return pieces[0]


def state_kernel(backward, step_ref, value_ref, lane_ref, rate_ref, out_ref):
    rows, width = step_ref.shape
    states = rate_ref.shape[0]
    rate = rate_ref[...] * LOG2E

    def block(index, state):
        base = pl.multiple_of((rows // 8 - 1 - index if backward else index) * 8, 8)
        for offset in range(8):
            at = base + (7 - offset if backward else offset)
            keep = jnp.exp2(rate * step_ref[pl.ds(at, 1), :])
            term = wide(lane_ref[at], width) * value_ref[pl.ds(at, 1), :]
            state = keep * (state + term) if backward else keep * state + term
        return state

    out_ref[0:states, :] = lax.fori_loop(0, rows // 8, block, jnp.zeros((states, width), jnp.float32))
    total = jnp.sum(step_ref[...], axis=0, keepdims=True)
    out_ref[states:, :] = jnp.broadcast_to(total, (out_ref.shape[0] - states, width))


def piece_state(step, value, lane, rate, backward):
    rows, width = step.shape
    states = rate.shape[0]
    tile = TILE
    return pl.pallas_call(
        functools.partial(state_kernel, backward),
        grid=(width // tile,),
        in_specs=[
            pl.BlockSpec((rows, tile), lambda i: (0, i)),
            pl.BlockSpec((rows, tile), lambda i: (0, i)),
            pl.BlockSpec((rows, states, 128), lambda i: (0, 0, 0)),
            pl.BlockSpec((states, tile), lambda i: (0, i)),
        ],
        out_specs=pl.BlockSpec((states + 8, tile), lambda i: (0, i)),
        out_shape=jax.ShapeDtypeStruct((states + 8, width), jnp.float32),
        compiler_params=pltpu.CompilerParams(vmem_limit_bytes=VMEM_LIMIT),
    )(step, value, lane, rate)


def entering(pieces_ref, rate, first, count, stride):
    states = rate.shape[0]

    def join(index, state):
        at = first + index * stride
        piece = pieces_ref[at]
        return jnp.exp2(rate * piece[states : states + 1]) * state + piece[:states]

    return lax.fori_loop(0, count, join, jnp.zeros(rate.shape, jnp.float32))


def forward_kernel(
    place_ref, step_ref, drive_ref, enter_ref, leave_ref, rate_ref, pieces_ref, out_ref, start_ref
):
    rows, width = step_ref.shape
    rate = rate_ref[...] * LOG2E
    start = entering(pieces_ref, rate, 0, place_ref[0], 1)
    start_ref[...] = start

    def block(index, state):
        base = pl.multiple_of(index * 8, 8)
        for offset in range(8):
            at = base + offset
            keep = jnp.exp2(rate * step_ref[pl.ds(at, 1), :])
            state = keep * state + wide(enter_ref[at], width) * drive_ref[pl.ds(at, 1), :]
            out_ref[pl.ds(at, 1), :] = jnp.sum(
                wide(leave_ref[at], width) * state, axis=0, keepdims=True
            )
        return state

    lax.fori_loop(0, rows // 8, block, start)


def scan_forward(place, step, drive, enter, leave, rate, pieces):
    rows, width = step.shape
    states = rate.shape[0]
    tile = TILE
    return pl.pallas_call(
        forward_kernel,
        grid=(width // tile,),
        in_specs=[
            pl.BlockSpec(memory_space=pltpu.SMEM),
            pl.BlockSpec((rows, tile), lambda i: (0, i)),
            pl.BlockSpec((rows, tile), lambda i: (0, i)),
            pl.BlockSpec((rows, states, 128), lambda i: (0, 0, 0)),
            pl.BlockSpec((rows, states, 128), lambda i: (0, 0, 0)),
            pl.BlockSpec((states, tile), lambda i: (0, i)),
            pl.BlockSpec((pieces.shape[0], states + 8, tile), lambda i: (0, 0, i)),
        ],
        out_specs=[
            pl.BlockSpec((rows, tile), lambda i: (0, i)),
            pl.BlockSpec((states, tile), lambda i: (0, i)),
        ],
        out_shape=[
            jax.ShapeDtypeStruct((rows, width), jnp.float32),
            jax.ShapeDtypeStruct((states, width), jnp.float32),
        ],
        compiler_params=pltpu.CompilerParams(vmem_limit_bytes=VMEM_LIMIT),
    )(place, step, drive, enter, leave, rate, pieces)


def backward_kernel(
    place_ref,
    step_ref,
    drive_ref,
    grad_ref,
    enter_ref,
    leave_ref,
    rate_ref,
    start_ref,
    pieces_ref,
    drive_grad_ref,
    step_grad_ref,
    decay_ref,
    enter_grad_ref,
    leave_grad_ref,
    kept_ref,
    state_ref,
):
    rows, width = step_ref.shape
    rate_own = rate_ref[...]
    rate = rate_own * LOG2E
    count = pieces_ref.shape[0]

    @pl.when(pl.program_id(0) == 0)
    def _():
        enter_grad_ref[...] = jnp.zeros_like(enter_grad_ref)
        leave_grad_ref[...] = jnp.zeros_like(leave_grad_ref)

    def again(index, state):
        base = pl.multiple_of(index * 8, 8)
        for offset in range(8):
            at = base + offset
            keep = jnp.exp2(rate * step_ref[pl.ds(at, 1), :])
            kept_ref[at] = keep
            state = keep * state + wide(enter_ref[at], width) * drive_ref[pl.ds(at, 1), :]
            state_ref[at + 1] = state
        return state

    start = start_ref[...]
    state_ref[0] = start
    lax.fori_loop(0, rows // 8, again, start)
    follow = entering(pieces_ref, rate, count - 1, count - 1 - place_ref[0], -1)

    def block(index, carry):
        follow, decay = carry
        base = pl.multiple_of((rows // 8 - 1 - index) * 8, 8)
        for offset in range(7, -1, -1):
            at = base + offset
            grad = grad_ref[pl.ds(at, 1), :]
            adjoint = wide(leave_ref[at], width) * grad + follow
            drive_grad_ref[pl.ds(at, 1), :] = jnp.sum(
                adjoint * wide(enter_ref[at], width), axis=0, keepdims=True
            )
            enter_grad_ref[at] += fold_lanes(adjoint * drive_ref[pl.ds(at, 1), :])
            leave_grad_ref[at] += fold_lanes(state_ref[at + 1] * grad)
            follow = kept_ref[at] * adjoint
            part = follow * state_ref[at]
            step_grad_ref[pl.ds(at, 1), :] = jnp.sum(part * rate_own, axis=0, keepdims=True)
            decay = decay + part * step_ref[pl.ds(at, 1), :]
        return follow, decay

    _, decay = lax.fori_loop(0, rows // 8, block, (follow, jnp.zeros_like(follow)))
    decay_ref[...] = decay * rate_own


def scan_backward(place, step, drive, grad, enter, leave, rate, start, pieces):
    rows, width = step.shape
    states = rate.shape[0]
    tile = TILE
    by_tile = pl.BlockSpec((rows, tile), lambda i: (0, i))
    by_state = pl.BlockSpec((states, tile), lambda i: (0, i))
    whole = pl.BlockSpec((rows, states, 128), lambda i: (0, 0, 0))
    return pl.pallas_call(
        backward_kernel,
        grid=(width // tile,),
        in_specs=[
            pl.BlockSpec(memory_space=pltpu.SMEM),
            by_tile,
            by_tile,
            by_tile,
            whole,
            whole,
            by_state,
            by_state,
            pl.BlockSpec((pieces.shape[0], states + 8, tile), lambda i: (0, 0, i)),
        ],
        out_specs=[by_tile, by_tile, by_state, whole, whole],
        out_shape=[
            jax.ShapeDtypeStruct((rows, width), jnp.float32),
            jax.ShapeDtypeStruct((rows, width), jnp.float32),
            jax.ShapeDtypeStruct((states, width), jnp.float32),
            jax.ShapeDtypeStruct((rows, states, 128), jnp.float32),
            jax.ShapeDtypeStruct((rows, states, 128), jnp.float32),
        ],
        scratch_shapes=[
            pltpu.VMEM((rows, states, tile), jnp.float32),
            pltpu.VMEM((rows + 1, states, tile), jnp.float32),
        ],
        compiler_params=pltpu.CompilerParams(vmem_limit_bytes=VMEM_LIMIT),
    )(place, step, drive, grad, enter, leave, rate, start, pieces)


def on_device(
    block_in,
    cotangent,
    segment_ids,
    norm_gain,
    in_weight,
    out_weight,
    conv_weight,
    conv_bias,
    select_weight,
    step_weight,
    step_bias,
    decay_log,
    skip_gain,
    norm_moment,
    in_rows,
    in_cols,
    out_rows,
    out_cols,
    conv_rows,
    conv_cols,
    bias_moment,
    select_rows,
    select_cols,
    step_rows,
    step_cols,
    step_moment,
    decay_rows,
    decay_cols,
    skip_moment,
):
    tp_count = lax.axis_size("tp")
    seq_index = lax.axis_index("seq")
    tp_index = lax.axis_index("tp")
    seq_first = (seq_index == 0).astype(jnp.float32)
    tp_first = (tp_index == 0).astype(jnp.float32)
    half_rows, model_dim = block_in.shape
    row_count = cotangent.shape[0]
    inner_dim = in_weight.shape[2]
    channels = inner_dim * tp_count
    conv_taps = conv_weight.shape[0]
    states = decay_log.shape[0]
    step_rank = step_weight.shape[0]
    row_share = in_weight.shape[0]
    id_padded = jnp.concatenate(
        [
            jnp.full((conv_taps - 1,), -1, jnp.int32),
            segment_ids,
            jnp.full((conv_taps - 1,), -2, jnp.int32),
        ]
    )
    window = lax.dynamic_slice_in_dim(
        id_padded, seq_index * row_count, row_count + 2 * (conv_taps - 1)
    )
    local_ids = window[conv_taps - 1 : conv_taps - 1 + row_count]
    keep_mask = (local_ids == window[conv_taps - 2 : conv_taps - 2 + row_count]).astype(jnp.float32)
    residual = block_in.astype(jnp.float32)
    mean_sq = jnp.mean(residual * residual, axis=1, keepdims=True)
    inv_rms = lax.rsqrt(mean_sq + EPS_NORM)
    normed = residual * inv_rms
    hidden = lax.all_gather(
        (normed * norm_gain[None, :]).astype(jnp.bfloat16), "tp", axis=0, tiled=True
    )
    in_full, out_full = (
        lax.all_gather(in_weight.astype(jnp.bfloat16), "seq", axis=0, tiled=True),
        lax.all_gather(out_weight.astype(jnp.bfloat16), "seq", axis=0, tiled=True),
    )
    projected = jnp.einsum("td,dke->tke", hidden, in_full, preferred_element_type=jnp.float32)
    conv_in = projected[:, 0].astype(jnp.bfloat16)
    gate_pre = projected[:, 1]
    rim_rows = passed_along(conv_in[row_count - (conv_taps - 1) :], "seq", 1)
    ext_rows = jnp.concatenate([rim_rows, conv_in], axis=0).astype(jnp.float32)
    same_docs = []
    conv_pre = jnp.zeros_like(gate_pre) + conv_bias[None, :]
    for shift_lag in range(conv_taps):
        first_row = conv_taps - 1 - shift_lag
        same_doc = (window[first_row : first_row + row_count] == local_ids).astype(jnp.float32)[
            :, None
        ]
        same_docs.append(same_doc)
        conv_pre = (
            conv_pre
            + conv_weight[shift_lag][None, :]
            * ext_rows[first_row : first_row + row_count]
            * same_doc
        )
    conv_out = jax.nn.silu(conv_pre).astype(jnp.bfloat16)
    conv_value = conv_out.astype(jnp.float32)
    select_low = select_weight.astype(jnp.bfloat16)
    select_out = lax.psum(
        jnp.einsum("te,ke->tk", conv_out, select_low, preferred_element_type=jnp.float32), "tp"
    )
    step_in = select_out[:, :step_rank].astype(jnp.bfloat16)
    state_in = select_out[:, step_rank : step_rank + states]
    state_out = select_out[:, step_rank + states :]
    step_low = step_weight.astype(jnp.bfloat16)
    step_pre = jnp.dot(step_in, step_low, preferred_element_type=jnp.float32) + step_bias[None, :]
    step_size = jax.nn.softplus(step_pre)
    decay_rate = -jnp.exp(decay_log)
    drive = step_size * conv_value
    place = seq_index[None]
    held_step = jnp.where(keep_mask[:, None] > 0.0, step_size, RESET)
    enter = jnp.broadcast_to(state_in[:, :, None], (row_count, states, 128))
    leave = jnp.broadcast_to(state_out[:, :, None], (row_count, states, 128))
    state_pieces = lax.all_gather(
        piece_state(held_step, drive, enter, decay_rate, False), "seq"
    )
    scanned, start = scan_forward(
        place, held_step, drive, enter, leave, decay_rate, state_pieces
    )
    mixed = scanned + skip_gain[None, :] * conv_value
    gate_act = jax.nn.silu(gate_pre)
    gated = (mixed * gate_act).astype(jnp.bfloat16)
    branch = jnp.einsum("te,de->td", gated, out_full, preferred_element_type=jnp.float32)
    block_out = residual + lax.psum_scatter(
        branch.astype(jnp.bfloat16), "tp", scatter_dimension=0, tiled=True
    ).astype(jnp.float32)
    in_back, out_back = (
        lax.all_gather(in_weight.astype(jnp.bfloat16), "seq", axis=0, tiled=True),
        lax.all_gather(out_weight.astype(jnp.bfloat16), "seq", axis=0, tiled=True),
    )
    d_gated = jnp.einsum("td,de->te", cotangent, out_back, preferred_element_type=jnp.float32)
    d_out_w = jnp.einsum("td,te->de", cotangent, gated, preferred_element_type=jnp.float32)
    d_mixed = d_gated * gate_act
    d_gate = (d_gated * mixed * silu_slope(gate_pre)).astype(jnp.bfloat16)
    skip_grad = jnp.sum(d_mixed * conv_value, axis=0)
    adjoint_pieces = lax.all_gather(
        piece_state(held_step, d_mixed, leave, decay_rate, True), "seq"
    )
    drive_grad, step_grad, decay_grad, enter_grad, leave_grad = scan_backward(
        place, held_step, drive, d_mixed, enter, leave, decay_rate, start, adjoint_pieces
    )
    enter_grad = jnp.sum(enter_grad, axis=2)
    leave_grad = jnp.sum(leave_grad, axis=2)
    d_step = drive_grad * conv_value + step_grad
    d_step_pre = (d_step * jax.nn.sigmoid(step_pre)).astype(jnp.bfloat16)
    step_bias_grad = jnp.sum(d_step_pre.astype(jnp.float32), axis=0)
    step_w_grad = jnp.einsum("tr,te->re", step_in, d_step_pre, preferred_element_type=jnp.float32)
    d_step_in = jnp.einsum("te,re->tr", d_step_pre, step_low, preferred_element_type=jnp.float32)
    select_grads = jnp.concatenate(
        [d_step_in, enter_grad, leave_grad],
        axis=1,
    )
    d_select = lax.psum(select_grads, "tp").astype(jnp.bfloat16)
    select_w_grad = jnp.einsum("tk,te->ke", d_select, conv_out, preferred_element_type=jnp.float32)
    d_conv = (
        drive_grad * step_size
        + d_mixed * skip_gain[None, :]
        + jnp.einsum("tk,ke->te", d_select, select_low, preferred_element_type=jnp.float32)
    )
    d_conv_pre = d_conv * silu_slope(conv_pre)
    rim_next = passed_along(d_conv_pre[: conv_taps - 1], "seq", -1)
    ext_grads = jnp.concatenate([d_conv_pre, rim_next], axis=0)
    ids_after = window[conv_taps - 1 :]
    d_conv_in = jnp.zeros_like(d_conv_pre)
    conv_w_rows = []
    for shift_lag in range(conv_taps):
        first_row = conv_taps - 1 - shift_lag
        later_same = (ids_after[shift_lag : shift_lag + row_count] == local_ids).astype(
            jnp.float32
        )[:, None]
        d_conv_in = (
            d_conv_in
            + conv_weight[shift_lag][None, :]
            * ext_grads[shift_lag : shift_lag + row_count]
            * later_same
        )
        conv_w_rows.append(
            jnp.sum(
                d_conv_pre * ext_rows[first_row : first_row + row_count] * same_docs[shift_lag],
                axis=0,
            )
        )
    conv_w_grad = jnp.stack(conv_w_rows, axis=0)
    conv_b_grad = jnp.sum(d_conv_pre, axis=0)
    d_projected = jnp.stack([d_conv_in.astype(jnp.bfloat16), d_gate], axis=1)
    d_hidden = lax.psum_scatter(
        jnp.einsum("tke,dke->td", d_projected, in_back, preferred_element_type=jnp.float32),
        "tp",
        scatter_dimension=0,
        tiled=True,
    )
    d_in_w = jnp.einsum("td,tke->dke", hidden, d_projected, preferred_element_type=jnp.float32)
    in_grad, out_grad = (
        lax.psum_scatter(d_in_w, "seq", scatter_dimension=0, tiled=True),
        lax.psum_scatter(d_out_w, "seq", scatter_dimension=0, tiled=True),
    )
    gain_part = jnp.sum(d_hidden * normed, axis=0)
    scaled = d_hidden * norm_gain[None, :]
    cot_half = lax.dynamic_slice_in_dim(cotangent, tp_index * half_rows, half_rows, 0).astype(
        jnp.float32
    )
    input_grad = cot_half + inv_rms * (
        scaled - normed * jnp.mean(scaled * normed, axis=1, keepdims=True)
    )
    in_square = in_grad * in_grad
    in_row_piece = (DECAY * in_rows + (1.0 - DECAY) * EPS_FACTOR) * tp_first + (
        1.0 - DECAY
    ) * jnp.sum(in_square, axis=(1, 2)) / (2 * channels)
    in_col_piece = (DECAY * in_cols + (1.0 - DECAY) * EPS_FACTOR) * seq_first + (
        1.0 - DECAY
    ) * jnp.sum(in_square, axis=0) / model_dim
    out_square = out_grad * out_grad
    out_row_piece = (DECAY * out_rows + (1.0 - DECAY) * EPS_FACTOR) * tp_first + (
        1.0 - DECAY
    ) * jnp.sum(out_square, axis=1) / channels
    out_col_piece = (DECAY * out_cols + (1.0 - DECAY) * EPS_FACTOR) * seq_first + (
        1.0 - DECAY
    ) * jnp.sum(out_square, axis=0) / model_dim
    vector_grads = jnp.stack([conv_b_grad, step_bias_grad, skip_grad], axis=0)
    (
        conv_full,
        vector_full,
        select_full,
        step_full,
        decay_full,
        gain_grad,
        in_rows_all,
        in_cols_all,
        out_rows_all,
        out_cols_all,
    ) = lax.psum(
        (
            widen_last(conv_w_grad, tp_index, channels),
            widen_last(vector_grads, tp_index, channels),
            widen_last(select_w_grad, tp_index, channels),
            widen_last(step_w_grad, tp_index, channels),
            widen_last(decay_grad, tp_index, channels),
            gain_part,
            widen_last(in_row_piece, seq_index, model_dim),
            widen_last(in_col_piece, tp_index, channels),
            widen_last(out_row_piece, seq_index, model_dim),
            widen_last(out_col_piece, tp_index, channels),
        ),
        ("seq", "tp"),
    )
    conv_local = narrow(conv_full, tp_index, inner_dim)
    vector_local = narrow(vector_full, tp_index, inner_dim)
    select_local = narrow(select_full, tp_index, inner_dim)
    step_local = narrow(step_full, tp_index, inner_dim)
    decay_local = narrow(decay_full, tp_index, inner_dim)
    conv_rows_new, conv_cols_new, conv_update = factor_update(
        conv_full, conv_local, conv_rows, conv_cols
    )
    select_rows_new, select_cols_new, select_update = factor_update(
        select_full, select_local, select_rows, select_cols
    )
    step_rows_new, step_cols_new, stepw_update = factor_update(
        step_full, step_local, step_rows, step_cols
    )
    decay_rows_new, decay_cols_new, decay_update = factor_update(
        decay_full, decay_local, decay_rows, decay_cols
    )
    bias_moment_new, convb_update = moment_update(vector_local[0], bias_moment)
    step_moment_new, stepb_update = moment_update(vector_local[1], step_moment)
    skip_moment_new, skip_update = moment_update(vector_local[2], skip_moment)
    gain_moment_new, gain_update = moment_update(gain_grad, norm_moment)
    in_rows_new = narrow(in_rows_all, seq_index, row_share)
    in_cols_new = narrow(in_cols_all, tp_index, inner_dim)
    in_update = in_grad * lax.rsqrt(
        in_rows_new[:, None, None] * in_cols_new[None] / jnp.mean(in_rows_all)
    )
    out_rows_new = narrow(out_rows_all, seq_index, row_share)
    out_cols_new = narrow(out_cols_all, tp_index, inner_dim)
    out_update = out_grad * lax.rsqrt(
        out_rows_new[:, None] * out_cols_new[None, :] / jnp.mean(out_rows_all)
    )
    clip_totals = lax.psum(
        jnp.stack(
            [
                sum_squares(in_update),
                sum_squares(out_update),
                seq_first * sum_squares(conv_update),
                seq_first * sum_squares(select_update),
                seq_first * sum_squares(stepw_update),
                seq_first * sum_squares(decay_update),
                seq_first * sum_squares(convb_update),
                seq_first * sum_squares(stepb_update),
                seq_first * sum_squares(skip_update),
            ]
        ),
        ("seq", "tp"),
    )
    gain_new = apply_step(norm_gain, gain_update, sum_squares(gain_update), model_dim, RATES[0])
    in_new = apply_step(in_weight, in_update, clip_totals[0], model_dim * 2 * channels, RATES[1])
    out_new = apply_step(out_weight, out_update, clip_totals[1], model_dim * channels, RATES[2])
    convw_new = apply_step(conv_weight, conv_update, clip_totals[2], conv_taps * channels, RATES[3])
    convb_new = apply_step(conv_bias, convb_update, clip_totals[6], channels, RATES[4])
    select_new = apply_step(
        select_weight, select_update, clip_totals[3], select_weight.shape[0] * channels, RATES[5]
    )
    stepw_new = apply_step(
        step_weight, stepw_update, clip_totals[4], step_rank * channels, RATES[6]
    )
    stepb_new = apply_step(step_bias, stepb_update, clip_totals[7], channels, RATES[7])
    decay_new = apply_step(decay_log, decay_update, clip_totals[5], states * channels, RATES[8])
    skip_new = apply_step(skip_gain, skip_update, clip_totals[8], channels, RATES[9])
    low_type = jnp.bfloat16
    return (
        block_out,
        input_grad,
        gain_grad,
        gain_new,
        gain_new.astype(low_type),
        gain_moment_new,
        in_grad,
        in_new,
        in_new.astype(low_type),
        in_rows_new,
        in_cols_new,
        out_grad,
        out_new,
        out_new.astype(low_type),
        out_rows_new,
        out_cols_new,
        conv_local,
        convw_new,
        convw_new.astype(low_type),
        conv_rows_new,
        conv_cols_new,
        vector_local[0],
        convb_new,
        convb_new.astype(low_type),
        bias_moment_new,
        select_local,
        select_new,
        select_new.astype(low_type),
        select_rows_new,
        select_cols_new,
        step_local,
        stepw_new,
        stepw_new.astype(low_type),
        step_rows_new,
        step_cols_new,
        vector_local[1],
        stepb_new,
        stepb_new.astype(low_type),
        step_moment_new,
        decay_local,
        decay_new,
        decay_new.astype(low_type),
        decay_rows_new,
        decay_cols_new,
        vector_local[2],
        skip_new,
        skip_new.astype(low_type),
        skip_moment_new,
    )


def solution(mesh):
    return jax.shard_map(
        on_device,
        mesh=mesh,
        in_specs=(
            P(("seq", "tp"), None),
            P("seq", None),
            P(),
            P(),
            P("seq", None, "tp"),
            P("seq", "tp"),
            P(None, "tp"),
            P("tp"),
            P(None, "tp"),
            P(None, "tp"),
            P("tp"),
            P(None, "tp"),
            P("tp"),
            P(),
            P("seq"),
            P(None, "tp"),
            P("seq"),
            P("tp"),
            P(),
            P("tp"),
            P("tp"),
            P(),
            P("tp"),
            P(),
            P("tp"),
            P("tp"),
            P(),
            P("tp"),
            P("tp"),
        ),
        out_specs=(
            P(("seq", "tp"), None),
            P(("seq", "tp"), None),
            P(),
            P(),
            P(),
            P(),
            P("seq", None, "tp"),
            P("seq", None, "tp"),
            P("seq", None, "tp"),
            P("seq"),
            P(None, "tp"),
            P("seq", "tp"),
            P("seq", "tp"),
            P("seq", "tp"),
            P("seq"),
            P("tp"),
            P(None, "tp"),
            P(None, "tp"),
            P(None, "tp"),
            P(),
            P("tp"),
            P("tp"),
            P("tp"),
            P("tp"),
            P("tp"),
            P(None, "tp"),
            P(None, "tp"),
            P(None, "tp"),
            P(),
            P("tp"),
            P(None, "tp"),
            P(None, "tp"),
            P(None, "tp"),
            P(),
            P("tp"),
            P("tp"),
            P("tp"),
            P("tp"),
            P("tp"),
            P(None, "tp"),
            P(None, "tp"),
            P(None, "tp"),
            P(),
            P("tp"),
            P("tp"),
            P("tp"),
            P("tp"),
            P("tp"),
        ),
        check_vma=False,
    )
```

```python
import functools

import jax
import jax.numpy as jnp
from jax import lax
from jax.experimental import pallas as pl
from jax.experimental.pallas import tpu as pltpu
from jax.sharding import PartitionSpec as P

EPS_NORM = 1e-05
EPS_FACTOR = 1e-30
DECAY = 0.5
CLIP = 0.5
RATES = (0.45, 0.02, 0.03, 0.1, 0.05, 0.016, 0.09, 1.8, 0.3, 0.45)
MESH = pl.DeviceIdType.MESH
LOG2E = 1.4426950408889634
RESET = 1e9
TILE = 512
VMEM_LIMIT = 48 * 1024 * 1024


def passed_along(value, axis, steps):
    count = lax.axis_size(axis)
    initial, last = (max(0, -steps), min(count, count - steps))
    return lax.ppermute(value, axis, [(source, source + steps) for source in range(initial, last)])


def silu_slope(values):
    sigmoid_v = jax.nn.sigmoid(values)
    return sigmoid_v * (1.0 + values * (1.0 - sigmoid_v))


def factor_update(grad, row_sums, rows_old, cols_old, channels):
    rows_new = DECAY * rows_old + (1.0 - DECAY) * (row_sums / channels + EPS_FACTOR)
    cols_new = DECAY * cols_old + (1.0 - DECAY) * (jnp.mean(grad * grad, axis=0) + EPS_FACTOR)
    scale_sq = rows_new[:, None] * cols_new[None, :] / jnp.mean(rows_new)
    return (rows_new, cols_new, grad * lax.rsqrt(scale_sq))


def moment_update(grad_in, moment_old):
    moment_new = DECAY * moment_old + (1.0 - DECAY) * (grad_in * grad_in + EPS_FACTOR)
    return (moment_new, grad_in * lax.rsqrt(moment_new))


def sum_squares(update):
    return jnp.sum(update * update)


def apply_step(weight, update, total_sum, count_all, step_rate):
    root_mean = jnp.sqrt(total_sum / count_all)
    return weight - step_rate * update / jnp.maximum(1.0, root_mean / CLIP)


def wide(tile, width):
    return jnp.concatenate([tile] * (width // tile.shape[1]), axis=1)


def fold_lanes(value):
    pieces = [value[:, at : at + 128] for at in range(0, value.shape[1], 128)]
    while len(pieces) > 1:
        pieces = [first + second for first, second in zip(pieces[::2], pieces[1::2])]
    return pieces[0]


def state_kernel(backward, step_ref, value_ref, lane_ref, rate_ref, out_ref):
    rows, width = step_ref.shape
    states = rate_ref.shape[0]
    rate = rate_ref[...] * LOG2E

    def block(index, state):
        base = pl.multiple_of((rows // 8 - 1 - index if backward else index) * 8, 8)
        for offset in range(8):
            at = base + (7 - offset if backward else offset)
            keep = jnp.exp2(rate * step_ref[pl.ds(at, 1), :])
            term = wide(lane_ref[at], width) * value_ref[pl.ds(at, 1), :]
            state = keep * (state + term) if backward else keep * state + term
        return state

    out_ref[0:states, :] = lax.fori_loop(0, rows // 8, block, jnp.zeros((states, width), jnp.float32))
    total = jnp.sum(step_ref[...], axis=0, keepdims=True)
    out_ref[states:, :] = jnp.broadcast_to(total, (out_ref.shape[0] - states, width))


def piece_state(step, value, lane, rate, backward):
    rows, width = step.shape
    states = rate.shape[0]
    tile = TILE
    return pl.pallas_call(
        functools.partial(state_kernel, backward),
        grid=(width // tile,),
        in_specs=[
            pl.BlockSpec((rows, tile), lambda i: (0, i)),
            pl.BlockSpec((rows, tile), lambda i: (0, i)),
            pl.BlockSpec((rows, states, 128), lambda i: (0, 0, 0)),
            pl.BlockSpec((states, tile), lambda i: (0, i)),
        ],
        out_specs=pl.BlockSpec((states + 8, tile), lambda i: (0, i)),
        out_shape=jax.ShapeDtypeStruct((states + 8, width), jnp.float32),
        compiler_params=pltpu.CompilerParams(vmem_limit_bytes=VMEM_LIMIT),
    )(step, value, lane, rate)


def entering(pieces_ref, rate, first, count, stride):
    states = rate.shape[0]

    def join(index, state):
        at = first + index * stride
        piece = pieces_ref[at]
        return jnp.exp2(rate * piece[states : states + 1]) * state + piece[:states]

    return lax.fori_loop(0, count, join, jnp.zeros(rate.shape, jnp.float32))


def forward_kernel(
    place_ref, step_ref, drive_ref, enter_ref, leave_ref, rate_ref, pieces_ref, out_ref, start_ref
):
    rows, width = step_ref.shape
    rate = rate_ref[...] * LOG2E
    start = entering(pieces_ref, rate, 0, place_ref[0], 1)
    start_ref[...] = start

    def block(index, state):
        base = pl.multiple_of(index * 8, 8)
        for offset in range(8):
            at = base + offset
            keep = jnp.exp2(rate * step_ref[pl.ds(at, 1), :])
            state = keep * state + wide(enter_ref[at], width) * drive_ref[pl.ds(at, 1), :]
            out_ref[pl.ds(at, 1), :] = jnp.sum(
                wide(leave_ref[at], width) * state, axis=0, keepdims=True
            )
        return state

    lax.fori_loop(0, rows // 8, block, start)


def scan_forward(place, step, drive, enter, leave, rate, pieces):
    rows, width = step.shape
    states = rate.shape[0]
    tile = TILE
    return pl.pallas_call(
        forward_kernel,
        grid=(width // tile,),
        in_specs=[
            pl.BlockSpec(memory_space=pltpu.SMEM),
            pl.BlockSpec((rows, tile), lambda i: (0, i)),
            pl.BlockSpec((rows, tile), lambda i: (0, i)),
            pl.BlockSpec((rows, states, 128), lambda i: (0, 0, 0)),
            pl.BlockSpec((rows, states, 128), lambda i: (0, 0, 0)),
            pl.BlockSpec((states, tile), lambda i: (0, i)),
            pl.BlockSpec((pieces.shape[0], states + 8, tile), lambda i: (0, 0, i)),
        ],
        out_specs=[
            pl.BlockSpec((rows, tile), lambda i: (0, i)),
            pl.BlockSpec((states, tile), lambda i: (0, i)),
        ],
        out_shape=[
            jax.ShapeDtypeStruct((rows, width), jnp.float32),
            jax.ShapeDtypeStruct((states, width), jnp.float32),
        ],
        compiler_params=pltpu.CompilerParams(vmem_limit_bytes=VMEM_LIMIT),
    )(place, step, drive, enter, leave, rate, pieces)


def backward_kernel(
    place_ref,
    step_ref,
    drive_ref,
    grad_ref,
    enter_ref,
    leave_ref,
    rate_ref,
    start_ref,
    pieces_ref,
    drive_grad_ref,
    step_grad_ref,
    decay_ref,
    enter_grad_ref,
    leave_grad_ref,
    kept_ref,
    state_ref,
):
    rows, width = step_ref.shape
    rate_own = rate_ref[...]
    rate = rate_own * LOG2E
    count = pieces_ref.shape[0]

    @pl.when(pl.program_id(0) == 0)
    def _():
        enter_grad_ref[...] = jnp.zeros_like(enter_grad_ref)
        leave_grad_ref[...] = jnp.zeros_like(leave_grad_ref)

    def again(index, state):
        base = pl.multiple_of(index * 8, 8)
        for offset in range(8):
            at = base + offset
            keep = jnp.exp2(rate * step_ref[pl.ds(at, 1), :])
            kept_ref[at] = keep
            state = keep * state + wide(enter_ref[at], width) * drive_ref[pl.ds(at, 1), :]
            state_ref[at + 1] = state
        return state

    start = start_ref[...]
    state_ref[0] = start
    lax.fori_loop(0, rows // 8, again, start)
    follow = entering(pieces_ref, rate, count - 1, count - 1 - place_ref[0], -1)

    def block(index, carry):
        follow, decay = carry
        base = pl.multiple_of((rows // 8 - 1 - index) * 8, 8)
        for offset in range(7, -1, -1):
            at = base + offset
            grad = grad_ref[pl.ds(at, 1), :]
            adjoint = wide(leave_ref[at], width) * grad + follow
            drive_grad_ref[pl.ds(at, 1), :] = jnp.sum(
                adjoint * wide(enter_ref[at], width), axis=0, keepdims=True
            )
            enter_grad_ref[at] += fold_lanes(adjoint * drive_ref[pl.ds(at, 1), :])
            leave_grad_ref[at] += fold_lanes(state_ref[at + 1] * grad)
            follow = kept_ref[at] * adjoint
            part = follow * state_ref[at]
            step_grad_ref[pl.ds(at, 1), :] = jnp.sum(part * rate_own, axis=0, keepdims=True)
            decay = decay + part * step_ref[pl.ds(at, 1), :]
        return follow, decay

    _, decay = lax.fori_loop(0, rows // 8, block, (follow, jnp.zeros_like(follow)))
    decay_ref[...] = decay * rate_own


def scan_backward(place, step, drive, grad, enter, leave, rate, start, pieces):
    rows, width = step.shape
    states = rate.shape[0]
    tile = TILE
    by_tile = pl.BlockSpec((rows, tile), lambda i: (0, i))
    by_state = pl.BlockSpec((states, tile), lambda i: (0, i))
    whole = pl.BlockSpec((rows, states, 128), lambda i: (0, 0, 0))
    return pl.pallas_call(
        backward_kernel,
        grid=(width // tile,),
        in_specs=[
            pl.BlockSpec(memory_space=pltpu.SMEM),
            by_tile,
            by_tile,
            by_tile,
            whole,
            whole,
            by_state,
            by_state,
            pl.BlockSpec((pieces.shape[0], states + 8, tile), lambda i: (0, 0, i)),
        ],
        out_specs=[by_tile, by_tile, by_state, whole, whole],
        out_shape=[
            jax.ShapeDtypeStruct((rows, width), jnp.float32),
            jax.ShapeDtypeStruct((rows, width), jnp.float32),
            jax.ShapeDtypeStruct((states, width), jnp.float32),
            jax.ShapeDtypeStruct((rows, states, 128), jnp.float32),
            jax.ShapeDtypeStruct((rows, states, 128), jnp.float32),
        ],
        scratch_shapes=[
            pltpu.VMEM((rows, states, tile), jnp.float32),
            pltpu.VMEM((rows + 1, states, tile), jnp.float32),
        ],
        compiler_params=pltpu.CompilerParams(vmem_limit_bytes=VMEM_LIMIT),
    )(place, step, drive, grad, enter, leave, rate, start, pieces)


def on_block():
    return lax.axis_size("seq") == 16 and lax.axis_size("tp") == 2


def position():
    place = lax.axis_index("seq")
    return lax.div(place, 4), lax.rem(lax.div(place, 2), 2), lax.rem(place, 2)


def device(z, x, core):
    return (z * 4 + x * 2 + core, lax.axis_index("tp"))


def other_half():
    return (lax.axis_index("seq"), 1 - lax.axis_index("tp"))


def greet(peers):
    barrier = pltpu.get_barrier_semaphore()
    for peer in peers:
        pl.semaphore_signal(barrier, inc=1, device_id=peer, device_id_type=MESH)
    pl.semaphore_wait(barrier, len(peers))


def remote(source, target, sent, arrived, peer):
    return pltpu.make_async_remote_copy(
        src_ref=source,
        dst_ref=target,
        send_sem=sent,
        recv_sem=arrived,
        device_id=peer,
        device_id_type=MESH,
    )


def sum_kernel(
    shared, mine_ref, pair_ref, out_ref, pair_out_ref, work, far, pair_far, sent, arrived
):
    z, x, core = position()
    seq_rows = mine_ref.shape[0]
    across = [device(lax.rem(z + step, 4), x, core) for step in (1, 2, 3)]
    peers = [device(z, x, 1 - core), device(z, 1 - x, core)] + across + [other_half()]
    greet(peers)
    pair = remote(pair_ref, pair_far, sent.at[0], arrived.at[0], peers[5])
    pair.start()
    first = remote(mine_ref, far.at[0], sent.at[1], arrived.at[1], peers[0])
    first.start()
    first.wait()
    work[4] = mine_ref[...] + far[0]
    second = remote(work.at[4], far.at[1], sent.at[2], arrived.at[2], peers[1])
    second.start()
    second.wait()
    work[z] = work[4] + far[1]
    copies = [
        remote(work.at[z], work.at[z], sent.at[3 + at], arrived.at[3 + at], across[at])
        for at in range(3)
    ]
    for copy in copies:
        copy.start()
    for copy in copies:
        copy.wait()
    out_ref[...] = (work[0] + work[1]) + (work[2] + work[3])
    last = remote(
        out_ref.at[seq_rows - shared :],
        far.at[2, seq_rows - shared :],
        sent.at[6],
        arrived.at[6],
        peers[5],
    )
    last.start()
    pair.wait()
    pair_out_ref[...] = pair_ref[...] + pair_far[...]
    last.wait()
    out_ref[seq_rows - shared :] = (
        out_ref[seq_rows - shared :] + far[2, seq_rows - shared :]
    )


def sum_over(seq_part, shared_part, tp_part, ident):
    mine = jnp.concatenate([seq_part, shared_part], axis=0)
    seq_rows, shared = mine.shape[0], shared_part.shape[0]
    if not on_block():
        total = lax.psum(mine, "seq")
        both = lax.psum(total[seq_rows - shared :], "tp")
        return total[: seq_rows - shared], both, lax.psum(tp_part, "tp")
    vmem = pl.BlockSpec(memory_space=pltpu.VMEM)
    total, pair = pl.pallas_call(
        functools.partial(sum_kernel, shared),
        in_specs=[vmem, vmem],
        out_specs=[vmem, vmem],
        out_shape=[
            jax.ShapeDtypeStruct(mine.shape, jnp.float32),
            jax.ShapeDtypeStruct(tp_part.shape, jnp.float32),
        ],
        scratch_shapes=[
            pltpu.VMEM((5,) + mine.shape, jnp.float32),
            pltpu.VMEM((3,) + mine.shape, jnp.float32),
            pltpu.VMEM(tp_part.shape, jnp.float32),
            pltpu.SemaphoreType.DMA((7,)),
            pltpu.SemaphoreType.DMA((7,)),
        ],
        compiler_params=pltpu.CompilerParams(collective_id=ident, has_side_effects=True),
    )(mine, tp_part)
    return total[: seq_rows - shared], total[seq_rows - shared :], pair


def reduce_kernel(
    hidden_ref,
    grads_ref,
    extra_ref,
    out_ref,
    full_ref,
    send_core,
    come_core,
    send_x,
    come_x,
    send_z,
    come_z,
    extra_come_core,
    extra_send_x,
    extra_come_x,
    extra_send_z,
    extra_come_z,
    sent_core,
    got_core,
    sent_x,
    got_x,
    sent_z,
    got_z,
    extra_sent,
    extra_got,
):
    z, x, core = position()
    chunks, width = send_core.shape[0], send_core.shape[3]
    away = [lax.rem(z + step, 4) for step in (1, 2, 3)]
    core_peer, x_peer = device(z, x, 1 - core), device(z, 1 - x, core)
    z_peers = [device(at, x, core) for at in away]
    greet([core_peer, x_peer] + z_peers)

    def product(chunk, block):
        return jnp.dot(
            hidden_ref[block],
            grads_ref[:, chunk * width : (chunk + 1) * width],
            preferred_element_type=jnp.float32,
        )

    def to_core(chunk):
        return remote(
            send_core.at[chunk], come_core.at[chunk], sent_core.at[chunk], got_core.at[chunk], core_peer
        )

    def to_x(chunk):
        return remote(send_x.at[chunk], come_x.at[chunk], sent_x.at[chunk], got_x.at[chunk], x_peer)

    def to_z(chunk, at):
        return remote(
            send_z.at[chunk, at],
            come_z.at[chunk, at],
            sent_z.at[chunk, at],
            got_z.at[chunk, at],
            z_peers[at],
        )

    def stage_core(chunk):
        def one(pair, _):
            send_core[chunk, pair] = product(chunk, pair * 2 + 1 - core).astype(jnp.bfloat16)
            return 0

        lax.fori_loop(0, 8, one, 0)
        to_core(chunk).start()

    def after_core(chunk, pair):
        return product(chunk, pair * 2 + core) + come_core[chunk, pair].astype(jnp.float32)

    def stage_x(chunk):
        to_core(chunk).wait_recv()

        def one(level, _):
            send_x[chunk, level] = after_core(chunk, level * 2 + 1 - x).astype(jnp.bfloat16)
            return 0

        lax.fori_loop(0, 4, one, 0)
        to_x(chunk).start()

    def stage_z(chunk):
        to_x(chunk).wait_recv()

        def after_x(level):
            return after_core(chunk, level * 2 + x) + come_x[chunk, level].astype(jnp.float32)

        def one(at, _):
            send_z[chunk, at] = after_x(lax.rem(z + 1 + at, 4)).astype(jnp.bfloat16)
            return 0

        lax.fori_loop(0, 3, one, 0)
        for at in range(3):
            to_z(chunk, at).start()
        out_ref[:, chunk * width : (chunk + 1) * width] = after_x(z)

    def stage_last(chunk):
        for at in range(3):
            to_z(chunk, at).wait_recv()
        total = come_z[chunk, 0].astype(jnp.float32) + come_z[chunk, 1].astype(jnp.float32)
        total = total + come_z[chunk, 2].astype(jnp.float32)
        columns = slice(chunk * width, (chunk + 1) * width)
        out_ref[:, columns] = out_ref[:, columns] + total

    extra_core = remote(
        extra_ref.at[:, 1 - core], extra_come_core, extra_sent.at[0], extra_got.at[0], core_peer
    )
    extra_x = remote(extra_send_x, extra_come_x, extra_sent.at[1], extra_got.at[1], x_peer)
    extra_z = [
        remote(
            extra_send_z.at[at], extra_come_z.at[at], extra_sent.at[2 + at], extra_got.at[2 + at], z_peers[at]
        )
        for at in range(3)
    ]
    own = full_ref.at[z, x, core]
    back_z = [
        remote(own, own, extra_sent.at[5 + at], extra_got.at[5 + at], z_peers[at]) for at in range(3)
    ]
    held = full_ref.at[:, x, core]
    back_x = remote(held, held, extra_sent.at[8], extra_got.at[8], x_peer)
    halves = full_ref.at[:, :, core]
    back_core = remote(halves, halves, extra_sent.at[9], extra_got.at[9], core_peer)

    def extra_after_core(pair):
        return extra_ref[pair, core].astype(jnp.float32) + extra_come_core[pair].astype(jnp.float32)

    def extra_stage_x():
        extra_core.wait_recv()

        def one(level, _):
            extra_send_x[level] = extra_after_core(level * 2 + 1 - x).astype(jnp.bfloat16)
            return 0

        lax.fori_loop(0, 4, one, 0)
        extra_x.start()

    def extra_after_x(level):
        return extra_after_core(level * 2 + x) + extra_come_x[level].astype(jnp.float32)

    def extra_stage_z():
        extra_x.wait_recv()

        def one(at, _):
            extra_send_z[at] = extra_after_x(lax.rem(z + 1 + at, 4)).astype(jnp.bfloat16)
            return 0

        lax.fori_loop(0, 3, one, 0)
        for copy in extra_z:
            copy.start()

    def extra_stage_last():
        for copy in extra_z:
            copy.wait_recv()
        total = extra_after_x(z)
        for at in range(3):
            total = total + extra_come_z[at].astype(jnp.float32)
        full_ref[z, x, core] = total.astype(full_ref.dtype)
        for copy in back_z:
            copy.start()

    def extra_back_x():
        for copy in back_z:
            copy.wait_recv()
        back_x.start()

    def extra_back_core():
        back_x.wait_recv()
        back_core.start()

    extra_core.start()
    extra_steps = {1: extra_stage_x, 3: extra_stage_z, 5: extra_stage_last, 7: extra_back_x, 9: extra_back_core}
    for step in range(max(chunks + 5, 10)):
        if step < chunks:
            stage_core(step)
        if 0 <= step - 1 < chunks:
            stage_x(step - 1)
        if 0 <= step - 3 < chunks:
            stage_z(step - 3)
        if 0 <= step - 5 < chunks:
            stage_last(step - 5)
        if step in extra_steps:
            extra_steps[step]()
    back_core.wait_recv()
    for chunk in range(chunks):
        to_core(chunk).wait_send()
        to_x(chunk).wait_send()
        for at in range(3):
            to_z(chunk, at).wait_send()
    for copy in [extra_core, extra_x] + extra_z + back_z + [back_x, back_core]:
        copy.wait_send()


def reduce_grads(hidden, grads, extra, ident):
    rows, model = hidden.shape
    columns = grads.shape[1]
    extra_columns = extra.shape[1]
    if not on_block():
        product = jnp.einsum("td,tn->dn", hidden, grads, preferred_element_type=jnp.float32)
        return (
            lax.psum_scatter(product, "seq", scatter_dimension=0, tiled=True),
            lax.psum(extra, "seq"),
        )
    share, extra_share = model // 16, extra.shape[0] // 16
    width = 512
    chunks = columns // width
    low = jnp.bfloat16
    vmem = pl.BlockSpec(memory_space=pltpu.VMEM)
    dma = pltpu.SemaphoreType.DMA
    out, full = pl.pallas_call(
        reduce_kernel,
        in_specs=[vmem, vmem, vmem],
        out_specs=[vmem, vmem],
        out_shape=[
            jax.ShapeDtypeStruct((share, columns), jnp.float32),
            jax.ShapeDtypeStruct((4, 2, 2, extra_share, extra_columns), low),
        ],
        scratch_shapes=[
            pltpu.VMEM((chunks, 8, share, width), low),
            pltpu.VMEM((chunks, 8, share, width), low),
            pltpu.VMEM((chunks, 4, share, width), low),
            pltpu.VMEM((chunks, 4, share, width), low),
            pltpu.VMEM((chunks, 3, share, width), low),
            pltpu.VMEM((chunks, 3, share, width), low),
            pltpu.VMEM((8, extra_share, extra_columns), low),
            pltpu.VMEM((4, extra_share, extra_columns), low),
            pltpu.VMEM((4, extra_share, extra_columns), low),
            pltpu.VMEM((3, extra_share, extra_columns), low),
            pltpu.VMEM((3, extra_share, extra_columns), low),
            dma((chunks,)),
            dma((chunks,)),
            dma((chunks,)),
            dma((chunks,)),
            dma((chunks, 3)),
            dma((chunks, 3)),
            dma((10,)),
            dma((10,)),
        ],
        compiler_params=pltpu.CompilerParams(
            collective_id=ident, has_side_effects=True, vmem_limit_bytes=VMEM_LIMIT
        ),
    )(
        hidden.T.reshape(16, share, rows),
        grads,
        extra.astype(low).reshape(8, 2, extra_share, extra_columns),
    )
    return out, full.reshape(extra.shape).astype(jnp.float32)


def on_device(
    block_in,
    cotangent,
    segment_ids,
    norm_gain,
    in_weight,
    out_weight,
    conv_weight,
    conv_bias,
    select_weight,
    step_weight,
    step_bias,
    decay_log,
    skip_gain,
    norm_moment,
    in_rows,
    in_cols,
    out_rows,
    out_cols,
    conv_rows,
    conv_cols,
    bias_moment,
    select_rows,
    select_cols,
    step_rows,
    step_cols,
    step_moment,
    decay_rows,
    decay_cols,
    skip_moment,
):
    tp_count = lax.axis_size("tp")
    seq_index = lax.axis_index("seq")
    tp_index = lax.axis_index("tp")
    seq_first = (seq_index == 0).astype(jnp.float32)
    tp_first = (tp_index == 0).astype(jnp.float32)
    half_rows, model_dim = block_in.shape
    row_count = cotangent.shape[0]
    inner_dim = in_weight.shape[2]
    channels = inner_dim * tp_count
    conv_taps = conv_weight.shape[0]
    states = decay_log.shape[0]
    step_rank = step_weight.shape[0]
    row_share = in_weight.shape[0]
    id_padded = jnp.concatenate(
        [
            jnp.full((conv_taps - 1,), -1, jnp.int32),
            segment_ids,
            jnp.full((conv_taps - 1,), -2, jnp.int32),
        ]
    )
    window = lax.dynamic_slice_in_dim(
        id_padded, seq_index * row_count, row_count + 2 * (conv_taps - 1)
    )
    local_ids = window[conv_taps - 1 : conv_taps - 1 + row_count]
    keep_mask = (local_ids == window[conv_taps - 2 : conv_taps - 2 + row_count]).astype(jnp.float32)
    residual = block_in.astype(jnp.float32)
    mean_sq = jnp.mean(residual * residual, axis=1, keepdims=True)
    inv_rms = lax.rsqrt(mean_sq + EPS_NORM)
    normed = residual * inv_rms
    hidden = lax.all_gather(
        (normed * norm_gain[None, :]).astype(jnp.bfloat16), "tp", axis=0, tiled=True
    )
    in_full, out_full = (
        lax.all_gather(in_weight.astype(jnp.bfloat16), "seq", axis=0, tiled=True),
        lax.all_gather(out_weight.astype(jnp.bfloat16), "seq", axis=0, tiled=True),
    )
    projected = jnp.einsum("td,dke->tke", hidden, in_full, preferred_element_type=jnp.float32)
    conv_in = projected[:, 0].astype(jnp.bfloat16)
    gate_pre = projected[:, 1]
    rim_rows = passed_along(conv_in[row_count - (conv_taps - 1) :], "seq", 1)
    ext_rows = jnp.concatenate([rim_rows, conv_in], axis=0).astype(jnp.float32)
    same_docs = []
    conv_pre = jnp.zeros_like(gate_pre) + conv_bias[None, :]
    for shift_lag in range(conv_taps):
        first_row = conv_taps - 1 - shift_lag
        same_doc = (window[first_row : first_row + row_count] == local_ids).astype(jnp.float32)[
            :, None
        ]
        same_docs.append(same_doc)
        conv_pre = (
            conv_pre
            + conv_weight[shift_lag][None, :]
            * ext_rows[first_row : first_row + row_count]
            * same_doc
        )
    conv_out = jax.nn.silu(conv_pre).astype(jnp.bfloat16)
    conv_value = conv_out.astype(jnp.float32)
    select_low = select_weight.astype(jnp.bfloat16)
    select_out = lax.psum(
        jnp.einsum("te,ke->tk", conv_out, select_low, preferred_element_type=jnp.float32), "tp"
    )
    step_in = select_out[:, :step_rank].astype(jnp.bfloat16)
    state_in = select_out[:, step_rank : step_rank + states]
    state_out = select_out[:, step_rank + states :]
    step_low = step_weight.astype(jnp.bfloat16)
    step_pre = jnp.dot(step_in, step_low, preferred_element_type=jnp.float32) + step_bias[None, :]
    step_size = jax.nn.softplus(step_pre)
    decay_rate = -jnp.exp(decay_log)
    drive = step_size * conv_value
    place = seq_index[None]
    held_step = jnp.where(keep_mask[:, None] > 0.0, step_size, RESET)
    enter = jnp.broadcast_to(state_in[:, :, None], (row_count, states, 128))
    leave = jnp.broadcast_to(state_out[:, :, None], (row_count, states, 128))
    state_pieces = lax.all_gather(
        piece_state(held_step, drive, enter, decay_rate, False), "seq"
    )
    scanned, start = scan_forward(
        place, held_step, drive, enter, leave, decay_rate, state_pieces
    )
    mixed = scanned + skip_gain[None, :] * conv_value
    gate_act = jax.nn.silu(gate_pre)
    gated = (mixed * gate_act).astype(jnp.bfloat16)
    branch = jnp.einsum("te,de->td", gated, out_full, preferred_element_type=jnp.float32)
    block_out = residual + lax.psum_scatter(
        branch.astype(jnp.bfloat16), "tp", scatter_dimension=0, tiled=True
    ).astype(jnp.float32)
    in_back, out_back = (
        lax.all_gather(in_weight.astype(jnp.bfloat16), "seq", axis=0, tiled=True),
        lax.all_gather(out_weight.astype(jnp.bfloat16), "seq", axis=0, tiled=True),
    )
    d_gated = jnp.einsum("td,de->te", cotangent, out_back, preferred_element_type=jnp.float32)
    d_out_w = jnp.einsum("td,te->de", cotangent, gated, preferred_element_type=jnp.float32)
    d_mixed = d_gated * gate_act
    d_gate = (d_gated * mixed * silu_slope(gate_pre)).astype(jnp.bfloat16)
    skip_grad = jnp.sum(d_mixed * conv_value, axis=0)
    adjoint_pieces = lax.all_gather(
        piece_state(held_step, d_mixed, leave, decay_rate, True), "seq"
    )
    drive_grad, step_grad, decay_grad, enter_grad, leave_grad = scan_backward(
        place, held_step, drive, d_mixed, enter, leave, decay_rate, start, adjoint_pieces
    )
    enter_grad = jnp.sum(enter_grad, axis=2)
    leave_grad = jnp.sum(leave_grad, axis=2)
    d_step = drive_grad * conv_value + step_grad
    d_step_pre = (d_step * jax.nn.sigmoid(step_pre)).astype(jnp.bfloat16)
    step_bias_grad = jnp.sum(d_step_pre.astype(jnp.float32), axis=0)
    step_w_grad = jnp.einsum("tr,te->re", step_in, d_step_pre, preferred_element_type=jnp.float32)
    d_step_in = jnp.einsum("te,re->tr", d_step_pre, step_low, preferred_element_type=jnp.float32)
    select_grads = jnp.concatenate(
        [d_step_in, enter_grad, leave_grad],
        axis=1,
    )
    d_select = lax.psum(select_grads, "tp").astype(jnp.bfloat16)
    select_w_grad = jnp.einsum("tk,te->ke", d_select, conv_out, preferred_element_type=jnp.float32)
    d_conv = (
        drive_grad * step_size
        + d_mixed * skip_gain[None, :]
        + jnp.einsum("tk,ke->te", d_select, select_low, preferred_element_type=jnp.float32)
    )
    d_conv_pre = d_conv * silu_slope(conv_pre)
    rim_next = passed_along(d_conv_pre[: conv_taps - 1], "seq", -1)
    ext_grads = jnp.concatenate([d_conv_pre, rim_next], axis=0)
    ids_after = window[conv_taps - 1 :]
    d_conv_in = jnp.zeros_like(d_conv_pre)
    conv_w_rows = []
    for shift_lag in range(conv_taps):
        first_row = conv_taps - 1 - shift_lag
        later_same = (ids_after[shift_lag : shift_lag + row_count] == local_ids).astype(
            jnp.float32
        )[:, None]
        d_conv_in = (
            d_conv_in
            + conv_weight[shift_lag][None, :]
            * ext_grads[shift_lag : shift_lag + row_count]
            * later_same
        )
        conv_w_rows.append(
            jnp.sum(
                d_conv_pre * ext_rows[first_row : first_row + row_count] * same_docs[shift_lag],
                axis=0,
            )
        )
    conv_w_grad = jnp.stack(conv_w_rows, axis=0)
    conv_b_grad = jnp.sum(d_conv_pre, axis=0)
    d_projected = jnp.concatenate([d_conv_in.astype(jnp.bfloat16), d_gate], axis=1)
    d_hidden = lax.psum_scatter(
        jnp.einsum(
            "tn,dn->td",
            d_projected,
            in_back.reshape(model_dim, 2 * inner_dim),
            preferred_element_type=jnp.float32,
        ),
        "tp",
        scatter_dimension=0,
        tiled=True,
    )
    vector_grads = jnp.stack([conv_b_grad, step_bias_grad, skip_grad], axis=0)
    small_grads = jnp.concatenate(
        [step_w_grad, select_w_grad, decay_grad, conv_w_grad, vector_grads], axis=0
    )
    small_count = small_grads.shape[0]
    small_grads = jnp.pad(small_grads, ((0, -small_count % 128), (0, 0)))
    in_grad, small_full = reduce_grads(hidden, d_projected, small_grads.T, 0)
    in_grad = in_grad.reshape(in_weight.shape)
    small_full = small_full.T
    out_grad = lax.psum_scatter(
        d_out_w.astype(jnp.bfloat16), "seq", scatter_dimension=0, tiled=True
    ).astype(jnp.float32)
    gain_part = jnp.sum(d_hidden * normed, axis=0)
    scaled = d_hidden * norm_gain[None, :]
    cot_half = lax.dynamic_slice_in_dim(cotangent, tp_index * half_rows, half_rows, 0).astype(
        jnp.float32
    )
    input_grad = cot_half + inv_rms * (
        scaled - normed * jnp.mean(scaled * normed, axis=1, keepdims=True)
    )
    edges = [step_rank, select_weight.shape[0], states, conv_taps, 3]
    edges = [sum(edges[:at]) for at in range(len(edges) + 1)]
    step_local, select_local, decay_local, conv_local, vector_local = [
        small_full[low:high] for low, high in zip(edges, edges[1:])
    ]
    in_square = in_grad * in_grad
    out_square = out_grad * out_grad
    in_row_part = jnp.sum(in_square, axis=(1, 2))
    out_row_part = jnp.sum(out_square, axis=1)
    small_row_part = jnp.sum(small_full * small_full, axis=1)
    in_total = jnp.sum(DECAY * in_rows + (1.0 - DECAY) * EPS_FACTOR) * tp_first + (
        1.0 - DECAY
    ) * jnp.sum(in_row_part) / (2 * channels)
    out_total = jnp.sum(DECAY * out_rows + (1.0 - DECAY) * EPS_FACTOR) * tp_first + (
        1.0 - DECAY
    ) * jnp.sum(out_row_part) / channels
    seq_part = jnp.concatenate(
        [jnp.sum(in_square, axis=0).reshape(-1, 128), jnp.sum(out_square, axis=0).reshape(-1, 128)]
    )
    shared_part = jnp.concatenate(
        [
            gain_part.reshape(-1, 128),
            jnp.broadcast_to(in_total, (8, 128)),
            jnp.broadcast_to(out_total, (8, 128)),
        ]
    )
    row_parts = jnp.concatenate([in_row_part, out_row_part, small_row_part])
    row_parts = jnp.pad(row_parts, (0, -row_parts.shape[0] % 1024)).reshape(-1, 128)
    col_sums, shared_sums, row_sums = sum_over(seq_part, shared_part, row_parts, 1)
    col_sums = col_sums.reshape(-1)
    in_col_sums = col_sums[: 2 * inner_dim].reshape(2, inner_dim)
    out_col_sums = col_sums[2 * inner_dim :]
    gain_grad = shared_sums[: model_dim // 128].reshape(-1)
    in_mean = shared_sums[model_dim // 128, 0] / model_dim
    out_mean = shared_sums[model_dim // 128 + 8, 0] / model_dim
    row_sums = row_sums.reshape(-1)
    in_row_sums = row_sums[:row_share]
    out_row_sums = row_sums[row_share : 2 * row_share]
    small_row_sums = row_sums[2 * row_share :]
    in_rows_new = DECAY * in_rows + (1.0 - DECAY) * (in_row_sums / (2 * channels) + EPS_FACTOR)
    in_cols_new = DECAY * in_cols + (1.0 - DECAY) * (in_col_sums / model_dim + EPS_FACTOR)
    out_rows_new = DECAY * out_rows + (1.0 - DECAY) * (out_row_sums / channels + EPS_FACTOR)
    out_cols_new = DECAY * out_cols + (1.0 - DECAY) * (out_col_sums / model_dim + EPS_FACTOR)
    step_rows_new, step_cols_new, stepw_update = factor_update(
        step_local, small_row_sums[edges[0] : edges[1]], step_rows, step_cols, channels
    )
    select_rows_new, select_cols_new, select_update = factor_update(
        select_local, small_row_sums[edges[1] : edges[2]], select_rows, select_cols, channels
    )
    decay_rows_new, decay_cols_new, decay_update = factor_update(
        decay_local, small_row_sums[edges[2] : edges[3]], decay_rows, decay_cols, channels
    )
    conv_rows_new, conv_cols_new, conv_update = factor_update(
        conv_local, small_row_sums[edges[3] : edges[4]], conv_rows, conv_cols, channels
    )
    bias_moment_new, convb_update = moment_update(vector_local[0], bias_moment)
    step_moment_new, stepb_update = moment_update(vector_local[1], step_moment)
    skip_moment_new, skip_update = moment_update(vector_local[2], skip_moment)
    gain_moment_new, gain_update = moment_update(gain_grad, norm_moment)
    in_update = in_grad * lax.rsqrt(in_rows_new[:, None, None] * in_cols_new[None] / in_mean)
    out_update = out_grad * lax.rsqrt(out_rows_new[:, None] * out_cols_new[None, :] / out_mean)
    squares = jnp.stack(
        [
            sum_squares(in_update),
            sum_squares(out_update),
            seq_first * sum_squares(conv_update),
            seq_first * sum_squares(select_update),
            seq_first * sum_squares(stepw_update),
            seq_first * sum_squares(decay_update),
            seq_first * sum_squares(convb_update),
            seq_first * sum_squares(stepb_update),
            seq_first * sum_squares(skip_update),
        ]
    )
    nothing = jnp.zeros((8, 128), jnp.float32)
    _, clip_totals, _ = sum_over(
        nothing, jnp.broadcast_to(jnp.pad(squares, (0, 7))[:, None], (16, 128)), nothing, 2
    )
    clip_totals = clip_totals[:, 0]
    gain_new = apply_step(norm_gain, gain_update, sum_squares(gain_update), model_dim, RATES[0])
    in_new = apply_step(in_weight, in_update, clip_totals[0], model_dim * 2 * channels, RATES[1])
    out_new = apply_step(out_weight, out_update, clip_totals[1], model_dim * channels, RATES[2])
    convw_new = apply_step(conv_weight, conv_update, clip_totals[2], conv_taps * channels, RATES[3])
    convb_new = apply_step(conv_bias, convb_update, clip_totals[6], channels, RATES[4])
    select_new = apply_step(
        select_weight, select_update, clip_totals[3], select_weight.shape[0] * channels, RATES[5]
    )
    stepw_new = apply_step(
        step_weight, stepw_update, clip_totals[4], step_rank * channels, RATES[6]
    )
    stepb_new = apply_step(step_bias, stepb_update, clip_totals[7], channels, RATES[7])
    decay_new = apply_step(decay_log, decay_update, clip_totals[5], states * channels, RATES[8])
    skip_new = apply_step(skip_gain, skip_update, clip_totals[8], channels, RATES[9])
    low_type = jnp.bfloat16
    return (
        block_out,
        input_grad,
        gain_grad,
        gain_new,
        gain_new.astype(low_type),
        gain_moment_new,
        in_grad,
        in_new,
        in_new.astype(low_type),
        in_rows_new,
        in_cols_new,
        out_grad,
        out_new,
        out_new.astype(low_type),
        out_rows_new,
        out_cols_new,
        conv_local,
        convw_new,
        convw_new.astype(low_type),
        conv_rows_new,
        conv_cols_new,
        vector_local[0],
        convb_new,
        convb_new.astype(low_type),
        bias_moment_new,
        select_local,
        select_new,
        select_new.astype(low_type),
        select_rows_new,
        select_cols_new,
        step_local,
        stepw_new,
        stepw_new.astype(low_type),
        step_rows_new,
        step_cols_new,
        vector_local[1],
        stepb_new,
        stepb_new.astype(low_type),
        step_moment_new,
        decay_local,
        decay_new,
        decay_new.astype(low_type),
        decay_rows_new,
        decay_cols_new,
        vector_local[2],
        skip_new,
        skip_new.astype(low_type),
        skip_moment_new,
    )


def solution(mesh):
    return jax.shard_map(
        on_device,
        mesh=mesh,
        in_specs=(
            P(("seq", "tp"), None),
            P("seq", None),
            P(),
            P(),
            P("seq", None, "tp"),
            P("seq", "tp"),
            P(None, "tp"),
            P("tp"),
            P(None, "tp"),
            P(None, "tp"),
            P("tp"),
            P(None, "tp"),
            P("tp"),
            P(),
            P("seq"),
            P(None, "tp"),
            P("seq"),
            P("tp"),
            P(),
            P("tp"),
            P("tp"),
            P(),
            P("tp"),
            P(),
            P("tp"),
            P("tp"),
            P(),
            P("tp"),
            P("tp"),
        ),
        out_specs=(
            P(("seq", "tp"), None),
            P(("seq", "tp"), None),
            P(),
            P(),
            P(),
            P(),
            P("seq", None, "tp"),
            P("seq", None, "tp"),
            P("seq", None, "tp"),
            P("seq"),
            P(None, "tp"),
            P("seq", "tp"),
            P("seq", "tp"),
            P("seq", "tp"),
            P("seq"),
            P("tp"),
            P(None, "tp"),
            P(None, "tp"),
            P(None, "tp"),
            P(),
            P("tp"),
            P("tp"),
            P("tp"),
            P("tp"),
            P("tp"),
            P(None, "tp"),
            P(None, "tp"),
            P(None, "tp"),
            P(),
            P("tp"),
            P(None, "tp"),
            P(None, "tp"),
            P(None, "tp"),
            P(),
            P("tp"),
            P("tp"),
            P("tp"),
            P("tp"),
            P("tp"),
            P(None, "tp"),
            P(None, "tp"),
            P(None, "tp"),
            P(),
            P("tp"),
            P("tp"),
            P("tp"),
            P("tp"),
            P("tp"),
        ),
        check_vma=False,
    )
```

```python
import functools
from types import SimpleNamespace
from typing import NamedTuple

import jax
import jax.numpy as jnp
from jax import lax
from jax.experimental import pallas as pl
from jax.experimental.pallas import tpu as pltpu
from jax.sharding import PartitionSpec as P

EPS_NORM = 1e-05
EPS_FACTOR = 1e-30
DECAY = 0.5
CLIP = 0.5
RATES = (0.45, 0.02, 0.03, 0.1, 0.05, 0.016, 0.09, 1.8, 0.3, 0.45)
MESH = pl.DeviceIdType.MESH
LOG2E = 1.4426950408889634
RESET = 1e9
TILE = 512
X_FIRST = (4, 8)
SHARE_WIDTH = 256
GATE_EARLY = 1024
RENEW_TILES = 4
VMEM_LIMIT = 48 * 1024 * 1024
FINISH_LIMIT = 63 * 1024 * 1024


def passed_along(value, axis, steps):
    count = lax.axis_size(axis)
    initial, last = (max(0, -steps), min(count, count - steps))
    return lax.ppermute(value, axis, [(source, source + steps) for source in range(initial, last)])


def silu_slope(values):
    sigmoid_v = jax.nn.sigmoid(values)
    return sigmoid_v * (1.0 + values * (1.0 - sigmoid_v))


def factor_update(grad, row_sums, rows_old, cols_old, channels):
    rows_new = DECAY * rows_old + (1.0 - DECAY) * (row_sums / channels + EPS_FACTOR)
    cols_new = DECAY * cols_old + (1.0 - DECAY) * (jnp.mean(grad * grad, axis=0) + EPS_FACTOR)
    scale_sq = rows_new[:, None] * cols_new[None, :] / jnp.mean(rows_new)
    return (rows_new, cols_new, grad * lax.rsqrt(scale_sq))


def moment_update(grad_in, moment_old):
    moment_new = DECAY * moment_old + (1.0 - DECAY) * (grad_in * grad_in + EPS_FACTOR)
    return (moment_new, grad_in * lax.rsqrt(moment_new))


def sum_squares(update):
    return jnp.sum(update * update)


def apply_step(weight, update, total_sum, count_all, step_rate):
    root_mean = jnp.sqrt(total_sum / count_all)
    return weight - step_rate * update / jnp.maximum(1.0, root_mean / CLIP)


def wide(tile, width):
    return jnp.concatenate([tile] * (width // tile.shape[1]), axis=1)


def fold_lanes(value):
    pieces = [value[:, at : at + 128] for at in range(0, value.shape[1], 128)]
    while len(pieces) > 1:
        pieces = [first + second for first, second in zip(pieces[::2], pieces[1::2])]
    return pieces[0]


def state_kernel(backward, step_ref, value_ref, lane_ref, rate_ref, out_ref):
    rows, width = step_ref.shape
    states = rate_ref.shape[0]
    rate = rate_ref[...] * LOG2E

    def block(index, state):
        base = pl.multiple_of((rows // 8 - 1 - index if backward else index) * 8, 8)
        for offset in range(8):
            at = base + (7 - offset if backward else offset)
            keep = jnp.exp2(rate * step_ref[pl.ds(at, 1), :])
            term = wide(lane_ref[at], width) * value_ref[pl.ds(at, 1), :]
            state = keep * (state + term) if backward else keep * state + term
        return state

    out_ref[0:states, :] = lax.fori_loop(0, rows // 8, block, jnp.zeros((states, width), jnp.float32))
    total = jnp.sum(step_ref[...], axis=0, keepdims=True)
    out_ref[states:, :] = jnp.broadcast_to(total, (out_ref.shape[0] - states, width))


def piece_state(step, value, lane, rate, backward):
    rows, width = step.shape
    states = rate.shape[0]
    tile = TILE
    return pl.pallas_call(
        functools.partial(state_kernel, backward),
        grid=(width // tile,),
        in_specs=[
            pl.BlockSpec((rows, tile), lambda i: (0, i)),
            pl.BlockSpec((rows, tile), lambda i: (0, i)),
            pl.BlockSpec((rows, states, 128), lambda i: (0, 0, 0)),
            pl.BlockSpec((states, tile), lambda i: (0, i)),
        ],
        out_specs=pl.BlockSpec((states + 8, tile), lambda i: (0, i)),
        out_shape=jax.ShapeDtypeStruct((states + 8, width), jnp.float32),
        compiler_params=pltpu.CompilerParams(vmem_limit_bytes=VMEM_LIMIT),
    )(step, value, lane, rate)


def forward_kernel(
    step_ref, drive_ref, enter_ref, leave_ref, rate_ref, start_ref, out_ref
):
    rows, width = step_ref.shape
    rate = rate_ref[...] * LOG2E

    def block(index, state):
        base = pl.multiple_of(index * 8, 8)
        for offset in range(8):
            at = base + offset
            keep = jnp.exp2(rate * step_ref[pl.ds(at, 1), :])
            state = keep * state + wide(enter_ref[at], width) * drive_ref[pl.ds(at, 1), :]
            out_ref[pl.ds(at, 1), :] = jnp.sum(
                wide(leave_ref[at], width) * state, axis=0, keepdims=True
            )
        return state

    lax.fori_loop(0, rows // 8, block, start_ref[...])


def scan_forward(step, drive, enter, leave, rate, start):
    rows, width = step.shape
    states = rate.shape[0]
    tile = TILE
    by_tile = pl.BlockSpec((rows, tile), lambda i: (0, i))
    by_state = pl.BlockSpec((states, tile), lambda i: (0, i))
    whole = pl.BlockSpec((rows, states, 128), lambda i: (0, 0, 0))
    return pl.pallas_call(
        forward_kernel,
        grid=(width // tile,),
        in_specs=[by_tile, by_tile, whole, whole, by_state, by_state],
        out_specs=by_tile,
        out_shape=jax.ShapeDtypeStruct((rows, width), jnp.float32),
        compiler_params=pltpu.CompilerParams(vmem_limit_bytes=VMEM_LIMIT),
    )(step, drive, enter, leave, rate, start)


def backward_kernel(
    step_ref,
    drive_ref,
    grad_ref,
    enter_ref,
    leave_ref,
    rate_ref,
    start_ref,
    follow_ref,
    drive_grad_ref,
    step_grad_ref,
    decay_ref,
    enter_grad_ref,
    leave_grad_ref,
    kept_ref,
    state_ref,
):
    rows, width = step_ref.shape
    rate_own = rate_ref[...]
    rate = rate_own * LOG2E

    @pl.when(pl.program_id(0) == 0)
    def _():
        enter_grad_ref[...] = jnp.zeros_like(enter_grad_ref)
        leave_grad_ref[...] = jnp.zeros_like(leave_grad_ref)

    def again(index, state):
        base = pl.multiple_of(index * 8, 8)
        for offset in range(8):
            at = base + offset
            keep = jnp.exp2(rate * step_ref[pl.ds(at, 1), :])
            kept_ref[at] = keep
            state = keep * state + wide(enter_ref[at], width) * drive_ref[pl.ds(at, 1), :]
            state_ref[at + 1] = state
        return state

    start = start_ref[...]
    state_ref[0] = start
    lax.fori_loop(0, rows // 8, again, start)
    follow = follow_ref[...]

    def block(index, carry):
        follow, decay = carry
        base = pl.multiple_of((rows // 8 - 1 - index) * 8, 8)
        for offset in range(7, -1, -1):
            at = base + offset
            grad = grad_ref[pl.ds(at, 1), :]
            adjoint = wide(leave_ref[at], width) * grad + follow
            drive_grad_ref[pl.ds(at, 1), :] = jnp.sum(
                adjoint * wide(enter_ref[at], width), axis=0, keepdims=True
            )
            enter_grad_ref[at] += fold_lanes(adjoint * drive_ref[pl.ds(at, 1), :])
            leave_grad_ref[at] += fold_lanes(state_ref[at + 1] * grad)
            follow = kept_ref[at] * adjoint
            part = follow * state_ref[at]
            step_grad_ref[pl.ds(at, 1), :] = jnp.sum(part * rate_own, axis=0, keepdims=True)
            decay = decay + part * step_ref[pl.ds(at, 1), :]
        return follow, decay

    _, decay = lax.fori_loop(0, rows // 8, block, (follow, jnp.zeros_like(follow)))
    decay_ref[...] = decay * rate_own


def scan_backward(step, drive, grad, enter, leave, rate, start, follow):
    rows, width = step.shape
    states = rate.shape[0]
    tile = TILE
    by_tile = pl.BlockSpec((rows, tile), lambda i: (0, i))
    by_state = pl.BlockSpec((states, tile), lambda i: (0, i))
    whole = pl.BlockSpec((rows, states, 128), lambda i: (0, 0, 0))
    return pl.pallas_call(
        backward_kernel,
        grid=(width // tile,),
        in_specs=[by_tile, by_tile, by_tile, whole, whole, by_state, by_state, by_state],
        out_specs=[by_tile, by_tile, by_state, whole, whole],
        out_shape=[
            jax.ShapeDtypeStruct((rows, width), jnp.float32),
            jax.ShapeDtypeStruct((rows, width), jnp.float32),
            jax.ShapeDtypeStruct((states, width), jnp.float32),
            jax.ShapeDtypeStruct((rows, states, 128), jnp.float32),
            jax.ShapeDtypeStruct((rows, states, 128), jnp.float32),
        ],
        scratch_shapes=[
            pltpu.VMEM((rows, states, tile), jnp.float32),
            pltpu.VMEM((rows + 1, states, tile), jnp.float32),
        ],
        compiler_params=pltpu.CompilerParams(vmem_limit_bytes=VMEM_LIMIT),
    )(step, drive, grad, enter, leave, rate, start, follow)


def on_block():
    return lax.axis_size("seq") == 16 and lax.axis_size("tp") == 2


def position():
    place = lax.axis_index("seq")
    return lax.div(place, 4), lax.rem(lax.div(place, 2), 2), lax.rem(place, 2)


def device(z, x, core):
    return (z * 4 + x * 2 + core, lax.axis_index("tp"))


def other_half():
    return (lax.axis_index("seq"), 1 - lax.axis_index("tp"))


def greet(peers):
    barrier = pltpu.get_barrier_semaphore()
    for peer in peers:
        pl.semaphore_signal(barrier, inc=1, device_id=peer, device_id_type=MESH)
    pl.semaphore_wait(barrier, len(peers))


def remote(source, target, sent, arrived, peer):
    return pltpu.make_async_remote_copy(
        src_ref=source,
        dst_ref=target,
        send_sem=sent,
        recv_sem=arrived,
        device_id=peer,
        device_id_type=MESH,
    )


def sum_over(seq_part, shared_part, tp_part):
    return lax.psum(seq_part, "seq"), lax.psum(shared_part, ("seq", "tp")), lax.psum(tp_part, "tp")


def project(half, weight, ident):
    hidden = lax.all_gather(half, "tp", axis=0, tiled=True)
    full = lax.all_gather(weight, "seq", axis=0, tiled=True)
    return jnp.dot(hidden, full, preferred_element_type=jnp.float32), hidden, full[None]


def pair_kernel(mine_ref, out_ref, far, sent, arrived):
    greet([other_half()])
    copy = remote(mine_ref, far, sent, arrived, other_half())
    copy.start()
    copy.wait()
    out_ref[...] = mine_ref[...] + far[...]


def pair_sum(value, ident):
    if not on_block():
        return lax.psum(value, "tp")
    vmem = pl.BlockSpec(memory_space=pltpu.VMEM)
    return pl.pallas_call(
        pair_kernel,
        in_specs=[vmem],
        out_specs=vmem,
        out_shape=jax.ShapeDtypeStruct(value.shape, value.dtype),
        scratch_shapes=[
            pltpu.VMEM(value.shape, value.dtype),
            pltpu.SemaphoreType.DMA,
            pltpu.SemaphoreType.DMA,
        ],
        compiler_params=pltpu.CompilerParams(collective_id=ident, has_side_effects=True),
    )(value)


def chain_kernel(backward, piece_ref, rate_ref, swap_ref, out_ref, swapped_ref, come, back, sems, swap_sems):
    place = lax.axis_index("seq")
    states = rate_ref.shape[0]
    peers = [(lax.rem(place + step, 16), lax.axis_index("tp")) for step in range(1, 16)]
    greet(peers + [other_half()])
    swap = remote(swap_ref, swapped_ref, swap_sems.at[0], swap_sems.at[1], other_half())
    swap.start()

    def lanes(at):
        return pl.ds(pl.multiple_of(at * 128, 128), 128)

    def out(at):
        return remote(
            piece_ref.at[:, lanes(peers[at][0])],
            come.at[place],
            sems.at[0, at],
            sems.at[1, at],
            peers[at],
        )

    def home(at):
        return remote(
            back.at[peers[at][0]],
            out_ref.at[:, lanes(place)],
            sems.at[2, at],
            sems.at[3, at],
            peers[at],
        )

    for at in range(15):
        out(at).start()
    come[place] = piece_ref[:, lanes(place)]
    rate = rate_ref[:, lanes(place)] * LOG2E
    for at in range(15):
        out(at).wait_recv()

    def join(index, state):
        at = 15 - index if backward else index
        back[at] = state
        piece = come[at]
        return jnp.exp2(rate * piece[states : states + 1]) * state + piece[:states]

    lax.fori_loop(0, 16, join, jnp.zeros((states, 128), jnp.float32))
    for at in range(15):
        home(at).start()
    out_ref[:, lanes(place)] = back[place]
    for at in range(15):
        home(at).wait_recv()
    for at in range(15):
        out(at).wait_send()
        home(at).wait_send()
    swap.wait()


def chain(piece, rate, swap, backward, ident):
    states, width = rate.shape
    if not on_block():
        count, place = lax.axis_size("seq"), lax.axis_index("seq")
        pieces = lax.all_gather(piece, "seq")

        def join(index, state):
            at = count - 1 - index if backward else index
            longer = (
                jnp.exp2(rate * LOG2E * pieces[at, states : states + 1]) * state + pieces[at, :states]
            )
            return jnp.where(at > place if backward else at < place, longer, state)

        state = lax.fori_loop(0, count, join, jnp.zeros((states, width), jnp.float32))
        order = [(0, 1), (1, 0)]
        return state, lax.ppermute(swap, "tp", order)
    vmem = pl.BlockSpec(memory_space=pltpu.VMEM)
    return pl.pallas_call(
        functools.partial(chain_kernel, backward),
        in_specs=[vmem, vmem, vmem],
        out_specs=[vmem, vmem],
        out_shape=[
            jax.ShapeDtypeStruct((states, width), jnp.float32),
            jax.ShapeDtypeStruct(swap.shape, swap.dtype),
        ],
        scratch_shapes=[
            pltpu.VMEM((16, states + 8, 128), jnp.float32),
            pltpu.VMEM((16, states, 128), jnp.float32),
            pltpu.SemaphoreType.DMA((4, 15)),
            pltpu.SemaphoreType.DMA((2,)),
        ],
        compiler_params=pltpu.CompilerParams(collective_id=ident, has_side_effects=True),
    )(piece, rate, swap)


def wait_all(copies):
    for copy in copies:
        copy.wait_recv()


def gathered(refs, *groups):
    named, at = {}, 0
    for group in groups:
        named.update(zip(group._fields, refs[at:]))
        at += len(group._fields)
    return SimpleNamespace(**named), list(refs[at:])


def shared(source, group):
    return {name: value for name, value in source._asdict().items() if name in group._fields}


class Reducer:
    def __init__(self, jobs, refs):
        self.jobs, self.at = jobs, 0
        self.send, self.come = refs[:3], refs[3:6]
        self.sent, self.got, self.total = refs[6:9], refs[9:12], refs[12]
        self.z, self.x, self.core = position()
        self.chunks, self.width = self.come[2].shape[0], self.come[2].shape[3]
        self.peers = [
            [device(self.z, self.x, 1 - self.core)],
            [device(self.z, 1 - self.x, self.core)],
            [device(lax.rem(self.z + step, 4), self.x, self.core) for step in (1, 2, 3)],
        ]

    def copies(self, level, chunk):
        slot = chunk % self.send[level].shape[0]
        if level < 2:
            return [
                remote(
                    self.send[level].at[slot],
                    self.come[level].at[chunk],
                    self.sent[level].at[chunk],
                    self.got[level].at[chunk],
                    self.peers[level][0],
                )
            ]
        return [
            remote(
                self.send[2].at[slot, 0, lax.rem(self.z + 1 + at, 4)],
                self.come[2].at[chunk, at],
                self.sent[2].at[chunk, at],
                self.got[2].at[chunk, at],
                self.peers[2][at],
            )
            for at in range(3)
        ]

    def free(self, level, chunk):
        older = chunk - self.send[level].shape[0]
        if older >= 0:
            for copy in self.copies(level, older):
                copy.wait_send()

    def product(self, chunk, first, count):
        left, right, start = self.jobs[chunk][:3]
        _, rows, depth = left.shape
        block = left[pl.ds(first, count)].reshape(count * rows, depth)
        value = jnp.dot(
            block, right[:, start : start + self.width], preferred_element_type=jnp.float32
        )
        return value.reshape(count, rows, self.width)

    def put(self, chunk, value, more):
        out, start = self.jobs[chunk][3:]
        here = slice(start, start + self.width)
        out[:, here] = out[:, here] + value if more else value

    def after_core(self, chunk, x):
        come = self.come[0][chunk, x].astype(jnp.float32)
        return self.product(chunk, self.core * 8 + x * 4, 4) + come

    def fill(self, level, chunk, values):
        self.free(level, chunk)
        slot = chunk % self.send[level].shape[0]
        for at, value in enumerate(values):
            self.send[level][slot, at] = value().astype(jnp.bfloat16)
        for copy in self.copies(level, chunk):
            copy.start()

    def stage(self, level, chunk):
        if not 0 <= chunk < self.chunks:
            return
        if level > 0:
            wait_all(self.copies(level - 1, chunk))
        if level == 0:
            away = (1 - self.core) * 8
            self.fill(
                0, chunk, [lambda at=at: self.product(chunk, away + at * 4, 4) for at in range(2)]
            )
        elif level == 1:
            self.fill(1, chunk, [lambda: self.after_core(chunk, 1 - self.x)])
        elif level == 2:
            come = self.come[1][chunk, 0].astype(jnp.float32)
            self.total[...] = self.after_core(chunk, self.x) + come
            self.fill(2, chunk, [lambda: self.total[...]])
            self.put(chunk, self.total[self.z], False)
        else:
            come = [self.come[2][chunk, at].astype(jnp.float32) for at in range(3)]
            self.put(chunk, (come[0] + come[1]) + come[2], True)

    def step(self, step):
        for level, lag in enumerate((0, 1, 3, 5)):
            self.stage(level, step - lag)

    def advance(self, count=1):
        for _ in range(count):
            if self.at < self.chunks + 5:
                self.step(self.at)
                self.at += 1

    def drain(self):
        for level in range(3):
            for chunk in range(max(0, self.chunks - self.send[level].shape[0]), self.chunks):
                for copy in self.copies(level, chunk):
                    copy.wait_send()


def reducer_scratch(columns, share, width):
    chunks = columns // width
    low, dma = jnp.bfloat16, pltpu.SemaphoreType.DMA
    return [
        pltpu.VMEM((4, 2, 4, share, width), low),
        pltpu.VMEM((4, 1, 4, share, width), low),
        pltpu.VMEM((4, 1, 4, share, width), low),
        pltpu.VMEM((chunks, 2, 4, share, width), low),
        pltpu.VMEM((chunks, 1, 4, share, width), low),
        pltpu.VMEM((chunks, 3, share, width), low),
        dma((chunks,)),
        dma((chunks,)),
        dma((chunks, 3)),
        dma((chunks,)),
        dma((chunks,)),
        dma((chunks, 3)),
        pltpu.VMEM((4, share, width), jnp.float32),
    ]


def rows_to_lanes(partial):
    return jnp.sum(partial.T, axis=0, keepdims=True)


def lanes_to_rows(row):
    return jnp.broadcast_to(row, (128, 128)).T


class FinishIn(NamedTuple):
    hidden_t: object
    d_value: object
    d_gate: object
    gate_grad: object
    extra: object
    weights: object
    block: object
    cot: object
    lanes: object
    out_grad: object
    norm_gain: object
    norm_moment: object
    in_cols: object
    out_cols: object
    step_cols: object
    select_cols: object
    decay_cols: object
    conv_cols: object
    bias_moment: object
    step_moment: object
    skip_moment: object
    conv_bias: object
    step_bias: object
    skip_gain: object


class FinishOut(NamedTuple):
    in_grad: object
    input_grad: object
    small: object
    scales: object
    lanes_new: object
    vectors_new: object


class FinishWork(NamedTuple):
    come_core: object
    send_x: object
    come_x: object
    send_z: object
    come_z: object
    full: object
    mine: object
    acc: object
    far: object
    pair: object
    pair_far: object
    totals: object
    totals_acc: object
    totals_far: object
    come_half: object
    d_hidden: object
    held: object
    held_sems: object
    extra_sent: object
    extra_got: object
    sums_sent: object
    sums_got: object
    half_sems: object


def finish_kernel(channels, model, *refs):
    r, rest = gathered(refs, FinishIn, FinishOut, FinishWork)
    z, x, core = position()
    place, tp = lax.axis_index("seq"), lax.axis_index("tp")
    core_peer, x_peer = device(z, x, 1 - core), device(z, 1 - x, core)
    z_peers = [device(lax.rem(z + step, 4), x, core) for step in (1, 2, 3)]
    others = [
        (lax.rem(z + step, 4) * 4 + x * 2 + core, 1 - lax.axis_index("tp")) for step in range(4)
    ]
    greet([core_peer, x_peer, device(z, 1 - x, 1 - core)] + z_peers + others)
    low = jnp.bfloat16
    half_rows = r.block.shape[0]
    own_half = pl.ds(pl.multiple_of(tp * half_rows, half_rows), half_rows)
    far_half = pl.ds(pl.multiple_of((1 - tp) * half_rows, half_rows), half_rows)
    d_hidden = r.d_hidden
    swap = remote(
        d_hidden.at[far_half], r.come_half, r.half_sems.at[0], r.half_sems.at[1], other_half()
    )
    sides = [r.d_value, r.d_gate]
    inner = r.out_grad.shape[1]
    early = r.gate_grad.shape[1]
    r.in_grad[:, inner : inner + early] = r.gate_grad[...]
    main = Reducer(
        [(r.hidden_t, r.d_value, at, r.in_grad, at) for at in range(0, inner, SHARE_WIDTH)]
        + [(r.hidden_t, r.d_gate, at, r.in_grad, inner + at) for at in range(early, inner, SHARE_WIDTH)],
        rest,
    )

    kept_chunks, _, kept_width = r.weights.shape

    def fetch(chunk):
        return pltpu.make_async_copy(
            r.weights.at[chunk], r.held.at[chunk % 2], r.held_sems.at[chunk]
        )

    def hidden_stage(chunk):
        fetch(chunk).wait()
        per_side = kept_chunks // 2
        at = chunk % per_side
        part = lax.dot_general(
            sides[chunk // per_side][:, at * kept_width : (at + 1) * kept_width],
            r.held[chunk % 2],
            (((1,), (1,)), ((), ())),
            preferred_element_type=jnp.float32,
        )
        d_hidden[...] = part if chunk == 0 else d_hidden[...] + part
        if chunk + 2 < kept_chunks:
            fetch(chunk + 2).start()
        if chunk == kept_chunks - 1:
            swap.start()

    fetch(0).start()
    fetch(1).start()

    sent, got = r.extra_sent, r.extra_got
    extra, full = r.extra, r.full
    extra_core = remote(extra.at[:, 1 - core], r.come_core, sent.at[0], got.at[0], core_peer)
    extra_x = remote(r.send_x, r.come_x, sent.at[1], got.at[1], x_peer)
    extra_z = [
        remote(r.send_z.at[at], r.come_z.at[at], sent.at[2 + at], got.at[2 + at], z_peers[at])
        for at in range(3)
    ]
    own, held, halves = full.at[z, x, core], full.at[:, x, core], full.at[:, :, core]
    back_z = [remote(own, own, sent.at[5 + at], got.at[5 + at], z_peers[at]) for at in range(3)]
    back_x = remote(held, held, sent.at[8], got.at[8], x_peer)
    back_core = remote(halves, halves, sent.at[9], got.at[9], core_peer)

    def extra_after_core(pair):
        return extra[pair, core].astype(jnp.float32) + r.come_core[pair].astype(jnp.float32)

    def extra_after_x(level):
        return extra_after_core(level * 2 + x) + r.come_x[level].astype(jnp.float32)

    def extra_stage_x():
        extra_core.wait_recv()

        def one(level, _):
            r.send_x[level] = extra_after_core(level * 2 + 1 - x).astype(low)
            return 0

        lax.fori_loop(0, 4, one, 0)
        extra_x.start()

    def extra_stage_z():
        extra_x.wait_recv()

        def one(at, _):
            r.send_z[at] = extra_after_x(lax.rem(z + 1 + at, 4)).astype(low)
            return 0

        lax.fori_loop(0, 3, one, 0)
        for copy in extra_z:
            copy.start()

    def extra_stage_last():
        wait_all(extra_z)
        total = extra_after_x(z)
        for at in range(3):
            total = total + r.come_z[at].astype(jnp.float32)
        full[z, x, core] = total.astype(low)
        for copy in back_z:
            copy.start()

    def extra_back_x():
        wait_all(back_z)
        back_x.start()

    def extra_back_core():
        back_x.wait_recv()
        back_core.start()

    mine = r.mine
    vectors_new = r.vectors_new

    def line(ref):
        return ref[...].reshape(1, -1)

    in_tiles, out_tiles = r.in_grad.shape[1] // 128, r.out_grad.shape[1] // 128
    seq_rows = in_tiles + out_tiles
    gain_tiles = model // 128

    def put(base, row):
        for at in range(row.shape[1] // 128):
            mine[base + at : base + at + 1, :] = row[:, at * 128 : (at + 1) * 128]

    def take(ref, base, tiles):
        return jnp.concatenate([ref[base + at : base + at + 1, :] for at in range(tiles)], axis=1)

    def residual_stage():
        swap.wait()
        total = d_hidden[own_half, :] + r.come_half[...]
        residual = r.block[...].astype(jnp.float32)
        inv_rms = lax.rsqrt(jnp.mean(residual * residual, axis=1, keepdims=True) + EPS_NORM)
        normed = residual * inv_rms
        put(seq_rows, jnp.sum(total * normed, axis=0, keepdims=True))
        scaled = total * line(r.norm_gain)
        mean = jnp.mean(scaled * normed, axis=1, keepdims=True)
        r.input_grad[...] = r.cot[own_half, :].astype(jnp.float32) + inv_rms * (scaled - normed * mean)

    span = 512
    wide_span = span // 128
    small = r.small
    groups = {"step": (0, 128), "select": (128, 288), "decay": (288, 304), "conv": (304, 308)}
    pair = r.pair

    def put_rows(at, partial):
        pair[at : at + 1, :] = rows_to_lanes(partial)

    def fold_square(value):
        return fold_lanes(value * value)

    def small_stage():
        back_core.wait_recv()
        for block in range(16):
            small[:, block * 128 : (block + 1) * 128] = full[
                block // 4, block // 2 % 2, block % 2
            ].astype(jnp.float32)
        for at in range(3):
            rows = min(128, small.shape[0] - at * 128)

            def one(index, partial):
                columns = pl.ds(pl.multiple_of(index * span, span), span)
                return partial + fold_square(small[at * 128 : at * 128 + rows, columns])

            partial = lax.fori_loop(
                0, small.shape[1] // span, one, jnp.zeros((rows, 128), jnp.float32)
            )
            if rows < 128:
                partial = jnp.concatenate(
                    [partial, jnp.zeros((128 - rows, 128), jnp.float32)], axis=0
                )
            put_rows(at, partial)

    def column_sums(ref, base):
        def one(index, partial):
            columns = pl.ds(pl.multiple_of(index * span, span), span)
            value = ref[:, columns]
            sums = jnp.sum(value * value, axis=0, keepdims=True)
            for at in range(wide_span):
                mine[pl.ds(base + index * wide_span + at, 1), :] = sums[:, at * 128 : (at + 1) * 128]
            return partial + fold_square(value)

        return lax.fori_loop(
            0, ref.shape[1] // span, one, jnp.zeros((ref.shape[0], 128), jnp.float32)
        )

    def out_stage():
        put_rows(4, column_sums(r.out_grad, in_tiles))

    pair[...] = jnp.zeros(pair.shape, jnp.float32)
    extra_core.start()
    extra_steps = {1: extra_stage_x, 3: extra_stage_z, 5: extra_stage_last, 7: extra_back_x, 9: extra_back_core}
    extra_steps.update({14: residual_stage, 12: out_stage, 11: small_stage})
    for step in range(max(main.chunks + 5, 16)):
        main.advance()
        if step < kept_chunks:
            hidden_stage(step)
        if step in extra_steps:
            extra_steps[step]()
    put_rows(3, column_sums(r.in_grad, 0))

    lanes = r.lanes
    row_at = lax.broadcasted_iota(jnp.int32, lanes.shape, 0)
    lane_at = lax.broadcasted_iota(jnp.int32, lanes.shape, 1)
    counts = jnp.where(row_at == 3, 2.0 * channels, 1.0 * channels)
    held_lanes = DECAY * lanes[...] + (1.0 - DECAY) * EPS_FACTOR
    part = jnp.where(tp == 0, held_lanes, 0.0) + (1.0 - DECAY) * pair[...] / counts

    def total(value):
        return jnp.sum(jnp.sum(value, axis=1, keepdims=True), axis=0, keepdims=True)

    base = seq_rows + gain_tiles
    for at in range(2):
        mean = total(jnp.where(row_at == 3 + at, part, 0.0)) / model
        mine[base + 8 * at : base + 8 * at + 8, :] = jnp.broadcast_to(mean, (8, 128))

    sums_sent, sums_got = r.sums_sent, r.sums_got

    def hop(at, source, target, peer):
        return remote(source, target, sums_sent.at[at], sums_got.at[at], peer)

    plane = x * 2 + core
    mates = [core_peer, x_peer, device(z, 1 - x, 1 - core)]
    across = [(lax.rem(z + step, 4) * 4 + plane, 1 - tp) for step in range(4)]

    def sum_hops(first, value, acc, far, shared):
        acc[plane] = value[...]
        copies = [hop(first + at, acc.at[plane], acc.at[plane], mates[at]) for at in range(3)]
        for copy in copies:
            copy.start()
        for copy in copies:
            copy.wait()
        acc[4 + z] = (acc[0] + acc[1]) + (acc[2] + acc[3])
        part = acc.at[4 + z]
        copies = [hop(first + 3 + at, part, part, z_peers[at]) for at in range(3)]
        copies += [
            hop(first + 6 + at, part.at[shared:], far.at[z], across[at]) for at in range(4)
        ]
        for copy in copies:
            copy.start()
        for copy in copies:
            copy.wait()
        value[...] = (acc[4] + acc[5]) + (acc[6] + acc[7])
        value[shared:] = value[shared:] + ((far[0] + far[1]) + (far[2] + far[3]))

    pair_copy = hop(20, pair, r.pair_far, other_half())
    pair_copy.start()
    sum_hops(0, mine, r.acc, r.far, seq_rows)
    pair_copy.wait()

    lanes_new = held_lanes + (1.0 - DECAY) * (pair[...] + r.pair_far[...]) / counts
    r.lanes_new[...] = lanes_new
    flat = row_at * 128 + lane_at
    means = jnp.where(row_at == 3, mine[base : base + 8, :], mine[base + 8 : base + 16, :])
    for low_edge, high_edge in groups.values():
        member = (flat >= low_edge) & (flat < high_edge)
        mean = total(jnp.where(member, lanes_new, 0.0)) / (high_edge - low_edge)
        means = jnp.where(member, mean, means)
    scale = lax.rsqrt(lanes_new / means)
    scales = [lanes_to_rows(scale[at : at + 1, :]) for at in range(5)]
    small_scale = jnp.concatenate(scales[:3], axis=0)
    in_scale, out_scale = scales[3], scales[4]

    def cols_new(old, sums, count):
        return DECAY * old + (1.0 - DECAY) * (sums / count + EPS_FACTOR)

    in_cols = cols_new(
        jnp.concatenate([r.in_cols[0:1, :], r.in_cols[1:2, :]], axis=1), take(mine, 0, in_tiles), model
    )
    half = in_cols.shape[1] // 2
    out_cols = cols_new(line(r.out_cols), take(mine, in_tiles, out_tiles), model)
    vectors_new[3:4, :] = in_cols[:, :half]
    vectors_new[4:5, :] = in_cols[:, half:]
    vectors_new[5:6, :] = out_cols

    def squares(ref, row_scale, first_row):
        def one(index, partial):
            columns = pl.ds(pl.multiple_of(index * span, span), span)
            col = vectors_new[pl.ds(first_row + lax.div(index, half // span), 1), pl.ds(
                pl.multiple_of(lax.rem(index, half // span) * span, span), span
            )]
            return partial + fold_square(ref[:, columns] * wide(row_scale, span) * lax.rsqrt(col))

        return total(
            lax.fori_loop(0, ref.shape[1] // span, one, jnp.zeros((ref.shape[0], 128), jnp.float32))
        )

    sums = [squares(r.in_grad, in_scale, 3), squares(r.out_grad, out_scale, 5)]
    group_cols = {
        "step": (line(r.step_cols), 8),
        "select": (line(r.select_cols), 7),
        "decay": (line(r.decay_cols), 9),
        "conv": (line(r.conv_cols), 6),
    }
    for name, (low_edge, high_edge) in groups.items():
        old_cols, new_row = group_cols[name]
        partial = jnp.zeros((high_edge - low_edge, 128), jnp.float32)
        for at in range(0, small.shape[1], span):
            columns = slice(at, at + span)
            value = small[low_edge:high_edge, columns]
            col = cols_new(
                old_cols[:, columns],
                jnp.sum(value * value, axis=0, keepdims=True),
                high_edge - low_edge,
            )
            vectors_new[new_row : new_row + 1, columns] = col
            row_scale = small_scale[low_edge:high_edge]
            partial = partial + fold_square(value * wide(row_scale, span) * lax.rsqrt(col))
        sums.append(total(partial))
    updates = []
    for at in range(3):
        value = small[308 + at : 309 + at, :]
        old = line((r.bias_moment, r.step_moment, r.skip_moment)[at])
        moment = DECAY * old + (1.0 - DECAY) * (value * value + EPS_FACTOR)
        vectors_new[24 + at : 25 + at, :] = moment
        vectors_new[18 + at : 19 + at, :] = value
        update = value * lax.rsqrt(moment)
        updates.append(update)
        sums.append(jnp.sum(update * update, axis=1, keepdims=True))
    totals = r.totals
    for at in range(9):
        totals[at : at + 1, :] = jnp.broadcast_to(sums[at], (1, 128))
    totals[9:16, :] = jnp.zeros((7, 128), jnp.float32)
    sum_hops(10, totals, r.totals_acc, r.totals_far, 0)

    def rate(at, count, step_rate, copies):
        root = jnp.sqrt(totals[at : at + 1, :] / (copies * count))
        return step_rate / jnp.maximum(1.0, root / CLIP)

    in_rate = rate(0, 2.0 * channels * model, RATES[1], 1)
    out_rate = rate(1, 1.0 * channels * model, RATES[2], 1)

    scales_out = r.scales
    scales_out[3] = in_scale * in_rate
    scales_out[4] = out_scale * out_rate
    small_rates = {"step": RATES[6], "select": RATES[5], "decay": RATES[8], "conv": RATES[3]}
    at_total = {"step": 2, "select": 3, "decay": 4, "conv": 5}
    row_number = lax.broadcasted_iota(jnp.int32, small_scale.shape, 0)
    for name, (low_edge, high_edge) in groups.items():
        step_rate = rate(
            at_total[name], 1.0 * (high_edge - low_edge) * channels, small_rates[name], 16
        )
        member = (row_number >= low_edge) & (row_number < high_edge)
        small_scale = jnp.where(member, small_scale * step_rate, small_scale)
    for at in range(3):
        scales_out[at] = small_scale[at * 128 : (at + 1) * 128, :]
    for at, step_rate in enumerate((RATES[4], RATES[7], RATES[9])):
        step_rate = rate(6 + at, 1.0 * channels, step_rate, 16)
        vectors_new[21 + at : 22 + at, :] = (
            line((r.conv_bias, r.step_bias, r.skip_gain)[at]) - wide(step_rate, half) * updates[at]
        )
    gain_grad = take(mine, seq_rows, gain_tiles)
    moment = DECAY * line(r.norm_moment) + (1.0 - DECAY) * (gain_grad * gain_grad + EPS_FACTOR)
    update = gain_grad * lax.rsqrt(moment)
    root = jnp.sqrt(jnp.mean(update * update, axis=1, keepdims=True))
    vectors_new[0:1, :] = gain_grad
    vectors_new[1:2, :] = line(r.norm_gain) - RATES[0] / jnp.maximum(1.0, root / CLIP) * update
    vectors_new[2:3, :] = moment
    vectors_new[10:18, :] = jnp.zeros((8, half), jnp.float32)
    vectors_new[27:32, :] = jnp.zeros((5, half), jnp.float32)

    main.drain()
    for copy in [extra_core, extra_x] + extra_z + back_z + [back_x, back_core]:
        copy.wait_send()


def finish(ident, channels, given):
    half_rows, model = given.block.shape
    share, inner = given.out_grad.shape
    columns = 2 * inner
    f32, low = jnp.float32, jnp.bfloat16
    small_rows = given.extra.shape[2]
    vmem = pl.BlockSpec(memory_space=pltpu.VMEM)
    dma = pltpu.SemaphoreType.DMA
    shape = jax.ShapeDtypeStruct
    seq_rows = columns // 128 + inner // 128 + model // 128 + 16
    kept_chunks, _, kept_width = given.weights.shape
    block = (small_rows, 128)
    outs = pl.pallas_call(
        functools.partial(finish_kernel, channels, model),
        in_specs=[
            pl.BlockSpec(memory_space=pltpu.HBM) if value is given.weights else vmem for value in given
        ],
        out_specs=[vmem] * len(FinishOut._fields),
        out_shape=[
            shape((share, columns), f32),
            shape((half_rows, model), f32),
            shape((small_rows, inner), f32),
            shape((5, 128, 128), f32),
            shape((8, 128), f32),
            shape((32, inner), f32),
        ],
        scratch_shapes=[
            pltpu.VMEM((8,) + block, low),
            pltpu.VMEM((4,) + block, low),
            pltpu.VMEM((4,) + block, low),
            pltpu.VMEM((3,) + block, low),
            pltpu.VMEM((3,) + block, low),
            pltpu.VMEM((4, 2, 2) + block, low),
            pltpu.VMEM((seq_rows, 128), f32),
            pltpu.VMEM((8, seq_rows, 128), f32),
            pltpu.VMEM((4, model // 128 + 16, 128), f32),
            pltpu.VMEM((8, 128), f32),
            pltpu.VMEM((8, 128), f32),
            pltpu.VMEM((16, 128), f32),
            pltpu.VMEM((8, 16, 128), f32),
            pltpu.VMEM((4, 16, 128), f32),
            pltpu.VMEM((half_rows, model), f32),
            pltpu.VMEM((2 * half_rows, model), f32),
            pltpu.VMEM((2, model, kept_width), low),
            dma((kept_chunks,)),
            dma((10,)),
            dma((10,)),
            dma((21,)),
            dma((21,)),
            dma((2,)),
        ]
        + reducer_scratch(columns - given.gate_grad.shape[1], share, SHARE_WIDTH),
        compiler_params=pltpu.CompilerParams(
            collective_id=ident, has_side_effects=True, vmem_limit_bytes=FINISH_LIMIT
        ),
    )(*given)
    return FinishOut(*outs)


class RenewIn(NamedTuple):
    value_grad: object
    gate_grad: object
    out_grad: object
    input_grad: object
    block_out: object
    small: object
    scales: object
    lanes_new: object
    vectors_new: object
    in_weight: object
    out_weight: object
    step_weight: object
    select_weight: object
    decay_log: object
    conv_weight: object


def renew_kernel(*refs):
    r, out = gathered(refs, RenewIn)
    cols, small, scales = r.vectors_new, r.small, r.scales
    span = small.shape[1]

    def write(*values):
        for value in values:
            ref = out.pop(0)
            ref[...] = value.astype(ref.dtype).reshape(ref.shape)

    def line(at):
        return cols[at : at + 1, :]

    def rows(low_edge, high_edge):
        flat = [r.lanes_new[at : at + 1, :] for at in range(5)]
        return jnp.concatenate(flat, axis=1)[:, low_edge:high_edge]

    def matrix(grad, weight, scale, col):
        new = weight - grad * wide(scale, span) * lax.rsqrt(line(col))
        write(grad, new, new)

    write(r.block_out[...], r.input_grad[...], line(0), line(1), line(1), line(2))
    in_refs = [out.pop(0) for _ in range(3)]
    for part, grad_ref in enumerate((r.value_grad, r.gate_grad)):
        grad = grad_ref[...]
        new = r.in_weight[:, part, :] - grad * wide(scales[3], span) * lax.rsqrt(line(3 + part))
        for ref, value in zip(in_refs, (grad, new, new)):
            ref[:, part, :] = value.astype(ref.dtype)
    write(rows(384, 512), cols[3:5, :])
    matrix(r.out_grad[...], r.out_weight[...], scales[4], 5)
    write(rows(512, 640), line(5))
    small_scale = jnp.concatenate([scales[0], scales[1], scales[2]], axis=0)
    matrix(small[304:308, :], r.conv_weight[...], small_scale[304:308], 6)
    write(rows(304, 308), line(6))
    write(line(18), line(21), line(21), line(24))
    matrix(small[128:288, :], r.select_weight[...], small_scale[128:288], 7)
    write(rows(128, 288), line(7))
    matrix(small[0:128, :], r.step_weight[...], small_scale[0:128], 8)
    write(rows(0, 128), line(8), line(19), line(22), line(22), line(25))
    matrix(small[288:304, :], r.decay_log[...], small_scale[288:304], 9)
    write(rows(288, 304), line(9))
    write(line(20), line(23), line(23), line(26))


def renew(given):
    f32, low = jnp.float32, jnp.bfloat16
    inner = given.out_grad.shape[1]
    shape = jax.ShapeDtypeStruct

    def three(ref):
        return [shape(ref.shape, f32), shape(ref.shape, f32), shape(ref.shape, low)]

    def vector(count):
        return shape((count,), f32)

    def trio(count):
        return [vector(count), vector(count), shape((count,), low)]

    model = given.block_out.shape[1]
    share = given.out_grad.shape[0]
    outs = (
        [shape(given.block_out.shape, f32), shape(given.input_grad.shape, f32)]
        + trio(model)
        + [vector(model)]
        + three(given.in_weight)
        + [vector(share), shape((2, inner), f32)]
        + three(given.out_weight)
        + [vector(share), vector(inner)]
        + three(given.conv_weight)
        + [vector(given.conv_weight.shape[0]), vector(inner)]
        + trio(inner)
        + [vector(inner)]
        + three(given.select_weight)
        + [vector(given.select_weight.shape[0]), vector(inner)]
        + three(given.step_weight)
        + [vector(given.step_weight.shape[0]), vector(inner)]
        + trio(inner)
        + [vector(inner)]
        + three(given.decay_log)
        + [vector(given.decay_log.shape[0]), vector(inner)]
        + trio(inner)
        + [vector(inner)]
    )
    span = inner // RENEW_TILES

    def by_tile(ref, first=0):
        *front, last = ref.shape
        if not front and last != inner:
            return pl.BlockSpec((last,), lambda i: (0,))
        zeros = (0,) * len(front)
        return pl.BlockSpec((*front, span), lambda i: zeros + (first + i,))

    def whole(ref):
        zeros = (0,) * len(ref.shape)
        return pl.BlockSpec(ref.shape, lambda i: zeros)

    specs = RenewIn(*[by_tile(ref) for ref in given])
    specs = specs._replace(
        gate_grad=by_tile(given.gate_grad, RENEW_TILES),
        scales=whole(given.scales),
        lanes_new=whole(given.lanes_new),
    )
    return tuple(
        pl.pallas_call(
            renew_kernel,
            grid=(RENEW_TILES,),
            in_specs=list(specs),
            out_specs=[by_tile(ref) for ref in outs],
            out_shape=outs,
            compiler_params=pltpu.CompilerParams(vmem_limit_bytes=FINISH_LIMIT),
        )(*given)
    )


class ForwardIn(NamedTuple):
    in_weight: object
    out_weight: object
    block: object
    cot: object
    norm_gain: object
    conv_weight: object
    conv_bias: object
    step_bias: object
    skip_gain: object
    masks: object
    select_weight: object
    step_weight: object
    decay_log: object


class ForwardOut(NamedTuple):
    hidden_t: object
    cot_t: object
    piece: object
    conv_in: object
    rim: object
    conv_pre: object
    conv_out: object
    select_out: object
    step_pre: object
    step_size: object
    held: object
    drive: object
    enter: object
    leave: object
    start: object
    gated: object
    d_mixed: object
    d_gate: object
    branch: object
    skip_grad: object
    weights: object


class ForwardWork(NamedTuple):
    hidden: object
    full: object
    ext: object
    gate: object
    scanned: object
    state_piece: object
    come: object
    back: object
    select_far: object
    z_sent: object
    z_got: object
    x_sent: object
    x_got: object
    core_sems: object
    kept: object
    rim_sems: object
    chain_sems: object
    pair_sems: object


def forward_block_kernel(*refs):
    r, _ = gathered(refs, ForwardIn, ForwardOut, ForwardWork)
    z, x, core = position()
    place, tp = lax.axis_index("seq"), lax.axis_index("tp")
    full, hidden = r.full, r.hidden

    def line(ref):
        return ref[...].reshape(1, -1)

    chunks, width = full.shape[0], full.shape[5]
    third = chunks // 3
    low = jnp.bfloat16
    z_peers = [device(lax.rem(z + step, 4), x, core) for step in (1, 2, 3)]
    x_peer, core_peer = device(z, 1 - x, core), device(z, x, 1 - core)
    seq_peers = [(lax.rem(place + step, 16), tp) for step in range(1, 16)]
    greet(seq_peers + [other_half()])

    def slot(chunk, level):
        if chunk in X_FIRST:
            return full.at[chunk, level, :, core]
        return full.at[chunk, level, x, core]

    def up(chunk, hop):
        ref = slot(chunk, z - hop)
        peer = device(z + 1, x, core)
        return remote(ref, ref, r.z_sent.at[chunk, hop], r.z_got.at[chunk, hop], peer)

    def down(chunk, hop):
        ref = slot(chunk, z + hop)
        peer = device(z - 1, x, core)
        return remote(ref, ref, r.z_sent.at[chunk, 3 + hop], r.z_got.at[chunk, 3 + hop], peer)

    def from_below(chunk, hop):
        ref = slot(chunk, z - hop)
        peer = device(z - 1, x, core)
        return remote(ref, ref, r.z_sent.at[chunk, hop - 1], r.z_got.at[chunk, hop - 1], peer)

    def from_above(chunk, hop):
        ref = slot(chunk, z + hop)
        peer = device(z + 1, x, core)
        return remote(ref, ref, r.z_sent.at[chunk, 2 + hop], r.z_got.at[chunk, 2 + hop], peer)

    def along_x(chunk, level):
        ref = full.at[chunk, level, x, core]
        return remote(ref, ref, r.x_sent.at[chunk, level], r.x_got.at[chunk, level], x_peer)

    def along_core(chunk):
        ref = full.at[chunk, :, :, core]
        return remote(ref, ref, r.core_sems.at[0, chunk], r.core_sems.at[1, chunk], core_peer)

    def keep(chunk):
        return pltpu.make_async_copy(full.at[chunk], r.weights.at[chunk], r.kept.at[chunk])

    def columns(at):
        return slice(at * width, (at + 1) * width)

    def when(condition, action):
        pl.when(condition)(action)

    def z_start(chunk):
        when(z < 3, lambda: up(chunk, 0).start())
        when(z > 0, lambda: down(chunk, 0).start())

    def z_hop(chunk, hop):
        def below():
            from_below(chunk, hop).wait_recv()
            if hop < 3:
                when(z < 3, lambda: up(chunk, hop).start())
            if chunk not in X_FIRST:
                along_x(chunk, z - hop).start()

        def above():
            from_above(chunk, hop).wait_recv()
            if hop < 3:
                when(z > 0, lambda: down(chunk, hop).start())
            if chunk not in X_FIRST:
                along_x(chunk, z + hop).start()

        when(z >= hop, below)
        when(z + hop < 4, above)

    def own_columns(chunk):
        if chunk < 2 * third:
            return r.in_weight[:, chunk // third, columns(chunk % third)]
        return r.out_weight[:, columns(chunk - 2 * third)]

    def ready(step):
        return 0 <= step < chunks

    def pump(step):
        for first in [step + 1] if step else range(2):
            if ready(first):
                full[first, z, x, core] = own_columns(first).astype(low)
                along_x(first, z).start()
                if first not in X_FIRST:
                    z_start(first)
        for hop in range(4):
            chunk = step - 1 - hop
            if not ready(chunk):
                continue
            late = 1 if chunk in X_FIRST else 0
            if late and hop == 0:
                along_x(chunk, z).wait_recv()
                z_start(chunk)
            elif hop + 1 - late < 4 and hop + 1 - late > 0:
                z_hop(chunk, hop + 1 - late)
            if hop == 3:
                if late == 0:
                    wait_all([along_x(chunk, level) for level in range(4)])
                along_core(chunk).start()
        if ready(step - 5):
            along_core(step - 5).wait_recv()
            if step - 5 < 2 * third:
                keep(step - 5).start()

    def weights(chunk):
        return full[chunk].reshape(hidden.shape[1], width)

    def dot(left, right):
        return jnp.dot(left, right, preferred_element_type=jnp.float32)

    def dot_last(left, right):
        return lax.dot_general(
            left, right, (((1,), (1,)), ((), ())), preferred_element_type=jnp.float32
        )

    half_rows = r.block.shape[0]
    mine = pl.ds(pl.multiple_of(tp * half_rows, half_rows), half_rows)
    residual = r.block[...].astype(jnp.float32)
    inv_rms = lax.rsqrt(jnp.mean(residual * residual, axis=1, keepdims=True) + EPS_NORM)
    hidden[mine] = (residual * inv_rms * line(r.norm_gain)).astype(low)
    pair_sems = r.pair_sems
    swap = remote(hidden.at[mine], hidden.at[mine], pair_sems.at[0], pair_sems.at[1], other_half())
    swap.start()

    rows = hidden.shape[0]
    conv_in, conv_pre, conv_out, rim, ext = (
        r.conv_in,
        r.conv_pre,
        r.conv_out,
        r.rim,
        r.ext,
    )

    def rim_copy(tile):
        return remote(
            conv_in.at[rows - 16 :, columns(tile)],
            rim.at[:, columns(tile)],
            r.rim_sems.at[0, tile],
            r.rim_sems.at[1, tile],
            seq_peers[0],
        )

    def value_tile(tile):
        conv_in[:, columns(tile)] = dot(hidden[...], weights(tile)).astype(low)
        rim_copy(tile).start()

    masks = r.masks
    select_out = r.select_out

    def conv_tile(tile):
        rim_copy(tile).wait_recv()
        ext[0:8, :] = rim[8:16, columns(tile)].astype(jnp.float32)
        ext[8:, :] = conv_in[:, columns(tile)].astype(jnp.float32)
        conv_weight = r.conv_weight
        total = line(r.conv_bias)[:, columns(tile)] + conv_weight[0:1, columns(tile)] * ext[8:, :]
        for lag in range(1, 4):
            total = total + conv_weight[lag : lag + 1, columns(tile)] * (
                ext[8 - lag : 8 - lag + rows, :] * wide(masks[lag - 1], width)
            )
        conv_pre[:, columns(tile)] = total
        out = (total * jax.nn.sigmoid(total)).astype(low)
        conv_out[:, columns(tile)] = out
        select_low = r.select_weight[:, columns(tile)].astype(low)
        spare = jnp.zeros((select_out.shape[1] - select_low.shape[0], width), low)
        part = dot_last(out, jnp.concatenate([select_low, spare], axis=0))
        select_out[...] = part if tile == 0 else select_out[...] + part

    select_swap = remote(
        select_out, r.select_far, pair_sems.at[2], pair_sems.at[3], other_half()
    )
    enter, leave = r.enter, r.leave
    states = r.decay_log.shape[0]
    step_rank = r.step_weight.shape[0]
    held, drive = r.held, r.drive

    def select_stage():
        select_swap.wait()
        select_out[...] = select_out[...] + r.select_far[...]
        turned = select_out[:, step_rank : step_rank + 128].T
        for at in range(rows):
            enter[at] = jnp.broadcast_to(turned[:states, at : at + 1], (states, 128))
            leave[at] = jnp.broadcast_to(turned[states : 2 * states, at : at + 1], (states, 128))

    def step_tile(tile):
        here = columns(tile)
        step_low = r.step_weight[:, here].astype(low)
        pre = dot(select_out[:, :step_rank].astype(low), step_low) + line(r.step_bias)[:, here]
        size = jnp.maximum(pre, 0.0) + jnp.log1p(jnp.exp(-jnp.abs(pre)))
        r.step_pre[:, here] = pre
        r.step_size[:, here] = size
        held[:, here] = jnp.where(wide(masks[0], width) > 0.0, size, RESET)
        drive[:, here] = size * conv_out[:, here].astype(jnp.float32)

    piece = r.state_piece

    def rate_of(here):
        return -jnp.exp(r.decay_log[:, here]) * LOG2E

    def state_tile(tile):
        here = columns(tile)
        rate = rate_of(here)

        def block(index, state):
            base = pl.multiple_of(index * 8, 8)
            for offset in range(8):
                at = base + offset
                kept = jnp.exp2(rate * held[pl.ds(at, 1), here])
                state = kept * state + wide(enter[at], width) * drive[pl.ds(at, 1), here]
            return state

        piece[0:states, here] = lax.fori_loop(
            0, rows // 8, block, jnp.zeros((states, width), jnp.float32)
        )
        total = jnp.sum(held[:, here], axis=0, keepdims=True)
        piece[states:, here] = jnp.broadcast_to(total, (8, width))

    chain_out, chain_home, chain_middle, chain_end = chain_parts(
        False, piece, lambda: rate_of(own_lanes(place)), r.start, r.come, r.back, r.chain_sems
    )
    scanned, start = r.scanned, r.start

    def scan_tile(tile):
        here = columns(tile)
        rate = rate_of(here)

        def block(index, state):
            base = pl.multiple_of(index * 8, 8)
            for offset in range(8):
                at = base + offset
                kept = jnp.exp2(rate * held[pl.ds(at, 1), here])
                state = kept * state + wide(enter[at], width) * drive[pl.ds(at, 1), here]
                scanned[pl.ds(at, 1), here] = jnp.sum(
                    wide(leave[at], width) * state, axis=0, keepdims=True
                )
            return state

        lax.fori_loop(0, rows // 8, block, start[:, here])

    gate = r.gate

    def gate_tile(tile):
        gate[:, columns(tile)] = dot(hidden[...], weights(third + tile))

    def out_tile(tile):
        here = columns(tile)
        out_weight = weights(2 * third + tile)
        value = conv_out[:, here].astype(jnp.float32)
        mixed = scanned[:, here] + line(r.skip_gain)[:, here] * value
        pre = gate[:, here]
        sigmoid = jax.nn.sigmoid(pre)
        act = pre * sigmoid
        gated = (mixed * act).astype(low)
        r.gated[:, here] = gated
        d_gated = dot(r.cot[...], out_weight)
        d_mixed = d_gated * act
        r.d_mixed[:, here] = d_mixed
        slope = sigmoid * (1.0 + pre * (1.0 - sigmoid))
        r.d_gate[:, here] = (d_gated * mixed * slope).astype(low)
        r.skip_grad[:, here] = jnp.sum(d_mixed * value, axis=0, keepdims=True)
        part = dot_last(gated, out_weight)
        r.branch[...] = part if tile == 0 else r.branch[...] + part

    def adjoint_tile(tile):
        here = columns(tile)
        rate = rate_of(here)

        def block(index, state):
            base = pl.multiple_of((rows // 8 - 1 - index) * 8, 8)
            for offset in range(7, -1, -1):
                at = base + offset
                kept = jnp.exp2(rate * held[pl.ds(at, 1), here])
                state = kept * (state + wide(leave[at], width) * r.d_mixed[pl.ds(at, 1), here])
            return state

        r.piece[0:states, here] = lax.fori_loop(
            0, rows // 8, block, jnp.zeros((states, width), jnp.float32)
        )
        total = jnp.sum(held[:, here], axis=0, keepdims=True)
        r.piece[states:, here] = jnp.broadcast_to(total, (8, width))

    def turn(source, target):
        for at in range(target.shape[0]):
            value = source[:, at * 128 : (at + 1) * 128].astype(jnp.float32)
            target[at % 2 * 8 + at // 2 % 2 * 4 + at // 4] = value.T.astype(low)

    for step in range(third + 5):
        pump(step)
        if step == 0:
            turn(r.cot, r.cot_t)
        if step == 2:
            swap.wait()
            turn(hidden, r.hidden_t)
        if step >= 5:
            value_tile(step - 5)
        if step >= 6:
            conv_tile(step - 6)
    conv_tile(third - 1)
    select_swap.start()
    pump(third + 5)
    gate_tile(0)
    select_stage()
    for tile in range(third):
        step_tile(tile)
    pump(third + 6)
    gate_tile(1)
    for tile in range(third):
        state_tile(tile)
    chain_out()
    chain_middle()
    pump(third + 7)
    gate_tile(2)
    chain_home()
    for tile in range(third):
        scan_tile(tile)
    pump(third + 8)
    gate_tile(3)
    for tile in range(third):
        pump(2 * third + 5 + tile)
        out_tile(tile)
        adjoint_tile(tile)
    chain_end()
    for chunk in range(chunks):
        for hop in range(3):
            when((z < 3) & (z >= hop), up(chunk, hop).wait_send)
            when((z > 0) & (z + hop < 4), down(chunk, hop).wait_send)
        for level in range(4):
            if chunk not in X_FIRST:
                along_x(chunk, level).wait_send()
        if chunk in X_FIRST:
            along_x(chunk, z).wait_send()
        along_core(chunk).wait_send()
        if chunk < 2 * third:
            keep(chunk).wait()
    for tile in range(third):
        rim_copy(tile).wait_send()


def own_lanes(at):
    return pl.ds(pl.multiple_of(at * 128, 128), 128)


def chain_parts(backward, piece, rate_own, out, come, back, sems):
    place = lax.axis_index("seq")
    peers = [(lax.rem(place + step, 16), lax.axis_index("tp")) for step in range(1, 16)]
    states = out.shape[0]

    def away(at):
        return remote(
            piece.at[:, own_lanes(peers[at][0])],
            come.at[place],
            sems.at[0, at],
            sems.at[1, at],
            peers[at],
        )

    def home(at):
        return remote(
            back.at[peers[at][0]],
            out.at[:, own_lanes(place)],
            sems.at[2, at],
            sems.at[3, at],
            peers[at],
        )

    def begin():
        for at in range(15):
            away(at).start()
        come[place] = piece[:, own_lanes(place)]

    def middle():
        rate = rate_own()
        for at in range(15):
            away(at).wait_recv()

        def join(index, state):
            at = 15 - index if backward else index
            back[at] = state
            part = come[at]
            return jnp.exp2(rate * part[states : states + 1]) * state + part[:states]

        lax.fori_loop(0, 16, join, jnp.zeros((states, 128), jnp.float32))
        for at in range(15):
            home(at).start()
        out[:, own_lanes(place)] = back[place]

    def arrive():
        for at in range(15):
            home(at).wait_recv()

    def end():
        for at in range(15):
            away(at).wait_send()
            home(at).wait_send()

    return begin, arrive, middle, end


def forward_block(ident, given):
    half_rows, model = given.block.shape
    rows = 2 * half_rows
    share, inner = given.out_weight.shape
    total = 3 * inner
    states = given.decay_log.shape[0]
    f32, low = jnp.float32, jnp.bfloat16
    vmem = pl.BlockSpec(memory_space=pltpu.VMEM)
    dma = pltpu.SemaphoreType.DMA
    width = 512
    chunks = total // width
    select_rows = 256

    def like(columns, dtype):
        return jax.ShapeDtypeStruct((rows, columns), dtype)

    lanes = jax.ShapeDtypeStruct((rows, states, 128), f32)
    outs = pl.pallas_call(
        forward_block_kernel,
        in_specs=[vmem] * len(ForwardIn._fields),
        out_specs=[vmem] * (len(ForwardOut._fields) - 1) + [pl.BlockSpec(memory_space=pltpu.HBM)],
        out_shape=[
            jax.ShapeDtypeStruct((16, share, rows), low),
            jax.ShapeDtypeStruct((16, share, rows), low),
            jax.ShapeDtypeStruct((states + 8, inner), f32),
            like(inner, low),
            jax.ShapeDtypeStruct((16, inner), low),
            like(inner, f32),
            like(inner, low),
            like(select_rows, f32),
            like(inner, f32),
            like(inner, f32),
            like(inner, f32),
            like(inner, f32),
            lanes,
            lanes,
            jax.ShapeDtypeStruct((states, inner), f32),
            like(inner, low),
            like(inner, f32),
            like(inner, low),
            like(model, f32),
            jax.ShapeDtypeStruct((1, inner), f32),
            jax.ShapeDtypeStruct((chunks * 2 // 3, 4, 2, 2, share, width), low),
        ],
        scratch_shapes=[
            pltpu.VMEM((rows, model), low),
            pltpu.VMEM((chunks, 4, 2, 2, share, width), low),
            pltpu.VMEM((rows + 8, width), f32),
            pltpu.VMEM((rows, inner), f32),
            pltpu.VMEM((rows, inner), f32),
            pltpu.VMEM((states + 8, inner), f32),
            pltpu.VMEM((16, states + 8, 128), f32),
            pltpu.VMEM((16, states, 128), f32),
            pltpu.VMEM((rows, select_rows), f32),
            dma((chunks, 6)),
            dma((chunks, 6)),
            dma((chunks, 4)),
            dma((chunks, 4)),
            dma((2, chunks)),
            dma((chunks,)),
            dma((2, chunks // 3)),
            dma((4, 15)),
            dma((4,)),
        ],
        compiler_params=pltpu.CompilerParams(
            collective_id=ident, has_side_effects=True, vmem_limit_bytes=FINISH_LIMIT
        ),
    )(*given)
    out = ForwardOut(*outs)
    return out._replace(weights=out.weights.reshape(-1, model, width))


class BackwardIn(NamedTuple):
    hidden_t: object
    cot_t: object
    gated: object
    d_gate: object
    piece: object
    d_mixed: object
    held: object
    drive: object
    enter: object
    leave: object
    start: object
    conv_out: object
    step_pre: object
    step_size: object
    conv_pre: object
    conv_in: object
    rim: object
    select_out: object
    branch: object
    block: object
    skip_grad: object
    masks: object
    masks_after: object
    conv_weight: object
    skip_gain: object
    select_weight: object
    step_weight: object
    decay_log: object


class BackwardOut(NamedTuple):
    out_grad: object
    gate_grad: object
    block_out: object
    d_value: object
    extra: object


class BackwardWork(NamedTuple):
    come: object
    back: object
    follow: object
    kept: object
    state: object
    drive_grad: object
    d_step_pre: object
    decay_grad: object
    enter_grad: object
    leave_grad: object
    select_grad: object
    select_far: object
    conv_grad: object
    rim_next: object
    ext: object
    branch_send: object
    branch_far: object
    chain_sems: object
    pair_sems: object
    rim_sems: object


def backward_block_kernel(*refs):
    r, rest = gathered(refs, BackwardIn, BackwardOut, BackwardWork)
    z, x, core = position()
    place, tp = lax.axis_index("seq"), lax.axis_index("tp")
    low = jnp.bfloat16
    seq_peers = [(lax.rem(place + step, 16), tp) for step in range(1, 16)]
    greet(seq_peers + [other_half()])
    rows, inner = r.held.shape
    main = Reducer(
        [(r.cot_t, r.gated, at, r.out_grad, at) for at in range(0, inner, SHARE_WIDTH)]
        + [
            (r.hidden_t, r.d_gate, at, r.gate_grad, at)
            for at in range(0, r.gate_grad.shape[1], SHARE_WIDTH)
        ],
        rest,
    )
    states = r.decay_log.shape[0]
    width = 512
    tiles = inner // width
    pair_sems = r.pair_sems

    def columns(at):
        return slice(at * width, (at + 1) * width)

    def dot(left, right):
        return jnp.dot(left, right, preferred_element_type=jnp.float32)

    def dot_last(left, right):
        return lax.dot_general(
            left, right, (((1,), (1,)), ((), ())), preferred_element_type=jnp.float32
        )

    def line(ref):
        return ref[...].reshape(1, -1)

    half_rows = r.block.shape[0]
    own_half = pl.ds(pl.multiple_of(tp * half_rows, half_rows), half_rows)
    far_half = pl.ds(pl.multiple_of((1 - tp) * half_rows, half_rows), half_rows)
    r.branch_send[...] = r.branch[far_half, :].astype(low)
    branch_swap = remote(
        r.branch_send, r.branch_far, pair_sems.at[0], pair_sems.at[1], other_half()
    )
    branch_swap.start()

    held, drive, grad = r.held, r.drive, r.d_mixed
    enter, leave, piece = r.enter, r.leave, r.piece

    def rate_of(here):
        return -jnp.exp(r.decay_log[:, here])

    chain_out, chain_home, chain_middle, chain_end = chain_parts(
        True,
        piece,
        lambda: rate_of(own_lanes(place)) * LOG2E,
        r.follow,
        r.come,
        r.back,
        r.chain_sems,
    )
    kept_all, state_all = r.kept, r.state
    drive_grad, d_step_pre = r.drive_grad, r.d_step_pre
    enter_grad, leave_grad = r.enter_grad, r.leave_grad

    def again_tile(tile):
        here = columns(tile)
        rate = rate_of(here) * LOG2E

        def block(index, state):
            base = pl.multiple_of(index * 8, 8)
            for offset in range(8):
                at = base + offset
                kept = jnp.exp2(rate * held[pl.ds(at, 1), here])
                kept_all[at] = kept
                state = kept * state + wide(enter[at], width) * drive[pl.ds(at, 1), here]
                state_all[at + 1] = state
            return state

        start = r.start[:, here]
        state_all[0] = start
        lax.fori_loop(0, rows // 8, block, start)

    def reverse_tile(tile):
        here = columns(tile)
        rate = rate_of(here)

        def block(index, carry):
            follow, decay = carry
            base = pl.multiple_of((rows // 8 - 1 - index) * 8, 8)
            for offset in range(7, -1, -1):
                at = base + offset
                now = grad[pl.ds(at, 1), here]
                adjoint = wide(leave[at], width) * now + follow
                drive_grad[pl.ds(at, 1), here] = jnp.sum(
                    adjoint * wide(enter[at], width), axis=0, keepdims=True
                )
                enters = fold_lanes(adjoint * drive[pl.ds(at, 1), here])
                leaves = fold_lanes(state_all[at + 1] * now)
                if tile == 0:
                    enter_grad[at], leave_grad[at] = enters, leaves
                else:
                    enter_grad[at] += enters
                    leave_grad[at] += leaves
                follow = kept_all[at] * adjoint
                part = follow * state_all[at]
                r.ext[pl.ds(at, 1), :] = jnp.sum(part * rate, axis=0, keepdims=True)
                decay = decay + part * held[pl.ds(at, 1), here]
            return follow, decay

        follow = r.follow[:, here]
        _, decay = lax.fori_loop(0, rows // 8, block, (follow, jnp.zeros_like(follow)))
        r.decay_grad[:, here] = decay * rate
        d_step = (
            drive_grad[:, here] * r.conv_out[:, here].astype(jnp.float32) + r.ext[0:rows, :]
        )
        d_step_pre[:, here] = (d_step * jax.nn.sigmoid(r.step_pre[:, here])).astype(low)

    step_rank = r.step_weight.shape[0]
    select_grad = r.select_grad
    extra = r.extra

    def turned(value):
        return value.astype(jnp.float32).T.astype(low)

    def store_extra(first, tile, value):
        for at in range(width // 128):
            owner = tile * (width // 128) + at
            extra[owner // 2, owner % 2, first : first + value.shape[0], :] = value[
                :, at * 128 : (at + 1) * 128
            ].astype(low)

    def select_start():
        step_in = turned(r.select_out[:, :step_rank])
        total = jnp.zeros((rows, step_rank), jnp.float32)
        for tile in range(tiles):
            here = columns(tile)
            total = total + dot_last(d_step_pre[:, here], r.step_weight[:, here].astype(low))
            store_extra(0, tile, dot(step_in, d_step_pre[:, here]))
        select_grad[:, :step_rank] = total
        row_at = lax.broadcasted_iota(jnp.int32, (8, states, 128), 1)
        lane_at = lax.broadcasted_iota(jnp.int32, (8, states, 128), 2)

        def block(index, _):
            base = pl.multiple_of(index * 8, 8)
            here = pl.ds(base, 8)
            enters = jnp.sum(enter_grad[here], axis=2, keepdims=True)
            leaves = jnp.sum(leave_grad[here], axis=2, keepdims=True)
            spread = jnp.where(lane_at == row_at, enters, 0.0)
            spread = jnp.where(lane_at == row_at + states, leaves, spread)
            select_grad[here, step_rank:] = jnp.sum(spread, axis=1)
            return 0

        lax.fori_loop(0, rows // 8, block, 0)
        select_swap.start()

    select_swap = remote(
        select_grad, r.select_far, pair_sems.at[2], pair_sems.at[3], other_half()
    )
    conv_grad, rim_next, ext = r.conv_grad, r.rim_next, r.ext

    def rim_copy(tile):
        return remote(
            conv_grad.at[0:8, columns(tile)],
            rim_next.at[:, columns(tile)],
            r.rim_sems.at[0, tile],
            r.rim_sems.at[1, tile],
            seq_peers[14],
        )

    select_count = r.select_weight.shape[0]

    def select_end():
        select_swap.wait()
        total = (select_grad[...] + r.select_far[...]).astype(low)
        select_low = total[:, :256]
        first, second = turned(select_low[:, :128]), turned(select_low[:, 128:])
        for tile in range(tiles):
            here = columns(tile)
            conv_out = r.conv_out[:, here]
            store_extra(step_rank, tile, dot(first, conv_out))
            store_extra(step_rank + 128, tile, dot(second[: select_count - 128], conv_out))
            weight = r.select_weight[:, here].astype(low)
            spare = jnp.zeros((256 - select_count, width), low)
            d_conv = (
                drive_grad[:, here] * r.step_size[:, here]
                + grad[:, here] * line(r.skip_gain)[:, here]
                + dot(select_low, jnp.concatenate([weight, spare], axis=0))
            )
            pre = r.conv_pre[:, here]
            sigmoid = jax.nn.sigmoid(pre)
            conv_grad[:, here] = d_conv * (sigmoid * (1.0 + pre * (1.0 - sigmoid)))
            rim_copy(tile).start()
            if tile % 2:
                main.advance()

    masks, masks_after = r.masks, r.masks_after

    def conv_tile(tile):
        here = columns(tile)
        value = conv_grad[:, here]
        weight = r.conv_weight
        lines = []
        ext[0:8, :] = r.rim[8:16, here].astype(jnp.float32)
        ext[8:, :] = r.conv_in[:, here].astype(jnp.float32)
        for lag in range(4):
            shifted = ext[8 - lag : 8 - lag + rows, :]
            if lag > 0:
                shifted = shifted * wide(masks[lag - 1], width)
            lines.append(jnp.sum(value * shifted, axis=0, keepdims=True))
        lines.append(jnp.sum(value, axis=0, keepdims=True))
        lines.append(
            jnp.sum(d_step_pre[:, here].astype(jnp.float32), axis=0, keepdims=True)
        )
        lines.append(r.skip_grad[:, here])
        lines.append(jnp.zeros((9, width), jnp.float32))
        first = step_rank + select_count
        store_extra(first, tile, r.decay_grad[:, here])
        store_extra(first + states, tile, jnp.concatenate(lines, axis=0))
        rim_copy(tile).wait_recv()
        ext[0:rows, :] = value
        ext[rows:, :] = rim_next[:, here]
        total = weight[0:1, here] * value
        for lag in range(1, 4):
            total = total + weight[lag : lag + 1, here] * (
                ext[lag : lag + rows, :] * wide(masks_after[lag - 1], width)
            )
        r.d_value[:, here] = total.astype(low)

    chain_out()
    main.advance(2)
    chain_middle()
    again_tile(0)
    main.advance(1)
    chain_home()
    for tile in range(tiles):
        if tile > 0:
            again_tile(tile)
            main.advance()
        reverse_tile(tile)
        main.advance()
    select_start()
    main.advance()
    branch_swap.wait()
    r.block_out[...] = (
        r.block[...].astype(jnp.float32)
        + r.branch[own_half, :]
        + r.branch_far[...].astype(jnp.float32)
    )
    select_end()
    main.advance()
    for tile in range(tiles):
        conv_tile(tile)
        main.advance()
    main.advance(main.chunks + 5)
    chain_end()
    main.drain()
    for tile in range(tiles):
        rim_copy(tile).wait_send()


def backward_block(ident, given):
    rows, inner = given.held.shape
    half_rows, model = given.block.shape
    states = given.decay_log.shape[0]
    small_rows = given.step_weight.shape[0] + given.select_weight.shape[0] + states + 16
    f32, low = jnp.float32, jnp.bfloat16
    vmem = pl.BlockSpec(memory_space=pltpu.VMEM)
    dma = pltpu.SemaphoreType.DMA
    share = model // 16
    outs = pl.pallas_call(
        backward_block_kernel,
        in_specs=[vmem] * len(BackwardIn._fields),
        out_specs=[vmem] * len(BackwardOut._fields),
        out_shape=[
            jax.ShapeDtypeStruct((share, inner), f32),
            jax.ShapeDtypeStruct((share, GATE_EARLY), f32),
            jax.ShapeDtypeStruct((half_rows, model), f32),
            jax.ShapeDtypeStruct((rows, inner), low),
            jax.ShapeDtypeStruct((8, 2, small_rows, 128), low),
        ],
        scratch_shapes=[
            pltpu.VMEM((16, states + 8, 128), f32),
            pltpu.VMEM((16, states, 128), f32),
            pltpu.VMEM((states, inner), f32),
            pltpu.VMEM((rows, states, 512), f32),
            pltpu.VMEM((rows + 1, states, 512), f32),
            pltpu.VMEM((rows, inner), f32),
            pltpu.VMEM((rows, inner), low),
            pltpu.VMEM((states, inner), f32),
            pltpu.VMEM((rows, states, 128), f32),
            pltpu.VMEM((rows, states, 128), f32),
            pltpu.VMEM((rows, 256), f32),
            pltpu.VMEM((rows, 256), f32),
            pltpu.VMEM((rows, inner), f32),
            pltpu.VMEM((8, inner), f32),
            pltpu.VMEM((rows + 8, 512), f32),
            pltpu.VMEM((half_rows, model), low),
            pltpu.VMEM((half_rows, model), low),
            dma((4, 15)),
            dma((4,)),
            dma((2, inner // 512)),
        ]
        + reducer_scratch(inner + GATE_EARLY, share, SHARE_WIDTH),
        compiler_params=pltpu.CompilerParams(
            collective_id=ident, has_side_effects=True, vmem_limit_bytes=FINISH_LIMIT
        ),
    )(*given)
    return BackwardOut(*outs)


def on_device(
    block_in,
    cotangent,
    segment_ids,
    norm_gain,
    in_weight,
    out_weight,
    conv_weight,
    conv_bias,
    select_weight,
    step_weight,
    step_bias,
    decay_log,
    skip_gain,
    norm_moment,
    in_rows,
    in_cols,
    out_rows,
    out_cols,
    conv_rows,
    conv_cols,
    bias_moment,
    select_rows,
    select_cols,
    step_rows,
    step_cols,
    step_moment,
    decay_rows,
    decay_cols,
    skip_moment,
):
    tp_count = lax.axis_size("tp")
    seq_index = lax.axis_index("seq")
    tp_index = lax.axis_index("tp")
    seq_first = (seq_index == 0).astype(jnp.float32)
    tp_first = (tp_index == 0).astype(jnp.float32)
    half_rows, model_dim = block_in.shape
    row_count = cotangent.shape[0]
    inner_dim = in_weight.shape[2]
    channels = inner_dim * tp_count
    conv_taps = conv_weight.shape[0]
    states = decay_log.shape[0]
    step_rank = step_weight.shape[0]
    row_share = in_weight.shape[0]
    id_padded = jnp.concatenate(
        [
            jnp.full((conv_taps - 1,), -1, jnp.int32),
            segment_ids,
            jnp.full((conv_taps - 1,), -2, jnp.int32),
        ]
    )
    window = lax.dynamic_slice_in_dim(
        id_padded, seq_index * row_count, row_count + 2 * (conv_taps - 1)
    )
    local_ids = window[conv_taps - 1 : conv_taps - 1 + row_count]
    keep_mask = (local_ids == window[conv_taps - 2 : conv_taps - 2 + row_count]).astype(jnp.float32)
    residual = block_in.astype(jnp.float32)
    mean_sq = jnp.mean(residual * residual, axis=1, keepdims=True)
    inv_rms = lax.rsqrt(mean_sq + EPS_NORM)
    normed = residual * inv_rms
    low_type = jnp.bfloat16
    projected, hidden, in_full = project(
        (normed * norm_gain[None, :]).astype(low_type),
        in_weight.astype(low_type).reshape(row_share, 2 * inner_dim),
        0,
    )
    out_low, projected = lax.optimization_barrier((out_weight.astype(low_type), projected))
    out_full = lax.all_gather(out_low, "seq", axis=0, tiled=True)
    conv_in = projected[:, :inner_dim].astype(jnp.bfloat16)
    gate_pre = projected[:, inner_dim:]
    rim_rows = passed_along(conv_in[row_count - (conv_taps - 1) :], "seq", 1)
    ext_rows = jnp.concatenate([rim_rows, conv_in], axis=0).astype(jnp.float32)
    same_docs = []
    conv_pre = jnp.zeros_like(gate_pre) + conv_bias[None, :]
    for shift_lag in range(conv_taps):
        first_row = conv_taps - 1 - shift_lag
        same_doc = (window[first_row : first_row + row_count] == local_ids).astype(jnp.float32)[
            :, None
        ]
        same_docs.append(same_doc)
        conv_pre = (
            conv_pre
            + conv_weight[shift_lag][None, :]
            * ext_rows[first_row : first_row + row_count]
            * same_doc
        )
    conv_out = jax.nn.silu(conv_pre).astype(jnp.bfloat16)
    conv_value = conv_out.astype(jnp.float32)
    select_low = select_weight.astype(jnp.bfloat16)
    select_out = pair_sum(
        jnp.einsum("te,ke->tk", conv_out, select_low, preferred_element_type=jnp.float32), 1
    )
    step_in = select_out[:, :step_rank].astype(jnp.bfloat16)
    state_in = select_out[:, step_rank : step_rank + states]
    state_out = select_out[:, step_rank + states :]
    step_low = step_weight.astype(jnp.bfloat16)
    step_pre = jnp.dot(step_in, step_low, preferred_element_type=jnp.float32) + step_bias[None, :]
    step_size = jax.nn.softplus(step_pre)
    decay_rate = -jnp.exp(decay_log)
    drive = step_size * conv_value
    held_step = jnp.where(keep_mask[:, None] > 0.0, step_size, RESET)
    enter = jnp.broadcast_to(state_in[:, :, None], (row_count, states, 128))
    leave = jnp.broadcast_to(state_out[:, :, None], (row_count, states, 128))
    nothing = jnp.zeros((8, 128), jnp.float32)
    start, _ = chain(
        piece_state(held_step, drive, enter, decay_rate, False), decay_rate, nothing, False, 2
    )
    scanned = scan_forward(held_step, drive, enter, leave, decay_rate, start)
    mixed = scanned + skip_gain[None, :] * conv_value
    gate_act = jax.nn.silu(gate_pre)
    gated = (mixed * gate_act).astype(jnp.bfloat16)
    branch = jnp.einsum("te,de->td", gated, out_full, preferred_element_type=jnp.float32)
    own_rows, far_rows = tp_index * half_rows, (1 - tp_index) * half_rows
    d_gated = jnp.einsum("td,de->te", cotangent, out_full, preferred_element_type=jnp.float32)
    d_out_w = jnp.einsum("td,te->de", cotangent, gated, preferred_element_type=jnp.float32)
    out_half = lax.psum_scatter(
        d_out_w.astype(low_type), "seq", scatter_dimension=0, tiled=True
    )
    d_mixed = d_gated * gate_act
    d_gate = (d_gated * mixed * silu_slope(gate_pre)).astype(jnp.bfloat16)
    skip_grad = jnp.sum(d_mixed * conv_value, axis=0)
    follow, branch_far = chain(
        piece_state(held_step, d_mixed, leave, decay_rate, True),
        decay_rate,
        lax.dynamic_slice_in_dim(branch, far_rows, half_rows, 0).astype(low_type),
        True,
        3,
    )
    block_out = (
        residual
        + lax.dynamic_slice_in_dim(branch, own_rows, half_rows, 0)
        + branch_far.astype(jnp.float32)
    )
    drive_grad, step_grad, decay_grad, enter_grad, leave_grad = scan_backward(
        held_step, drive, d_mixed, enter, leave, decay_rate, start, follow
    )
    enter_grad = jnp.sum(enter_grad, axis=2)
    leave_grad = jnp.sum(leave_grad, axis=2)
    d_step = drive_grad * conv_value + step_grad
    d_step_pre = (d_step * jax.nn.sigmoid(step_pre)).astype(jnp.bfloat16)
    step_bias_grad = jnp.sum(d_step_pre.astype(jnp.float32), axis=0)
    step_w_grad = jnp.einsum("tr,te->re", step_in, d_step_pre, preferred_element_type=jnp.float32)
    d_step_in = jnp.einsum("te,re->tr", d_step_pre, step_low, preferred_element_type=jnp.float32)
    select_grads = jnp.concatenate(
        [d_step_in, enter_grad, leave_grad],
        axis=1,
    )
    d_select = pair_sum(select_grads, 4).astype(jnp.bfloat16)
    select_w_grad = jnp.einsum("tk,te->ke", d_select, conv_out, preferred_element_type=jnp.float32)
    d_conv = (
        drive_grad * step_size
        + d_mixed * skip_gain[None, :]
        + jnp.einsum("tk,ke->te", d_select, select_low, preferred_element_type=jnp.float32)
    )
    d_conv_pre = d_conv * silu_slope(conv_pre)
    rim_next = passed_along(d_conv_pre[: conv_taps - 1], "seq", -1)
    ext_grads = jnp.concatenate([d_conv_pre, rim_next], axis=0)
    ids_after = window[conv_taps - 1 :]
    d_conv_in = jnp.zeros_like(d_conv_pre)
    conv_w_rows = []
    for shift_lag in range(conv_taps):
        first_row = conv_taps - 1 - shift_lag
        later_same = (ids_after[shift_lag : shift_lag + row_count] == local_ids).astype(
            jnp.float32
        )[:, None]
        d_conv_in = (
            d_conv_in
            + conv_weight[shift_lag][None, :]
            * ext_grads[shift_lag : shift_lag + row_count]
            * later_same
        )
        conv_w_rows.append(
            jnp.sum(
                d_conv_pre * ext_rows[first_row : first_row + row_count] * same_docs[shift_lag],
                axis=0,
            )
        )
    conv_w_grad = jnp.stack(conv_w_rows, axis=0)
    conv_b_grad = jnp.sum(d_conv_pre, axis=0)
    d_projected = jnp.concatenate([d_conv_in.astype(jnp.bfloat16), d_gate], axis=1)
    d_hidden = jnp.einsum(
        "tkn,kdn->td",
        d_projected.reshape(row_count, in_full.shape[0], -1),
        in_full,
        preferred_element_type=jnp.float32,
    )
    vector_grads = jnp.stack([conv_b_grad, step_bias_grad, skip_grad], axis=0)
    small_grads = jnp.concatenate(
        [step_w_grad, select_w_grad, decay_grad, conv_w_grad, vector_grads], axis=0
    )
    out_grad = out_half.astype(jnp.float32)
    in_grad = lax.psum_scatter(
        jnp.einsum("td,tn->dn", hidden, d_projected, preferred_element_type=jnp.float32),
        "seq",
        scatter_dimension=0,
        tiled=True,
    )
    small_full = lax.psum(small_grads, "seq")
    d_hidden = lax.psum_scatter(d_hidden, "tp", scatter_dimension=0, tiled=True)
    in_grad = in_grad.reshape(in_weight.shape)
    gain_part = jnp.sum(d_hidden * normed, axis=0)
    scaled = d_hidden * norm_gain[None, :]
    cot_half = lax.dynamic_slice_in_dim(cotangent, own_rows, half_rows, 0).astype(
        jnp.float32
    )
    input_grad = cot_half + inv_rms * (
        scaled - normed * jnp.mean(scaled * normed, axis=1, keepdims=True)
    )
    edges = [step_rank, select_weight.shape[0], states, conv_taps, 3]
    edges = [sum(edges[:at]) for at in range(len(edges) + 1)]
    step_local, select_local, decay_local, conv_local, vector_local = [
        small_full[low:high] for low, high in zip(edges, edges[1:])
    ]
    in_square = in_grad * in_grad
    out_square = out_grad * out_grad
    in_row_part = jnp.sum(in_square, axis=(1, 2))
    out_row_part = jnp.sum(out_square, axis=1)
    small_row_part = jnp.sum(small_full * small_full, axis=1)
    in_total = jnp.sum(DECAY * in_rows + (1.0 - DECAY) * EPS_FACTOR) * tp_first + (
        1.0 - DECAY
    ) * jnp.sum(in_row_part) / (2 * channels)
    out_total = jnp.sum(DECAY * out_rows + (1.0 - DECAY) * EPS_FACTOR) * tp_first + (
        1.0 - DECAY
    ) * jnp.sum(out_row_part) / channels
    seq_part = jnp.concatenate(
        [jnp.sum(in_square, axis=0).reshape(-1, 128), jnp.sum(out_square, axis=0).reshape(-1, 128)]
    )
    shared_part = jnp.concatenate(
        [
            gain_part.reshape(-1, 128),
            jnp.broadcast_to(in_total, (8, 128)),
            jnp.broadcast_to(out_total, (8, 128)),
        ]
    )
    row_parts = jnp.concatenate([in_row_part, out_row_part, small_row_part])
    row_parts = jnp.pad(row_parts, (0, -row_parts.shape[0] % 1024)).reshape(-1, 128)
    col_sums, shared_sums, row_sums = sum_over(seq_part, shared_part, row_parts)
    col_sums = col_sums.reshape(-1)
    in_col_sums = col_sums[: 2 * inner_dim].reshape(2, inner_dim)
    out_col_sums = col_sums[2 * inner_dim :]
    gain_grad = shared_sums[: model_dim // 128].reshape(-1)
    in_mean = shared_sums[model_dim // 128, 0] / model_dim
    out_mean = shared_sums[model_dim // 128 + 8, 0] / model_dim
    row_sums = row_sums.reshape(-1)
    in_row_sums = row_sums[:row_share]
    out_row_sums = row_sums[row_share : 2 * row_share]
    small_row_sums = row_sums[2 * row_share :]
    in_rows_new = DECAY * in_rows + (1.0 - DECAY) * (in_row_sums / (2 * channels) + EPS_FACTOR)
    in_cols_new = DECAY * in_cols + (1.0 - DECAY) * (in_col_sums / model_dim + EPS_FACTOR)
    out_rows_new = DECAY * out_rows + (1.0 - DECAY) * (out_row_sums / channels + EPS_FACTOR)
    out_cols_new = DECAY * out_cols + (1.0 - DECAY) * (out_col_sums / model_dim + EPS_FACTOR)
    step_rows_new, step_cols_new, stepw_update = factor_update(
        step_local, small_row_sums[edges[0] : edges[1]], step_rows, step_cols, channels
    )
    select_rows_new, select_cols_new, select_update = factor_update(
        select_local, small_row_sums[edges[1] : edges[2]], select_rows, select_cols, channels
    )
    decay_rows_new, decay_cols_new, decay_update = factor_update(
        decay_local, small_row_sums[edges[2] : edges[3]], decay_rows, decay_cols, channels
    )
    conv_rows_new, conv_cols_new, conv_update = factor_update(
        conv_local, small_row_sums[edges[3] : edges[4]], conv_rows, conv_cols, channels
    )
    bias_moment_new, convb_update = moment_update(vector_local[0], bias_moment)
    step_moment_new, stepb_update = moment_update(vector_local[1], step_moment)
    skip_moment_new, skip_update = moment_update(vector_local[2], skip_moment)
    gain_moment_new, gain_update = moment_update(gain_grad, norm_moment)
    in_update = in_grad * lax.rsqrt(in_rows_new[:, None, None] * in_cols_new[None] / in_mean)
    out_update = out_grad * lax.rsqrt(out_rows_new[:, None] * out_cols_new[None, :] / out_mean)
    squares = jnp.stack(
        [
            sum_squares(in_update),
            sum_squares(out_update),
            seq_first * sum_squares(conv_update),
            seq_first * sum_squares(select_update),
            seq_first * sum_squares(stepw_update),
            seq_first * sum_squares(decay_update),
            seq_first * sum_squares(convb_update),
            seq_first * sum_squares(stepb_update),
            seq_first * sum_squares(skip_update),
        ]
    )
    _, clip_totals, _ = sum_over(
        nothing, jnp.broadcast_to(jnp.pad(squares, (0, 7))[:, None], (16, 128)), nothing
    )
    clip_totals = clip_totals[:, 0]
    gain_new = apply_step(norm_gain, gain_update, sum_squares(gain_update), model_dim, RATES[0])
    in_new = apply_step(in_weight, in_update, clip_totals[0], model_dim * 2 * channels, RATES[1])
    out_new = apply_step(out_weight, out_update, clip_totals[1], model_dim * channels, RATES[2])
    convw_new = apply_step(conv_weight, conv_update, clip_totals[2], conv_taps * channels, RATES[3])
    convb_new = apply_step(conv_bias, convb_update, clip_totals[6], channels, RATES[4])
    select_new = apply_step(
        select_weight, select_update, clip_totals[3], select_weight.shape[0] * channels, RATES[5]
    )
    stepw_new = apply_step(
        step_weight, stepw_update, clip_totals[4], step_rank * channels, RATES[6]
    )
    stepb_new = apply_step(step_bias, stepb_update, clip_totals[7], channels, RATES[7])
    decay_new = apply_step(decay_log, decay_update, clip_totals[5], states * channels, RATES[8])
    skip_new = apply_step(skip_gain, skip_update, clip_totals[8], channels, RATES[9])
    return (
        block_out,
        input_grad,
        gain_grad,
        gain_new,
        gain_new.astype(low_type),
        gain_moment_new,
        in_grad,
        in_new,
        in_new.astype(low_type),
        in_rows_new,
        in_cols_new,
        out_grad,
        out_new,
        out_new.astype(low_type),
        out_rows_new,
        out_cols_new,
        conv_local,
        convw_new,
        convw_new.astype(low_type),
        conv_rows_new,
        conv_cols_new,
        vector_local[0],
        convb_new,
        convb_new.astype(low_type),
        bias_moment_new,
        select_local,
        select_new,
        select_new.astype(low_type),
        select_rows_new,
        select_cols_new,
        step_local,
        stepw_new,
        stepw_new.astype(low_type),
        step_rows_new,
        step_cols_new,
        vector_local[1],
        stepb_new,
        stepb_new.astype(low_type),
        step_moment_new,
        decay_local,
        decay_new,
        decay_new.astype(low_type),
        decay_rows_new,
        decay_cols_new,
        vector_local[2],
        skip_new,
        skip_new.astype(low_type),
        skip_moment_new,
    )


def on_block_device(
    block_in,
    cotangent,
    segment_ids,
    norm_gain,
    in_weight,
    out_weight,
    conv_weight,
    conv_bias,
    select_weight,
    step_weight,
    step_bias,
    decay_log,
    skip_gain,
    norm_moment,
    in_rows,
    in_cols,
    out_rows,
    out_cols,
    conv_rows,
    conv_cols,
    bias_moment,
    select_rows,
    select_cols,
    step_rows,
    step_cols,
    step_moment,
    decay_rows,
    decay_cols,
    skip_moment,
):
    tp_count = lax.axis_size("tp")
    seq_index = lax.axis_index("seq")
    tp_index = lax.axis_index("tp")
    half_rows, model_dim = block_in.shape
    row_count = cotangent.shape[0]
    inner_dim = in_weight.shape[2]
    channels = inner_dim * tp_count
    conv_taps = conv_weight.shape[0]
    states = decay_log.shape[0]
    step_rank = step_weight.shape[0]
    row_share = in_weight.shape[0]
    low_type = jnp.bfloat16
    id_padded = jnp.concatenate(
        [
            jnp.full((conv_taps - 1,), -1, jnp.int32),
            segment_ids,
            jnp.full((conv_taps - 1,), -2, jnp.int32),
        ]
    )
    window = lax.dynamic_slice_in_dim(
        id_padded, seq_index * row_count, row_count + 2 * (conv_taps - 1)
    )
    local_ids = window[conv_taps - 1 : conv_taps - 1 + row_count]
    same_docs = [
        (window[conv_taps - 1 - lag : conv_taps - 1 - lag + row_count] == local_ids).astype(
            jnp.float32
        )[:, None]
        for lag in range(conv_taps)
    ]
    masks = jnp.broadcast_to(jnp.stack(same_docs[1:]), (conv_taps - 1, row_count, 128))
    ids_after = window[conv_taps - 1 :]
    same_after = [
        (ids_after[lag : lag + row_count] == local_ids).astype(jnp.float32)[:, None]
        for lag in range(1, conv_taps)
    ]
    masks_after = jnp.broadcast_to(jnp.stack(same_after), (conv_taps - 1, row_count, 128))
    lanes = jnp.concatenate(
        [step_rows, select_rows, decay_rows, conv_rows, jnp.ones((76,), jnp.float32)]
        + [in_rows, out_rows, jnp.ones((384,), jnp.float32)]
    ).reshape(8, 128)
    f = forward_block(
        0,
        ForwardIn(
        in_weight=in_weight,
        out_weight=out_weight,
        block=block_in,
        cot=cotangent,
        norm_gain=norm_gain,
        conv_weight=conv_weight,
        conv_bias=conv_bias,
        step_bias=step_bias,
        skip_gain=skip_gain,
        masks=masks,
        select_weight=select_weight,
        step_weight=step_weight,
        decay_log=decay_log,
        ),
    )
    back = backward_block(
        1,
        BackwardIn(
            block=block_in,
            masks=masks,
            masks_after=masks_after,
            conv_weight=conv_weight,
            skip_gain=skip_gain,
            select_weight=select_weight,
            step_weight=step_weight,
            decay_log=decay_log,
            **shared(f, BackwardIn),
        ),
    )
    new = finish(
        2,
        channels,
        FinishIn(
            hidden_t=f.hidden_t,
            d_gate=f.d_gate,
            weights=f.weights,
            block=block_in,
            cot=cotangent,
            lanes=lanes,
            norm_gain=norm_gain,
            norm_moment=norm_moment,
            in_cols=in_cols,
            out_cols=out_cols,
            step_cols=step_cols,
            select_cols=select_cols,
            decay_cols=decay_cols,
            conv_cols=conv_cols,
            bias_moment=bias_moment,
            step_moment=step_moment,
            skip_moment=skip_moment,
            conv_bias=conv_bias,
            step_bias=step_bias,
            skip_gain=skip_gain,
            **shared(back, FinishIn),
        ),
    )
    return renew(
        RenewIn(
            value_grad=new.in_grad,
            gate_grad=new.in_grad,
            out_grad=back.out_grad,
            block_out=back.block_out,
            in_weight=in_weight,
            out_weight=out_weight,
            step_weight=step_weight,
            select_weight=select_weight,
            decay_log=decay_log,
            conv_weight=conv_weight,
            **shared(new, RenewIn),
        )
    )


def solution(mesh):
    on_slice = mesh.shape["seq"] == 16 and mesh.shape["tp"] == 2
    return jax.shard_map(
        on_block_device if on_slice else on_device,
        mesh=mesh,
        in_specs=(
            P(("seq", "tp"), None),
            P("seq", None),
            P(),
            P(),
            P("seq", None, "tp"),
            P("seq", "tp"),
            P(None, "tp"),
            P("tp"),
            P(None, "tp"),
            P(None, "tp"),
            P("tp"),
            P(None, "tp"),
            P("tp"),
            P(),
            P("seq"),
            P(None, "tp"),
            P("seq"),
            P("tp"),
            P(),
            P("tp"),
            P("tp"),
            P(),
            P("tp"),
            P(),
            P("tp"),
            P("tp"),
            P(),
            P("tp"),
            P("tp"),
        ),
        out_specs=(
            P(("seq", "tp"), None),
            P(("seq", "tp"), None),
            P(),
            P(),
            P(),
            P(),
            P("seq", None, "tp"),
            P("seq", None, "tp"),
            P("seq", None, "tp"),
            P("seq"),
            P(None, "tp"),
            P("seq", "tp"),
            P("seq", "tp"),
            P("seq", "tp"),
            P("seq"),
            P("tp"),
            P(None, "tp"),
            P(None, "tp"),
            P(None, "tp"),
            P(),
            P("tp"),
            P("tp"),
            P("tp"),
            P("tp"),
            P("tp"),
            P(None, "tp"),
            P(None, "tp"),
            P(None, "tp"),
            P(),
            P("tp"),
            P(None, "tp"),
            P(None, "tp"),
            P(None, "tp"),
            P(),
            P("tp"),
            P("tp"),
            P("tp"),
            P("tp"),
            P("tp"),
            P(None, "tp"),
            P(None, "tp"),
            P(None, "tp"),
            P(),
            P("tp"),
            P("tp"),
            P("tp"),
            P("tp"),
            P("tp"),
        ),
        check_vma=False,
    )
```

```python
import functools
from types import SimpleNamespace
from typing import NamedTuple

import jax
import jax.numpy as jnp
from jax import lax
from jax.experimental import pallas as pl
from jax.experimental.pallas import tpu as pltpu
from jax.sharding import PartitionSpec as P

EPS_NORM = 1e-05
EPS_FACTOR = 1e-30
DECAY = 0.5
CLIP = 0.5
RATES = (0.45, 0.02, 0.03, 0.1, 0.05, 0.016, 0.09, 1.8, 0.3, 0.45)
MESH = pl.DeviceIdType.MESH
LOG2E = 1.4426950408889634
RESET = 1e9
TILE = 512
X_FIRST = (4, 8)
SHARE_WIDTH = 256
SLOTS = 8
RENEW_TILES = 4
VMEM_LIMIT = 48 * 1024 * 1024
FINISH_LIMIT = 63 * 1024 * 1024


def passed_along(value, axis, steps):
    count = lax.axis_size(axis)
    initial, last = (max(0, -steps), min(count, count - steps))
    return lax.ppermute(value, axis, [(source, source + steps) for source in range(initial, last)])


def silu_slope(values):
    sigmoid_v = jax.nn.sigmoid(values)
    return sigmoid_v * (1.0 + values * (1.0 - sigmoid_v))


def factor_update(grad, row_sums, rows_old, cols_old, channels):
    rows_new = DECAY * rows_old + (1.0 - DECAY) * (row_sums / channels + EPS_FACTOR)
    cols_new = DECAY * cols_old + (1.0 - DECAY) * (jnp.mean(grad * grad, axis=0) + EPS_FACTOR)
    scale_sq = rows_new[:, None] * cols_new[None, :] / jnp.mean(rows_new)
    return (rows_new, cols_new, grad * lax.rsqrt(scale_sq))


def moment_update(grad_in, moment_old):
    moment_new = DECAY * moment_old + (1.0 - DECAY) * (grad_in * grad_in + EPS_FACTOR)
    return (moment_new, grad_in * lax.rsqrt(moment_new))


def sum_squares(update):
    return jnp.sum(update * update)


def apply_step(weight, update, total_sum, count_all, step_rate):
    root_mean = jnp.sqrt(total_sum / count_all)
    return weight - step_rate * update / jnp.maximum(1.0, root_mean / CLIP)


def wide(tile, width):
    return jnp.concatenate([tile] * (width // tile.shape[1]), axis=1)


def fold_lanes(value):
    pieces = [value[:, at : at + 128] for at in range(0, value.shape[1], 128)]
    while len(pieces) > 1:
        pieces = [first + second for first, second in zip(pieces[::2], pieces[1::2])]
    return pieces[0]


def state_kernel(backward, step_ref, value_ref, lane_ref, rate_ref, out_ref):
    rows, width = step_ref.shape
    states = rate_ref.shape[0]
    rate = rate_ref[...] * LOG2E

    def block(index, state):
        base = pl.multiple_of((rows // 8 - 1 - index if backward else index) * 8, 8)
        for offset in range(8):
            at = base + (7 - offset if backward else offset)
            keep = jnp.exp2(rate * step_ref[pl.ds(at, 1), :])
            term = wide(lane_ref[at], width) * value_ref[pl.ds(at, 1), :]
            state = keep * (state + term) if backward else keep * state + term
        return state

    out_ref[0:states, :] = lax.fori_loop(0, rows // 8, block, jnp.zeros((states, width), jnp.float32))
    total = jnp.sum(step_ref[...], axis=0, keepdims=True)
    out_ref[states:, :] = jnp.broadcast_to(total, (out_ref.shape[0] - states, width))


def piece_state(step, value, lane, rate, backward):
    rows, width = step.shape
    states = rate.shape[0]
    tile = TILE
    return pl.pallas_call(
        functools.partial(state_kernel, backward),
        grid=(width // tile,),
        in_specs=[
            pl.BlockSpec((rows, tile), lambda i: (0, i)),
            pl.BlockSpec((rows, tile), lambda i: (0, i)),
            pl.BlockSpec((rows, states, 128), lambda i: (0, 0, 0)),
            pl.BlockSpec((states, tile), lambda i: (0, i)),
        ],
        out_specs=pl.BlockSpec((states + 8, tile), lambda i: (0, i)),
        out_shape=jax.ShapeDtypeStruct((states + 8, width), jnp.float32),
        compiler_params=pltpu.CompilerParams(vmem_limit_bytes=VMEM_LIMIT),
    )(step, value, lane, rate)


def forward_kernel(
    step_ref, drive_ref, enter_ref, leave_ref, rate_ref, start_ref, out_ref
):
    rows, width = step_ref.shape
    rate = rate_ref[...] * LOG2E

    def block(index, state):
        base = pl.multiple_of(index * 8, 8)
        for offset in range(8):
            at = base + offset
            keep = jnp.exp2(rate * step_ref[pl.ds(at, 1), :])
            state = keep * state + wide(enter_ref[at], width) * drive_ref[pl.ds(at, 1), :]
            out_ref[pl.ds(at, 1), :] = jnp.sum(
                wide(leave_ref[at], width) * state, axis=0, keepdims=True
            )
        return state

    lax.fori_loop(0, rows // 8, block, start_ref[...])


def scan_forward(step, drive, enter, leave, rate, start):
    rows, width = step.shape
    states = rate.shape[0]
    tile = TILE
    by_tile = pl.BlockSpec((rows, tile), lambda i: (0, i))
    by_state = pl.BlockSpec((states, tile), lambda i: (0, i))
    whole = pl.BlockSpec((rows, states, 128), lambda i: (0, 0, 0))
    return pl.pallas_call(
        forward_kernel,
        grid=(width // tile,),
        in_specs=[by_tile, by_tile, whole, whole, by_state, by_state],
        out_specs=by_tile,
        out_shape=jax.ShapeDtypeStruct((rows, width), jnp.float32),
        compiler_params=pltpu.CompilerParams(vmem_limit_bytes=VMEM_LIMIT),
    )(step, drive, enter, leave, rate, start)


def backward_kernel(
    step_ref,
    drive_ref,
    grad_ref,
    enter_ref,
    leave_ref,
    rate_ref,
    start_ref,
    follow_ref,
    drive_grad_ref,
    step_grad_ref,
    decay_ref,
    enter_grad_ref,
    leave_grad_ref,
    kept_ref,
    state_ref,
):
    rows, width = step_ref.shape
    rate_own = rate_ref[...]
    rate = rate_own * LOG2E

    @pl.when(pl.program_id(0) == 0)
    def _():
        enter_grad_ref[...] = jnp.zeros_like(enter_grad_ref)
        leave_grad_ref[...] = jnp.zeros_like(leave_grad_ref)

    def again(index, state):
        base = pl.multiple_of(index * 8, 8)
        for offset in range(8):
            at = base + offset
            keep = jnp.exp2(rate * step_ref[pl.ds(at, 1), :])
            kept_ref[at] = keep
            state = keep * state + wide(enter_ref[at], width) * drive_ref[pl.ds(at, 1), :]
            state_ref[at + 1] = state
        return state

    start = start_ref[...]
    state_ref[0] = start
    lax.fori_loop(0, rows // 8, again, start)
    follow = follow_ref[...]

    def block(index, carry):
        follow, decay = carry
        base = pl.multiple_of((rows // 8 - 1 - index) * 8, 8)
        for offset in range(7, -1, -1):
            at = base + offset
            grad = grad_ref[pl.ds(at, 1), :]
            adjoint = wide(leave_ref[at], width) * grad + follow
            drive_grad_ref[pl.ds(at, 1), :] = jnp.sum(
                adjoint * wide(enter_ref[at], width), axis=0, keepdims=True
            )
            enter_grad_ref[at] += fold_lanes(adjoint * drive_ref[pl.ds(at, 1), :])
            leave_grad_ref[at] += fold_lanes(state_ref[at + 1] * grad)
            follow = kept_ref[at] * adjoint
            part = follow * state_ref[at]
            step_grad_ref[pl.ds(at, 1), :] = jnp.sum(part * rate_own, axis=0, keepdims=True)
            decay = decay + part * step_ref[pl.ds(at, 1), :]
        return follow, decay

    _, decay = lax.fori_loop(0, rows // 8, block, (follow, jnp.zeros_like(follow)))
    decay_ref[...] = decay * rate_own


def scan_backward(step, drive, grad, enter, leave, rate, start, follow):
    rows, width = step.shape
    states = rate.shape[0]
    tile = TILE
    by_tile = pl.BlockSpec((rows, tile), lambda i: (0, i))
    by_state = pl.BlockSpec((states, tile), lambda i: (0, i))
    whole = pl.BlockSpec((rows, states, 128), lambda i: (0, 0, 0))
    return pl.pallas_call(
        backward_kernel,
        grid=(width // tile,),
        in_specs=[by_tile, by_tile, by_tile, whole, whole, by_state, by_state, by_state],
        out_specs=[by_tile, by_tile, by_state, whole, whole],
        out_shape=[
            jax.ShapeDtypeStruct((rows, width), jnp.float32),
            jax.ShapeDtypeStruct((rows, width), jnp.float32),
            jax.ShapeDtypeStruct((states, width), jnp.float32),
            jax.ShapeDtypeStruct((rows, states, 128), jnp.float32),
            jax.ShapeDtypeStruct((rows, states, 128), jnp.float32),
        ],
        scratch_shapes=[
            pltpu.VMEM((rows, states, tile), jnp.float32),
            pltpu.VMEM((rows + 1, states, tile), jnp.float32),
        ],
        compiler_params=pltpu.CompilerParams(vmem_limit_bytes=VMEM_LIMIT),
    )(step, drive, grad, enter, leave, rate, start, follow)


def on_block():
    return lax.axis_size("seq") == 16 and lax.axis_size("tp") == 2


def position():
    place = lax.axis_index("seq")
    return lax.div(place, 4), lax.rem(lax.div(place, 2), 2), lax.rem(place, 2)


def device(z, x, core):
    return (z * 4 + x * 2 + core, lax.axis_index("tp"))


def other_half():
    return (lax.axis_index("seq"), 1 - lax.axis_index("tp"))


def greet(peers):
    barrier = pltpu.get_barrier_semaphore()
    for peer in peers:
        pl.semaphore_signal(barrier, inc=1, device_id=peer, device_id_type=MESH)
    pl.semaphore_wait(barrier, len(peers))


def remote(source, target, sent, arrived, peer):
    return pltpu.make_async_remote_copy(
        src_ref=source,
        dst_ref=target,
        send_sem=sent,
        recv_sem=arrived,
        device_id=peer,
        device_id_type=MESH,
    )


def sum_over(seq_part, shared_part, tp_part):
    return lax.psum(seq_part, "seq"), lax.psum(shared_part, ("seq", "tp")), lax.psum(tp_part, "tp")


def project(half, weight, ident):
    hidden = lax.all_gather(half, "tp", axis=0, tiled=True)
    full = lax.all_gather(weight, "seq", axis=0, tiled=True)
    return jnp.dot(hidden, full, preferred_element_type=jnp.float32), hidden, full[None]


def pair_kernel(mine_ref, out_ref, far, sent, arrived):
    greet([other_half()])
    copy = remote(mine_ref, far, sent, arrived, other_half())
    copy.start()
    copy.wait()
    out_ref[...] = mine_ref[...] + far[...]


def pair_sum(value, ident):
    if not on_block():
        return lax.psum(value, "tp")
    vmem = pl.BlockSpec(memory_space=pltpu.VMEM)
    return pl.pallas_call(
        pair_kernel,
        in_specs=[vmem],
        out_specs=vmem,
        out_shape=jax.ShapeDtypeStruct(value.shape, value.dtype),
        scratch_shapes=[
            pltpu.VMEM(value.shape, value.dtype),
            pltpu.SemaphoreType.DMA,
            pltpu.SemaphoreType.DMA,
        ],
        compiler_params=pltpu.CompilerParams(collective_id=ident, has_side_effects=True),
    )(value)


def chain_kernel(backward, piece_ref, rate_ref, swap_ref, out_ref, swapped_ref, come, back, sems, swap_sems):
    place = lax.axis_index("seq")
    states = rate_ref.shape[0]
    peers = [(lax.rem(place + step, 16), lax.axis_index("tp")) for step in range(1, 16)]
    greet(peers + [other_half()])
    swap = remote(swap_ref, swapped_ref, swap_sems.at[0], swap_sems.at[1], other_half())
    swap.start()

    def lanes(at):
        return pl.ds(pl.multiple_of(at * 128, 128), 128)

    def out(at):
        return remote(
            piece_ref.at[:, lanes(peers[at][0])],
            come.at[place],
            sems.at[0, at],
            sems.at[1, at],
            peers[at],
        )

    def home(at):
        return remote(
            back.at[peers[at][0]],
            out_ref.at[:, lanes(place)],
            sems.at[2, at],
            sems.at[3, at],
            peers[at],
        )

    for at in range(15):
        out(at).start()
    come[place] = piece_ref[:, lanes(place)]
    rate = rate_ref[:, lanes(place)] * LOG2E
    for at in range(15):
        out(at).wait_recv()

    def join(index, state):
        at = 15 - index if backward else index
        back[at] = state
        piece = come[at]
        return jnp.exp2(rate * piece[states : states + 1]) * state + piece[:states]

    lax.fori_loop(0, 16, join, jnp.zeros((states, 128), jnp.float32))
    for at in range(15):
        home(at).start()
    out_ref[:, lanes(place)] = back[place]
    for at in range(15):
        home(at).wait_recv()
    for at in range(15):
        out(at).wait_send()
        home(at).wait_send()
    swap.wait()


def chain(piece, rate, swap, backward, ident):
    states, width = rate.shape
    if not on_block():
        count, place = lax.axis_size("seq"), lax.axis_index("seq")
        pieces = lax.all_gather(piece, "seq")

        def join(index, state):
            at = count - 1 - index if backward else index
            longer = (
                jnp.exp2(rate * LOG2E * pieces[at, states : states + 1]) * state + pieces[at, :states]
            )
            return jnp.where(at > place if backward else at < place, longer, state)

        state = lax.fori_loop(0, count, join, jnp.zeros((states, width), jnp.float32))
        order = [(0, 1), (1, 0)]
        return state, lax.ppermute(swap, "tp", order)
    vmem = pl.BlockSpec(memory_space=pltpu.VMEM)
    return pl.pallas_call(
        functools.partial(chain_kernel, backward),
        in_specs=[vmem, vmem, vmem],
        out_specs=[vmem, vmem],
        out_shape=[
            jax.ShapeDtypeStruct((states, width), jnp.float32),
            jax.ShapeDtypeStruct(swap.shape, swap.dtype),
        ],
        scratch_shapes=[
            pltpu.VMEM((16, states + 8, 128), jnp.float32),
            pltpu.VMEM((16, states, 128), jnp.float32),
            pltpu.SemaphoreType.DMA((4, 15)),
            pltpu.SemaphoreType.DMA((2,)),
        ],
        compiler_params=pltpu.CompilerParams(collective_id=ident, has_side_effects=True),
    )(piece, rate, swap)


def wait_all(copies):
    for copy in copies:
        copy.wait_recv()


def gathered(refs, *groups):
    named, at = {}, 0
    for group in groups:
        named.update(zip(group._fields, refs[at:]))
        at += len(group._fields)
    return SimpleNamespace(**named), list(refs[at:])


def shared(source, group):
    return {name: value for name, value in source._asdict().items() if name in group._fields}


class Reducer:
    def __init__(self, jobs, refs):
        self.jobs, self.at = jobs, 0
        self.send, self.come = refs[:3], refs[3:6]
        self.sent, self.got, self.total = refs[6:9], refs[9:12], refs[12]
        self.z, self.x, self.core = position()
        self.chunks, self.width = len(jobs), self.come[2].shape[3]
        self.peers = [
            [device(self.z, self.x, 1 - self.core)],
            [device(self.z, 1 - self.x, self.core)],
            [device(lax.rem(self.z + step, 4), self.x, self.core) for step in (1, 2, 3)],
        ]

    def copies(self, level, chunk):
        slot = chunk % self.send[level].shape[0]
        if level < 2:
            return [
                remote(
                    self.send[level].at[slot],
                    self.come[level].at[chunk % SLOTS],
                    self.sent[level].at[chunk],
                    self.got[level].at[chunk],
                    self.peers[level][0],
                )
            ]
        return [
            remote(
                self.send[2].at[slot, 0, lax.rem(self.z + 1 + at, 4)],
                self.come[2].at[chunk % SLOTS, at],
                self.sent[2].at[chunk, at],
                self.got[2].at[chunk, at],
                self.peers[2][at],
            )
            for at in range(3)
        ]

    def free(self, level, chunk):
        older = chunk - self.send[level].shape[0]
        if older >= 0:
            for copy in self.copies(level, older):
                copy.wait_send()

    def product(self, chunk, first, count):
        left, right, start = self.jobs[chunk][:3]
        _, rows, depth = left.shape
        block = left[pl.ds(first, count)].reshape(count * rows, depth)
        value = jnp.dot(
            block, right[:, start : start + self.width], preferred_element_type=jnp.float32
        )
        return value.reshape(count, rows, self.width)

    def put(self, chunk, value, more):
        out, start = self.jobs[chunk][3:]
        here = slice(start, start + self.width)
        out[:, here] = out[:, here] + value if more else value

    def after_core(self, chunk, x):
        come = self.come[0][chunk % SLOTS, x].astype(jnp.float32)
        return self.product(chunk, self.core * 8 + x * 4, 4) + come

    def fill(self, level, chunk, values):
        self.free(level, chunk)
        slot = chunk % self.send[level].shape[0]
        for at, value in enumerate(values):
            self.send[level][slot, at] = value().astype(jnp.bfloat16)
        for copy in self.copies(level, chunk):
            copy.start()

    def stage(self, level, chunk):
        if not 0 <= chunk < self.chunks:
            return
        if level > 0:
            wait_all(self.copies(level - 1, chunk))
        if level == 0:
            away = (1 - self.core) * 8
            self.fill(
                0, chunk, [lambda at=at: self.product(chunk, away + at * 4, 4) for at in range(2)]
            )
        elif level == 1:
            self.fill(1, chunk, [lambda: self.after_core(chunk, 1 - self.x)])
        elif level == 2:
            come = self.come[1][chunk % SLOTS, 0].astype(jnp.float32)
            self.total[...] = self.after_core(chunk, self.x) + come
            self.fill(2, chunk, [lambda: self.total[...]])
            self.put(chunk, self.total[self.z], False)
        else:
            come = [self.come[2][chunk % SLOTS, at].astype(jnp.float32) for at in range(3)]
            self.put(chunk, (come[0] + come[1]) + come[2], True)

    def step(self, step):
        for level, lag in enumerate((0, 1, 3, 5)):
            self.stage(level, step - lag)

    def advance(self, count=1):
        for _ in range(count):
            if self.at < self.chunks + 5:
                self.step(self.at)
                self.at += 1

    def drain(self):
        for level in range(3):
            for chunk in range(max(0, self.chunks - self.send[level].shape[0]), self.chunks):
                for copy in self.copies(level, chunk):
                    copy.wait_send()


def reducer_scratch(columns, share, width):
    chunks = columns // width
    low, dma = jnp.bfloat16, pltpu.SemaphoreType.DMA
    return [
        pltpu.VMEM((4, 2, 4, share, width), low),
        pltpu.VMEM((4, 1, 4, share, width), low),
        pltpu.VMEM((4, 1, 4, share, width), low),
        pltpu.VMEM((SLOTS, 2, 4, share, width), low),
        pltpu.VMEM((SLOTS, 1, 4, share, width), low),
        pltpu.VMEM((SLOTS, 3, share, width), low),
        dma((chunks,)),
        dma((chunks,)),
        dma((chunks, 3)),
        dma((chunks,)),
        dma((chunks,)),
        dma((chunks, 3)),
        pltpu.VMEM((4, share, width), jnp.float32),
    ]


def rows_to_lanes(partial):
    return jnp.sum(partial.T, axis=0, keepdims=True)


def lanes_to_rows(row):
    return jnp.broadcast_to(row, (128, 128)).T


def finish_part(channels, model, r, main):
    z, x, core = position()
    place, tp = lax.axis_index("seq"), lax.axis_index("tp")
    core_peer, x_peer = device(z, x, 1 - core), device(z, 1 - x, core)
    z_peers = [device(lax.rem(z + step, 4), x, core) for step in (1, 2, 3)]
    low = jnp.bfloat16
    half_rows = r.block.shape[0]
    own_half = pl.ds(pl.multiple_of(tp * half_rows, half_rows), half_rows)
    far_half = pl.ds(pl.multiple_of((1 - tp) * half_rows, half_rows), half_rows)
    d_hidden = r.d_hidden
    swap = remote(
        d_hidden.at[far_half], r.come_half, r.half_sems.at[0], r.half_sems.at[1], other_half()
    )
    sides = [r.d_value, r.d_gate]
    kept_chunks, _, kept_width = r.weights.shape

    def fetch(chunk):
        return pltpu.make_async_copy(
            r.weights.at[chunk], r.fetched.at[chunk % 2], r.fetched_sems.at[chunk]
        )

    def hidden_stage(chunk):
        fetch(chunk).wait()
        per_side = kept_chunks // 2
        at = chunk % per_side
        part = lax.dot_general(
            sides[chunk // per_side][:, at * kept_width : (at + 1) * kept_width],
            r.fetched[chunk % 2],
            (((1,), (1,)), ((), ())),
            preferred_element_type=jnp.float32,
        )
        d_hidden[...] = part if chunk == 0 else d_hidden[...] + part
        if chunk + 2 < kept_chunks:
            fetch(chunk + 2).start()
        if chunk == kept_chunks - 1:
            swap.start()

    fetch(0).start()
    fetch(1).start()

    sent, got = r.extra_sent, r.extra_got
    extra, full = r.extra, r.full
    extra_core = remote(extra.at[:, 1 - core], r.come_core, sent.at[0], got.at[0], core_peer)
    extra_x = remote(r.send_x, r.come_x, sent.at[1], got.at[1], x_peer)
    extra_z = [
        remote(r.send_z.at[at], r.come_z.at[at], sent.at[2 + at], got.at[2 + at], z_peers[at])
        for at in range(3)
    ]
    own, held, halves = full.at[z, x, core], full.at[:, x, core], full.at[:, :, core]
    back_z = [remote(own, own, sent.at[5 + at], got.at[5 + at], z_peers[at]) for at in range(3)]
    back_x = remote(held, held, sent.at[8], got.at[8], x_peer)
    back_core = remote(halves, halves, sent.at[9], got.at[9], core_peer)

    def extra_after_core(pair):
        return extra[pair, core].astype(jnp.float32) + r.come_core[pair].astype(jnp.float32)

    def extra_after_x(level):
        return extra_after_core(level * 2 + x) + r.come_x[level].astype(jnp.float32)

    def extra_stage_x():
        extra_core.wait_recv()

        def one(level, _):
            r.send_x[level] = extra_after_core(level * 2 + 1 - x).astype(low)
            return 0

        lax.fori_loop(0, 4, one, 0)
        extra_x.start()

    def extra_stage_z():
        extra_x.wait_recv()

        def one(at, _):
            r.send_z[at] = extra_after_x(lax.rem(z + 1 + at, 4)).astype(low)
            return 0

        lax.fori_loop(0, 3, one, 0)
        for copy in extra_z:
            copy.start()

    def extra_stage_last():
        wait_all(extra_z)
        total = extra_after_x(z)
        for at in range(3):
            total = total + r.come_z[at].astype(jnp.float32)
        full[z, x, core] = total.astype(low)
        for copy in back_z:
            copy.start()

    def extra_back_x():
        wait_all(back_z)
        back_x.start()

    def extra_back_core():
        back_x.wait_recv()
        back_core.start()

    mine = r.mine
    vectors_new = r.vectors_new

    def line(ref):
        return ref[...].reshape(1, -1)

    in_tiles, out_tiles = r.in_grad.shape[1] // 128, r.out_grad.shape[1] // 128
    seq_rows = in_tiles + out_tiles
    gain_tiles = model // 128

    def put(base, row):
        for at in range(row.shape[1] // 128):
            mine[base + at : base + at + 1, :] = row[:, at * 128 : (at + 1) * 128]

    def take(ref, base, tiles):
        return jnp.concatenate([ref[base + at : base + at + 1, :] for at in range(tiles)], axis=1)

    def residual_stage():
        swap.wait()
        total = d_hidden[own_half, :] + r.come_half[...]
        residual = r.block[...].astype(jnp.float32)
        inv_rms = lax.rsqrt(jnp.mean(residual * residual, axis=1, keepdims=True) + EPS_NORM)
        normed = residual * inv_rms
        put(seq_rows, jnp.sum(total * normed, axis=0, keepdims=True))
        scaled = total * line(r.norm_gain)
        mean = jnp.mean(scaled * normed, axis=1, keepdims=True)
        r.input_grad[...] = r.cot[own_half, :].astype(jnp.float32) + inv_rms * (scaled - normed * mean)

    span = 512
    wide_span = span // 128
    small = r.small
    groups = {"step": (0, 128), "select": (128, 288), "decay": (288, 304), "conv": (304, 308)}
    pair = r.pair

    def put_rows(at, partial):
        pair[at : at + 1, :] = rows_to_lanes(partial)

    def fold_square(value):
        return fold_lanes(value * value)

    def small_stage():
        back_core.wait_recv()
        for block in range(16):
            small[:, block * 128 : (block + 1) * 128] = full[
                block // 4, block // 2 % 2, block % 2
            ].astype(jnp.float32)
        for at in range(3):
            rows = min(128, small.shape[0] - at * 128)

            def one(index, partial):
                columns = pl.ds(pl.multiple_of(index * span, span), span)
                return partial + fold_square(small[at * 128 : at * 128 + rows, columns])

            partial = lax.fori_loop(
                0, small.shape[1] // span, one, jnp.zeros((rows, 128), jnp.float32)
            )
            if rows < 128:
                partial = jnp.concatenate(
                    [partial, jnp.zeros((128 - rows, 128), jnp.float32)], axis=0
                )
            put_rows(at, partial)

    def column_sums(ref, base):
        def one(index, partial):
            columns = pl.ds(pl.multiple_of(index * span, span), span)
            value = ref[:, columns]
            sums = jnp.sum(value * value, axis=0, keepdims=True)
            for at in range(wide_span):
                mine[pl.ds(base + index * wide_span + at, 1), :] = sums[:, at * 128 : (at + 1) * 128]
            return partial + fold_square(value)

        return lax.fori_loop(
            0, ref.shape[1] // span, one, jnp.zeros((ref.shape[0], 128), jnp.float32)
        )

    def out_stage():
        put_rows(4, column_sums(r.out_grad, in_tiles))

    pair[...] = jnp.zeros(pair.shape, jnp.float32)
    extra_core.start()
    extra_steps = {1: extra_stage_x, 3: extra_stage_z, 5: extra_stage_last, 7: extra_back_x, 9: extra_back_core}
    extra_steps.update({14: residual_stage, 12: out_stage, 11: small_stage})
    for step in range(max(main.chunks + 5 - main.at, 16)):
        main.advance()
        if step < kept_chunks:
            hidden_stage(step)
        if step in extra_steps:
            extra_steps[step]()
    put_rows(3, column_sums(r.in_grad, 0))

    lanes = r.lanes
    row_at = lax.broadcasted_iota(jnp.int32, lanes.shape, 0)
    lane_at = lax.broadcasted_iota(jnp.int32, lanes.shape, 1)
    counts = jnp.where(row_at == 3, 2.0 * channels, 1.0 * channels)
    held_lanes = DECAY * lanes[...] + (1.0 - DECAY) * EPS_FACTOR
    part = jnp.where(tp == 0, held_lanes, 0.0) + (1.0 - DECAY) * pair[...] / counts

    def total(value):
        return jnp.sum(jnp.sum(value, axis=1, keepdims=True), axis=0, keepdims=True)

    base = seq_rows + gain_tiles
    for at in range(2):
        mean = total(jnp.where(row_at == 3 + at, part, 0.0)) / model
        mine[base + 8 * at : base + 8 * at + 8, :] = jnp.broadcast_to(mean, (8, 128))

    sums_sent, sums_got = r.sums_sent, r.sums_got

    def hop(at, source, target, peer):
        return remote(source, target, sums_sent.at[at], sums_got.at[at], peer)

    plane = x * 2 + core
    mates = [core_peer, x_peer, device(z, 1 - x, 1 - core)]
    across = [(lax.rem(z + step, 4) * 4 + plane, 1 - tp) for step in range(4)]

    def sum_hops(first, value, acc, far, shared):
        acc[plane] = value[...]
        copies = [hop(first + at, acc.at[plane], acc.at[plane], mates[at]) for at in range(3)]
        for copy in copies:
            copy.start()
        for copy in copies:
            copy.wait()
        acc[4 + z] = (acc[0] + acc[1]) + (acc[2] + acc[3])
        part = acc.at[4 + z]
        copies = [hop(first + 3 + at, part, part, z_peers[at]) for at in range(3)]
        copies += [
            hop(first + 6 + at, part.at[shared:], far.at[z], across[at]) for at in range(4)
        ]
        for copy in copies:
            copy.start()
        for copy in copies:
            copy.wait()
        value[...] = (acc[4] + acc[5]) + (acc[6] + acc[7])
        value[shared:] = value[shared:] + ((far[0] + far[1]) + (far[2] + far[3]))

    pair_copy = hop(20, pair, r.pair_far, other_half())
    pair_copy.start()
    sum_hops(0, mine, r.acc, r.far, seq_rows)
    pair_copy.wait()

    lanes_new = held_lanes + (1.0 - DECAY) * (pair[...] + r.pair_far[...]) / counts
    r.lanes_new[...] = lanes_new
    flat = row_at * 128 + lane_at
    means = jnp.where(row_at == 3, mine[base : base + 8, :], mine[base + 8 : base + 16, :])
    for low_edge, high_edge in groups.values():
        member = (flat >= low_edge) & (flat < high_edge)
        mean = total(jnp.where(member, lanes_new, 0.0)) / (high_edge - low_edge)
        means = jnp.where(member, mean, means)
    scale = lax.rsqrt(lanes_new / means)
    scales = [lanes_to_rows(scale[at : at + 1, :]) for at in range(5)]
    small_scale = jnp.concatenate(scales[:3], axis=0)
    in_scale, out_scale = scales[3], scales[4]

    def cols_new(old, sums, count):
        return DECAY * old + (1.0 - DECAY) * (sums / count + EPS_FACTOR)

    in_cols = cols_new(
        jnp.concatenate([r.in_cols[0:1, :], r.in_cols[1:2, :]], axis=1), take(mine, 0, in_tiles), model
    )
    half = in_cols.shape[1] // 2
    out_cols = cols_new(line(r.out_cols), take(mine, in_tiles, out_tiles), model)
    vectors_new[3:4, :] = in_cols[:, :half]
    vectors_new[4:5, :] = in_cols[:, half:]
    vectors_new[5:6, :] = out_cols

    def squares(ref, row_scale, first_row):
        def one(index, partial):
            columns = pl.ds(pl.multiple_of(index * span, span), span)
            col = vectors_new[pl.ds(first_row + lax.div(index, half // span), 1), pl.ds(
                pl.multiple_of(lax.rem(index, half // span) * span, span), span
            )]
            return partial + fold_square(ref[:, columns] * wide(row_scale, span) * lax.rsqrt(col))

        return total(
            lax.fori_loop(0, ref.shape[1] // span, one, jnp.zeros((ref.shape[0], 128), jnp.float32))
        )

    sums = [squares(r.in_grad, in_scale, 3), squares(r.out_grad, out_scale, 5)]
    group_cols = {
        "step": (line(r.step_cols), 8),
        "select": (line(r.select_cols), 7),
        "decay": (line(r.decay_cols), 9),
        "conv": (line(r.conv_cols), 6),
    }
    for name, (low_edge, high_edge) in groups.items():
        old_cols, new_row = group_cols[name]
        partial = jnp.zeros((high_edge - low_edge, 128), jnp.float32)
        for at in range(0, small.shape[1], span):
            columns = slice(at, at + span)
            value = small[low_edge:high_edge, columns]
            col = cols_new(
                old_cols[:, columns],
                jnp.sum(value * value, axis=0, keepdims=True),
                high_edge - low_edge,
            )
            vectors_new[new_row : new_row + 1, columns] = col
            row_scale = small_scale[low_edge:high_edge]
            partial = partial + fold_square(value * wide(row_scale, span) * lax.rsqrt(col))
        sums.append(total(partial))
    updates = []
    for at in range(3):
        value = small[308 + at : 309 + at, :]
        old = line((r.bias_moment, r.step_moment, r.skip_moment)[at])
        moment = DECAY * old + (1.0 - DECAY) * (value * value + EPS_FACTOR)
        vectors_new[24 + at : 25 + at, :] = moment
        vectors_new[18 + at : 19 + at, :] = value
        update = value * lax.rsqrt(moment)
        updates.append(update)
        sums.append(jnp.sum(update * update, axis=1, keepdims=True))
    totals = r.totals
    for at in range(9):
        totals[at : at + 1, :] = jnp.broadcast_to(sums[at], (1, 128))
    totals[9:16, :] = jnp.zeros((7, 128), jnp.float32)
    sum_hops(10, totals, r.totals_acc, r.totals_far, 0)

    def rate(at, count, step_rate, copies):
        root = jnp.sqrt(totals[at : at + 1, :] / (copies * count))
        return step_rate / jnp.maximum(1.0, root / CLIP)

    in_rate = rate(0, 2.0 * channels * model, RATES[1], 1)
    out_rate = rate(1, 1.0 * channels * model, RATES[2], 1)

    scales_out = r.scales
    scales_out[3] = in_scale * in_rate
    scales_out[4] = out_scale * out_rate
    small_rates = {"step": RATES[6], "select": RATES[5], "decay": RATES[8], "conv": RATES[3]}
    at_total = {"step": 2, "select": 3, "decay": 4, "conv": 5}
    row_number = lax.broadcasted_iota(jnp.int32, small_scale.shape, 0)
    for name, (low_edge, high_edge) in groups.items():
        step_rate = rate(
            at_total[name], 1.0 * (high_edge - low_edge) * channels, small_rates[name], 16
        )
        member = (row_number >= low_edge) & (row_number < high_edge)
        small_scale = jnp.where(member, small_scale * step_rate, small_scale)
    for at in range(3):
        scales_out[at] = small_scale[at * 128 : (at + 1) * 128, :]
    for at, step_rate in enumerate((RATES[4], RATES[7], RATES[9])):
        step_rate = rate(6 + at, 1.0 * channels, step_rate, 16)
        vectors_new[21 + at : 22 + at, :] = (
            line((r.conv_bias, r.step_bias, r.skip_gain)[at]) - wide(step_rate, half) * updates[at]
        )
    gain_grad = take(mine, seq_rows, gain_tiles)
    moment = DECAY * line(r.norm_moment) + (1.0 - DECAY) * (gain_grad * gain_grad + EPS_FACTOR)
    update = gain_grad * lax.rsqrt(moment)
    root = jnp.sqrt(jnp.mean(update * update, axis=1, keepdims=True))
    vectors_new[0:1, :] = gain_grad
    vectors_new[1:2, :] = line(r.norm_gain) - RATES[0] / jnp.maximum(1.0, root / CLIP) * update
    vectors_new[2:3, :] = moment
    vectors_new[10:18, :] = jnp.zeros((8, half), jnp.float32)
    vectors_new[27:32, :] = jnp.zeros((5, half), jnp.float32)

    for copy in [extra_core, extra_x] + extra_z + back_z + [back_x, back_core]:
        copy.wait_send()


class RenewIn(NamedTuple):
    value_grad: object
    gate_grad: object
    out_grad: object
    input_grad: object
    block_out: object
    small: object
    scales: object
    lanes_new: object
    vectors_new: object
    in_weight: object
    out_weight: object
    step_weight: object
    select_weight: object
    decay_log: object
    conv_weight: object


def renew_kernel(*refs):
    r, out = gathered(refs, RenewIn)
    cols, small, scales = r.vectors_new, r.small, r.scales
    span = small.shape[1]

    def write(*values):
        for value in values:
            ref = out.pop(0)
            ref[...] = value.astype(ref.dtype).reshape(ref.shape)

    def line(at):
        return cols[at : at + 1, :]

    def rows(low_edge, high_edge):
        flat = [r.lanes_new[at : at + 1, :] for at in range(5)]
        return jnp.concatenate(flat, axis=1)[:, low_edge:high_edge]

    def matrix(grad, weight, scale, col):
        new = weight - grad * wide(scale, span) * lax.rsqrt(line(col))
        write(grad, new, new)

    write(r.block_out[...], r.input_grad[...], line(0), line(1), line(1), line(2))
    in_refs = [out.pop(0) for _ in range(3)]
    for part, grad_ref in enumerate((r.value_grad, r.gate_grad)):
        grad = grad_ref[...]
        new = r.in_weight[:, part, :] - grad * wide(scales[3], span) * lax.rsqrt(line(3 + part))
        for ref, value in zip(in_refs, (grad, new, new)):
            ref[:, part, :] = value.astype(ref.dtype)
    write(rows(384, 512), cols[3:5, :])
    matrix(r.out_grad[...], r.out_weight[...], scales[4], 5)
    write(rows(512, 640), line(5))
    small_scale = jnp.concatenate([scales[0], scales[1], scales[2]], axis=0)
    matrix(small[304:308, :], r.conv_weight[...], small_scale[304:308], 6)
    write(rows(304, 308), line(6))
    write(line(18), line(21), line(21), line(24))
    matrix(small[128:288, :], r.select_weight[...], small_scale[128:288], 7)
    write(rows(128, 288), line(7))
    matrix(small[0:128, :], r.step_weight[...], small_scale[0:128], 8)
    write(rows(0, 128), line(8), line(19), line(22), line(22), line(25))
    matrix(small[288:304, :], r.decay_log[...], small_scale[288:304], 9)
    write(rows(288, 304), line(9))
    write(line(20), line(23), line(23), line(26))


def renew(given):
    f32, low = jnp.float32, jnp.bfloat16
    inner = given.out_grad.shape[1]
    shape = jax.ShapeDtypeStruct

    def three(ref):
        return [shape(ref.shape, f32), shape(ref.shape, f32), shape(ref.shape, low)]

    def vector(count):
        return shape((count,), f32)

    def trio(count):
        return [vector(count), vector(count), shape((count,), low)]

    model = given.block_out.shape[1]
    share = given.out_grad.shape[0]
    outs = (
        [shape(given.block_out.shape, f32), shape(given.input_grad.shape, f32)]
        + trio(model)
        + [vector(model)]
        + three(given.in_weight)
        + [vector(share), shape((2, inner), f32)]
        + three(given.out_weight)
        + [vector(share), vector(inner)]
        + three(given.conv_weight)
        + [vector(given.conv_weight.shape[0]), vector(inner)]
        + trio(inner)
        + [vector(inner)]
        + three(given.select_weight)
        + [vector(given.select_weight.shape[0]), vector(inner)]
        + three(given.step_weight)
        + [vector(given.step_weight.shape[0]), vector(inner)]
        + trio(inner)
        + [vector(inner)]
        + three(given.decay_log)
        + [vector(given.decay_log.shape[0]), vector(inner)]
        + trio(inner)
        + [vector(inner)]
    )
    span = inner // RENEW_TILES

    def by_tile(ref, first=0):
        *front, last = ref.shape
        if not front and last != inner:
            return pl.BlockSpec((last,), lambda i: (0,))
        zeros = (0,) * len(front)
        return pl.BlockSpec((*front, span), lambda i: zeros + (first + i,))

    def whole(ref):
        zeros = (0,) * len(ref.shape)
        return pl.BlockSpec(ref.shape, lambda i: zeros)

    specs = RenewIn(*[by_tile(ref) for ref in given])
    specs = specs._replace(
        gate_grad=by_tile(given.gate_grad, RENEW_TILES),
        scales=whole(given.scales),
        lanes_new=whole(given.lanes_new),
    )
    return tuple(
        pl.pallas_call(
            renew_kernel,
            grid=(RENEW_TILES,),
            in_specs=list(specs),
            out_specs=[by_tile(ref) for ref in outs],
            out_shape=outs,
            compiler_params=pltpu.CompilerParams(vmem_limit_bytes=FINISH_LIMIT),
        )(*given)
    )


class ForwardIn(NamedTuple):
    in_weight: object
    out_weight: object
    block: object
    cot: object
    norm_gain: object
    conv_weight: object
    conv_bias: object
    step_bias: object
    skip_gain: object
    masks: object
    select_weight: object
    step_weight: object
    decay_log: object


class ForwardOut(NamedTuple):
    hidden_t: object
    cot_t: object
    piece: object
    conv_in: object
    rim: object
    conv_pre: object
    conv_out: object
    select_out: object
    step_pre: object
    step_size: object
    held: object
    drive: object
    enter: object
    leave: object
    start: object
    gated: object
    d_mixed: object
    d_gate: object
    branch: object
    skip_grad: object
    weights: object


class ForwardWork(NamedTuple):
    hidden: object
    full: object
    ext: object
    gate: object
    scanned: object
    state_piece: object
    come: object
    back: object
    select_far: object
    z_sent: object
    z_got: object
    x_sent: object
    x_got: object
    core_sems: object
    kept: object
    rim_sems: object
    chain_sems: object
    pair_sems: object


def forward_block_kernel(*refs):
    r, _ = gathered(refs, ForwardIn, ForwardOut, ForwardWork)
    z, x, core = position()
    place, tp = lax.axis_index("seq"), lax.axis_index("tp")
    full, hidden = r.full, r.hidden

    def line(ref):
        return ref[...].reshape(1, -1)

    chunks, width = full.shape[0], full.shape[5]
    third = chunks // 3
    low = jnp.bfloat16
    z_peers = [device(lax.rem(z + step, 4), x, core) for step in (1, 2, 3)]
    x_peer, core_peer = device(z, 1 - x, core), device(z, x, 1 - core)
    seq_peers = [(lax.rem(place + step, 16), tp) for step in range(1, 16)]
    greet(seq_peers + [other_half()])

    def slot(chunk, level):
        if chunk in X_FIRST:
            return full.at[chunk, level, :, core]
        return full.at[chunk, level, x, core]

    def up(chunk, hop):
        ref = slot(chunk, z - hop)
        peer = device(z + 1, x, core)
        return remote(ref, ref, r.z_sent.at[chunk, hop], r.z_got.at[chunk, hop], peer)

    def down(chunk, hop):
        ref = slot(chunk, z + hop)
        peer = device(z - 1, x, core)
        return remote(ref, ref, r.z_sent.at[chunk, 3 + hop], r.z_got.at[chunk, 3 + hop], peer)

    def from_below(chunk, hop):
        ref = slot(chunk, z - hop)
        peer = device(z - 1, x, core)
        return remote(ref, ref, r.z_sent.at[chunk, hop - 1], r.z_got.at[chunk, hop - 1], peer)

    def from_above(chunk, hop):
        ref = slot(chunk, z + hop)
        peer = device(z + 1, x, core)
        return remote(ref, ref, r.z_sent.at[chunk, 2 + hop], r.z_got.at[chunk, 2 + hop], peer)

    def along_x(chunk, level):
        ref = full.at[chunk, level, x, core]
        return remote(ref, ref, r.x_sent.at[chunk, level], r.x_got.at[chunk, level], x_peer)

    def along_core(chunk):
        ref = full.at[chunk, :, :, core]
        return remote(ref, ref, r.core_sems.at[0, chunk], r.core_sems.at[1, chunk], core_peer)

    def keep(chunk):
        return pltpu.make_async_copy(full.at[chunk], r.weights.at[chunk], r.kept.at[chunk])

    def columns(at):
        return slice(at * width, (at + 1) * width)

    def when(condition, action):
        pl.when(condition)(action)

    def z_start(chunk):
        when(z < 3, lambda: up(chunk, 0).start())
        when(z > 0, lambda: down(chunk, 0).start())

    def z_hop(chunk, hop):
        def below():
            from_below(chunk, hop).wait_recv()
            if hop < 3:
                when(z < 3, lambda: up(chunk, hop).start())
            if chunk not in X_FIRST:
                along_x(chunk, z - hop).start()

        def above():
            from_above(chunk, hop).wait_recv()
            if hop < 3:
                when(z > 0, lambda: down(chunk, hop).start())
            if chunk not in X_FIRST:
                along_x(chunk, z + hop).start()

        when(z >= hop, below)
        when(z + hop < 4, above)

    def own_columns(chunk):
        if chunk < 2 * third:
            return r.in_weight[:, chunk // third, columns(chunk % third)]
        return r.out_weight[:, columns(chunk - 2 * third)]

    def ready(step):
        return 0 <= step < chunks

    def pump(step):
        for first in [step + 1] if step else range(2):
            if ready(first):
                full[first, z, x, core] = own_columns(first).astype(low)
                along_x(first, z).start()
                if first not in X_FIRST:
                    z_start(first)
        for hop in range(4):
            chunk = step - 1 - hop
            if not ready(chunk):
                continue
            late = 1 if chunk in X_FIRST else 0
            if late and hop == 0:
                along_x(chunk, z).wait_recv()
                z_start(chunk)
            elif hop + 1 - late < 4 and hop + 1 - late > 0:
                z_hop(chunk, hop + 1 - late)
            if hop == 3:
                if late == 0:
                    wait_all([along_x(chunk, level) for level in range(4)])
                along_core(chunk).start()
        if ready(step - 5):
            along_core(step - 5).wait_recv()
            if step - 5 < 2 * third:
                keep(step - 5).start()

    def weights(chunk):
        return full[chunk].reshape(hidden.shape[1], width)

    def dot(left, right):
        return jnp.dot(left, right, preferred_element_type=jnp.float32)

    def dot_last(left, right):
        return lax.dot_general(
            left, right, (((1,), (1,)), ((), ())), preferred_element_type=jnp.float32
        )

    half_rows = r.block.shape[0]
    mine = pl.ds(pl.multiple_of(tp * half_rows, half_rows), half_rows)
    residual = r.block[...].astype(jnp.float32)
    inv_rms = lax.rsqrt(jnp.mean(residual * residual, axis=1, keepdims=True) + EPS_NORM)
    hidden[mine] = (residual * inv_rms * line(r.norm_gain)).astype(low)
    pair_sems = r.pair_sems
    swap = remote(hidden.at[mine], hidden.at[mine], pair_sems.at[0], pair_sems.at[1], other_half())
    swap.start()

    rows = hidden.shape[0]
    conv_in, conv_pre, conv_out, rim, ext = (
        r.conv_in,
        r.conv_pre,
        r.conv_out,
        r.rim,
        r.ext,
    )

    def rim_copy(tile):
        return remote(
            conv_in.at[rows - 16 :, columns(tile)],
            rim.at[:, columns(tile)],
            r.rim_sems.at[0, tile],
            r.rim_sems.at[1, tile],
            seq_peers[0],
        )

    def value_tile(tile):
        conv_in[:, columns(tile)] = dot(hidden[...], weights(tile)).astype(low)
        rim_copy(tile).start()

    masks = r.masks
    select_out = r.select_out

    def conv_tile(tile):
        rim_copy(tile).wait_recv()
        ext[0:8, :] = rim[8:16, columns(tile)].astype(jnp.float32)
        ext[8:, :] = conv_in[:, columns(tile)].astype(jnp.float32)
        conv_weight = r.conv_weight
        total = line(r.conv_bias)[:, columns(tile)] + conv_weight[0:1, columns(tile)] * ext[8:, :]
        for lag in range(1, 4):
            total = total + conv_weight[lag : lag + 1, columns(tile)] * (
                ext[8 - lag : 8 - lag + rows, :] * wide(masks[lag - 1], width)
            )
        conv_pre[:, columns(tile)] = total
        out = (total * jax.nn.sigmoid(total)).astype(low)
        conv_out[:, columns(tile)] = out
        select_low = r.select_weight[:, columns(tile)].astype(low)
        spare = jnp.zeros((select_out.shape[1] - select_low.shape[0], width), low)
        part = dot_last(out, jnp.concatenate([select_low, spare], axis=0))
        select_out[...] = part if tile == 0 else select_out[...] + part

    select_swap = remote(
        select_out, r.select_far, pair_sems.at[2], pair_sems.at[3], other_half()
    )
    enter, leave = r.enter, r.leave
    states = r.decay_log.shape[0]
    step_rank = r.step_weight.shape[0]
    held, drive = r.held, r.drive

    def select_stage():
        select_swap.wait()
        select_out[...] = select_out[...] + r.select_far[...]
        turned = select_out[:, step_rank : step_rank + 128].T
        for at in range(rows):
            enter[at] = jnp.broadcast_to(turned[:states, at : at + 1], (states, 128))
            leave[at] = jnp.broadcast_to(turned[states : 2 * states, at : at + 1], (states, 128))

    def step_tile(tile):
        here = columns(tile)
        step_low = r.step_weight[:, here].astype(low)
        pre = dot(select_out[:, :step_rank].astype(low), step_low) + line(r.step_bias)[:, here]
        size = jnp.maximum(pre, 0.0) + jnp.log1p(jnp.exp(-jnp.abs(pre)))
        r.step_pre[:, here] = pre
        r.step_size[:, here] = size
        held[:, here] = jnp.where(wide(masks[0], width) > 0.0, size, RESET)
        drive[:, here] = size * conv_out[:, here].astype(jnp.float32)

    piece = r.state_piece

    def rate_of(here):
        return -jnp.exp(r.decay_log[:, here]) * LOG2E

    def state_tile(tile):
        here = columns(tile)
        rate = rate_of(here)

        def block(index, state):
            base = pl.multiple_of(index * 8, 8)
            for offset in range(8):
                at = base + offset
                kept = jnp.exp2(rate * held[pl.ds(at, 1), here])
                state = kept * state + wide(enter[at], width) * drive[pl.ds(at, 1), here]
            return state

        piece[0:states, here] = lax.fori_loop(
            0, rows // 8, block, jnp.zeros((states, width), jnp.float32)
        )
        total = jnp.sum(held[:, here], axis=0, keepdims=True)
        piece[states:, here] = jnp.broadcast_to(total, (8, width))

    chain_out, chain_home, chain_middle, chain_end = chain_parts(
        False, piece, lambda: rate_of(own_lanes(place)), r.start, r.come, r.back, r.chain_sems
    )
    scanned, start = r.scanned, r.start

    def scan_tile(tile):
        here = columns(tile)
        rate = rate_of(here)

        def block(index, state):
            base = pl.multiple_of(index * 8, 8)
            for offset in range(8):
                at = base + offset
                kept = jnp.exp2(rate * held[pl.ds(at, 1), here])
                state = kept * state + wide(enter[at], width) * drive[pl.ds(at, 1), here]
                scanned[pl.ds(at, 1), here] = jnp.sum(
                    wide(leave[at], width) * state, axis=0, keepdims=True
                )
            return state

        lax.fori_loop(0, rows // 8, block, start[:, here])

    gate = r.gate

    def gate_tile(tile):
        gate[:, columns(tile)] = dot(hidden[...], weights(third + tile))

    def out_tile(tile):
        here = columns(tile)
        out_weight = weights(2 * third + tile)
        value = conv_out[:, here].astype(jnp.float32)
        mixed = scanned[:, here] + line(r.skip_gain)[:, here] * value
        pre = gate[:, here]
        sigmoid = jax.nn.sigmoid(pre)
        act = pre * sigmoid
        gated = (mixed * act).astype(low)
        r.gated[:, here] = gated
        d_gated = dot(r.cot[...], out_weight)
        d_mixed = d_gated * act
        r.d_mixed[:, here] = d_mixed
        slope = sigmoid * (1.0 + pre * (1.0 - sigmoid))
        r.d_gate[:, here] = (d_gated * mixed * slope).astype(low)
        r.skip_grad[:, here] = jnp.sum(d_mixed * value, axis=0, keepdims=True)
        part = dot_last(gated, out_weight)
        r.branch[...] = part if tile == 0 else r.branch[...] + part

    def adjoint_tile(tile):
        here = columns(tile)
        rate = rate_of(here)

        def block(index, state):
            base = pl.multiple_of((rows // 8 - 1 - index) * 8, 8)
            for offset in range(7, -1, -1):
                at = base + offset
                kept = jnp.exp2(rate * held[pl.ds(at, 1), here])
                state = kept * (state + wide(leave[at], width) * r.d_mixed[pl.ds(at, 1), here])
            return state

        r.piece[0:states, here] = lax.fori_loop(
            0, rows // 8, block, jnp.zeros((states, width), jnp.float32)
        )
        total = jnp.sum(held[:, here], axis=0, keepdims=True)
        r.piece[states:, here] = jnp.broadcast_to(total, (8, width))

    def turn(source, target):
        for at in range(target.shape[0]):
            value = source[:, at * 128 : (at + 1) * 128].astype(jnp.float32)
            target[at % 2 * 8 + at // 2 % 2 * 4 + at // 4] = value.T.astype(low)

    for step in range(third + 5):
        pump(step)
        if step == 0:
            turn(r.cot, r.cot_t)
        if step == 2:
            swap.wait()
            turn(hidden, r.hidden_t)
        if step >= 5:
            value_tile(step - 5)
        if step >= 6:
            conv_tile(step - 6)
    conv_tile(third - 1)
    select_swap.start()
    pump(third + 5)
    gate_tile(0)
    select_stage()
    for tile in range(third):
        step_tile(tile)
    pump(third + 6)
    gate_tile(1)
    for tile in range(third):
        state_tile(tile)
    chain_out()
    chain_middle()
    pump(third + 7)
    gate_tile(2)
    chain_home()
    for tile in range(third):
        scan_tile(tile)
    pump(third + 8)
    gate_tile(3)
    for tile in range(third):
        pump(2 * third + 5 + tile)
        out_tile(tile)
        adjoint_tile(tile)
    chain_end()
    for chunk in range(chunks):
        for hop in range(3):
            when((z < 3) & (z >= hop), up(chunk, hop).wait_send)
            when((z > 0) & (z + hop < 4), down(chunk, hop).wait_send)
        for level in range(4):
            if chunk not in X_FIRST:
                along_x(chunk, level).wait_send()
        if chunk in X_FIRST:
            along_x(chunk, z).wait_send()
        along_core(chunk).wait_send()
        if chunk < 2 * third:
            keep(chunk).wait()
    for tile in range(third):
        rim_copy(tile).wait_send()


def own_lanes(at):
    return pl.ds(pl.multiple_of(at * 128, 128), 128)


def chain_parts(backward, piece, rate_own, out, come, back, sems):
    place = lax.axis_index("seq")
    peers = [(lax.rem(place + step, 16), lax.axis_index("tp")) for step in range(1, 16)]
    states = out.shape[0]

    def away(at):
        return remote(
            piece.at[:, own_lanes(peers[at][0])],
            come.at[place],
            sems.at[0, at],
            sems.at[1, at],
            peers[at],
        )

    def home(at):
        return remote(
            back.at[peers[at][0]],
            out.at[:, own_lanes(place)],
            sems.at[2, at],
            sems.at[3, at],
            peers[at],
        )

    def begin():
        for at in range(15):
            away(at).start()
        come[place] = piece[:, own_lanes(place)]

    def middle():
        rate = rate_own()
        for at in range(15):
            away(at).wait_recv()

        def join(index, state):
            at = 15 - index if backward else index
            back[at] = state
            part = come[at]
            return jnp.exp2(rate * part[states : states + 1]) * state + part[:states]

        lax.fori_loop(0, 16, join, jnp.zeros((states, 128), jnp.float32))
        for at in range(15):
            home(at).start()
        out[:, own_lanes(place)] = back[place]

    def arrive():
        for at in range(15):
            home(at).wait_recv()

    def end():
        for at in range(15):
            away(at).wait_send()
            home(at).wait_send()

    return begin, arrive, middle, end


def forward_block(ident, given):
    half_rows, model = given.block.shape
    rows = 2 * half_rows
    share, inner = given.out_weight.shape
    total = 3 * inner
    states = given.decay_log.shape[0]
    f32, low = jnp.float32, jnp.bfloat16
    vmem = pl.BlockSpec(memory_space=pltpu.VMEM)
    dma = pltpu.SemaphoreType.DMA
    width = 512
    chunks = total // width
    select_rows = 256

    def like(columns, dtype):
        return jax.ShapeDtypeStruct((rows, columns), dtype)

    lanes = jax.ShapeDtypeStruct((rows, states, 128), f32)
    outs = pl.pallas_call(
        forward_block_kernel,
        in_specs=[vmem] * len(ForwardIn._fields),
        out_specs=[vmem] * (len(ForwardOut._fields) - 1) + [pl.BlockSpec(memory_space=pltpu.HBM)],
        out_shape=[
            jax.ShapeDtypeStruct((16, share, rows), low),
            jax.ShapeDtypeStruct((16, share, rows), low),
            jax.ShapeDtypeStruct((states + 8, inner), f32),
            like(inner, low),
            jax.ShapeDtypeStruct((16, inner), low),
            like(inner, f32),
            like(inner, low),
            like(select_rows, f32),
            like(inner, f32),
            like(inner, f32),
            like(inner, f32),
            like(inner, f32),
            lanes,
            lanes,
            jax.ShapeDtypeStruct((states, inner), f32),
            like(inner, low),
            like(inner, f32),
            like(inner, low),
            like(model, f32),
            jax.ShapeDtypeStruct((1, inner), f32),
            jax.ShapeDtypeStruct((chunks * 2 // 3, 4, 2, 2, share, width), low),
        ],
        scratch_shapes=[
            pltpu.VMEM((rows, model), low),
            pltpu.VMEM((chunks, 4, 2, 2, share, width), low),
            pltpu.VMEM((rows + 8, width), f32),
            pltpu.VMEM((rows, inner), f32),
            pltpu.VMEM((rows, inner), f32),
            pltpu.VMEM((states + 8, inner), f32),
            pltpu.VMEM((16, states + 8, 128), f32),
            pltpu.VMEM((16, states, 128), f32),
            pltpu.VMEM((rows, select_rows), f32),
            dma((chunks, 6)),
            dma((chunks, 6)),
            dma((chunks, 4)),
            dma((chunks, 4)),
            dma((2, chunks)),
            dma((chunks,)),
            dma((2, chunks // 3)),
            dma((4, 15)),
            dma((4,)),
        ],
        compiler_params=pltpu.CompilerParams(
            collective_id=ident, has_side_effects=True, vmem_limit_bytes=FINISH_LIMIT
        ),
    )(*given)
    out = ForwardOut(*outs)
    return out._replace(weights=out.weights.reshape(-1, model, width))


def backward_part(r, main):
    z, x, core = position()
    place, tp = lax.axis_index("seq"), lax.axis_index("tp")
    low = jnp.bfloat16
    seq_peers = [(lax.rem(place + step, 16), tp) for step in range(1, 16)]
    rows, inner = r.held.shape
    states = r.decay_log.shape[0]
    width = 512
    tiles = inner // width
    pair_sems = r.pair_sems

    def columns(at):
        return slice(at * width, (at + 1) * width)

    def dot(left, right):
        return jnp.dot(left, right, preferred_element_type=jnp.float32)

    def dot_last(left, right):
        return lax.dot_general(
            left, right, (((1,), (1,)), ((), ())), preferred_element_type=jnp.float32
        )

    def line(ref):
        return ref[...].reshape(1, -1)

    half_rows = r.block.shape[0]
    own_half = pl.ds(pl.multiple_of(tp * half_rows, half_rows), half_rows)
    far_half = pl.ds(pl.multiple_of((1 - tp) * half_rows, half_rows), half_rows)
    r.branch_send[...] = r.branch[far_half, :].astype(low)
    branch_swap = remote(
        r.branch_send, r.branch_far, pair_sems.at[0], pair_sems.at[1], other_half()
    )
    branch_swap.start()

    held, drive, grad = r.held, r.drive, r.d_mixed
    enter, leave, piece = r.enter, r.leave, r.piece

    def rate_of(here):
        return -jnp.exp(r.decay_log[:, here])

    chain_out, chain_home, chain_middle, chain_end = chain_parts(
        True,
        piece,
        lambda: rate_of(own_lanes(place)) * LOG2E,
        r.follow,
        r.come,
        r.back,
        r.chain_sems,
    )
    kept_all, state_all = r.kept, r.state
    drive_grad, d_step_pre = r.drive_grad, r.d_step_pre
    enter_grad, leave_grad = r.enter_grad, r.leave_grad

    def again_tile(tile):
        here = columns(tile)
        rate = rate_of(here) * LOG2E

        def block(index, state):
            base = pl.multiple_of(index * 8, 8)
            for offset in range(8):
                at = base + offset
                kept = jnp.exp2(rate * held[pl.ds(at, 1), here])
                kept_all[at] = kept
                state = kept * state + wide(enter[at], width) * drive[pl.ds(at, 1), here]
                state_all[at + 1] = state
            return state

        start = r.start[:, here]
        state_all[0] = start
        lax.fori_loop(0, rows // 8, block, start)

    def reverse_tile(tile):
        here = columns(tile)
        rate = rate_of(here)

        def block(index, carry):
            follow, decay = carry
            base = pl.multiple_of((rows // 8 - 1 - index) * 8, 8)
            for offset in range(7, -1, -1):
                at = base + offset
                now = grad[pl.ds(at, 1), here]
                adjoint = wide(leave[at], width) * now + follow
                drive_grad[pl.ds(at, 1), here] = jnp.sum(
                    adjoint * wide(enter[at], width), axis=0, keepdims=True
                )
                enters = fold_lanes(adjoint * drive[pl.ds(at, 1), here])
                leaves = fold_lanes(state_all[at + 1] * now)
                if tile == 0:
                    enter_grad[at], leave_grad[at] = enters, leaves
                else:
                    enter_grad[at] += enters
                    leave_grad[at] += leaves
                follow = kept_all[at] * adjoint
                part = follow * state_all[at]
                r.ext[pl.ds(at, 1), :] = jnp.sum(part * rate, axis=0, keepdims=True)
                decay = decay + part * held[pl.ds(at, 1), here]
            return follow, decay

        follow = r.follow[:, here]
        _, decay = lax.fori_loop(0, rows // 8, block, (follow, jnp.zeros_like(follow)))
        r.decay_grad[:, here] = decay * rate
        d_step = (
            drive_grad[:, here] * r.conv_out[:, here].astype(jnp.float32) + r.ext[0:rows, :]
        )
        d_step_pre[:, here] = (d_step * jax.nn.sigmoid(r.step_pre[:, here])).astype(low)

    step_rank = r.step_weight.shape[0]
    select_grad = r.select_grad
    extra = r.extra

    def turned(value):
        return value.astype(jnp.float32).T.astype(low)

    def store_extra(first, tile, value):
        for at in range(width // 128):
            owner = tile * (width // 128) + at
            extra[owner // 2, owner % 2, first : first + value.shape[0], :] = value[
                :, at * 128 : (at + 1) * 128
            ].astype(low)

    def select_start():
        step_in = turned(r.select_out[:, :step_rank])
        total = jnp.zeros((rows, step_rank), jnp.float32)
        for tile in range(tiles):
            here = columns(tile)
            total = total + dot_last(d_step_pre[:, here], r.step_weight[:, here].astype(low))
            store_extra(0, tile, dot(step_in, d_step_pre[:, here]))
        select_grad[:, :step_rank] = total
        row_at = lax.broadcasted_iota(jnp.int32, (8, states, 128), 1)
        lane_at = lax.broadcasted_iota(jnp.int32, (8, states, 128), 2)

        def block(index, _):
            base = pl.multiple_of(index * 8, 8)
            here = pl.ds(base, 8)
            enters = jnp.sum(enter_grad[here], axis=2, keepdims=True)
            leaves = jnp.sum(leave_grad[here], axis=2, keepdims=True)
            spread = jnp.where(lane_at == row_at, enters, 0.0)
            spread = jnp.where(lane_at == row_at + states, leaves, spread)
            select_grad[here, step_rank:] = jnp.sum(spread, axis=1)
            return 0

        lax.fori_loop(0, rows // 8, block, 0)
        select_swap.start()

    select_swap = remote(
        select_grad, r.select_far, pair_sems.at[2], pair_sems.at[3], other_half()
    )
    conv_grad, rim_next, ext = r.conv_grad, r.rim_next, r.ext

    def rim_copy(tile):
        return remote(
            conv_grad.at[0:8, columns(tile)],
            rim_next.at[:, columns(tile)],
            r.rim_sems.at[0, tile],
            r.rim_sems.at[1, tile],
            seq_peers[14],
        )

    select_count = r.select_weight.shape[0]

    def select_end():
        select_swap.wait()
        total = (select_grad[...] + r.select_far[...]).astype(low)
        select_low = total[:, :256]
        first, second = turned(select_low[:, :128]), turned(select_low[:, 128:])
        for tile in range(tiles):
            here = columns(tile)
            conv_out = r.conv_out[:, here]
            store_extra(step_rank, tile, dot(first, conv_out))
            store_extra(step_rank + 128, tile, dot(second[: select_count - 128], conv_out))
            weight = r.select_weight[:, here].astype(low)
            spare = jnp.zeros((256 - select_count, width), low)
            d_conv = (
                drive_grad[:, here] * r.step_size[:, here]
                + grad[:, here] * line(r.skip_gain)[:, here]
                + dot(select_low, jnp.concatenate([weight, spare], axis=0))
            )
            pre = r.conv_pre[:, here]
            sigmoid = jax.nn.sigmoid(pre)
            conv_grad[:, here] = d_conv * (sigmoid * (1.0 + pre * (1.0 - sigmoid)))
            rim_copy(tile).start()
            if tile % 2:
                main.advance()

    masks, masks_after = r.masks, r.masks_after

    def conv_tile(tile):
        here = columns(tile)
        value = conv_grad[:, here]
        weight = r.conv_weight
        lines = []
        ext[0:8, :] = r.rim[8:16, here].astype(jnp.float32)
        ext[8:, :] = r.conv_in[:, here].astype(jnp.float32)
        for lag in range(4):
            shifted = ext[8 - lag : 8 - lag + rows, :]
            if lag > 0:
                shifted = shifted * wide(masks[lag - 1], width)
            lines.append(jnp.sum(value * shifted, axis=0, keepdims=True))
        lines.append(jnp.sum(value, axis=0, keepdims=True))
        lines.append(
            jnp.sum(d_step_pre[:, here].astype(jnp.float32), axis=0, keepdims=True)
        )
        lines.append(r.skip_grad[:, here])
        lines.append(jnp.zeros((9, width), jnp.float32))
        first = step_rank + select_count
        store_extra(first, tile, r.decay_grad[:, here])
        store_extra(first + states, tile, jnp.concatenate(lines, axis=0))
        rim_copy(tile).wait_recv()
        ext[0:rows, :] = value
        ext[rows:, :] = rim_next[:, here]
        total = weight[0:1, here] * value
        for lag in range(1, 4):
            total = total + weight[lag : lag + 1, here] * (
                ext[lag : lag + rows, :] * wide(masks_after[lag - 1], width)
            )
        r.d_value[:, here] = total.astype(low)

    chain_out()
    main.advance(2)
    chain_middle()
    again_tile(0)
    main.advance(1)
    chain_home()
    for tile in range(tiles):
        if tile > 0:
            again_tile(tile)
            main.advance()
        reverse_tile(tile)
        main.advance()
    select_start()
    main.advance()
    branch_swap.wait()
    r.block_out[...] = (
        r.block[...].astype(jnp.float32)
        + r.branch[own_half, :]
        + r.branch_far[...].astype(jnp.float32)
    )
    select_end()
    main.advance()
    for tile in range(tiles):
        conv_tile(tile)
        main.advance()

    def end():
        chain_end()
        for tile in range(tiles):
            rim_copy(tile).wait_send()

    return end


def rest_kernel(channels, model, *refs):
    r, reducer_refs = gathered(refs, RestIn, RestOut, RestWork)
    z, x, core = position()
    place, tp = lax.axis_index("seq"), lax.axis_index("tp")
    seq_peers = [(lax.rem(place + step, 16), tp) for step in range(1, 16)]
    across = [(lax.rem(z + step, 4) * 4 + x * 2 + core, 1 - tp) for step in range(4)]
    greet(seq_peers + across)
    inner = r.out_grad.shape[1]
    starts = range(0, inner, SHARE_WIDTH)
    main = Reducer(
        [(r.cot_t, r.gated, at, r.out_grad, at) for at in starts]
        + [(r.hidden_t, r.d_gate, at, r.in_grad, inner + at) for at in starts]
        + [(r.hidden_t, r.d_value, at, r.in_grad, at) for at in starts],
        reducer_refs,
    )
    end = backward_part(r, main)
    finish_part(channels, model, r, main)
    end()
    main.drain()


class RestIn(NamedTuple):
    hidden_t: object
    cot_t: object
    gated: object
    d_gate: object
    piece: object
    d_mixed: object
    held: object
    drive: object
    enter: object
    leave: object
    start: object
    conv_out: object
    step_pre: object
    step_size: object
    conv_pre: object
    conv_in: object
    rim: object
    select_out: object
    branch: object
    block: object
    skip_grad: object
    masks: object
    masks_after: object
    conv_weight: object
    skip_gain: object
    select_weight: object
    step_weight: object
    decay_log: object
    weights: object
    cot: object
    lanes: object
    norm_gain: object
    norm_moment: object
    in_cols: object
    out_cols: object
    step_cols: object
    select_cols: object
    decay_cols: object
    conv_cols: object
    bias_moment: object
    step_moment: object
    skip_moment: object
    conv_bias: object
    step_bias: object


class RestOut(NamedTuple):
    out_grad: object
    block_out: object
    in_grad: object
    input_grad: object
    small: object
    scales: object
    lanes_new: object
    vectors_new: object


class RestWork(NamedTuple):
    d_value: object
    extra: object
    come: object
    back: object
    follow: object
    kept: object
    state: object
    drive_grad: object
    d_step_pre: object
    decay_grad: object
    enter_grad: object
    leave_grad: object
    select_grad: object
    select_far: object
    conv_grad: object
    rim_next: object
    ext: object
    branch_send: object
    branch_far: object
    chain_sems: object
    pair_sems: object
    rim_sems: object
    come_core: object
    send_x: object
    come_x: object
    send_z: object
    come_z: object
    full: object
    mine: object
    acc: object
    far: object
    pair: object
    pair_far: object
    totals: object
    totals_acc: object
    totals_far: object
    come_half: object
    d_hidden: object
    fetched: object
    fetched_sems: object
    extra_sent: object
    extra_got: object
    sums_sent: object
    sums_got: object
    half_sems: object


def rest_block(ident, channels, given):
    rows, inner = given.held.shape
    half_rows, model = given.block.shape
    states = given.decay_log.shape[0]
    small_rows = given.step_weight.shape[0] + given.select_weight.shape[0] + states + 16
    columns = 2 * inner
    f32, low = jnp.float32, jnp.bfloat16
    dma = pltpu.SemaphoreType.DMA
    share = model // 16
    seq_rows = columns // 128 + inner // 128 + model // 128 + 16
    kept_chunks, _, kept_width = given.weights.shape
    block = (small_rows, 128)
    shape, space = jax.ShapeDtypeStruct, pltpu.VMEM
    vmem = pl.BlockSpec(memory_space=pltpu.VMEM)
    specs = RestIn(*[vmem] * len(given))._replace(
        weights=pl.BlockSpec(memory_space=pltpu.HBM)
    )
    outs = pl.pallas_call(
        functools.partial(rest_kernel, channels, model),
        in_specs=list(specs),
        out_specs=[vmem] * len(RestOut._fields),
        out_shape=[
            shape((share, inner), f32),
            shape((half_rows, model), f32),
            shape((share, columns), f32),
            shape((half_rows, model), f32),
            shape((small_rows, inner), f32),
            shape((5, 128, 128), f32),
            shape((8, 128), f32),
            shape((32, inner), f32),
        ],
        scratch_shapes=[
            space((rows, inner), low),
            space((8, 2, small_rows, 128), low),
            space((16, states + 8, 128), f32),
            space((16, states, 128), f32),
            space((states, inner), f32),
            space((rows, states, 512), f32),
            space((rows + 1, states, 512), f32),
            space((rows, inner), f32),
            space((rows, inner), low),
            space((states, inner), f32),
            space((rows, states, 128), f32),
            space((rows, states, 128), f32),
            space((rows, 256), f32),
            space((rows, 256), f32),
            space((rows, inner), f32),
            space((8, inner), f32),
            space((rows + 8, 512), f32),
            space((half_rows, model), low),
            space((half_rows, model), low),
            dma((4, 15)),
            dma((4,)),
            dma((2, inner // 512)),
            space((8,) + block, low),
            space((4,) + block, low),
            space((4,) + block, low),
            space((3,) + block, low),
            space((3,) + block, low),
            space((4, 2, 2) + block, low),
            space((seq_rows, 128), f32),
            space((8, seq_rows, 128), f32),
            space((4, model // 128 + 16, 128), f32),
            space((8, 128), f32),
            space((8, 128), f32),
            space((16, 128), f32),
            space((8, 16, 128), f32),
            space((4, 16, 128), f32),
            space((half_rows, model), f32),
            space((2 * half_rows, model), f32),
            space((2, model, kept_width), low),
            dma((kept_chunks,)),
            dma((10,)),
            dma((10,)),
            dma((21,)),
            dma((21,)),
            dma((2,)),
        ]
        + reducer_scratch(inner + columns, share, SHARE_WIDTH),
        compiler_params=pltpu.CompilerParams(
            collective_id=ident, has_side_effects=True, vmem_limit_bytes=FINISH_LIMIT
        ),
    )(*given)
    return RestOut(*outs)


def on_device(
    block_in,
    cotangent,
    segment_ids,
    norm_gain,
    in_weight,
    out_weight,
    conv_weight,
    conv_bias,
    select_weight,
    step_weight,
    step_bias,
    decay_log,
    skip_gain,
    norm_moment,
    in_rows,
    in_cols,
    out_rows,
    out_cols,
    conv_rows,
    conv_cols,
    bias_moment,
    select_rows,
    select_cols,
    step_rows,
    step_cols,
    step_moment,
    decay_rows,
    decay_cols,
    skip_moment,
):
    tp_count = lax.axis_size("tp")
    seq_index = lax.axis_index("seq")
    tp_index = lax.axis_index("tp")
    seq_first = (seq_index == 0).astype(jnp.float32)
    tp_first = (tp_index == 0).astype(jnp.float32)
    half_rows, model_dim = block_in.shape
    row_count = cotangent.shape[0]
    inner_dim = in_weight.shape[2]
    channels = inner_dim * tp_count
    conv_taps = conv_weight.shape[0]
    states = decay_log.shape[0]
    step_rank = step_weight.shape[0]
    row_share = in_weight.shape[0]
    id_padded = jnp.concatenate(
        [
            jnp.full((conv_taps - 1,), -1, jnp.int32),
            segment_ids,
            jnp.full((conv_taps - 1,), -2, jnp.int32),
        ]
    )
    window = lax.dynamic_slice_in_dim(
        id_padded, seq_index * row_count, row_count + 2 * (conv_taps - 1)
    )
    local_ids = window[conv_taps - 1 : conv_taps - 1 + row_count]
    keep_mask = (local_ids == window[conv_taps - 2 : conv_taps - 2 + row_count]).astype(jnp.float32)
    residual = block_in.astype(jnp.float32)
    mean_sq = jnp.mean(residual * residual, axis=1, keepdims=True)
    inv_rms = lax.rsqrt(mean_sq + EPS_NORM)
    normed = residual * inv_rms
    low_type = jnp.bfloat16
    projected, hidden, in_full = project(
        (normed * norm_gain[None, :]).astype(low_type),
        in_weight.astype(low_type).reshape(row_share, 2 * inner_dim),
        0,
    )
    out_low, projected = lax.optimization_barrier((out_weight.astype(low_type), projected))
    out_full = lax.all_gather(out_low, "seq", axis=0, tiled=True)
    conv_in = projected[:, :inner_dim].astype(jnp.bfloat16)
    gate_pre = projected[:, inner_dim:]
    rim_rows = passed_along(conv_in[row_count - (conv_taps - 1) :], "seq", 1)
    ext_rows = jnp.concatenate([rim_rows, conv_in], axis=0).astype(jnp.float32)
    same_docs = []
    conv_pre = jnp.zeros_like(gate_pre) + conv_bias[None, :]
    for shift_lag in range(conv_taps):
        first_row = conv_taps - 1 - shift_lag
        same_doc = (window[first_row : first_row + row_count] == local_ids).astype(jnp.float32)[
            :, None
        ]
        same_docs.append(same_doc)
        conv_pre = (
            conv_pre
            + conv_weight[shift_lag][None, :]
            * ext_rows[first_row : first_row + row_count]
            * same_doc
        )
    conv_out = jax.nn.silu(conv_pre).astype(jnp.bfloat16)
    conv_value = conv_out.astype(jnp.float32)
    select_low = select_weight.astype(jnp.bfloat16)
    select_out = pair_sum(
        jnp.einsum("te,ke->tk", conv_out, select_low, preferred_element_type=jnp.float32), 1
    )
    step_in = select_out[:, :step_rank].astype(jnp.bfloat16)
    state_in = select_out[:, step_rank : step_rank + states]
    state_out = select_out[:, step_rank + states :]
    step_low = step_weight.astype(jnp.bfloat16)
    step_pre = jnp.dot(step_in, step_low, preferred_element_type=jnp.float32) + step_bias[None, :]
    step_size = jax.nn.softplus(step_pre)
    decay_rate = -jnp.exp(decay_log)
    drive = step_size * conv_value
    held_step = jnp.where(keep_mask[:, None] > 0.0, step_size, RESET)
    enter = jnp.broadcast_to(state_in[:, :, None], (row_count, states, 128))
    leave = jnp.broadcast_to(state_out[:, :, None], (row_count, states, 128))
    nothing = jnp.zeros((8, 128), jnp.float32)
    start, _ = chain(
        piece_state(held_step, drive, enter, decay_rate, False), decay_rate, nothing, False, 2
    )
    scanned = scan_forward(held_step, drive, enter, leave, decay_rate, start)
    mixed = scanned + skip_gain[None, :] * conv_value
    gate_act = jax.nn.silu(gate_pre)
    gated = (mixed * gate_act).astype(jnp.bfloat16)
    branch = jnp.einsum("te,de->td", gated, out_full, preferred_element_type=jnp.float32)
    own_rows, far_rows = tp_index * half_rows, (1 - tp_index) * half_rows
    d_gated = jnp.einsum("td,de->te", cotangent, out_full, preferred_element_type=jnp.float32)
    d_out_w = jnp.einsum("td,te->de", cotangent, gated, preferred_element_type=jnp.float32)
    out_half = lax.psum_scatter(
        d_out_w.astype(low_type), "seq", scatter_dimension=0, tiled=True
    )
    d_mixed = d_gated * gate_act
    d_gate = (d_gated * mixed * silu_slope(gate_pre)).astype(jnp.bfloat16)
    skip_grad = jnp.sum(d_mixed * conv_value, axis=0)
    follow, branch_far = chain(
        piece_state(held_step, d_mixed, leave, decay_rate, True),
        decay_rate,
        lax.dynamic_slice_in_dim(branch, far_rows, half_rows, 0).astype(low_type),
        True,
        3,
    )
    block_out = (
        residual
        + lax.dynamic_slice_in_dim(branch, own_rows, half_rows, 0)
        + branch_far.astype(jnp.float32)
    )
    drive_grad, step_grad, decay_grad, enter_grad, leave_grad = scan_backward(
        held_step, drive, d_mixed, enter, leave, decay_rate, start, follow
    )
    enter_grad = jnp.sum(enter_grad, axis=2)
    leave_grad = jnp.sum(leave_grad, axis=2)
    d_step = drive_grad * conv_value + step_grad
    d_step_pre = (d_step * jax.nn.sigmoid(step_pre)).astype(jnp.bfloat16)
    step_bias_grad = jnp.sum(d_step_pre.astype(jnp.float32), axis=0)
    step_w_grad = jnp.einsum("tr,te->re", step_in, d_step_pre, preferred_element_type=jnp.float32)
    d_step_in = jnp.einsum("te,re->tr", d_step_pre, step_low, preferred_element_type=jnp.float32)
    select_grads = jnp.concatenate(
        [d_step_in, enter_grad, leave_grad],
        axis=1,
    )
    d_select = pair_sum(select_grads, 4).astype(jnp.bfloat16)
    select_w_grad = jnp.einsum("tk,te->ke", d_select, conv_out, preferred_element_type=jnp.float32)
    d_conv = (
        drive_grad * step_size
        + d_mixed * skip_gain[None, :]
        + jnp.einsum("tk,ke->te", d_select, select_low, preferred_element_type=jnp.float32)
    )
    d_conv_pre = d_conv * silu_slope(conv_pre)
    rim_next = passed_along(d_conv_pre[: conv_taps - 1], "seq", -1)
    ext_grads = jnp.concatenate([d_conv_pre, rim_next], axis=0)
    ids_after = window[conv_taps - 1 :]
    d_conv_in = jnp.zeros_like(d_conv_pre)
    conv_w_rows = []
    for shift_lag in range(conv_taps):
        first_row = conv_taps - 1 - shift_lag
        later_same = (ids_after[shift_lag : shift_lag + row_count] == local_ids).astype(
            jnp.float32
        )[:, None]
        d_conv_in = (
            d_conv_in
            + conv_weight[shift_lag][None, :]
            * ext_grads[shift_lag : shift_lag + row_count]
            * later_same
        )
        conv_w_rows.append(
            jnp.sum(
                d_conv_pre * ext_rows[first_row : first_row + row_count] * same_docs[shift_lag],
                axis=0,
            )
        )
    conv_w_grad = jnp.stack(conv_w_rows, axis=0)
    conv_b_grad = jnp.sum(d_conv_pre, axis=0)
    d_projected = jnp.concatenate([d_conv_in.astype(jnp.bfloat16), d_gate], axis=1)
    d_hidden = jnp.einsum(
        "tkn,kdn->td",
        d_projected.reshape(row_count, in_full.shape[0], -1),
        in_full,
        preferred_element_type=jnp.float32,
    )
    vector_grads = jnp.stack([conv_b_grad, step_bias_grad, skip_grad], axis=0)
    small_grads = jnp.concatenate(
        [step_w_grad, select_w_grad, decay_grad, conv_w_grad, vector_grads], axis=0
    )
    out_grad = out_half.astype(jnp.float32)
    in_grad = lax.psum_scatter(
        jnp.einsum("td,tn->dn", hidden, d_projected, preferred_element_type=jnp.float32),
        "seq",
        scatter_dimension=0,
        tiled=True,
    )
    small_full = lax.psum(small_grads, "seq")
    d_hidden = lax.psum_scatter(d_hidden, "tp", scatter_dimension=0, tiled=True)
    in_grad = in_grad.reshape(in_weight.shape)
    gain_part = jnp.sum(d_hidden * normed, axis=0)
    scaled = d_hidden * norm_gain[None, :]
    cot_half = lax.dynamic_slice_in_dim(cotangent, own_rows, half_rows, 0).astype(
        jnp.float32
    )
    input_grad = cot_half + inv_rms * (
        scaled - normed * jnp.mean(scaled * normed, axis=1, keepdims=True)
    )
    edges = [step_rank, select_weight.shape[0], states, conv_taps, 3]
    edges = [sum(edges[:at]) for at in range(len(edges) + 1)]
    step_local, select_local, decay_local, conv_local, vector_local = [
        small_full[low:high] for low, high in zip(edges, edges[1:])
    ]
    in_square = in_grad * in_grad
    out_square = out_grad * out_grad
    in_row_part = jnp.sum(in_square, axis=(1, 2))
    out_row_part = jnp.sum(out_square, axis=1)
    small_row_part = jnp.sum(small_full * small_full, axis=1)
    in_total = jnp.sum(DECAY * in_rows + (1.0 - DECAY) * EPS_FACTOR) * tp_first + (
        1.0 - DECAY
    ) * jnp.sum(in_row_part) / (2 * channels)
    out_total = jnp.sum(DECAY * out_rows + (1.0 - DECAY) * EPS_FACTOR) * tp_first + (
        1.0 - DECAY
    ) * jnp.sum(out_row_part) / channels
    seq_part = jnp.concatenate(
        [jnp.sum(in_square, axis=0).reshape(-1, 128), jnp.sum(out_square, axis=0).reshape(-1, 128)]
    )
    shared_part = jnp.concatenate(
        [
            gain_part.reshape(-1, 128),
            jnp.broadcast_to(in_total, (8, 128)),
            jnp.broadcast_to(out_total, (8, 128)),
        ]
    )
    row_parts = jnp.concatenate([in_row_part, out_row_part, small_row_part])
    row_parts = jnp.pad(row_parts, (0, -row_parts.shape[0] % 1024)).reshape(-1, 128)
    col_sums, shared_sums, row_sums = sum_over(seq_part, shared_part, row_parts)
    col_sums = col_sums.reshape(-1)
    in_col_sums = col_sums[: 2 * inner_dim].reshape(2, inner_dim)
    out_col_sums = col_sums[2 * inner_dim :]
    gain_grad = shared_sums[: model_dim // 128].reshape(-1)
    in_mean = shared_sums[model_dim // 128, 0] / model_dim
    out_mean = shared_sums[model_dim // 128 + 8, 0] / model_dim
    row_sums = row_sums.reshape(-1)
    in_row_sums = row_sums[:row_share]
    out_row_sums = row_sums[row_share : 2 * row_share]
    small_row_sums = row_sums[2 * row_share :]
    in_rows_new = DECAY * in_rows + (1.0 - DECAY) * (in_row_sums / (2 * channels) + EPS_FACTOR)
    in_cols_new = DECAY * in_cols + (1.0 - DECAY) * (in_col_sums / model_dim + EPS_FACTOR)
    out_rows_new = DECAY * out_rows + (1.0 - DECAY) * (out_row_sums / channels + EPS_FACTOR)
    out_cols_new = DECAY * out_cols + (1.0 - DECAY) * (out_col_sums / model_dim + EPS_FACTOR)
    step_rows_new, step_cols_new, stepw_update = factor_update(
        step_local, small_row_sums[edges[0] : edges[1]], step_rows, step_cols, channels
    )
    select_rows_new, select_cols_new, select_update = factor_update(
        select_local, small_row_sums[edges[1] : edges[2]], select_rows, select_cols, channels
    )
    decay_rows_new, decay_cols_new, decay_update = factor_update(
        decay_local, small_row_sums[edges[2] : edges[3]], decay_rows, decay_cols, channels
    )
    conv_rows_new, conv_cols_new, conv_update = factor_update(
        conv_local, small_row_sums[edges[3] : edges[4]], conv_rows, conv_cols, channels
    )
    bias_moment_new, convb_update = moment_update(vector_local[0], bias_moment)
    step_moment_new, stepb_update = moment_update(vector_local[1], step_moment)
    skip_moment_new, skip_update = moment_update(vector_local[2], skip_moment)
    gain_moment_new, gain_update = moment_update(gain_grad, norm_moment)
    in_update = in_grad * lax.rsqrt(in_rows_new[:, None, None] * in_cols_new[None] / in_mean)
    out_update = out_grad * lax.rsqrt(out_rows_new[:, None] * out_cols_new[None, :] / out_mean)
    squares = jnp.stack(
        [
            sum_squares(in_update),
            sum_squares(out_update),
            seq_first * sum_squares(conv_update),
            seq_first * sum_squares(select_update),
            seq_first * sum_squares(stepw_update),
            seq_first * sum_squares(decay_update),
            seq_first * sum_squares(convb_update),
            seq_first * sum_squares(stepb_update),
            seq_first * sum_squares(skip_update),
        ]
    )
    _, clip_totals, _ = sum_over(
        nothing, jnp.broadcast_to(jnp.pad(squares, (0, 7))[:, None], (16, 128)), nothing
    )
    clip_totals = clip_totals[:, 0]
    gain_new = apply_step(norm_gain, gain_update, sum_squares(gain_update), model_dim, RATES[0])
    in_new = apply_step(in_weight, in_update, clip_totals[0], model_dim * 2 * channels, RATES[1])
    out_new = apply_step(out_weight, out_update, clip_totals[1], model_dim * channels, RATES[2])
    convw_new = apply_step(conv_weight, conv_update, clip_totals[2], conv_taps * channels, RATES[3])
    convb_new = apply_step(conv_bias, convb_update, clip_totals[6], channels, RATES[4])
    select_new = apply_step(
        select_weight, select_update, clip_totals[3], select_weight.shape[0] * channels, RATES[5]
    )
    stepw_new = apply_step(
        step_weight, stepw_update, clip_totals[4], step_rank * channels, RATES[6]
    )
    stepb_new = apply_step(step_bias, stepb_update, clip_totals[7], channels, RATES[7])
    decay_new = apply_step(decay_log, decay_update, clip_totals[5], states * channels, RATES[8])
    skip_new = apply_step(skip_gain, skip_update, clip_totals[8], channels, RATES[9])
    return (
        block_out,
        input_grad,
        gain_grad,
        gain_new,
        gain_new.astype(low_type),
        gain_moment_new,
        in_grad,
        in_new,
        in_new.astype(low_type),
        in_rows_new,
        in_cols_new,
        out_grad,
        out_new,
        out_new.astype(low_type),
        out_rows_new,
        out_cols_new,
        conv_local,
        convw_new,
        convw_new.astype(low_type),
        conv_rows_new,
        conv_cols_new,
        vector_local[0],
        convb_new,
        convb_new.astype(low_type),
        bias_moment_new,
        select_local,
        select_new,
        select_new.astype(low_type),
        select_rows_new,
        select_cols_new,
        step_local,
        stepw_new,
        stepw_new.astype(low_type),
        step_rows_new,
        step_cols_new,
        vector_local[1],
        stepb_new,
        stepb_new.astype(low_type),
        step_moment_new,
        decay_local,
        decay_new,
        decay_new.astype(low_type),
        decay_rows_new,
        decay_cols_new,
        vector_local[2],
        skip_new,
        skip_new.astype(low_type),
        skip_moment_new,
    )


def on_block_device(
    block_in,
    cotangent,
    segment_ids,
    norm_gain,
    in_weight,
    out_weight,
    conv_weight,
    conv_bias,
    select_weight,
    step_weight,
    step_bias,
    decay_log,
    skip_gain,
    norm_moment,
    in_rows,
    in_cols,
    out_rows,
    out_cols,
    conv_rows,
    conv_cols,
    bias_moment,
    select_rows,
    select_cols,
    step_rows,
    step_cols,
    step_moment,
    decay_rows,
    decay_cols,
    skip_moment,
):
    tp_count = lax.axis_size("tp")
    seq_index = lax.axis_index("seq")
    tp_index = lax.axis_index("tp")
    half_rows, model_dim = block_in.shape
    row_count = cotangent.shape[0]
    inner_dim = in_weight.shape[2]
    channels = inner_dim * tp_count
    conv_taps = conv_weight.shape[0]
    states = decay_log.shape[0]
    step_rank = step_weight.shape[0]
    row_share = in_weight.shape[0]
    low_type = jnp.bfloat16
    id_padded = jnp.concatenate(
        [
            jnp.full((conv_taps - 1,), -1, jnp.int32),
            segment_ids,
            jnp.full((conv_taps - 1,), -2, jnp.int32),
        ]
    )
    window = lax.dynamic_slice_in_dim(
        id_padded, seq_index * row_count, row_count + 2 * (conv_taps - 1)
    )
    local_ids = window[conv_taps - 1 : conv_taps - 1 + row_count]
    same_docs = [
        (window[conv_taps - 1 - lag : conv_taps - 1 - lag + row_count] == local_ids).astype(
            jnp.float32
        )[:, None]
        for lag in range(conv_taps)
    ]
    masks = jnp.broadcast_to(jnp.stack(same_docs[1:]), (conv_taps - 1, row_count, 128))
    ids_after = window[conv_taps - 1 :]
    same_after = [
        (ids_after[lag : lag + row_count] == local_ids).astype(jnp.float32)[:, None]
        for lag in range(1, conv_taps)
    ]
    masks_after = jnp.broadcast_to(jnp.stack(same_after), (conv_taps - 1, row_count, 128))
    lanes = jnp.concatenate(
        [step_rows, select_rows, decay_rows, conv_rows, jnp.ones((76,), jnp.float32)]
        + [in_rows, out_rows, jnp.ones((384,), jnp.float32)]
    ).reshape(8, 128)
    f = forward_block(
        0,
        ForwardIn(
        in_weight=in_weight,
        out_weight=out_weight,
        block=block_in,
        cot=cotangent,
        norm_gain=norm_gain,
        conv_weight=conv_weight,
        conv_bias=conv_bias,
        step_bias=step_bias,
        skip_gain=skip_gain,
        masks=masks,
        select_weight=select_weight,
        step_weight=step_weight,
        decay_log=decay_log,
        ),
    )
    rest = rest_block(
        1,
        channels,
        RestIn(
            block=block_in,
            cot=cotangent,
            lanes=lanes,
            masks=masks,
            masks_after=masks_after,
            conv_weight=conv_weight,
            select_weight=select_weight,
            step_weight=step_weight,
            decay_log=decay_log,
            norm_gain=norm_gain,
            norm_moment=norm_moment,
            in_cols=in_cols,
            out_cols=out_cols,
            step_cols=step_cols,
            select_cols=select_cols,
            decay_cols=decay_cols,
            conv_cols=conv_cols,
            bias_moment=bias_moment,
            step_moment=step_moment,
            skip_moment=skip_moment,
            conv_bias=conv_bias,
            step_bias=step_bias,
            skip_gain=skip_gain,
            **shared(f, RestIn),
        ),
    )
    return renew(
        RenewIn(
            value_grad=rest.in_grad,
            gate_grad=rest.in_grad,
            in_weight=in_weight,
            out_weight=out_weight,
            step_weight=step_weight,
            select_weight=select_weight,
            decay_log=decay_log,
            conv_weight=conv_weight,
            **shared(rest, RenewIn),
        )
    )


def solution(mesh):
    on_slice = mesh.shape["seq"] == 16 and mesh.shape["tp"] == 2
    return jax.shard_map(
        on_block_device if on_slice else on_device,
        mesh=mesh,
        in_specs=(
            P(("seq", "tp"), None),
            P("seq", None),
            P(),
            P(),
            P("seq", None, "tp"),
            P("seq", "tp"),
            P(None, "tp"),
            P("tp"),
            P(None, "tp"),
            P(None, "tp"),
            P("tp"),
            P(None, "tp"),
            P("tp"),
            P(),
            P("seq"),
            P(None, "tp"),
            P("seq"),
            P("tp"),
            P(),
            P("tp"),
            P("tp"),
            P(),
            P("tp"),
            P(),
            P("tp"),
            P("tp"),
            P(),
            P("tp"),
            P("tp"),
        ),
        out_specs=(
            P(("seq", "tp"), None),
            P(("seq", "tp"), None),
            P(),
            P(),
            P(),
            P(),
            P("seq", None, "tp"),
            P("seq", None, "tp"),
            P("seq", None, "tp"),
            P("seq"),
            P(None, "tp"),
            P("seq", "tp"),
            P("seq", "tp"),
            P("seq", "tp"),
            P("seq"),
            P("tp"),
            P(None, "tp"),
            P(None, "tp"),
            P(None, "tp"),
            P(),
            P("tp"),
            P("tp"),
            P("tp"),
            P("tp"),
            P("tp"),
            P(None, "tp"),
            P(None, "tp"),
            P(None, "tp"),
            P(),
            P("tp"),
            P(None, "tp"),
            P(None, "tp"),
            P(None, "tp"),
            P(),
            P("tp"),
            P("tp"),
            P("tp"),
            P("tp"),
            P("tp"),
            P(None, "tp"),
            P(None, "tp"),
            P(None, "tp"),
            P(),
            P("tp"),
            P("tp"),
            P("tp"),
            P("tp"),
            P("tp"),
        ),
        check_vma=False,
    )
```

```python
import functools
from types import SimpleNamespace
from typing import NamedTuple

import jax
import jax.numpy as jnp
from jax import lax
from jax.experimental import pallas as pl
from jax.experimental.pallas import tpu as pltpu
from jax.sharding import PartitionSpec as P

EPS_NORM = 1e-05
EPS_FACTOR = 1e-30
DECAY = 0.5
CLIP = 0.5
RATES = (0.45, 0.02, 0.03, 0.1, 0.05, 0.016, 0.09, 1.8, 0.3, 0.45)
MESH = pl.DeviceIdType.MESH
LOG2E = 1.4426950408889634
RESET = 1e9
TILE = 512
X_FIRST = (4, 8)
SHARE_WIDTH = 256
SLOTS = 8
RENEW_TILES = 2
VMEM_LIMIT = 48 * 1024 * 1024
FINISH_LIMIT = 63 * 1024 * 1024


def passed_along(value, axis, steps):
    count = lax.axis_size(axis)
    initial, last = (max(0, -steps), min(count, count - steps))
    return lax.ppermute(value, axis, [(source, source + steps) for source in range(initial, last)])


def silu_slope(values):
    sigmoid_v = jax.nn.sigmoid(values)
    return sigmoid_v * (1.0 + values * (1.0 - sigmoid_v))


def factor_update(grad, row_sums, rows_old, cols_old, channels):
    rows_new = DECAY * rows_old + (1.0 - DECAY) * (row_sums / channels + EPS_FACTOR)
    cols_new = DECAY * cols_old + (1.0 - DECAY) * (jnp.mean(grad * grad, axis=0) + EPS_FACTOR)
    scale_sq = rows_new[:, None] * cols_new[None, :] / jnp.mean(rows_new)
    return (rows_new, cols_new, grad * lax.rsqrt(scale_sq))


def moment_update(grad_in, moment_old):
    moment_new = DECAY * moment_old + (1.0 - DECAY) * (grad_in * grad_in + EPS_FACTOR)
    return (moment_new, grad_in * lax.rsqrt(moment_new))


def sum_squares(update):
    return jnp.sum(update * update)


def apply_step(weight, update, total_sum, count_all, step_rate):
    root_mean = jnp.sqrt(total_sum / count_all)
    return weight - step_rate * update / jnp.maximum(1.0, root_mean / CLIP)


def wide(tile, width):
    return jnp.concatenate([tile] * (width // tile.shape[1]), axis=1)


def fold_lanes(value):
    pieces = [value[:, at : at + 128] for at in range(0, value.shape[1], 128)]
    while len(pieces) > 1:
        pieces = [first + second for first, second in zip(pieces[::2], pieces[1::2])]
    return pieces[0]


def state_kernel(backward, step_ref, value_ref, lane_ref, rate_ref, out_ref):
    rows, width = step_ref.shape
    states = rate_ref.shape[0]
    rate = rate_ref[...] * LOG2E

    def block(index, state):
        base = pl.multiple_of((rows // 8 - 1 - index if backward else index) * 8, 8)
        for offset in range(8):
            at = base + (7 - offset if backward else offset)
            keep = jnp.exp2(rate * step_ref[pl.ds(at, 1), :])
            term = wide(lane_ref[at], width) * value_ref[pl.ds(at, 1), :]
            state = keep * (state + term) if backward else keep * state + term
        return state

    out_ref[0:states, :] = lax.fori_loop(0, rows // 8, block, jnp.zeros((states, width), jnp.float32))
    total = jnp.sum(step_ref[...], axis=0, keepdims=True)
    out_ref[states:, :] = jnp.broadcast_to(total, (out_ref.shape[0] - states, width))


def piece_state(step, value, lane, rate, backward):
    rows, width = step.shape
    states = rate.shape[0]
    tile = TILE
    return pl.pallas_call(
        functools.partial(state_kernel, backward),
        grid=(width // tile,),
        in_specs=[
            pl.BlockSpec((rows, tile), lambda i: (0, i)),
            pl.BlockSpec((rows, tile), lambda i: (0, i)),
            pl.BlockSpec((rows, states, 128), lambda i: (0, 0, 0)),
            pl.BlockSpec((states, tile), lambda i: (0, i)),
        ],
        out_specs=pl.BlockSpec((states + 8, tile), lambda i: (0, i)),
        out_shape=jax.ShapeDtypeStruct((states + 8, width), jnp.float32),
        compiler_params=pltpu.CompilerParams(vmem_limit_bytes=VMEM_LIMIT),
    )(step, value, lane, rate)


def forward_kernel(
    step_ref, drive_ref, enter_ref, leave_ref, rate_ref, start_ref, out_ref
):
    rows, width = step_ref.shape
    rate = rate_ref[...] * LOG2E

    def block(index, state):
        base = pl.multiple_of(index * 8, 8)
        for offset in range(8):
            at = base + offset
            keep = jnp.exp2(rate * step_ref[pl.ds(at, 1), :])
            state = keep * state + wide(enter_ref[at], width) * drive_ref[pl.ds(at, 1), :]
            out_ref[pl.ds(at, 1), :] = jnp.sum(
                wide(leave_ref[at], width) * state, axis=0, keepdims=True
            )
        return state

    lax.fori_loop(0, rows // 8, block, start_ref[...])


def scan_forward(step, drive, enter, leave, rate, start):
    rows, width = step.shape
    states = rate.shape[0]
    tile = TILE
    by_tile = pl.BlockSpec((rows, tile), lambda i: (0, i))
    by_state = pl.BlockSpec((states, tile), lambda i: (0, i))
    whole = pl.BlockSpec((rows, states, 128), lambda i: (0, 0, 0))
    return pl.pallas_call(
        forward_kernel,
        grid=(width // tile,),
        in_specs=[by_tile, by_tile, whole, whole, by_state, by_state],
        out_specs=by_tile,
        out_shape=jax.ShapeDtypeStruct((rows, width), jnp.float32),
        compiler_params=pltpu.CompilerParams(vmem_limit_bytes=VMEM_LIMIT),
    )(step, drive, enter, leave, rate, start)


def backward_kernel(
    step_ref,
    drive_ref,
    grad_ref,
    enter_ref,
    leave_ref,
    rate_ref,
    start_ref,
    follow_ref,
    drive_grad_ref,
    step_grad_ref,
    decay_ref,
    enter_grad_ref,
    leave_grad_ref,
    kept_ref,
    state_ref,
):
    rows, width = step_ref.shape
    rate_own = rate_ref[...]
    rate = rate_own * LOG2E

    @pl.when(pl.program_id(0) == 0)
    def _():
        enter_grad_ref[...] = jnp.zeros_like(enter_grad_ref)
        leave_grad_ref[...] = jnp.zeros_like(leave_grad_ref)

    def again(index, state):
        base = pl.multiple_of(index * 8, 8)
        for offset in range(8):
            at = base + offset
            keep = jnp.exp2(rate * step_ref[pl.ds(at, 1), :])
            kept_ref[at] = keep
            state = keep * state + wide(enter_ref[at], width) * drive_ref[pl.ds(at, 1), :]
            state_ref[at + 1] = state
        return state

    start = start_ref[...]
    state_ref[0] = start
    lax.fori_loop(0, rows // 8, again, start)
    follow = follow_ref[...]

    def block(index, carry):
        follow, decay = carry
        base = pl.multiple_of((rows // 8 - 1 - index) * 8, 8)
        for offset in range(7, -1, -1):
            at = base + offset
            grad = grad_ref[pl.ds(at, 1), :]
            adjoint = wide(leave_ref[at], width) * grad + follow
            drive_grad_ref[pl.ds(at, 1), :] = jnp.sum(
                adjoint * wide(enter_ref[at], width), axis=0, keepdims=True
            )
            enter_grad_ref[at] += fold_lanes(adjoint * drive_ref[pl.ds(at, 1), :])
            leave_grad_ref[at] += fold_lanes(state_ref[at + 1] * grad)
            follow = kept_ref[at] * adjoint
            part = follow * state_ref[at]
            step_grad_ref[pl.ds(at, 1), :] = jnp.sum(part * rate_own, axis=0, keepdims=True)
            decay = decay + part * step_ref[pl.ds(at, 1), :]
        return follow, decay

    _, decay = lax.fori_loop(0, rows // 8, block, (follow, jnp.zeros_like(follow)))
    decay_ref[...] = decay * rate_own


def scan_backward(step, drive, grad, enter, leave, rate, start, follow):
    rows, width = step.shape
    states = rate.shape[0]
    tile = TILE
    by_tile = pl.BlockSpec((rows, tile), lambda i: (0, i))
    by_state = pl.BlockSpec((states, tile), lambda i: (0, i))
    whole = pl.BlockSpec((rows, states, 128), lambda i: (0, 0, 0))
    return pl.pallas_call(
        backward_kernel,
        grid=(width // tile,),
        in_specs=[by_tile, by_tile, by_tile, whole, whole, by_state, by_state, by_state],
        out_specs=[by_tile, by_tile, by_state, whole, whole],
        out_shape=[
            jax.ShapeDtypeStruct((rows, width), jnp.float32),
            jax.ShapeDtypeStruct((rows, width), jnp.float32),
            jax.ShapeDtypeStruct((states, width), jnp.float32),
            jax.ShapeDtypeStruct((rows, states, 128), jnp.float32),
            jax.ShapeDtypeStruct((rows, states, 128), jnp.float32),
        ],
        scratch_shapes=[
            pltpu.VMEM((rows, states, tile), jnp.float32),
            pltpu.VMEM((rows + 1, states, tile), jnp.float32),
        ],
        compiler_params=pltpu.CompilerParams(vmem_limit_bytes=VMEM_LIMIT),
    )(step, drive, grad, enter, leave, rate, start, follow)


def on_block():
    return lax.axis_size("seq") == 16 and lax.axis_size("tp") == 2


def position():
    place = lax.axis_index("seq")
    return lax.div(place, 4), lax.rem(lax.div(place, 2), 2), lax.rem(place, 2)


def device(z, x, core):
    return (z * 4 + x * 2 + core, lax.axis_index("tp"))


def other_half():
    return (lax.axis_index("seq"), 1 - lax.axis_index("tp"))


def greet(peers):
    barrier = pltpu.get_barrier_semaphore()
    for peer in peers:
        pl.semaphore_signal(barrier, inc=1, device_id=peer, device_id_type=MESH)
    pl.semaphore_wait(barrier, len(peers))


def remote(source, target, sent, arrived, peer):
    return pltpu.make_async_remote_copy(
        src_ref=source,
        dst_ref=target,
        send_sem=sent,
        recv_sem=arrived,
        device_id=peer,
        device_id_type=MESH,
    )


def sum_over(seq_part, shared_part, tp_part):
    return lax.psum(seq_part, "seq"), lax.psum(shared_part, ("seq", "tp")), lax.psum(tp_part, "tp")


def project(half, weight, ident):
    hidden = lax.all_gather(half, "tp", axis=0, tiled=True)
    full = lax.all_gather(weight, "seq", axis=0, tiled=True)
    return jnp.dot(hidden, full, preferred_element_type=jnp.float32), hidden, full[None]


def pair_kernel(mine_ref, out_ref, far, sent, arrived):
    greet([other_half()])
    copy = remote(mine_ref, far, sent, arrived, other_half())
    copy.start()
    copy.wait()
    out_ref[...] = mine_ref[...] + far[...]


def pair_sum(value, ident):
    if not on_block():
        return lax.psum(value, "tp")
    vmem = pl.BlockSpec(memory_space=pltpu.VMEM)
    return pl.pallas_call(
        pair_kernel,
        in_specs=[vmem],
        out_specs=vmem,
        out_shape=jax.ShapeDtypeStruct(value.shape, value.dtype),
        scratch_shapes=[
            pltpu.VMEM(value.shape, value.dtype),
            pltpu.SemaphoreType.DMA,
            pltpu.SemaphoreType.DMA,
        ],
        compiler_params=pltpu.CompilerParams(collective_id=ident, has_side_effects=True),
    )(value)


def chain_kernel(backward, piece_ref, rate_ref, swap_ref, out_ref, swapped_ref, come, back, sems, swap_sems):
    place = lax.axis_index("seq")
    states = rate_ref.shape[0]
    peers = [(lax.rem(place + step, 16), lax.axis_index("tp")) for step in range(1, 16)]
    greet(peers + [other_half()])
    swap = remote(swap_ref, swapped_ref, swap_sems.at[0], swap_sems.at[1], other_half())
    swap.start()

    def lanes(at):
        return pl.ds(pl.multiple_of(at * 128, 128), 128)

    def out(at):
        return remote(
            piece_ref.at[:, lanes(peers[at][0])],
            come.at[place],
            sems.at[0, at],
            sems.at[1, at],
            peers[at],
        )

    def home(at):
        return remote(
            back.at[peers[at][0]],
            out_ref.at[:, lanes(place)],
            sems.at[2, at],
            sems.at[3, at],
            peers[at],
        )

    for at in range(15):
        out(at).start()
    come[place] = piece_ref[:, lanes(place)]
    rate = rate_ref[:, lanes(place)] * LOG2E
    for at in range(15):
        out(at).wait_recv()

    def join(index, state):
        at = 15 - index if backward else index
        back[at] = state
        piece = come[at]
        return jnp.exp2(rate * piece[states : states + 1]) * state + piece[:states]

    lax.fori_loop(0, 16, join, jnp.zeros((states, 128), jnp.float32))
    for at in range(15):
        home(at).start()
    out_ref[:, lanes(place)] = back[place]
    for at in range(15):
        home(at).wait_recv()
    for at in range(15):
        out(at).wait_send()
        home(at).wait_send()
    swap.wait()


def chain(piece, rate, swap, backward, ident):
    states, width = rate.shape
    if not on_block():
        count, place = lax.axis_size("seq"), lax.axis_index("seq")
        pieces = lax.all_gather(piece, "seq")

        def join(index, state):
            at = count - 1 - index if backward else index
            longer = (
                jnp.exp2(rate * LOG2E * pieces[at, states : states + 1]) * state + pieces[at, :states]
            )
            return jnp.where(at > place if backward else at < place, longer, state)

        state = lax.fori_loop(0, count, join, jnp.zeros((states, width), jnp.float32))
        order = [(0, 1), (1, 0)]
        return state, lax.ppermute(swap, "tp", order)
    vmem = pl.BlockSpec(memory_space=pltpu.VMEM)
    return pl.pallas_call(
        functools.partial(chain_kernel, backward),
        in_specs=[vmem, vmem, vmem],
        out_specs=[vmem, vmem],
        out_shape=[
            jax.ShapeDtypeStruct((states, width), jnp.float32),
            jax.ShapeDtypeStruct(swap.shape, swap.dtype),
        ],
        scratch_shapes=[
            pltpu.VMEM((16, states + 8, 128), jnp.float32),
            pltpu.VMEM((16, states, 128), jnp.float32),
            pltpu.SemaphoreType.DMA((4, 15)),
            pltpu.SemaphoreType.DMA((2,)),
        ],
        compiler_params=pltpu.CompilerParams(collective_id=ident, has_side_effects=True),
    )(piece, rate, swap)


def wait_all(copies):
    for copy in copies:
        copy.wait_recv()


def gathered(refs, *groups):
    named, at = {}, 0
    for group in groups:
        named.update(zip(group._fields, refs[at:]))
        at += len(group._fields)
    return SimpleNamespace(**named), list(refs[at:])


def mirrored(r, group, near, sems, outward):
    copies = []
    for at, name in enumerate(group._fields):
        ends = (near[at], getattr(r, name)) if outward else (getattr(r, name), near[at])
        copies.append(pltpu.make_async_copy(*ends, sems.at[at]))
        setattr(r, name, near[at])
    return group(*copies)


def mirrors(group, shapes):
    named = shapes._asdict()
    picked = [named[name] for name in group._fields]
    return [pltpu.VMEM(ref.shape, ref.dtype) for ref in picked] + [
        pltpu.SemaphoreType.DMA((len(picked),))
    ]


def placed(group, *lazy):
    names = [name for other in lazy for name in other._fields]
    return [
        pl.BlockSpec(memory_space=pltpu.HBM if name in names else pltpu.VMEM)
        for name in group._fields
    ]


def shared(source, group):
    return {name: value for name, value in source._asdict().items() if name in group._fields}


class Reducer:
    def __init__(self, jobs, refs):
        self.jobs, self.at = jobs, 0
        self.send, self.come = refs[:3], refs[3:6]
        self.sent, self.got, self.total = refs[6:9], refs[9:12], refs[12]
        self.z, self.x, self.core = position()
        self.chunks, self.width = len(jobs), self.come[2].shape[3]
        self.peers = [
            [device(self.z, self.x, 1 - self.core)],
            [device(self.z, 1 - self.x, self.core)],
            [device(lax.rem(self.z + step, 4), self.x, self.core) for step in (1, 2, 3)],
        ]

    def copies(self, level, chunk):
        slot = chunk % self.send[level].shape[0]
        if level < 2:
            return [
                remote(
                    self.send[level].at[slot],
                    self.come[level].at[chunk % SLOTS],
                    self.sent[level].at[chunk],
                    self.got[level].at[chunk],
                    self.peers[level][0],
                )
            ]
        return [
            remote(
                self.send[2].at[slot, 0, lax.rem(self.z + 1 + at, 4)],
                self.come[2].at[chunk % SLOTS, at],
                self.sent[2].at[chunk, at],
                self.got[2].at[chunk, at],
                self.peers[2][at],
            )
            for at in range(3)
        ]

    def free(self, level, chunk):
        older = chunk - self.send[level].shape[0]
        if older >= 0:
            for copy in self.copies(level, older):
                copy.wait_send()

    def product(self, chunk, first, count):
        left, right, start = self.jobs[chunk][:3]
        _, rows, depth = left.shape
        block = left[pl.ds(first, count)].reshape(count * rows, depth)
        value = jnp.dot(
            block, right[:, start : start + self.width], preferred_element_type=jnp.float32
        )
        return value.reshape(count, rows, self.width)

    def put(self, chunk, value, more):
        out, start = self.jobs[chunk][3:]
        here = slice(start, start + self.width)
        out[:, here] = out[:, here] + value if more else value

    def after_core(self, chunk, x):
        come = self.come[0][chunk % SLOTS, x].astype(jnp.float32)
        return self.product(chunk, self.core * 8 + x * 4, 4) + come

    def fill(self, level, chunk, values):
        self.free(level, chunk)
        slot = chunk % self.send[level].shape[0]
        for at, value in enumerate(values):
            self.send[level][slot, at] = value().astype(jnp.bfloat16)
        for copy in self.copies(level, chunk):
            copy.start()

    def stage(self, level, chunk):
        if not 0 <= chunk < self.chunks:
            return
        if level > 0:
            wait_all(self.copies(level - 1, chunk))
        if level == 0:
            away = (1 - self.core) * 8
            self.fill(
                0, chunk, [lambda at=at: self.product(chunk, away + at * 4, 4) for at in range(2)]
            )
        elif level == 1:
            self.fill(1, chunk, [lambda: self.after_core(chunk, 1 - self.x)])
        elif level == 2:
            come = self.come[1][chunk % SLOTS, 0].astype(jnp.float32)
            self.total[...] = self.after_core(chunk, self.x) + come
            self.fill(2, chunk, [lambda: self.total[...]])
            self.put(chunk, self.total[self.z], False)
        else:
            come = [self.come[2][chunk % SLOTS, at].astype(jnp.float32) for at in range(3)]
            self.put(chunk, (come[0] + come[1]) + come[2], True)

    def step(self, step):
        for level, lag in enumerate((0, 1, 3, 5)):
            self.stage(level, step - lag)

    def advance(self, count=1):
        for _ in range(count):
            if self.at < self.chunks + 5:
                self.step(self.at)
                self.at += 1

    def drain(self):
        for level in range(3):
            for chunk in range(max(0, self.chunks - self.send[level].shape[0]), self.chunks):
                for copy in self.copies(level, chunk):
                    copy.wait_send()


def reducer_scratch(columns, share, width):
    chunks = columns // width
    low, dma = jnp.bfloat16, pltpu.SemaphoreType.DMA
    return [
        pltpu.VMEM((4, 2, 4, share, width), low),
        pltpu.VMEM((4, 1, 4, share, width), low),
        pltpu.VMEM((4, 1, 4, share, width), low),
        pltpu.VMEM((SLOTS, 2, 4, share, width), low),
        pltpu.VMEM((SLOTS, 1, 4, share, width), low),
        pltpu.VMEM((SLOTS, 3, share, width), low),
        dma((chunks,)),
        dma((chunks,)),
        dma((chunks, 3)),
        dma((chunks,)),
        dma((chunks,)),
        dma((chunks, 3)),
        pltpu.VMEM((4, share, width), jnp.float32),
    ]


def rows_to_lanes(partial):
    return jnp.sum(partial.T, axis=0, keepdims=True)


def lanes_to_rows(row):
    return jnp.broadcast_to(row, (128, 128)).T


def finish_part(channels, model, r, main, stores):
    z, x, core = position()
    place, tp = lax.axis_index("seq"), lax.axis_index("tp")
    core_peer, x_peer = device(z, x, 1 - core), device(z, 1 - x, core)
    z_peers = [device(lax.rem(z + step, 4), x, core) for step in (1, 2, 3)]
    low = jnp.bfloat16
    half_rows = r.block.shape[0]
    own_half = pl.ds(pl.multiple_of(tp * half_rows, half_rows), half_rows)
    far_half = pl.ds(pl.multiple_of((1 - tp) * half_rows, half_rows), half_rows)
    d_hidden = r.d_hidden
    swap = remote(
        d_hidden.at[far_half], r.come_half, r.half_sems.at[0], r.half_sems.at[1], other_half()
    )
    sides = [r.d_value, r.d_gate]
    kept_chunks, _, kept_width = r.weights.shape

    def fetch(chunk):
        return pltpu.make_async_copy(
            r.weights.at[chunk], r.fetched.at[chunk % 2], r.fetched_sems.at[chunk]
        )

    def hidden_stage(chunk):
        fetch(chunk).wait()
        per_side = kept_chunks // 2
        at = chunk % per_side
        part = lax.dot_general(
            sides[chunk // per_side][:, at * kept_width : (at + 1) * kept_width],
            r.fetched[chunk % 2],
            (((1,), (1,)), ((), ())),
            preferred_element_type=jnp.float32,
        )
        d_hidden[...] = part if chunk == 0 else d_hidden[...] + part
        if chunk + 2 < kept_chunks:
            fetch(chunk + 2).start()
        if chunk == kept_chunks - 1:
            swap.start()

    fetch(0).start()
    fetch(1).start()

    sent, got = r.extra_sent, r.extra_got
    extra, full = r.extra, r.full
    extra_core = remote(extra.at[:, 1 - core], r.come_core, sent.at[0], got.at[0], core_peer)
    extra_x = remote(r.send_x, r.come_x, sent.at[1], got.at[1], x_peer)
    extra_z = [
        remote(r.send_z.at[at], r.come_z.at[at], sent.at[2 + at], got.at[2 + at], z_peers[at])
        for at in range(3)
    ]
    own, held, halves = full.at[z, x, core], full.at[:, x, core], full.at[:, :, core]
    back_z = [remote(own, own, sent.at[5 + at], got.at[5 + at], z_peers[at]) for at in range(3)]
    back_x = remote(held, held, sent.at[8], got.at[8], x_peer)
    back_core = remote(halves, halves, sent.at[9], got.at[9], core_peer)

    def extra_after_core(pair):
        return extra[pair, core].astype(jnp.float32) + r.come_core[pair].astype(jnp.float32)

    def extra_after_x(level):
        return extra_after_core(level * 2 + x) + r.come_x[level].astype(jnp.float32)

    def extra_stage_x():
        extra_core.wait_recv()

        def one(level, _):
            r.send_x[level] = extra_after_core(level * 2 + 1 - x).astype(low)
            return 0

        lax.fori_loop(0, 4, one, 0)
        extra_x.start()

    def extra_stage_z():
        extra_x.wait_recv()

        def one(at, _):
            r.send_z[at] = extra_after_x(lax.rem(z + 1 + at, 4)).astype(low)
            return 0

        lax.fori_loop(0, 3, one, 0)
        for copy in extra_z:
            copy.start()

    def extra_stage_last():
        wait_all(extra_z)
        total = extra_after_x(z)
        for at in range(3):
            total = total + r.come_z[at].astype(jnp.float32)
        full[z, x, core] = total.astype(low)
        for copy in back_z:
            copy.start()

    def extra_back_x():
        wait_all(back_z)
        back_x.start()

    def extra_back_core():
        back_x.wait_recv()
        back_core.start()

    mine = r.mine
    vectors_new = r.vectors_new

    def line(ref):
        return ref[...].reshape(1, -1)

    half = r.out_grad.shape[1]
    tiles = half // 128
    gain_tiles = model // 128

    def put(base, row):
        for at in range(row.shape[1] // 128):
            mine[base + at : base + at + 1, :] = row[:, at * 128 : (at + 1) * 128]

    def take(ref, base, tiles):
        return jnp.concatenate([ref[base + at : base + at + 1, :] for at in range(tiles)], axis=1)

    def residual_stage():
        swap.wait()
        total = d_hidden[own_half, :] + r.come_half[...]
        residual = r.block[...].astype(jnp.float32)
        inv_rms = lax.rsqrt(jnp.mean(residual * residual, axis=1, keepdims=True) + EPS_NORM)
        normed = residual * inv_rms
        put(2 * tiles, jnp.sum(total * normed, axis=0, keepdims=True))
        scaled = total * line(r.norm_gain)
        mean = jnp.mean(scaled * normed, axis=1, keepdims=True)
        r.input_grad[...] = r.cot[own_half, :].astype(jnp.float32) + inv_rms * (scaled - normed * mean)

    span = 512
    wide_span = span // 128
    small = r.small
    groups = {"step": (0, 128), "select": (128, 288), "decay": (288, 304), "conv": (304, 308)}
    pair = r.pair

    def put_rows(at, partial):
        pair[at : at + 1, :] = rows_to_lanes(partial)

    def fold_square(value):
        return fold_lanes(value * value)

    def small_stage():
        back_core.wait_recv()
        for block in range(16):
            small[:, block * 128 : (block + 1) * 128] = full[
                block // 4, block // 2 % 2, block % 2
            ].astype(jnp.float32)
        for at in range(3):
            rows = min(128, small.shape[0] - at * 128)

            def one(index, partial):
                columns = pl.ds(pl.multiple_of(index * span, span), span)
                return partial + fold_square(small[at * 128 : at * 128 + rows, columns])

            partial = lax.fori_loop(
                0, small.shape[1] // span, one, jnp.zeros((rows, 128), jnp.float32)
            )
            if rows < 128:
                partial = jnp.concatenate(
                    [partial, jnp.zeros((128 - rows, 128), jnp.float32)], axis=0
                )
            put_rows(at, partial)

    late = 2 * tiles + gain_tiles + 8
    row_sums = r.row_sums

    def square_sums(ref, start, width, base):
        value = ref[:, start : start + width]
        put(base, jnp.sum(value * value, axis=0, keepdims=True))
        return fold_square(value)

    def in_stage(chunk):
        start = (chunk - main.chunks // 3) * main.width
        if start < 0 or chunk >= main.chunks:
            return
        gate = start < half
        base = start // 128 if gate else late + (start - half) // 128
        start = half + start if gate else start - half
        part = square_sums(r.in_grad, start, main.width, base)
        row_sums[...] = part if base == 0 else row_sums[...] + part

    def out_stage():
        part = jnp.zeros((r.out_grad.shape[0], 128), jnp.float32)
        for start in range(0, half, span):
            part = part + square_sums(r.out_grad, start, span, tiles + start // 128)
        put_rows(4, part)

    lanes = r.lanes
    row_at = lax.broadcasted_iota(jnp.int32, lanes.shape, 0)
    lane_at = lax.broadcasted_iota(jnp.int32, lanes.shape, 1)
    counts = jnp.where(row_at == 3, 2.0 * channels, 1.0 * channels)
    held_lanes = DECAY * lanes[...] + (1.0 - DECAY) * EPS_FACTOR
    def total(value):
        return jnp.sum(jnp.sum(value, axis=1, keepdims=True), axis=0, keepdims=True)

    def put_mean(at, sums, first):
        part = jnp.where(tp == 0, held_lanes, 0.0) + (1.0 - DECAY) * sums[...] / counts
        mean = total(jnp.where(row_at == at, part, 0.0)) / model
        mine[first : first + 8, :] = jnp.broadcast_to(mean, (8, 128))

    sums_sent, sums_got = r.sums_sent, r.sums_got

    def hop(at, source, target, peer):
        return remote(source, target, sums_sent.at[at], sums_got.at[at], peer)

    plane = x * 2 + core
    mates = [core_peer, x_peer, device(z, 1 - x, 1 - core)]
    across = [(lax.rem(z + step, 4) * 4 + plane, 1 - tp) for step in range(4)]

    def sum_hops(first, value, acc, far, shared):
        plane_copies = [hop(first + at, acc.at[plane], acc.at[plane], mates[at]) for at in range(3)]
        part = acc.at[4 + z]
        z_copies = [hop(first + 3 + at, part, part, z_peers[at]) for at in range(3)]
        z_copies += [hop(first + 6 + at, part.at[shared:], far.at[z], across[at]) for at in range(4)]

        def begin():
            acc[plane] = value[...]
            for copy in plane_copies:
                copy.start()

        def middle():
            for copy in plane_copies:
                copy.wait()
            acc[4 + z] = (acc[0] + acc[1]) + (acc[2] + acc[3])
            for copy in z_copies:
                copy.start()

        def end():
            for copy in z_copies:
                copy.wait()
            value[...] = (acc[4] + acc[5]) + (acc[6] + acc[7])
            value[shared:] = value[shared:] + ((far[0] + far[1]) + (far[2] + far[3]))

        return begin, middle, end

    def cols_new(old, sums, count):
        return DECAY * old + (1.0 - DECAY) * (sums / count + EPS_FACTOR)

    def part_hops(first, low_row, high_row, low_far, high_far):
        return sum_hops(
            first,
            mine.at[low_row:high_row],
            r.acc.at[:, low_row:high_row],
            r.far.at[:, low_far:high_far],
            high_row - low_row - (high_far - low_far),
        )

    shared_rows = gain_tiles + 8
    early_hops = part_hops(0, 0, late, 0, shared_rows)
    late_hops = part_hops(20, late, late + tiles + 8, shared_rows, shared_rows + 8)
    pair_copy = hop(30, pair, r.pair_far, other_half())
    last_copy = hop(31, r.pair_last, r.pair_last_far, other_half())
    scales_out = r.scales
    sums = {}

    def early_begin():
        put_mean(4, pair, 2 * tiles + gain_tiles)
        pair_copy.start()
        early_hops[0]()

    def squares(ref, row_scale, first_row):
        def one(index, partial):
            columns = pl.ds(pl.multiple_of(index * span, span), span)
            col = vectors_new[pl.ds(first_row + lax.div(index, half // span), 1), pl.ds(
                pl.multiple_of(lax.rem(index, half // span) * span, span), span
            )]
            return partial + fold_square(ref[:, columns] * wide(row_scale, span) * lax.rsqrt(col))

        return total(
            lax.fori_loop(0, ref.shape[1] // span, one, jnp.zeros((ref.shape[0], 128), jnp.float32))
        )

    group_cols = {
        "step": (r.step_cols, 8),
        "select": (r.select_cols, 7),
        "decay": (r.decay_cols, 9),
        "conv": (r.conv_cols, 6),
    }

    def early_end():
        early_hops[2]()
        pair_copy.wait()
        lanes_new = held_lanes + (1.0 - DECAY) * (pair[...] + r.pair_far[...]) / counts
        r.lanes_new[...] = lanes_new
        flat = row_at * 128 + lane_at
        base = 2 * tiles + gain_tiles
        means = mine[base : base + 8, :]
        for low_edge, high_edge in groups.values():
            member = (flat >= low_edge) & (flat < high_edge)
            mean = total(jnp.where(member, lanes_new, 0.0)) / (high_edge - low_edge)
            means = jnp.where(member, mean, means)
        scale = lax.rsqrt(lanes_new / means)
        for at in (0, 1, 2, 4):
            scales_out[at] = lanes_to_rows(scale[at : at + 1, :])
        vectors_new[4:5, :] = cols_new(r.in_cols[1:2, :], take(mine, 0, tiles), model)
        vectors_new[5:6, :] = cols_new(line(r.out_cols), take(mine, tiles, tiles), model)
        sums["out"] = squares(r.out_grad, scales_out[4], 5)
        small_scale = jnp.concatenate([scales_out[0], scales_out[1], scales_out[2]], axis=0)
        for name, (low_edge, high_edge) in groups.items():
            old_cols, new_row = line(group_cols[name][0]), group_cols[name][1]
            partial = jnp.zeros((high_edge - low_edge, 128), jnp.float32)
            for at in range(0, small.shape[1], span):
                columns = slice(at, at + span)
                value = small[low_edge:high_edge, columns]
                col = cols_new(
                    old_cols[:, columns],
                    jnp.sum(value * value, axis=0, keepdims=True),
                    high_edge - low_edge,
                )
                vectors_new[new_row : new_row + 1, columns] = col
                row_scale = small_scale[low_edge:high_edge]
                partial = partial + fold_square(value * wide(row_scale, span) * lax.rsqrt(col))
            sums[name] = total(partial)
        for at in range(3):
            value = small[308 + at : 309 + at, :]
            old = line((r.bias_moment, r.step_moment, r.skip_moment)[at])
            moment = DECAY * old + (1.0 - DECAY) * (value * value + EPS_FACTOR)
            vectors_new[24 + at : 25 + at, :] = moment
            vectors_new[18 + at : 19 + at, :] = value
            update = value * lax.rsqrt(moment)
            vectors_new[21 + at : 22 + at, :] = update
            sums[at] = jnp.sum(update * update, axis=1, keepdims=True)
        gain_grad = take(mine, 2 * tiles, gain_tiles)
        moment = DECAY * line(r.norm_moment) + (1.0 - DECAY) * (gain_grad * gain_grad + EPS_FACTOR)
        update = gain_grad * lax.rsqrt(moment)
        root = jnp.sqrt(jnp.mean(update * update, axis=1, keepdims=True))
        vectors_new[0:1, :] = gain_grad
        vectors_new[1:2, :] = line(r.norm_gain) - RATES[0] / jnp.maximum(1.0, root / CLIP) * update
        vectors_new[2:3, :] = moment
        vectors_new[10:18, :] = jnp.zeros((8, half), jnp.float32)
        vectors_new[27:32, :] = jnp.zeros((5, half), jnp.float32)

    pair[...] = jnp.zeros(pair.shape, jnp.float32)
    r.pair_last[...] = jnp.zeros(pair.shape, jnp.float32)
    extra_core.start()
    extra_steps = {1: extra_stage_x, 3: extra_stage_z, 5: extra_stage_last, 7: extra_back_x, 9: extra_back_core}
    extra_steps.update({2: out_stage, 10: residual_stage, 11: small_stage})
    extra_steps.update({12: early_begin, 13: early_hops[1], 14: early_end})
    for step in range(max(main.chunks + 5 - main.at, 15)):
        main.advance()
        in_stage(main.at - 6)
        if step < kept_chunks:
            hidden_stage(step)
        if step in extra_steps:
            extra_steps[step]()
        if step == 11:
            for copy in stores:
                copy.start()

    r.pair_last[3:4, :] = rows_to_lanes(row_sums[...])
    last_copy.start()
    put_mean(3, r.pair_last, late + tiles)
    for action in late_hops:
        action()
    last_copy.wait()
    sums_in = (r.pair_last[...] + r.pair_last_far[...]) / counts
    lanes_new = jnp.where(row_at == 3, held_lanes + (1.0 - DECAY) * sums_in, r.lanes_new[...])
    r.lanes_new[...] = lanes_new
    in_mean = mine[late + tiles : late + tiles + 1, :]
    in_scale = lanes_to_rows(lax.rsqrt(lanes_new[3:4, :] / in_mean))
    vectors_new[3:4, :] = cols_new(r.in_cols[0:1, :], take(mine, late, tiles), model)
    in_sum = squares(r.in_grad, in_scale, 3)
    totals = r.totals
    for at, value in enumerate([in_sum, *sums.values()]):
        totals[at : at + 1, :] = jnp.broadcast_to(value, (1, 128))
    totals[9:16, :] = jnp.zeros((7, 128), jnp.float32)
    for action in sum_hops(10, totals, r.totals_acc, r.totals_far, 0):
        action()

    def rate(at, count, step_rate, copies):
        root = jnp.sqrt(totals[at : at + 1, :] / (copies * count))
        return step_rate / jnp.maximum(1.0, root / CLIP)

    in_rate = rate(0, 2.0 * channels * model, RATES[1], 1)
    out_rate = rate(1, 1.0 * channels * model, RATES[2], 1)

    scales_out[3] = in_scale * in_rate
    scales_out[4] = scales_out[4] * out_rate
    small_scale = jnp.concatenate([scales_out[0], scales_out[1], scales_out[2]], axis=0)
    small_rates = {"step": RATES[6], "select": RATES[5], "decay": RATES[8], "conv": RATES[3]}
    at_total = {"step": 2, "select": 3, "decay": 4, "conv": 5}
    row_number = lax.broadcasted_iota(jnp.int32, small_scale.shape, 0)
    for name, (low_edge, high_edge) in groups.items():
        step_rate = rate(
            at_total[name], 1.0 * (high_edge - low_edge) * channels, small_rates[name], 16
        )
        member = (row_number >= low_edge) & (row_number < high_edge)
        small_scale = jnp.where(member, small_scale * step_rate, small_scale)
    for at in range(3):
        scales_out[at] = small_scale[at * 128 : (at + 1) * 128, :]
    for at, step_rate in enumerate((RATES[4], RATES[7], RATES[9])):
        step_rate = rate(6 + at, 1.0 * channels, step_rate, 16)
        vectors_new[21 + at : 22 + at, :] = (
            line((r.conv_bias, r.step_bias, r.skip_gain)[at])
            - wide(step_rate, half) * vectors_new[21 + at : 22 + at, :]
        )

    for copy in [extra_core, extra_x] + extra_z + back_z + [back_x, back_core]:
        copy.wait_send()


class RenewIn(NamedTuple):
    value_grad: object
    gate_grad: object
    out_grad: object
    input_grad: object
    block_out: object
    small: object
    scales: object
    lanes_new: object
    vectors_new: object
    in_weight: object
    out_weight: object
    step_weight: object
    select_weight: object
    decay_log: object
    conv_weight: object


def renew_kernel(*refs):
    r, out = gathered(refs, RenewIn)
    cols, small, scales = r.vectors_new, r.small, r.scales
    span = small.shape[1]

    def write(*values):
        for value in values:
            ref = out.pop(0)
            ref[...] = value.astype(ref.dtype).reshape(ref.shape)

    def line(at):
        return cols[at : at + 1, :]

    def rows(low_edge, high_edge):
        flat = [r.lanes_new[at : at + 1, :] for at in range(5)]
        return jnp.concatenate(flat, axis=1)[:, low_edge:high_edge]

    def matrix(grad, weight, scale, col):
        new = weight - grad * wide(scale, span) * lax.rsqrt(line(col))
        write(grad, new, new)

    write(r.block_out[...], r.input_grad[...], line(0), line(1), line(1), line(2))
    in_refs = [out.pop(0) for _ in range(3)]
    for part, grad_ref in enumerate((r.value_grad, r.gate_grad)):
        grad = grad_ref[...]
        new = r.in_weight[:, part, :] - grad * wide(scales[3], span) * lax.rsqrt(line(3 + part))
        for ref, value in zip(in_refs, (grad, new, new)):
            ref[:, part, :] = value.astype(ref.dtype)
    write(rows(384, 512), cols[3:5, :])
    matrix(r.out_grad[...], r.out_weight[...], scales[4], 5)
    write(rows(512, 640), line(5))
    small_scale = jnp.concatenate([scales[0], scales[1], scales[2]], axis=0)
    matrix(small[304:308, :], r.conv_weight[...], small_scale[304:308], 6)
    write(rows(304, 308), line(6))
    write(line(18), line(21), line(21), line(24))
    matrix(small[128:288, :], r.select_weight[...], small_scale[128:288], 7)
    write(rows(128, 288), line(7))
    matrix(small[0:128, :], r.step_weight[...], small_scale[0:128], 8)
    write(rows(0, 128), line(8), line(19), line(22), line(22), line(25))
    matrix(small[288:304, :], r.decay_log[...], small_scale[288:304], 9)
    write(rows(288, 304), line(9))
    write(line(20), line(23), line(23), line(26))


def renew(given):
    f32, low = jnp.float32, jnp.bfloat16
    inner = given.out_grad.shape[1]
    shape = jax.ShapeDtypeStruct

    def three(ref):
        return [shape(ref.shape, f32), shape(ref.shape, f32), shape(ref.shape, low)]

    def vector(count):
        return shape((count,), f32)

    def trio(count):
        return [vector(count), vector(count), shape((count,), low)]

    model = given.block_out.shape[1]
    share = given.out_grad.shape[0]
    outs = (
        [shape(given.block_out.shape, f32), shape(given.input_grad.shape, f32)]
        + trio(model)
        + [vector(model)]
        + three(given.in_weight)
        + [vector(share), shape((2, inner), f32)]
        + three(given.out_weight)
        + [vector(share), vector(inner)]
        + three(given.conv_weight)
        + [vector(given.conv_weight.shape[0]), vector(inner)]
        + trio(inner)
        + [vector(inner)]
        + three(given.select_weight)
        + [vector(given.select_weight.shape[0]), vector(inner)]
        + three(given.step_weight)
        + [vector(given.step_weight.shape[0]), vector(inner)]
        + trio(inner)
        + [vector(inner)]
        + three(given.decay_log)
        + [vector(given.decay_log.shape[0]), vector(inner)]
        + trio(inner)
        + [vector(inner)]
    )
    span = inner // RENEW_TILES

    def by_tile(ref, first=0):
        *front, last = ref.shape
        if not front and last != inner:
            return pl.BlockSpec((last,), lambda i: (0,))
        zeros = (0,) * len(front)
        return pl.BlockSpec((*front, span), lambda i: zeros + (first + i,))

    def whole(ref):
        zeros = (0,) * len(ref.shape)
        return pl.BlockSpec(ref.shape, lambda i: zeros)

    specs = RenewIn(*[by_tile(ref) for ref in given])
    specs = specs._replace(
        gate_grad=by_tile(given.gate_grad, RENEW_TILES),
        scales=whole(given.scales),
        lanes_new=whole(given.lanes_new),
    )
    return tuple(
        pl.pallas_call(
            renew_kernel,
            grid=(RENEW_TILES,),
            in_specs=list(specs),
            out_specs=[by_tile(ref) for ref in outs],
            out_shape=outs,
            compiler_params=pltpu.CompilerParams(vmem_limit_bytes=FINISH_LIMIT),
        )(*given)
    )


class ForwardIn(NamedTuple):
    in_weight: object
    out_weight: object
    block: object
    cot: object
    norm_gain: object
    conv_weight: object
    conv_bias: object
    step_bias: object
    skip_gain: object
    masks: object
    select_weight: object
    step_weight: object
    decay_log: object


class ForwardOut(NamedTuple):
    hidden_t: object
    cot_t: object
    piece: object
    conv_in: object
    rim: object
    conv_pre: object
    conv_out: object
    select_out: object
    step_pre: object
    step_size: object
    held: object
    drive: object
    enter: object
    leave: object
    start: object
    gated: object
    d_mixed: object
    d_gate: object
    branch: object
    skip_grad: object
    weights: object


class ForwardLazy(NamedTuple):
    in_weight: object
    masks: object
    select_weight: object
    cot: object
    out_weight: object
    step_weight: object
    decay_log: object


class ForwardEarly(NamedTuple):
    hidden_t: object
    cot_t: object
    conv_in: object
    conv_pre: object
    conv_out: object
    step_pre: object
    step_size: object
    held: object
    drive: object
    enter: object
    leave: object
    start: object


class ForwardWork(NamedTuple):
    hidden: object
    full: object
    ext: object
    gate: object
    scanned: object
    state_piece: object
    come: object
    back: object
    select_far: object
    z_sent: object
    z_got: object
    x_sent: object
    x_got: object
    core_sems: object
    kept: object
    rim_sems: object
    chain_sems: object
    pair_sems: object


def forward_block_kernel(*refs):
    r, left = gathered(refs, ForwardIn, ForwardOut, ForwardWork)
    lazy, early = len(ForwardLazy._fields), len(ForwardEarly._fields)
    loads = mirrored(r, ForwardLazy, left[:lazy], left[lazy], False)
    stores = mirrored(r, ForwardEarly, left[lazy + 1 :], left[lazy + 1 + early], True)
    for copy in loads:
        copy.start()
    z, x, core = position()
    place, tp = lax.axis_index("seq"), lax.axis_index("tp")
    full, hidden = r.full, r.hidden

    def line(ref):
        return ref[...].reshape(1, -1)

    chunks, width = full.shape[0], full.shape[5]
    third = chunks // 3
    low = jnp.bfloat16
    z_peers = [device(lax.rem(z + step, 4), x, core) for step in (1, 2, 3)]
    x_peer, core_peer = device(z, 1 - x, core), device(z, x, 1 - core)
    seq_peers = [(lax.rem(place + step, 16), tp) for step in range(1, 16)]
    greet(seq_peers + [other_half()])

    def slot(chunk, level):
        if chunk in X_FIRST:
            return full.at[chunk, level, :, core]
        return full.at[chunk, level, x, core]

    def up(chunk, hop):
        ref = slot(chunk, z - hop)
        peer = device(z + 1, x, core)
        return remote(ref, ref, r.z_sent.at[chunk, hop], r.z_got.at[chunk, hop], peer)

    def down(chunk, hop):
        ref = slot(chunk, z + hop)
        peer = device(z - 1, x, core)
        return remote(ref, ref, r.z_sent.at[chunk, 3 + hop], r.z_got.at[chunk, 3 + hop], peer)

    def from_below(chunk, hop):
        ref = slot(chunk, z - hop)
        peer = device(z - 1, x, core)
        return remote(ref, ref, r.z_sent.at[chunk, hop - 1], r.z_got.at[chunk, hop - 1], peer)

    def from_above(chunk, hop):
        ref = slot(chunk, z + hop)
        peer = device(z + 1, x, core)
        return remote(ref, ref, r.z_sent.at[chunk, 2 + hop], r.z_got.at[chunk, 2 + hop], peer)

    def along_x(chunk, level):
        ref = full.at[chunk, level, x, core]
        return remote(ref, ref, r.x_sent.at[chunk, level], r.x_got.at[chunk, level], x_peer)

    def along_core(chunk):
        ref = full.at[chunk, :, :, core]
        return remote(ref, ref, r.core_sems.at[0, chunk], r.core_sems.at[1, chunk], core_peer)

    def keep(chunk):
        return pltpu.make_async_copy(full.at[chunk], r.weights.at[chunk], r.kept.at[chunk])

    def columns(at):
        return slice(at * width, (at + 1) * width)

    def when(condition, action):
        pl.when(condition)(action)

    def z_start(chunk):
        when(z < 3, lambda: up(chunk, 0).start())
        when(z > 0, lambda: down(chunk, 0).start())

    def z_hop(chunk, hop):
        def below():
            from_below(chunk, hop).wait_recv()
            if hop < 3:
                when(z < 3, lambda: up(chunk, hop).start())
            if chunk not in X_FIRST:
                along_x(chunk, z - hop).start()

        def above():
            from_above(chunk, hop).wait_recv()
            if hop < 3:
                when(z > 0, lambda: down(chunk, hop).start())
            if chunk not in X_FIRST:
                along_x(chunk, z + hop).start()

        when(z >= hop, below)
        when(z + hop < 4, above)

    def own_columns(chunk):
        if chunk < 2 * third:
            return r.in_weight[:, chunk // third, columns(chunk % third)]
        return r.out_weight[:, columns(chunk - 2 * third)]

    def ready(step):
        return 0 <= step < chunks

    def pump(step):
        for first in [step + 1] if step else range(2):
            if ready(first):
                full[first, z, x, core] = own_columns(first).astype(low)
                along_x(first, z).start()
                if first not in X_FIRST:
                    z_start(first)
        for hop in range(4):
            chunk = step - 1 - hop
            if not ready(chunk):
                continue
            late = 1 if chunk in X_FIRST else 0
            if late and hop == 0:
                along_x(chunk, z).wait_recv()
                z_start(chunk)
            elif hop + 1 - late < 4 and hop + 1 - late > 0:
                z_hop(chunk, hop + 1 - late)
            if hop == 3:
                if late == 0:
                    wait_all([along_x(chunk, level) for level in range(4)])
                along_core(chunk).start()
        if ready(step - 5):
            along_core(step - 5).wait_recv()
            if step - 5 < 2 * third:
                keep(step - 5).start()

    def weights(chunk):
        return full[chunk].reshape(hidden.shape[1], width)

    def dot(left, right):
        return jnp.dot(left, right, preferred_element_type=jnp.float32)

    def dot_last(left, right):
        return lax.dot_general(
            left, right, (((1,), (1,)), ((), ())), preferred_element_type=jnp.float32
        )

    half_rows = r.block.shape[0]
    mine = pl.ds(pl.multiple_of(tp * half_rows, half_rows), half_rows)
    residual = r.block[...].astype(jnp.float32)
    inv_rms = lax.rsqrt(jnp.mean(residual * residual, axis=1, keepdims=True) + EPS_NORM)
    hidden[mine] = (residual * inv_rms * line(r.norm_gain)).astype(low)
    pair_sems = r.pair_sems
    swap = remote(hidden.at[mine], hidden.at[mine], pair_sems.at[0], pair_sems.at[1], other_half())
    swap.start()
    loads.in_weight.wait()

    rows = hidden.shape[0]
    conv_in, conv_pre, conv_out, rim, ext = (
        r.conv_in,
        r.conv_pre,
        r.conv_out,
        r.rim,
        r.ext,
    )

    def rim_copy(tile):
        return remote(
            conv_in.at[rows - 16 :, columns(tile)],
            rim.at[:, columns(tile)],
            r.rim_sems.at[0, tile],
            r.rim_sems.at[1, tile],
            seq_peers[0],
        )

    def value_tile(tile):
        conv_in[:, columns(tile)] = dot(hidden[...], weights(tile)).astype(low)
        rim_copy(tile).start()

    masks = r.masks
    select_out = r.select_out

    def conv_tile(tile):
        rim_copy(tile).wait_recv()
        ext[0:8, :] = rim[8:16, columns(tile)].astype(jnp.float32)
        ext[8:, :] = conv_in[:, columns(tile)].astype(jnp.float32)
        conv_weight = r.conv_weight
        total = line(r.conv_bias)[:, columns(tile)] + conv_weight[0:1, columns(tile)] * ext[8:, :]
        for lag in range(1, 4):
            total = total + conv_weight[lag : lag + 1, columns(tile)] * (
                ext[8 - lag : 8 - lag + rows, :] * wide(masks[lag - 1], width)
            )
        conv_pre[:, columns(tile)] = total
        out = (total * jax.nn.sigmoid(total)).astype(low)
        conv_out[:, columns(tile)] = out
        select_low = r.select_weight[:, columns(tile)].astype(low)
        spare = jnp.zeros((select_out.shape[1] - select_low.shape[0], width), low)
        part = dot_last(out, jnp.concatenate([select_low, spare], axis=0))
        select_out[...] = part if tile == 0 else select_out[...] + part

    select_swap = remote(
        select_out, r.select_far, pair_sems.at[2], pair_sems.at[3], other_half()
    )
    enter, leave = r.enter, r.leave
    states = r.decay_log.shape[0]
    step_rank = r.step_weight.shape[0]
    held, drive = r.held, r.drive

    def select_stage():
        select_swap.wait()
        select_out[...] = select_out[...] + r.select_far[...]
        turned = select_out[:, step_rank : step_rank + 128].T
        for at in range(rows):
            enter[at] = jnp.broadcast_to(turned[:states, at : at + 1], (states, 128))
            leave[at] = jnp.broadcast_to(turned[states : 2 * states, at : at + 1], (states, 128))

    def step_tile(tile):
        here = columns(tile)
        step_low = r.step_weight[:, here].astype(low)
        pre = dot(select_out[:, :step_rank].astype(low), step_low) + line(r.step_bias)[:, here]
        size = jnp.maximum(pre, 0.0) + jnp.log1p(jnp.exp(-jnp.abs(pre)))
        r.step_pre[:, here] = pre
        r.step_size[:, here] = size
        held[:, here] = jnp.where(wide(masks[0], width) > 0.0, size, RESET)
        drive[:, here] = size * conv_out[:, here].astype(jnp.float32)

    piece = r.state_piece

    def rate_of(here):
        return -jnp.exp(r.decay_log[:, here]) * LOG2E

    def state_tile(tile):
        here = columns(tile)
        rate = rate_of(here)

        def block(index, state):
            base = pl.multiple_of(index * 8, 8)
            for offset in range(8):
                at = base + offset
                kept = jnp.exp2(rate * held[pl.ds(at, 1), here])
                state = kept * state + wide(enter[at], width) * drive[pl.ds(at, 1), here]
            return state

        piece[0:states, here] = lax.fori_loop(
            0, rows // 8, block, jnp.zeros((states, width), jnp.float32)
        )
        total = jnp.sum(held[:, here], axis=0, keepdims=True)
        piece[states:, here] = jnp.broadcast_to(total, (8, width))

    chain_out, chain_home, chain_middle, chain_end = chain_parts(
        False, piece, lambda: rate_of(own_lanes(place)), r.start, r.come, r.back, r.chain_sems
    )
    scanned, start = r.scanned, r.start

    def scan_tile(tile):
        here = columns(tile)
        rate = rate_of(here)

        def block(index, state):
            base = pl.multiple_of(index * 8, 8)
            for offset in range(8):
                at = base + offset
                kept = jnp.exp2(rate * held[pl.ds(at, 1), here])
                state = kept * state + wide(enter[at], width) * drive[pl.ds(at, 1), here]
                scanned[pl.ds(at, 1), here] = jnp.sum(
                    wide(leave[at], width) * state, axis=0, keepdims=True
                )
            return state

        lax.fori_loop(0, rows // 8, block, start[:, here])

    gate = r.gate

    def gate_tile(tile):
        gate[:, columns(tile)] = dot(hidden[...], weights(third + tile))

    def out_tile(tile):
        here = columns(tile)
        out_weight = weights(2 * third + tile)
        value = conv_out[:, here].astype(jnp.float32)
        mixed = scanned[:, here] + line(r.skip_gain)[:, here] * value
        pre = gate[:, here]
        sigmoid = jax.nn.sigmoid(pre)
        act = pre * sigmoid
        gated = (mixed * act).astype(low)
        r.gated[:, here] = gated
        d_gated = dot(r.cot[...], out_weight)
        d_mixed = d_gated * act
        r.d_mixed[:, here] = d_mixed
        slope = sigmoid * (1.0 + pre * (1.0 - sigmoid))
        r.d_gate[:, here] = (d_gated * mixed * slope).astype(low)
        r.skip_grad[:, here] = jnp.sum(d_mixed * value, axis=0, keepdims=True)
        part = dot_last(gated, out_weight)
        r.branch[...] = part if tile == 0 else r.branch[...] + part

    def adjoint_tile(tile):
        here = columns(tile)
        rate = rate_of(here)

        def block(index, state):
            base = pl.multiple_of((rows // 8 - 1 - index) * 8, 8)
            for offset in range(7, -1, -1):
                at = base + offset
                kept = jnp.exp2(rate * held[pl.ds(at, 1), here])
                state = kept * (state + wide(leave[at], width) * r.d_mixed[pl.ds(at, 1), here])
            return state

        r.piece[0:states, here] = lax.fori_loop(
            0, rows // 8, block, jnp.zeros((states, width), jnp.float32)
        )
        total = jnp.sum(held[:, here], axis=0, keepdims=True)
        r.piece[states:, here] = jnp.broadcast_to(total, (8, width))

    def turn(source, target):
        for at in range(target.shape[0]):
            value = source[:, at * 128 : (at + 1) * 128].astype(jnp.float32)
            target[at % 2 * 8 + at // 2 % 2 * 4 + at // 4] = value.T.astype(low)

    for step in range(third + 5):
        pump(step)
        if step == 2:
            swap.wait()
            for copy in loads[1:]:
                copy.wait()
        if step >= 5:
            value_tile(step - 5)
        if step >= 6:
            conv_tile(step - 6)
    conv_tile(third - 1)
    select_swap.start()
    pump(third + 5)
    gate_tile(0)
    select_stage()
    for tile in range(third):
        step_tile(tile)
    pump(third + 6)
    gate_tile(1)
    for tile in range(third):
        state_tile(tile)
    chain_out()
    turn(r.cot, r.cot_t)
    chain_middle()
    turn(hidden, r.hidden_t)
    pump(third + 7)
    gate_tile(2)
    chain_home()
    for tile in range(third):
        scan_tile(tile)
    pump(third + 8)
    gate_tile(3)
    for copy in stores:
        copy.start()
    for tile in range(third):
        pump(2 * third + 5 + tile)
        out_tile(tile)
        adjoint_tile(tile)
    chain_end()
    for chunk in range(chunks):
        for hop in range(3):
            when((z < 3) & (z >= hop), up(chunk, hop).wait_send)
            when((z > 0) & (z + hop < 4), down(chunk, hop).wait_send)
        for level in range(4):
            if chunk not in X_FIRST:
                along_x(chunk, level).wait_send()
        if chunk in X_FIRST:
            along_x(chunk, z).wait_send()
        along_core(chunk).wait_send()
        if chunk < 2 * third:
            keep(chunk).wait()
    for tile in range(third):
        rim_copy(tile).wait_send()
    for copy in stores:
        copy.wait()


def own_lanes(at):
    return pl.ds(pl.multiple_of(at * 128, 128), 128)


def chain_parts(backward, piece, rate_own, out, come, back, sems):
    place = lax.axis_index("seq")
    peers = [(lax.rem(place + step, 16), lax.axis_index("tp")) for step in range(1, 16)]
    states = out.shape[0]

    def away(at):
        return remote(
            piece.at[:, own_lanes(peers[at][0])],
            come.at[place],
            sems.at[0, at],
            sems.at[1, at],
            peers[at],
        )

    def home(at):
        return remote(
            back.at[peers[at][0]],
            out.at[:, own_lanes(place)],
            sems.at[2, at],
            sems.at[3, at],
            peers[at],
        )

    def begin():
        for at in range(15):
            away(at).start()
        come[place] = piece[:, own_lanes(place)]

    def middle():
        rate = rate_own()
        for at in range(15):
            away(at).wait_recv()

        def join(index, state):
            at = 15 - index if backward else index
            back[at] = state
            part = come[at]
            return jnp.exp2(rate * part[states : states + 1]) * state + part[:states]

        lax.fori_loop(0, 16, join, jnp.zeros((states, 128), jnp.float32))
        for at in range(15):
            home(at).start()
        out[:, own_lanes(place)] = back[place]

    def arrive():
        for at in range(15):
            home(at).wait_recv()

    def end():
        for at in range(15):
            away(at).wait_send()
            home(at).wait_send()

    return begin, arrive, middle, end


def forward_block(ident, given):
    half_rows, model = given.block.shape
    rows = 2 * half_rows
    share, inner = given.out_weight.shape
    total = 3 * inner
    states = given.decay_log.shape[0]
    f32, low = jnp.float32, jnp.bfloat16
    vmem = pl.BlockSpec(memory_space=pltpu.VMEM)
    dma = pltpu.SemaphoreType.DMA
    width = 512
    chunks = total // width
    select_rows = 256

    def like(columns, dtype):
        return jax.ShapeDtypeStruct((rows, columns), dtype)

    lanes = jax.ShapeDtypeStruct((rows, states, 128), f32)
    shapes = ForwardOut(*[
        jax.ShapeDtypeStruct((16, share, rows), low),
        jax.ShapeDtypeStruct((16, share, rows), low),
        jax.ShapeDtypeStruct((states + 8, inner), f32),
        like(inner, low),
        jax.ShapeDtypeStruct((16, inner), low),
        like(inner, f32),
        like(inner, low),
        like(select_rows, f32),
        like(inner, f32),
        like(inner, f32),
        like(inner, f32),
        like(inner, f32),
        lanes,
        lanes,
        jax.ShapeDtypeStruct((states, inner), f32),
        like(inner, low),
        like(inner, f32),
        like(inner, low),
        like(model, f32),
        jax.ShapeDtypeStruct((1, inner), f32),
        jax.ShapeDtypeStruct((chunks * 2 // 3, 4, 2, 2, share, width), low),
    ])
    specs = ForwardOut(*placed(ForwardOut, ForwardEarly))._replace(
        weights=pl.BlockSpec(memory_space=pltpu.HBM)
    )
    outs = pl.pallas_call(
        forward_block_kernel,
        in_specs=placed(ForwardIn, ForwardLazy),
        out_specs=list(specs),
        out_shape=list(shapes),
        scratch_shapes=[
            pltpu.VMEM((rows, model), low),
            pltpu.VMEM((chunks, 4, 2, 2, share, width), low),
            pltpu.VMEM((rows + 8, width), f32),
            pltpu.VMEM((rows, inner), f32),
            pltpu.VMEM((rows, inner), f32),
            pltpu.VMEM((states + 8, inner), f32),
            pltpu.VMEM((16, states + 8, 128), f32),
            pltpu.VMEM((16, states, 128), f32),
            pltpu.VMEM((rows, select_rows), f32),
            dma((chunks, 6)),
            dma((chunks, 6)),
            dma((chunks, 4)),
            dma((chunks, 4)),
            dma((2, chunks)),
            dma((chunks,)),
            dma((2, chunks // 3)),
            dma((4, 15)),
            dma((4,)),
        ]
        + mirrors(ForwardLazy, given)
        + mirrors(ForwardEarly, shapes),
        compiler_params=pltpu.CompilerParams(
            collective_id=ident, has_side_effects=True, vmem_limit_bytes=FINISH_LIMIT
        ),
    )(*given)
    out = ForwardOut(*outs)
    return out._replace(weights=out.weights.reshape(-1, model, width))


def backward_part(r, main, loads):
    z, x, core = position()
    place, tp = lax.axis_index("seq"), lax.axis_index("tp")
    low = jnp.bfloat16
    seq_peers = [(lax.rem(place + step, 16), tp) for step in range(1, 16)]
    rows, inner = r.held.shape
    states = r.decay_log.shape[0]
    width = 512
    tiles = inner // width
    pair_sems = r.pair_sems

    def columns(at):
        return slice(at * width, (at + 1) * width)

    def dot(left, right):
        return jnp.dot(left, right, preferred_element_type=jnp.float32)

    def dot_last(left, right):
        return lax.dot_general(
            left, right, (((1,), (1,)), ((), ())), preferred_element_type=jnp.float32
        )

    def line(ref):
        return ref[...].reshape(1, -1)

    half_rows = r.block.shape[0]
    own_half = pl.ds(pl.multiple_of(tp * half_rows, half_rows), half_rows)
    far_half = pl.ds(pl.multiple_of((1 - tp) * half_rows, half_rows), half_rows)
    branch_swap = remote(
        r.branch_send, r.branch_far, pair_sems.at[0], pair_sems.at[1], other_half()
    )

    held, drive, grad = r.held, r.drive, r.d_mixed
    enter, leave, piece = r.enter, r.leave, r.piece

    def rate_of(here):
        return -jnp.exp(r.decay_log[:, here])

    chain_out, chain_home, chain_middle, chain_end = chain_parts(
        True,
        piece,
        lambda: rate_of(own_lanes(place)) * LOG2E,
        r.follow,
        r.come,
        r.back,
        r.chain_sems,
    )
    kept_all, state_all = r.kept, r.state
    drive_grad, d_step_pre = r.drive_grad, r.d_step_pre
    enter_grad, leave_grad = r.enter_grad, r.leave_grad

    def again_tile(tile):
        here = columns(tile)
        rate = rate_of(here) * LOG2E

        def block(index, state):
            base = pl.multiple_of(index * 8, 8)
            for offset in range(8):
                at = base + offset
                kept = jnp.exp2(rate * held[pl.ds(at, 1), here])
                kept_all[at] = kept
                state = kept * state + wide(enter[at], width) * drive[pl.ds(at, 1), here]
                state_all[at + 1] = state
            return state

        start = r.start[:, here]
        state_all[0] = start
        lax.fori_loop(0, rows // 8, block, start)

    def reverse_tile(tile):
        here = columns(tile)
        rate = rate_of(here)

        def block(index, carry):
            follow, decay = carry
            base = pl.multiple_of((rows // 8 - 1 - index) * 8, 8)
            for offset in range(7, -1, -1):
                at = base + offset
                now = grad[pl.ds(at, 1), here]
                adjoint = wide(leave[at], width) * now + follow
                drive_grad[pl.ds(at, 1), here] = jnp.sum(
                    adjoint * wide(enter[at], width), axis=0, keepdims=True
                )
                enters = fold_lanes(adjoint * drive[pl.ds(at, 1), here])
                leaves = fold_lanes(state_all[at + 1] * now)
                if tile == 0:
                    enter_grad[at], leave_grad[at] = enters, leaves
                else:
                    enter_grad[at] += enters
                    leave_grad[at] += leaves
                follow = kept_all[at] * adjoint
                part = follow * state_all[at]
                r.ext[pl.ds(at, 1), :] = jnp.sum(part * rate, axis=0, keepdims=True)
                decay = decay + part * held[pl.ds(at, 1), here]
            return follow, decay

        follow = r.follow[:, here]
        _, decay = lax.fori_loop(0, rows // 8, block, (follow, jnp.zeros_like(follow)))
        r.decay_grad[:, here] = decay * rate
        d_step = (
            drive_grad[:, here] * r.conv_out[:, here].astype(jnp.float32) + r.ext[0:rows, :]
        )
        d_step_pre[:, here] = (d_step * jax.nn.sigmoid(r.step_pre[:, here])).astype(low)

    step_rank = r.step_weight.shape[0]
    select_grad = r.select_grad
    extra = r.extra

    def turned(value):
        return value.astype(jnp.float32).T.astype(low)

    def store_extra(first, tile, value):
        for at in range(width // 128):
            owner = tile * (width // 128) + at
            extra[owner // 2, owner % 2, first : first + value.shape[0], :] = value[
                :, at * 128 : (at + 1) * 128
            ].astype(low)

    def select_start():
        step_in = turned(r.select_out[:, :step_rank])
        total = jnp.zeros((rows, step_rank), jnp.float32)
        for tile in range(tiles):
            here = columns(tile)
            total = total + dot_last(d_step_pre[:, here], r.step_weight[:, here].astype(low))
            store_extra(0, tile, dot(step_in, d_step_pre[:, here]))
        select_grad[:, :step_rank] = total
        row_at = lax.broadcasted_iota(jnp.int32, (8, states, 128), 1)
        lane_at = lax.broadcasted_iota(jnp.int32, (8, states, 128), 2)

        def block(index, _):
            base = pl.multiple_of(index * 8, 8)
            here = pl.ds(base, 8)
            enters = jnp.sum(enter_grad[here], axis=2, keepdims=True)
            leaves = jnp.sum(leave_grad[here], axis=2, keepdims=True)
            spread = jnp.where(lane_at == row_at, enters, 0.0)
            spread = jnp.where(lane_at == row_at + states, leaves, spread)
            select_grad[here, step_rank:] = jnp.sum(spread, axis=1)
            return 0

        lax.fori_loop(0, rows // 8, block, 0)
        select_swap.start()

    select_swap = remote(
        select_grad, r.select_far, pair_sems.at[2], pair_sems.at[3], other_half()
    )
    conv_grad, rim_next, ext = r.conv_grad, r.rim_next, r.ext

    def rim_copy(tile):
        return remote(
            conv_grad.at[0:8, columns(tile)],
            rim_next.at[:, columns(tile)],
            r.rim_sems.at[0, tile],
            r.rim_sems.at[1, tile],
            seq_peers[14],
        )

    select_count = r.select_weight.shape[0]

    def select_end():
        select_swap.wait()
        total = (select_grad[...] + r.select_far[...]).astype(low)
        select_low = total[:, :256]
        first, second = turned(select_low[:, :128]), turned(select_low[:, 128:])
        for tile in range(tiles):
            here = columns(tile)
            conv_out = r.conv_out[:, here]
            store_extra(step_rank, tile, dot(first, conv_out))
            store_extra(step_rank + 128, tile, dot(second[: select_count - 128], conv_out))
            weight = r.select_weight[:, here].astype(low)
            spare = jnp.zeros((256 - select_count, width), low)
            d_conv = (
                drive_grad[:, here] * r.step_size[:, here]
                + grad[:, here] * line(r.skip_gain)[:, here]
                + dot(select_low, jnp.concatenate([weight, spare], axis=0))
            )
            pre = r.conv_pre[:, here]
            sigmoid = jax.nn.sigmoid(pre)
            conv_grad[:, here] = d_conv * (sigmoid * (1.0 + pre * (1.0 - sigmoid)))
            rim_copy(tile).start()
            if tile == 1:
                main.advance()

    masks, masks_after = r.masks, r.masks_after

    def conv_tile(tile):
        here = columns(tile)
        value = conv_grad[:, here]
        weight = r.conv_weight
        lines = []
        ext[0:8, :] = r.rim[8:16, here].astype(jnp.float32)
        ext[8:, :] = r.conv_in[:, here].astype(jnp.float32)
        for lag in range(4):
            shifted = ext[8 - lag : 8 - lag + rows, :]
            if lag > 0:
                shifted = shifted * wide(masks[lag - 1], width)
            lines.append(jnp.sum(value * shifted, axis=0, keepdims=True))
        lines.append(jnp.sum(value, axis=0, keepdims=True))
        lines.append(
            jnp.sum(d_step_pre[:, here].astype(jnp.float32), axis=0, keepdims=True)
        )
        lines.append(r.skip_grad[:, here])
        lines.append(jnp.zeros((9, width), jnp.float32))
        first = step_rank + select_count
        store_extra(first, tile, r.decay_grad[:, here])
        store_extra(first + states, tile, jnp.concatenate(lines, axis=0))
        rim_copy(tile).wait_recv()
        ext[0:rows, :] = value
        ext[rows:, :] = rim_next[:, here]
        total = weight[0:1, here] * value
        for lag in range(1, 4):
            total = total + weight[lag : lag + 1, here] * (
                ext[lag : lag + rows, :] * wide(masks_after[lag - 1], width)
            )
        r.d_value[:, here] = total.astype(low)

    for copy in loads[:3]:
        copy.wait()
    main.advance()
    chain_out()
    main.advance()
    for copy in loads[3:]:
        copy.wait()
    r.branch_send[...] = r.branch[far_half, :].astype(low)
    branch_swap.start()
    chain_middle()
    again_tile(0)
    main.advance(1)
    chain_home()
    for tile in range(tiles):
        if tile > 0:
            again_tile(tile)
        reverse_tile(tile)
        main.advance()
    select_start()
    main.advance()
    branch_swap.wait()
    r.block_out[...] = (
        r.block[...].astype(jnp.float32)
        + r.branch[own_half, :]
        + r.branch_far[...].astype(jnp.float32)
    )
    select_end()
    main.advance()
    for tile in range(tiles):
        conv_tile(tile)
        if tile % 2:
            main.advance()

    def end():
        chain_end()
        for tile in range(tiles):
            rim_copy(tile).wait_send()

    return end


def rest_kernel(channels, model, *refs):
    r, left = gathered(refs, RestIn, RestOut, RestWork)
    lazy, early = len(RestLazy._fields), len(RestEarly._fields)
    loads = mirrored(r, RestLazy, left, left[lazy], False)
    left = left[lazy + 1 :]
    stores = mirrored(r, RestEarly, left, left[early], True)
    for copy in loads:
        copy.start()
    reducer_refs = left[early + 1 :]
    z, x, core = position()
    place, tp = lax.axis_index("seq"), lax.axis_index("tp")
    seq_peers = [(lax.rem(place + step, 16), tp) for step in range(1, 16)]
    across = [(lax.rem(z + step, 4) * 4 + x * 2 + core, 1 - tp) for step in range(4)]
    greet(seq_peers + across)
    inner = r.out_grad.shape[1]
    starts = range(0, inner, SHARE_WIDTH)
    main = Reducer(
        [(r.cot_t, r.gated, at, r.out_grad, at) for at in starts]
        + [(r.hidden_t, r.d_gate, at, r.in_grad, inner + at) for at in starts]
        + [(r.hidden_t, r.d_value, at, r.in_grad, at) for at in starts],
        reducer_refs,
    )
    end = backward_part(r, main, loads)
    finish_part(channels, model, r, main, stores)
    end()
    main.drain()
    for copy in stores:
        copy.wait()


class RestIn(NamedTuple):
    hidden_t: object
    cot_t: object
    gated: object
    d_gate: object
    piece: object
    d_mixed: object
    held: object
    drive: object
    enter: object
    leave: object
    start: object
    conv_out: object
    step_pre: object
    step_size: object
    conv_pre: object
    conv_in: object
    rim: object
    select_out: object
    branch: object
    block: object
    skip_grad: object
    masks: object
    masks_after: object
    conv_weight: object
    skip_gain: object
    select_weight: object
    step_weight: object
    decay_log: object
    weights: object
    cot: object
    lanes: object
    norm_gain: object
    norm_moment: object
    in_cols: object
    out_cols: object
    step_cols: object
    select_cols: object
    decay_cols: object
    conv_cols: object
    bias_moment: object
    step_moment: object
    skip_moment: object
    conv_bias: object
    step_bias: object


class RestOut(NamedTuple):
    out_grad: object
    block_out: object
    in_grad: object
    input_grad: object
    small: object
    scales: object
    lanes_new: object
    vectors_new: object


class RestLazy(NamedTuple):
    cot_t: object
    gated: object
    piece: object
    branch: object
    held: object
    drive: object
    enter: object
    start: object
    leave: object
    d_mixed: object
    conv_out: object
    step_pre: object
    step_weight: object
    select_weight: object
    step_size: object
    conv_pre: object
    conv_in: object
    hidden_t: object
    d_gate: object
    masks: object
    masks_after: object


class RestEarly(NamedTuple):
    out_grad: object
    block_out: object
    input_grad: object
    small: object


class RestWork(NamedTuple):
    d_value: object
    extra: object
    come: object
    back: object
    follow: object
    kept: object
    state: object
    drive_grad: object
    d_step_pre: object
    decay_grad: object
    enter_grad: object
    leave_grad: object
    select_grad: object
    select_far: object
    conv_grad: object
    rim_next: object
    ext: object
    branch_send: object
    branch_far: object
    chain_sems: object
    pair_sems: object
    rim_sems: object
    come_core: object
    send_x: object
    come_x: object
    send_z: object
    come_z: object
    full: object
    mine: object
    acc: object
    far: object
    row_sums: object
    pair: object
    pair_far: object
    pair_last: object
    pair_last_far: object
    totals: object
    totals_acc: object
    totals_far: object
    come_half: object
    d_hidden: object
    fetched: object
    fetched_sems: object
    extra_sent: object
    extra_got: object
    sums_sent: object
    sums_got: object
    half_sems: object


def rest_block(ident, channels, given):
    rows, inner = given.held.shape
    half_rows, model = given.block.shape
    states = given.decay_log.shape[0]
    small_rows = given.step_weight.shape[0] + given.select_weight.shape[0] + states + 16
    columns = 2 * inner
    f32, low = jnp.float32, jnp.bfloat16
    dma = pltpu.SemaphoreType.DMA
    share = model // 16
    seq_rows = columns // 128 + inner // 128 + model // 128 + 16
    kept_chunks, _, kept_width = given.weights.shape
    block = (small_rows, 128)
    shape, space = jax.ShapeDtypeStruct, pltpu.VMEM
    vmem = pl.BlockSpec(memory_space=pltpu.VMEM)
    specs = RestIn(*placed(RestIn, RestLazy))._replace(
        weights=pl.BlockSpec(memory_space=pltpu.HBM)
    )
    shapes = RestOut(
        shape((share, inner), f32),
        shape((half_rows, model), f32),
        shape((share, columns), f32),
        shape((half_rows, model), f32),
        shape((small_rows, inner), f32),
        shape((5, 128, 128), f32),
        shape((8, 128), f32),
        shape((32, inner), f32),
    )
    outs = pl.pallas_call(
        functools.partial(rest_kernel, channels, model),
        in_specs=list(specs),
        out_specs=placed(RestOut, RestEarly),
        out_shape=list(shapes),
        scratch_shapes=[
            space((rows, inner), low),
            space((8, 2, small_rows, 128), low),
            space((16, states + 8, 128), f32),
            space((16, states, 128), f32),
            space((states, inner), f32),
            space((rows, states, 512), f32),
            space((rows + 1, states, 512), f32),
            space((rows, inner), f32),
            space((rows, inner), low),
            space((states, inner), f32),
            space((rows, states, 128), f32),
            space((rows, states, 128), f32),
            space((rows, 256), f32),
            space((rows, 256), f32),
            space((rows, inner), f32),
            space((8, inner), f32),
            space((rows + 8, 512), f32),
            space((half_rows, model), low),
            space((half_rows, model), low),
            dma((4, 15)),
            dma((4,)),
            dma((2, inner // 512)),
            space((8,) + block, low),
            space((4,) + block, low),
            space((4,) + block, low),
            space((3,) + block, low),
            space((3,) + block, low),
            space((4, 2, 2) + block, low),
            space((seq_rows, 128), f32),
            space((8, seq_rows, 128), f32),
            space((4, model // 128 + 16, 128), f32),
            space((share, 128), f32),
            space((8, 128), f32),
            space((8, 128), f32),
            space((8, 128), f32),
            space((8, 128), f32),
            space((16, 128), f32),
            space((8, 16, 128), f32),
            space((4, 16, 128), f32),
            space((half_rows, model), f32),
            space((2 * half_rows, model), f32),
            space((2, model, kept_width), low),
            dma((kept_chunks,)),
            dma((10,)),
            dma((10,)),
            dma((32,)),
            dma((32,)),
            dma((2,)),
        ]
        + mirrors(RestLazy, given)
        + mirrors(RestEarly, shapes)
        + reducer_scratch(inner + columns, share, SHARE_WIDTH),
        compiler_params=pltpu.CompilerParams(
            collective_id=ident, has_side_effects=True, vmem_limit_bytes=FINISH_LIMIT
        ),
    )(*given)
    return RestOut(*outs)


def on_device(
    block_in,
    cotangent,
    segment_ids,
    norm_gain,
    in_weight,
    out_weight,
    conv_weight,
    conv_bias,
    select_weight,
    step_weight,
    step_bias,
    decay_log,
    skip_gain,
    norm_moment,
    in_rows,
    in_cols,
    out_rows,
    out_cols,
    conv_rows,
    conv_cols,
    bias_moment,
    select_rows,
    select_cols,
    step_rows,
    step_cols,
    step_moment,
    decay_rows,
    decay_cols,
    skip_moment,
):
    tp_count = lax.axis_size("tp")
    seq_index = lax.axis_index("seq")
    tp_index = lax.axis_index("tp")
    seq_first = (seq_index == 0).astype(jnp.float32)
    tp_first = (tp_index == 0).astype(jnp.float32)
    half_rows, model_dim = block_in.shape
    row_count = cotangent.shape[0]
    inner_dim = in_weight.shape[2]
    channels = inner_dim * tp_count
    conv_taps = conv_weight.shape[0]
    states = decay_log.shape[0]
    step_rank = step_weight.shape[0]
    row_share = in_weight.shape[0]
    id_padded = jnp.concatenate(
        [
            jnp.full((conv_taps - 1,), -1, jnp.int32),
            segment_ids,
            jnp.full((conv_taps - 1,), -2, jnp.int32),
        ]
    )
    window = lax.dynamic_slice_in_dim(
        id_padded, seq_index * row_count, row_count + 2 * (conv_taps - 1)
    )
    local_ids = window[conv_taps - 1 : conv_taps - 1 + row_count]
    keep_mask = (local_ids == window[conv_taps - 2 : conv_taps - 2 + row_count]).astype(jnp.float32)
    residual = block_in.astype(jnp.float32)
    mean_sq = jnp.mean(residual * residual, axis=1, keepdims=True)
    inv_rms = lax.rsqrt(mean_sq + EPS_NORM)
    normed = residual * inv_rms
    low_type = jnp.bfloat16
    projected, hidden, in_full = project(
        (normed * norm_gain[None, :]).astype(low_type),
        in_weight.astype(low_type).reshape(row_share, 2 * inner_dim),
        0,
    )
    out_low, projected = lax.optimization_barrier((out_weight.astype(low_type), projected))
    out_full = lax.all_gather(out_low, "seq", axis=0, tiled=True)
    conv_in = projected[:, :inner_dim].astype(jnp.bfloat16)
    gate_pre = projected[:, inner_dim:]
    rim_rows = passed_along(conv_in[row_count - (conv_taps - 1) :], "seq", 1)
    ext_rows = jnp.concatenate([rim_rows, conv_in], axis=0).astype(jnp.float32)
    same_docs = []
    conv_pre = jnp.zeros_like(gate_pre) + conv_bias[None, :]
    for shift_lag in range(conv_taps):
        first_row = conv_taps - 1 - shift_lag
        same_doc = (window[first_row : first_row + row_count] == local_ids).astype(jnp.float32)[
            :, None
        ]
        same_docs.append(same_doc)
        conv_pre = (
            conv_pre
            + conv_weight[shift_lag][None, :]
            * ext_rows[first_row : first_row + row_count]
            * same_doc
        )
    conv_out = jax.nn.silu(conv_pre).astype(jnp.bfloat16)
    conv_value = conv_out.astype(jnp.float32)
    select_low = select_weight.astype(jnp.bfloat16)
    select_out = pair_sum(
        jnp.einsum("te,ke->tk", conv_out, select_low, preferred_element_type=jnp.float32), 1
    )
    step_in = select_out[:, :step_rank].astype(jnp.bfloat16)
    state_in = select_out[:, step_rank : step_rank + states]
    state_out = select_out[:, step_rank + states :]
    step_low = step_weight.astype(jnp.bfloat16)
    step_pre = jnp.dot(step_in, step_low, preferred_element_type=jnp.float32) + step_bias[None, :]
    step_size = jax.nn.softplus(step_pre)
    decay_rate = -jnp.exp(decay_log)
    drive = step_size * conv_value
    held_step = jnp.where(keep_mask[:, None] > 0.0, step_size, RESET)
    enter = jnp.broadcast_to(state_in[:, :, None], (row_count, states, 128))
    leave = jnp.broadcast_to(state_out[:, :, None], (row_count, states, 128))
    nothing = jnp.zeros((8, 128), jnp.float32)
    start, _ = chain(
        piece_state(held_step, drive, enter, decay_rate, False), decay_rate, nothing, False, 2
    )
    scanned = scan_forward(held_step, drive, enter, leave, decay_rate, start)
    mixed = scanned + skip_gain[None, :] * conv_value
    gate_act = jax.nn.silu(gate_pre)
    gated = (mixed * gate_act).astype(jnp.bfloat16)
    branch = jnp.einsum("te,de->td", gated, out_full, preferred_element_type=jnp.float32)
    own_rows, far_rows = tp_index * half_rows, (1 - tp_index) * half_rows
    d_gated = jnp.einsum("td,de->te", cotangent, out_full, preferred_element_type=jnp.float32)
    d_out_w = jnp.einsum("td,te->de", cotangent, gated, preferred_element_type=jnp.float32)
    out_half = lax.psum_scatter(
        d_out_w.astype(low_type), "seq", scatter_dimension=0, tiled=True
    )
    d_mixed = d_gated * gate_act
    d_gate = (d_gated * mixed * silu_slope(gate_pre)).astype(jnp.bfloat16)
    skip_grad = jnp.sum(d_mixed * conv_value, axis=0)
    follow, branch_far = chain(
        piece_state(held_step, d_mixed, leave, decay_rate, True),
        decay_rate,
        lax.dynamic_slice_in_dim(branch, far_rows, half_rows, 0).astype(low_type),
        True,
        3,
    )
    block_out = (
        residual
        + lax.dynamic_slice_in_dim(branch, own_rows, half_rows, 0)
        + branch_far.astype(jnp.float32)
    )
    drive_grad, step_grad, decay_grad, enter_grad, leave_grad = scan_backward(
        held_step, drive, d_mixed, enter, leave, decay_rate, start, follow
    )
    enter_grad = jnp.sum(enter_grad, axis=2)
    leave_grad = jnp.sum(leave_grad, axis=2)
    d_step = drive_grad * conv_value + step_grad
    d_step_pre = (d_step * jax.nn.sigmoid(step_pre)).astype(jnp.bfloat16)
    step_bias_grad = jnp.sum(d_step_pre.astype(jnp.float32), axis=0)
    step_w_grad = jnp.einsum("tr,te->re", step_in, d_step_pre, preferred_element_type=jnp.float32)
    d_step_in = jnp.einsum("te,re->tr", d_step_pre, step_low, preferred_element_type=jnp.float32)
    select_grads = jnp.concatenate(
        [d_step_in, enter_grad, leave_grad],
        axis=1,
    )
    d_select = pair_sum(select_grads, 4).astype(jnp.bfloat16)
    select_w_grad = jnp.einsum("tk,te->ke", d_select, conv_out, preferred_element_type=jnp.float32)
    d_conv = (
        drive_grad * step_size
        + d_mixed * skip_gain[None, :]
        + jnp.einsum("tk,ke->te", d_select, select_low, preferred_element_type=jnp.float32)
    )
    d_conv_pre = d_conv * silu_slope(conv_pre)
    rim_next = passed_along(d_conv_pre[: conv_taps - 1], "seq", -1)
    ext_grads = jnp.concatenate([d_conv_pre, rim_next], axis=0)
    ids_after = window[conv_taps - 1 :]
    d_conv_in = jnp.zeros_like(d_conv_pre)
    conv_w_rows = []
    for shift_lag in range(conv_taps):
        first_row = conv_taps - 1 - shift_lag
        later_same = (ids_after[shift_lag : shift_lag + row_count] == local_ids).astype(
            jnp.float32
        )[:, None]
        d_conv_in = (
            d_conv_in
            + conv_weight[shift_lag][None, :]
            * ext_grads[shift_lag : shift_lag + row_count]
            * later_same
        )
        conv_w_rows.append(
            jnp.sum(
                d_conv_pre * ext_rows[first_row : first_row + row_count] * same_docs[shift_lag],
                axis=0,
            )
        )
    conv_w_grad = jnp.stack(conv_w_rows, axis=0)
    conv_b_grad = jnp.sum(d_conv_pre, axis=0)
    d_projected = jnp.concatenate([d_conv_in.astype(jnp.bfloat16), d_gate], axis=1)
    d_hidden = jnp.einsum(
        "tkn,kdn->td",
        d_projected.reshape(row_count, in_full.shape[0], -1),
        in_full,
        preferred_element_type=jnp.float32,
    )
    vector_grads = jnp.stack([conv_b_grad, step_bias_grad, skip_grad], axis=0)
    small_grads = jnp.concatenate(
        [step_w_grad, select_w_grad, decay_grad, conv_w_grad, vector_grads], axis=0
    )
    out_grad = out_half.astype(jnp.float32)
    in_grad = lax.psum_scatter(
        jnp.einsum("td,tn->dn", hidden, d_projected, preferred_element_type=jnp.float32),
        "seq",
        scatter_dimension=0,
        tiled=True,
    )
    small_full = lax.psum(small_grads, "seq")
    d_hidden = lax.psum_scatter(d_hidden, "tp", scatter_dimension=0, tiled=True)
    in_grad = in_grad.reshape(in_weight.shape)
    gain_part = jnp.sum(d_hidden * normed, axis=0)
    scaled = d_hidden * norm_gain[None, :]
    cot_half = lax.dynamic_slice_in_dim(cotangent, own_rows, half_rows, 0).astype(
        jnp.float32
    )
    input_grad = cot_half + inv_rms * (
        scaled - normed * jnp.mean(scaled * normed, axis=1, keepdims=True)
    )
    edges = [step_rank, select_weight.shape[0], states, conv_taps, 3]
    edges = [sum(edges[:at]) for at in range(len(edges) + 1)]
    step_local, select_local, decay_local, conv_local, vector_local = [
        small_full[low:high] for low, high in zip(edges, edges[1:])
    ]
    in_square = in_grad * in_grad
    out_square = out_grad * out_grad
    in_row_part = jnp.sum(in_square, axis=(1, 2))
    out_row_part = jnp.sum(out_square, axis=1)
    small_row_part = jnp.sum(small_full * small_full, axis=1)
    in_total = jnp.sum(DECAY * in_rows + (1.0 - DECAY) * EPS_FACTOR) * tp_first + (
        1.0 - DECAY
    ) * jnp.sum(in_row_part) / (2 * channels)
    out_total = jnp.sum(DECAY * out_rows + (1.0 - DECAY) * EPS_FACTOR) * tp_first + (
        1.0 - DECAY
    ) * jnp.sum(out_row_part) / channels
    seq_part = jnp.concatenate(
        [jnp.sum(in_square, axis=0).reshape(-1, 128), jnp.sum(out_square, axis=0).reshape(-1, 128)]
    )
    shared_part = jnp.concatenate(
        [
            gain_part.reshape(-1, 128),
            jnp.broadcast_to(in_total, (8, 128)),
            jnp.broadcast_to(out_total, (8, 128)),
        ]
    )
    row_parts = jnp.concatenate([in_row_part, out_row_part, small_row_part])
    row_parts = jnp.pad(row_parts, (0, -row_parts.shape[0] % 1024)).reshape(-1, 128)
    col_sums, shared_sums, row_sums = sum_over(seq_part, shared_part, row_parts)
    col_sums = col_sums.reshape(-1)
    in_col_sums = col_sums[: 2 * inner_dim].reshape(2, inner_dim)
    out_col_sums = col_sums[2 * inner_dim :]
    gain_grad = shared_sums[: model_dim // 128].reshape(-1)
    in_mean = shared_sums[model_dim // 128, 0] / model_dim
    out_mean = shared_sums[model_dim // 128 + 8, 0] / model_dim
    row_sums = row_sums.reshape(-1)
    in_row_sums = row_sums[:row_share]
    out_row_sums = row_sums[row_share : 2 * row_share]
    small_row_sums = row_sums[2 * row_share :]
    in_rows_new = DECAY * in_rows + (1.0 - DECAY) * (in_row_sums / (2 * channels) + EPS_FACTOR)
    in_cols_new = DECAY * in_cols + (1.0 - DECAY) * (in_col_sums / model_dim + EPS_FACTOR)
    out_rows_new = DECAY * out_rows + (1.0 - DECAY) * (out_row_sums / channels + EPS_FACTOR)
    out_cols_new = DECAY * out_cols + (1.0 - DECAY) * (out_col_sums / model_dim + EPS_FACTOR)
    step_rows_new, step_cols_new, stepw_update = factor_update(
        step_local, small_row_sums[edges[0] : edges[1]], step_rows, step_cols, channels
    )
    select_rows_new, select_cols_new, select_update = factor_update(
        select_local, small_row_sums[edges[1] : edges[2]], select_rows, select_cols, channels
    )
    decay_rows_new, decay_cols_new, decay_update = factor_update(
        decay_local, small_row_sums[edges[2] : edges[3]], decay_rows, decay_cols, channels
    )
    conv_rows_new, conv_cols_new, conv_update = factor_update(
        conv_local, small_row_sums[edges[3] : edges[4]], conv_rows, conv_cols, channels
    )
    bias_moment_new, convb_update = moment_update(vector_local[0], bias_moment)
    step_moment_new, stepb_update = moment_update(vector_local[1], step_moment)
    skip_moment_new, skip_update = moment_update(vector_local[2], skip_moment)
    gain_moment_new, gain_update = moment_update(gain_grad, norm_moment)
    in_update = in_grad * lax.rsqrt(in_rows_new[:, None, None] * in_cols_new[None] / in_mean)
    out_update = out_grad * lax.rsqrt(out_rows_new[:, None] * out_cols_new[None, :] / out_mean)
    squares = jnp.stack(
        [
            sum_squares(in_update),
            sum_squares(out_update),
            seq_first * sum_squares(conv_update),
            seq_first * sum_squares(select_update),
            seq_first * sum_squares(stepw_update),
            seq_first * sum_squares(decay_update),
            seq_first * sum_squares(convb_update),
            seq_first * sum_squares(stepb_update),
            seq_first * sum_squares(skip_update),
        ]
    )
    _, clip_totals, _ = sum_over(
        nothing, jnp.broadcast_to(jnp.pad(squares, (0, 7))[:, None], (16, 128)), nothing
    )
    clip_totals = clip_totals[:, 0]
    gain_new = apply_step(norm_gain, gain_update, sum_squares(gain_update), model_dim, RATES[0])
    in_new = apply_step(in_weight, in_update, clip_totals[0], model_dim * 2 * channels, RATES[1])
    out_new = apply_step(out_weight, out_update, clip_totals[1], model_dim * channels, RATES[2])
    convw_new = apply_step(conv_weight, conv_update, clip_totals[2], conv_taps * channels, RATES[3])
    convb_new = apply_step(conv_bias, convb_update, clip_totals[6], channels, RATES[4])
    select_new = apply_step(
        select_weight, select_update, clip_totals[3], select_weight.shape[0] * channels, RATES[5]
    )
    stepw_new = apply_step(
        step_weight, stepw_update, clip_totals[4], step_rank * channels, RATES[6]
    )
    stepb_new = apply_step(step_bias, stepb_update, clip_totals[7], channels, RATES[7])
    decay_new = apply_step(decay_log, decay_update, clip_totals[5], states * channels, RATES[8])
    skip_new = apply_step(skip_gain, skip_update, clip_totals[8], channels, RATES[9])
    return (
        block_out,
        input_grad,
        gain_grad,
        gain_new,
        gain_new.astype(low_type),
        gain_moment_new,
        in_grad,
        in_new,
        in_new.astype(low_type),
        in_rows_new,
        in_cols_new,
        out_grad,
        out_new,
        out_new.astype(low_type),
        out_rows_new,
        out_cols_new,
        conv_local,
        convw_new,
        convw_new.astype(low_type),
        conv_rows_new,
        conv_cols_new,
        vector_local[0],
        convb_new,
        convb_new.astype(low_type),
        bias_moment_new,
        select_local,
        select_new,
        select_new.astype(low_type),
        select_rows_new,
        select_cols_new,
        step_local,
        stepw_new,
        stepw_new.astype(low_type),
        step_rows_new,
        step_cols_new,
        vector_local[1],
        stepb_new,
        stepb_new.astype(low_type),
        step_moment_new,
        decay_local,
        decay_new,
        decay_new.astype(low_type),
        decay_rows_new,
        decay_cols_new,
        vector_local[2],
        skip_new,
        skip_new.astype(low_type),
        skip_moment_new,
    )


def on_block_device(
    block_in,
    cotangent,
    segment_ids,
    norm_gain,
    in_weight,
    out_weight,
    conv_weight,
    conv_bias,
    select_weight,
    step_weight,
    step_bias,
    decay_log,
    skip_gain,
    norm_moment,
    in_rows,
    in_cols,
    out_rows,
    out_cols,
    conv_rows,
    conv_cols,
    bias_moment,
    select_rows,
    select_cols,
    step_rows,
    step_cols,
    step_moment,
    decay_rows,
    decay_cols,
    skip_moment,
):
    tp_count = lax.axis_size("tp")
    seq_index = lax.axis_index("seq")
    tp_index = lax.axis_index("tp")
    half_rows, model_dim = block_in.shape
    row_count = cotangent.shape[0]
    inner_dim = in_weight.shape[2]
    channels = inner_dim * tp_count
    conv_taps = conv_weight.shape[0]
    states = decay_log.shape[0]
    step_rank = step_weight.shape[0]
    row_share = in_weight.shape[0]
    low_type = jnp.bfloat16
    id_padded = jnp.concatenate(
        [
            jnp.full((conv_taps - 1,), -1, jnp.int32),
            segment_ids,
            jnp.full((conv_taps - 1,), -2, jnp.int32),
        ]
    )
    window = lax.dynamic_slice_in_dim(
        id_padded, seq_index * row_count, row_count + 2 * (conv_taps - 1)
    )
    local_ids = window[conv_taps - 1 : conv_taps - 1 + row_count]
    same_docs = [
        (window[conv_taps - 1 - lag : conv_taps - 1 - lag + row_count] == local_ids).astype(
            jnp.float32
        )[:, None]
        for lag in range(conv_taps)
    ]
    masks = jnp.broadcast_to(jnp.stack(same_docs[1:]), (conv_taps - 1, row_count, 128))
    ids_after = window[conv_taps - 1 :]
    same_after = [
        (ids_after[lag : lag + row_count] == local_ids).astype(jnp.float32)[:, None]
        for lag in range(1, conv_taps)
    ]
    masks_after = jnp.broadcast_to(jnp.stack(same_after), (conv_taps - 1, row_count, 128))
    lanes = jnp.concatenate(
        [step_rows, select_rows, decay_rows, conv_rows, jnp.ones((76,), jnp.float32)]
        + [in_rows, out_rows, jnp.ones((384,), jnp.float32)]
    ).reshape(8, 128)
    f = forward_block(
        0,
        ForwardIn(
        in_weight=in_weight,
        out_weight=out_weight,
        block=block_in,
        cot=cotangent,
        norm_gain=norm_gain,
        conv_weight=conv_weight,
        conv_bias=conv_bias,
        step_bias=step_bias,
        skip_gain=skip_gain,
        masks=masks,
        select_weight=select_weight,
        step_weight=step_weight,
        decay_log=decay_log,
        ),
    )
    rest = rest_block(
        1,
        channels,
        RestIn(
            block=block_in,
            cot=cotangent,
            lanes=lanes,
            masks=masks,
            masks_after=masks_after,
            conv_weight=conv_weight,
            select_weight=select_weight,
            step_weight=step_weight,
            decay_log=decay_log,
            norm_gain=norm_gain,
            norm_moment=norm_moment,
            in_cols=in_cols,
            out_cols=out_cols,
            step_cols=step_cols,
            select_cols=select_cols,
            decay_cols=decay_cols,
            conv_cols=conv_cols,
            bias_moment=bias_moment,
            step_moment=step_moment,
            skip_moment=skip_moment,
            conv_bias=conv_bias,
            step_bias=step_bias,
            skip_gain=skip_gain,
            **shared(f, RestIn),
        ),
    )
    return renew(
        RenewIn(
            value_grad=rest.in_grad,
            gate_grad=rest.in_grad,
            in_weight=in_weight,
            out_weight=out_weight,
            step_weight=step_weight,
            select_weight=select_weight,
            decay_log=decay_log,
            conv_weight=conv_weight,
            **shared(rest, RenewIn),
        )
    )


def solution(mesh):
    on_slice = mesh.shape["seq"] == 16 and mesh.shape["tp"] == 2
    return jax.shard_map(
        on_block_device if on_slice else on_device,
        mesh=mesh,
        in_specs=(
            P(("seq", "tp"), None),
            P("seq", None),
            P(),
            P(),
            P("seq", None, "tp"),
            P("seq", "tp"),
            P(None, "tp"),
            P("tp"),
            P(None, "tp"),
            P(None, "tp"),
            P("tp"),
            P(None, "tp"),
            P("tp"),
            P(),
            P("seq"),
            P(None, "tp"),
            P("seq"),
            P("tp"),
            P(),
            P("tp"),
            P("tp"),
            P(),
            P("tp"),
            P(),
            P("tp"),
            P("tp"),
            P(),
            P("tp"),
            P("tp"),
        ),
        out_specs=(
            P(("seq", "tp"), None),
            P(("seq", "tp"), None),
            P(),
            P(),
            P(),
            P(),
            P("seq", None, "tp"),
            P("seq", None, "tp"),
            P("seq", None, "tp"),
            P("seq"),
            P(None, "tp"),
            P("seq", "tp"),
            P("seq", "tp"),
            P("seq", "tp"),
            P("seq"),
            P("tp"),
            P(None, "tp"),
            P(None, "tp"),
            P(None, "tp"),
            P(),
            P("tp"),
            P("tp"),
            P("tp"),
            P("tp"),
            P("tp"),
            P(None, "tp"),
            P(None, "tp"),
            P(None, "tp"),
            P(),
            P("tp"),
            P(None, "tp"),
            P(None, "tp"),
            P(None, "tp"),
            P(),
            P("tp"),
            P("tp"),
            P("tp"),
            P("tp"),
            P("tp"),
            P(None, "tp"),
            P(None, "tp"),
            P(None, "tp"),
            P(),
            P("tp"),
            P("tp"),
            P("tp"),
            P("tp"),
            P("tp"),
        ),
        check_vma=False,
    )
```

```python
import functools
from types import SimpleNamespace
from typing import NamedTuple

import jax
import jax.numpy as jnp
from jax import lax
from jax.experimental import pallas as pl
from jax.experimental.pallas import tpu as pltpu
from jax.sharding import PartitionSpec as P

EPS_NORM = 1e-05
EPS_FACTOR = 1e-30
DECAY = 0.5
CLIP = 0.5
RATES = (0.45, 0.02, 0.03, 0.1, 0.05, 0.016, 0.09, 1.8, 0.3, 0.45)
MESH = pl.DeviceIdType.MESH
LOG2E = 1.4426950408889634
RESET = 1e9
TILE = 512
X_FIRST = (4, 8)
SHARE_WIDTH = 256
SLOTS = 8
LAGS = (0, 1, 3, 5)
RENEW_TILES = 2
VMEM_LIMIT = 48 * 1024 * 1024
FINISH_LIMIT = 63 * 1024 * 1024


def passed_along(value, axis, steps):
    count = lax.axis_size(axis)
    initial, last = (max(0, -steps), min(count, count - steps))
    return lax.ppermute(value, axis, [(source, source + steps) for source in range(initial, last)])


def silu_slope(values):
    sigmoid_v = jax.nn.sigmoid(values)
    return sigmoid_v * (1.0 + values * (1.0 - sigmoid_v))


def factor_update(grad, row_sums, rows_old, cols_old, channels):
    rows_new = DECAY * rows_old + (1.0 - DECAY) * (row_sums / channels + EPS_FACTOR)
    cols_new = DECAY * cols_old + (1.0 - DECAY) * (jnp.mean(grad * grad, axis=0) + EPS_FACTOR)
    scale_sq = rows_new[:, None] * cols_new[None, :] / jnp.mean(rows_new)
    return (rows_new, cols_new, grad * lax.rsqrt(scale_sq))


def moment_update(grad_in, moment_old):
    moment_new = DECAY * moment_old + (1.0 - DECAY) * (grad_in * grad_in + EPS_FACTOR)
    return (moment_new, grad_in * lax.rsqrt(moment_new))


def sum_squares(update):
    return jnp.sum(update * update)


def apply_step(weight, update, total_sum, count_all, step_rate):
    root_mean = jnp.sqrt(total_sum / count_all)
    return weight - step_rate * update / jnp.maximum(1.0, root_mean / CLIP)


def wide(tile, width):
    return jnp.concatenate([tile] * (width // tile.shape[1]), axis=1)


def fold_lanes(value):
    pieces = [value[:, at : at + 128] for at in range(0, value.shape[1], 128)]
    while len(pieces) > 1:
        pieces = [first + second for first, second in zip(pieces[::2], pieces[1::2])]
    return pieces[0]


def state_kernel(backward, step_ref, value_ref, lane_ref, rate_ref, out_ref):
    rows, width = step_ref.shape
    states = rate_ref.shape[0]
    rate = rate_ref[...] * LOG2E

    def block(index, state):
        base = pl.multiple_of((rows // 8 - 1 - index if backward else index) * 8, 8)
        for offset in range(8):
            at = base + (7 - offset if backward else offset)
            keep = jnp.exp2(rate * step_ref[pl.ds(at, 1), :])
            term = wide(lane_ref[at], width) * value_ref[pl.ds(at, 1), :]
            state = keep * (state + term) if backward else keep * state + term
        return state

    out_ref[0:states, :] = lax.fori_loop(0, rows // 8, block, jnp.zeros((states, width), jnp.float32))
    total = jnp.sum(step_ref[...], axis=0, keepdims=True)
    out_ref[states:, :] = jnp.broadcast_to(total, (out_ref.shape[0] - states, width))


def piece_state(step, value, lane, rate, backward):
    rows, width = step.shape
    states = rate.shape[0]
    tile = TILE
    return pl.pallas_call(
        functools.partial(state_kernel, backward),
        grid=(width // tile,),
        in_specs=[
            pl.BlockSpec((rows, tile), lambda i: (0, i)),
            pl.BlockSpec((rows, tile), lambda i: (0, i)),
            pl.BlockSpec((rows, states, 128), lambda i: (0, 0, 0)),
            pl.BlockSpec((states, tile), lambda i: (0, i)),
        ],
        out_specs=pl.BlockSpec((states + 8, tile), lambda i: (0, i)),
        out_shape=jax.ShapeDtypeStruct((states + 8, width), jnp.float32),
        compiler_params=pltpu.CompilerParams(vmem_limit_bytes=VMEM_LIMIT),
    )(step, value, lane, rate)


def forward_kernel(
    step_ref, drive_ref, enter_ref, leave_ref, rate_ref, start_ref, out_ref
):
    rows, width = step_ref.shape
    rate = rate_ref[...] * LOG2E

    def block(index, state):
        base = pl.multiple_of(index * 8, 8)
        for offset in range(8):
            at = base + offset
            keep = jnp.exp2(rate * step_ref[pl.ds(at, 1), :])
            state = keep * state + wide(enter_ref[at], width) * drive_ref[pl.ds(at, 1), :]
            out_ref[pl.ds(at, 1), :] = jnp.sum(
                wide(leave_ref[at], width) * state, axis=0, keepdims=True
            )
        return state

    lax.fori_loop(0, rows // 8, block, start_ref[...])


def scan_forward(step, drive, enter, leave, rate, start):
    rows, width = step.shape
    states = rate.shape[0]
    tile = TILE
    by_tile = pl.BlockSpec((rows, tile), lambda i: (0, i))
    by_state = pl.BlockSpec((states, tile), lambda i: (0, i))
    whole = pl.BlockSpec((rows, states, 128), lambda i: (0, 0, 0))
    return pl.pallas_call(
        forward_kernel,
        grid=(width // tile,),
        in_specs=[by_tile, by_tile, whole, whole, by_state, by_state],
        out_specs=by_tile,
        out_shape=jax.ShapeDtypeStruct((rows, width), jnp.float32),
        compiler_params=pltpu.CompilerParams(vmem_limit_bytes=VMEM_LIMIT),
    )(step, drive, enter, leave, rate, start)


def backward_kernel(
    step_ref,
    drive_ref,
    grad_ref,
    enter_ref,
    leave_ref,
    rate_ref,
    start_ref,
    follow_ref,
    drive_grad_ref,
    step_grad_ref,
    decay_ref,
    enter_grad_ref,
    leave_grad_ref,
    kept_ref,
    state_ref,
):
    rows, width = step_ref.shape
    rate_own = rate_ref[...]
    rate = rate_own * LOG2E

    @pl.when(pl.program_id(0) == 0)
    def _():
        enter_grad_ref[...] = jnp.zeros_like(enter_grad_ref)
        leave_grad_ref[...] = jnp.zeros_like(leave_grad_ref)

    def again(index, state):
        base = pl.multiple_of(index * 8, 8)
        for offset in range(8):
            at = base + offset
            keep = jnp.exp2(rate * step_ref[pl.ds(at, 1), :])
            kept_ref[at] = keep
            state = keep * state + wide(enter_ref[at], width) * drive_ref[pl.ds(at, 1), :]
            state_ref[at + 1] = state
        return state

    start = start_ref[...]
    state_ref[0] = start
    lax.fori_loop(0, rows // 8, again, start)
    follow = follow_ref[...]

    def block(index, carry):
        follow, decay = carry
        base = pl.multiple_of((rows // 8 - 1 - index) * 8, 8)
        for offset in range(7, -1, -1):
            at = base + offset
            grad = grad_ref[pl.ds(at, 1), :]
            adjoint = wide(leave_ref[at], width) * grad + follow
            drive_grad_ref[pl.ds(at, 1), :] = jnp.sum(
                adjoint * wide(enter_ref[at], width), axis=0, keepdims=True
            )
            enter_grad_ref[at] += fold_lanes(adjoint * drive_ref[pl.ds(at, 1), :])
            leave_grad_ref[at] += fold_lanes(state_ref[at + 1] * grad)
            follow = kept_ref[at] * adjoint
            part = follow * state_ref[at]
            step_grad_ref[pl.ds(at, 1), :] = jnp.sum(part * rate_own, axis=0, keepdims=True)
            decay = decay + part * step_ref[pl.ds(at, 1), :]
        return follow, decay

    _, decay = lax.fori_loop(0, rows // 8, block, (follow, jnp.zeros_like(follow)))
    decay_ref[...] = decay * rate_own


def scan_backward(step, drive, grad, enter, leave, rate, start, follow):
    rows, width = step.shape
    states = rate.shape[0]
    tile = TILE
    by_tile = pl.BlockSpec((rows, tile), lambda i: (0, i))
    by_state = pl.BlockSpec((states, tile), lambda i: (0, i))
    whole = pl.BlockSpec((rows, states, 128), lambda i: (0, 0, 0))
    return pl.pallas_call(
        backward_kernel,
        grid=(width // tile,),
        in_specs=[by_tile, by_tile, by_tile, whole, whole, by_state, by_state, by_state],
        out_specs=[by_tile, by_tile, by_state, whole, whole],
        out_shape=[
            jax.ShapeDtypeStruct((rows, width), jnp.float32),
            jax.ShapeDtypeStruct((rows, width), jnp.float32),
            jax.ShapeDtypeStruct((states, width), jnp.float32),
            jax.ShapeDtypeStruct((rows, states, 128), jnp.float32),
            jax.ShapeDtypeStruct((rows, states, 128), jnp.float32),
        ],
        scratch_shapes=[
            pltpu.VMEM((rows, states, tile), jnp.float32),
            pltpu.VMEM((rows + 1, states, tile), jnp.float32),
        ],
        compiler_params=pltpu.CompilerParams(vmem_limit_bytes=VMEM_LIMIT),
    )(step, drive, grad, enter, leave, rate, start, follow)


def on_block():
    return lax.axis_size("seq") == 16 and lax.axis_size("tp") == 2


def position():
    place = lax.axis_index("seq")
    return lax.div(place, 4), lax.rem(lax.div(place, 2), 2), lax.rem(place, 2)


def device(z, x, core):
    return (z * 4 + x * 2 + core, lax.axis_index("tp"))


def other_half():
    return (lax.axis_index("seq"), 1 - lax.axis_index("tp"))


def greet(peers):
    barrier = pltpu.get_barrier_semaphore()
    for peer in peers:
        pl.semaphore_signal(barrier, inc=1, device_id=peer, device_id_type=MESH)
    pl.semaphore_wait(barrier, len(peers))


def remote(source, target, sent, arrived, peer):
    return pltpu.make_async_remote_copy(
        src_ref=source,
        dst_ref=target,
        send_sem=sent,
        recv_sem=arrived,
        device_id=peer,
        device_id_type=MESH,
    )


def sum_over(seq_part, shared_part, tp_part):
    return lax.psum(seq_part, "seq"), lax.psum(shared_part, ("seq", "tp")), lax.psum(tp_part, "tp")


def project(half, weight, ident):
    hidden = lax.all_gather(half, "tp", axis=0, tiled=True)
    full = lax.all_gather(weight, "seq", axis=0, tiled=True)
    return jnp.dot(hidden, full, preferred_element_type=jnp.float32), hidden, full[None]


def pair_kernel(mine_ref, out_ref, far, sent, arrived):
    greet([other_half()])
    copy = remote(mine_ref, far, sent, arrived, other_half())
    copy.start()
    copy.wait()
    out_ref[...] = mine_ref[...] + far[...]


def pair_sum(value, ident):
    if not on_block():
        return lax.psum(value, "tp")
    vmem = pl.BlockSpec(memory_space=pltpu.VMEM)
    return pl.pallas_call(
        pair_kernel,
        in_specs=[vmem],
        out_specs=vmem,
        out_shape=jax.ShapeDtypeStruct(value.shape, value.dtype),
        scratch_shapes=[
            pltpu.VMEM(value.shape, value.dtype),
            pltpu.SemaphoreType.DMA,
            pltpu.SemaphoreType.DMA,
        ],
        compiler_params=pltpu.CompilerParams(collective_id=ident, has_side_effects=True),
    )(value)


def chain_kernel(backward, piece_ref, rate_ref, swap_ref, out_ref, swapped_ref, come, back, sems, swap_sems):
    place = lax.axis_index("seq")
    states = rate_ref.shape[0]
    peers = [(lax.rem(place + step, 16), lax.axis_index("tp")) for step in range(1, 16)]
    greet(peers + [other_half()])
    swap = remote(swap_ref, swapped_ref, swap_sems.at[0], swap_sems.at[1], other_half())
    swap.start()

    def lanes(at):
        return pl.ds(pl.multiple_of(at * 128, 128), 128)

    def out(at):
        return remote(
            piece_ref.at[:, lanes(peers[at][0])],
            come.at[place],
            sems.at[0, at],
            sems.at[1, at],
            peers[at],
        )

    def home(at):
        return remote(
            back.at[peers[at][0]],
            out_ref.at[:, lanes(place)],
            sems.at[2, at],
            sems.at[3, at],
            peers[at],
        )

    for at in range(15):
        out(at).start()
    come[place] = piece_ref[:, lanes(place)]
    rate = rate_ref[:, lanes(place)] * LOG2E
    for at in range(15):
        out(at).wait_recv()

    def join(index, state):
        at = 15 - index if backward else index
        back[at] = state
        piece = come[at]
        return jnp.exp2(rate * piece[states : states + 1]) * state + piece[:states]

    lax.fori_loop(0, 16, join, jnp.zeros((states, 128), jnp.float32))
    for at in range(15):
        home(at).start()
    out_ref[:, lanes(place)] = back[place]
    for at in range(15):
        home(at).wait_recv()
    for at in range(15):
        out(at).wait_send()
        home(at).wait_send()
    swap.wait()


def chain(piece, rate, swap, backward, ident):
    states, width = rate.shape
    if not on_block():
        count, place = lax.axis_size("seq"), lax.axis_index("seq")
        pieces = lax.all_gather(piece, "seq")

        def join(index, state):
            at = count - 1 - index if backward else index
            longer = (
                jnp.exp2(rate * LOG2E * pieces[at, states : states + 1]) * state + pieces[at, :states]
            )
            return jnp.where(at > place if backward else at < place, longer, state)

        state = lax.fori_loop(0, count, join, jnp.zeros((states, width), jnp.float32))
        order = [(0, 1), (1, 0)]
        return state, lax.ppermute(swap, "tp", order)
    vmem = pl.BlockSpec(memory_space=pltpu.VMEM)
    return pl.pallas_call(
        functools.partial(chain_kernel, backward),
        in_specs=[vmem, vmem, vmem],
        out_specs=[vmem, vmem],
        out_shape=[
            jax.ShapeDtypeStruct((states, width), jnp.float32),
            jax.ShapeDtypeStruct(swap.shape, swap.dtype),
        ],
        scratch_shapes=[
            pltpu.VMEM((16, states + 8, 128), jnp.float32),
            pltpu.VMEM((16, states, 128), jnp.float32),
            pltpu.SemaphoreType.DMA((4, 15)),
            pltpu.SemaphoreType.DMA((2,)),
        ],
        compiler_params=pltpu.CompilerParams(collective_id=ident, has_side_effects=True),
    )(piece, rate, swap)


def wait_all(copies):
    for copy in copies:
        copy.wait_recv()


def gathered(refs, *groups):
    named, at = {}, 0
    for group in groups:
        named.update(zip(group._fields, refs[at:]))
        at += len(group._fields)
    return SimpleNamespace(**named), list(refs[at:])


def mirrored(r, group, near, sems, outward):
    copies = []
    for at, name in enumerate(group._fields):
        ends = (near[at], getattr(r, name)) if outward else (getattr(r, name), near[at])
        copies.append(pltpu.make_async_copy(*ends, sems.at[at]))
        setattr(r, name, near[at])
    return group(*copies)


def mirrors(group, shapes):
    named = shapes._asdict()
    picked = [named[name] for name in group._fields]
    return [pltpu.VMEM(ref.shape, ref.dtype) for ref in picked] + [
        pltpu.SemaphoreType.DMA((len(picked),))
    ]


def placed(group, *lazy):
    names = [name for other in lazy for name in other._fields]
    return [
        pl.BlockSpec(memory_space=pltpu.HBM if name in names else pltpu.VMEM)
        for name in group._fields
    ]


def shared(source, group):
    return {name: value for name, value in source._asdict().items() if name in group._fields}


class Reducer:
    def __init__(self, jobs, refs):
        self.jobs, self.at = jobs, 0
        self.send, self.come = refs[:3], refs[3:6]
        self.sent, self.got, self.total = refs[6:9], refs[9:12], refs[12]
        self.z, self.x, self.core = position()
        self.chunks, self.width = len(jobs), self.come[2].shape[3]
        self.peers = [
            [device(self.z, self.x, 1 - self.core)],
            [device(self.z, 1 - self.x, self.core)],
            [device(lax.rem(self.z + step, 4), self.x, self.core) for step in (1, 2, 3)],
        ]

    def copies(self, level, chunk):
        slot = chunk % self.send[level].shape[0]
        if level < 2:
            return [
                remote(
                    self.send[level].at[slot],
                    self.come[level].at[chunk % SLOTS],
                    self.sent[level].at[chunk],
                    self.got[level].at[chunk],
                    self.peers[level][0],
                )
            ]
        return [
            remote(
                self.send[2].at[slot, 0, lax.rem(self.z + 1 + at, 4)],
                self.come[2].at[chunk % SLOTS, at],
                self.sent[2].at[chunk, at],
                self.got[2].at[chunk, at],
                self.peers[2][at],
            )
            for at in range(3)
        ]

    def free(self, level, chunk):
        older = chunk - self.send[level].shape[0]
        if older >= 0:
            for copy in self.copies(level, older):
                copy.wait_send()

    def product(self, chunk, first, count):
        left, right, start = self.jobs[chunk][:3]
        _, rows, depth = left.shape
        block = left[pl.ds(first, count)].reshape(count * rows, depth)
        value = jnp.dot(
            block, right[:, start : start + self.width], preferred_element_type=jnp.float32
        )
        return value.reshape(count, rows, self.width)

    def put(self, chunk, value, more):
        out, start = self.jobs[chunk][3:]
        here = slice(start, start + self.width)
        out[:, here] = out[:, here] + value if more else value

    def after_core(self, chunk, x):
        come = self.come[0][chunk % SLOTS, x].astype(jnp.float32)
        return self.product(chunk, self.core * 8 + x * 4, 4) + come

    def fill(self, level, chunk, values):
        self.free(level, chunk)
        slot = chunk % self.send[level].shape[0]
        for at, value in enumerate(values):
            self.send[level][slot, at] = value().astype(jnp.bfloat16)
        for copy in self.copies(level, chunk):
            copy.start()

    def stage(self, level, chunk):
        if not 0 <= chunk < self.chunks:
            return
        if level > 0:
            wait_all(self.copies(level - 1, chunk))
        if level == 0:
            away = (1 - self.core) * 8
            self.fill(
                0, chunk, [lambda at=at: self.product(chunk, away + at * 4, 4) for at in range(2)]
            )
        elif level == 1:
            self.fill(1, chunk, [lambda: self.after_core(chunk, 1 - self.x)])
        elif level == 2:
            come = self.come[1][chunk % SLOTS, 0].astype(jnp.float32)
            self.total[...] = self.after_core(chunk, self.x) + come
            self.fill(2, chunk, [lambda: self.total[...]])
            self.put(chunk, self.total[self.z], False)
        else:
            come = [self.come[2][chunk % SLOTS, at].astype(jnp.float32) for at in range(3)]
            self.put(chunk, (come[0] + come[1]) + come[2], True)

    def step(self, step):
        for level, lag in enumerate(LAGS):
            self.stage(level, step - lag)

    def advance(self, count=1):
        for _ in range(count):
            if self.at < self.chunks + LAGS[3]:
                self.step(self.at)
                self.at += 1

    def drain(self):
        for level in range(3):
            for chunk in range(max(0, self.chunks - self.send[level].shape[0]), self.chunks):
                for copy in self.copies(level, chunk):
                    copy.wait_send()


def reducer_scratch(columns, share, width):
    chunks = columns // width
    low, dma = jnp.bfloat16, pltpu.SemaphoreType.DMA
    return [
        pltpu.VMEM((4, 2, 4, share, width), low),
        pltpu.VMEM((4, 1, 4, share, width), low),
        pltpu.VMEM((4, 1, 4, share, width), low),
        pltpu.VMEM((SLOTS, 2, 4, share, width), low),
        pltpu.VMEM((SLOTS, 1, 4, share, width), low),
        pltpu.VMEM((SLOTS, 3, share, width), low),
        dma((chunks,)),
        dma((chunks,)),
        dma((chunks, 3)),
        dma((chunks,)),
        dma((chunks,)),
        dma((chunks, 3)),
        pltpu.VMEM((4, share, width), jnp.float32),
    ]


def rows_to_lanes(partial):
    return jnp.sum(partial.T, axis=0, keepdims=True)


def lanes_to_rows(row):
    return jnp.broadcast_to(row, (128, 128)).T


def finish_part(channels, model, r, main, stores):
    z, x, core = position()
    place, tp = lax.axis_index("seq"), lax.axis_index("tp")
    core_peer, x_peer = device(z, x, 1 - core), device(z, 1 - x, core)
    z_peers = [device(lax.rem(z + step, 4), x, core) for step in (1, 2, 3)]
    low = jnp.bfloat16
    half_rows = r.block.shape[0]
    own_half = pl.ds(pl.multiple_of(tp * half_rows, half_rows), half_rows)
    far_half = pl.ds(pl.multiple_of((1 - tp) * half_rows, half_rows), half_rows)
    d_hidden = r.d_hidden
    swap = remote(
        d_hidden.at[far_half], r.come_half, r.half_sems.at[0], r.half_sems.at[1], other_half()
    )
    sides = [r.d_value, r.d_gate]
    kept_chunks, _, kept_width = r.weights.shape

    def fetch(chunk):
        return pltpu.make_async_copy(
            r.weights.at[chunk], r.fetched.at[chunk % 2], r.fetched_sems.at[chunk]
        )

    def hidden_stage(chunk):
        fetch(chunk).wait()
        per_side = kept_chunks // 2
        at = chunk % per_side
        part = lax.dot_general(
            sides[chunk // per_side][:, at * kept_width : (at + 1) * kept_width],
            r.fetched[chunk % 2],
            (((1,), (1,)), ((), ())),
            preferred_element_type=jnp.float32,
        )
        d_hidden[...] = part if chunk == 0 else d_hidden[...] + part
        if chunk + 2 < kept_chunks:
            fetch(chunk + 2).start()
        if chunk == kept_chunks - 1:
            swap.start()

    fetch(0).start()
    fetch(1).start()

    sent, got = r.extra_sent, r.extra_got
    extra, full = r.extra, r.full
    extra_core = remote(extra.at[:, 1 - core], r.come_core, sent.at[0], got.at[0], core_peer)
    extra_x = remote(r.send_x, r.come_x, sent.at[1], got.at[1], x_peer)
    extra_z = [
        remote(r.send_z.at[at], r.come_z.at[at], sent.at[2 + at], got.at[2 + at], z_peers[at])
        for at in range(3)
    ]
    own, held, halves = full.at[z, x, core], full.at[:, x, core], full.at[:, :, core]
    back_z = [remote(own, own, sent.at[5 + at], got.at[5 + at], z_peers[at]) for at in range(3)]
    back_x = remote(held, held, sent.at[8], got.at[8], x_peer)
    back_core = remote(halves, halves, sent.at[9], got.at[9], core_peer)

    def extra_after_core(pair):
        return extra[pair, core].astype(jnp.float32) + r.come_core[pair].astype(jnp.float32)

    def extra_after_x(level):
        return extra_after_core(level * 2 + x) + r.come_x[level].astype(jnp.float32)

    def extra_stage_x():
        extra_core.wait_recv()

        def one(level, _):
            r.send_x[level] = extra_after_core(level * 2 + 1 - x).astype(low)
            return 0

        lax.fori_loop(0, 4, one, 0)
        extra_x.start()

    def extra_stage_z():
        extra_x.wait_recv()

        def one(at, _):
            r.send_z[at] = extra_after_x(lax.rem(z + 1 + at, 4)).astype(low)
            return 0

        lax.fori_loop(0, 3, one, 0)
        for copy in extra_z:
            copy.start()

    def extra_stage_last():
        wait_all(extra_z)
        total = extra_after_x(z)
        for at in range(3):
            total = total + r.come_z[at].astype(jnp.float32)
        full[z, x, core] = total.astype(low)
        for copy in back_z:
            copy.start()

    def extra_back_x():
        wait_all(back_z)
        back_x.start()

    def extra_back_core():
        back_x.wait_recv()
        back_core.start()

    mine = r.mine
    vectors_new = r.vectors_new

    def line(ref):
        return ref[...].reshape(1, -1)

    half = r.out_grad.shape[1]
    tiles = half // 128
    gain_tiles = model // 128

    def put(base, row):
        for at in range(row.shape[1] // 128):
            mine[base + at : base + at + 1, :] = row[:, at * 128 : (at + 1) * 128]

    def take(ref, base, tiles):
        return jnp.concatenate([ref[base + at : base + at + 1, :] for at in range(tiles)], axis=1)

    def residual_stage():
        swap.wait()
        total = d_hidden[own_half, :] + r.come_half[...]
        residual = r.block[...].astype(jnp.float32)
        inv_rms = lax.rsqrt(jnp.mean(residual * residual, axis=1, keepdims=True) + EPS_NORM)
        normed = residual * inv_rms
        put(2 * tiles, jnp.sum(total * normed, axis=0, keepdims=True))
        scaled = total * line(r.norm_gain)
        mean = jnp.mean(scaled * normed, axis=1, keepdims=True)
        r.input_grad[...] = r.cot[own_half, :].astype(jnp.float32) + inv_rms * (scaled - normed * mean)

    span = 512
    wide_span = span // 128
    small = r.small
    groups = {"step": (0, 128), "select": (128, 288), "decay": (288, 304), "conv": (304, 308)}
    pair = r.pair

    def put_rows(at, partial):
        pair[at : at + 1, :] = rows_to_lanes(partial)

    def fold_square(value):
        return fold_lanes(value * value)

    def small_stage():
        back_core.wait_recv()
        for block in range(16):
            small[:, block * 128 : (block + 1) * 128] = full[
                block // 4, block // 2 % 2, block % 2
            ].astype(jnp.float32)
        for at in range(3):
            rows = min(128, small.shape[0] - at * 128)

            def one(index, partial):
                columns = pl.ds(pl.multiple_of(index * span, span), span)
                return partial + fold_square(small[at * 128 : at * 128 + rows, columns])

            partial = lax.fori_loop(
                0, small.shape[1] // span, one, jnp.zeros((rows, 128), jnp.float32)
            )
            if rows < 128:
                partial = jnp.concatenate(
                    [partial, jnp.zeros((128 - rows, 128), jnp.float32)], axis=0
                )
            put_rows(at, partial)

    late = 2 * tiles + gain_tiles + 8
    row_sums = r.row_sums

    def square_sums(ref, start, width, base):
        value = ref[:, start : start + width]
        put(base, jnp.sum(value * value, axis=0, keepdims=True))
        return fold_square(value)

    def in_stage(chunk):
        start = (chunk - main.chunks // 3) * main.width
        if start < 0 or chunk >= main.chunks:
            return
        gate = start < half
        base = start // 128 if gate else late + (start - half) // 128
        start = half + start if gate else start - half
        part = square_sums(r.in_grad, start, main.width, base)
        row_sums[...] = part if base == 0 else row_sums[...] + part

    def out_stage():
        part = jnp.zeros((r.out_grad.shape[0], 128), jnp.float32)
        for start in range(0, half, span):
            part = part + square_sums(r.out_grad, start, span, tiles + start // 128)
        put_rows(4, part)

    lanes = r.lanes
    ones = jnp.ones((3, 128), jnp.float32)
    packed = jnp.concatenate(
        [line(r.select_rows), line(r.decay_rows), line(r.conv_rows), ones[:1, :76]], axis=1
    )
    lanes[0:1, :] = line(r.step_rows)
    lanes[1:2, :] = packed[:, :128]
    lanes[2:3, :] = packed[:, 128:]
    lanes[3:4, :] = line(r.in_rows)
    lanes[4:5, :] = line(r.out_rows)
    lanes[5:8, :] = ones
    row_at = lax.broadcasted_iota(jnp.int32, lanes.shape, 0)
    lane_at = lax.broadcasted_iota(jnp.int32, lanes.shape, 1)
    counts = jnp.where(row_at == 3, 2.0 * channels, 1.0 * channels)
    held_lanes = DECAY * lanes[...] + (1.0 - DECAY) * EPS_FACTOR
    def total(value):
        return jnp.sum(jnp.sum(value, axis=1, keepdims=True), axis=0, keepdims=True)

    def put_mean(at, sums, first):
        part = jnp.where(tp == 0, held_lanes, 0.0) + (1.0 - DECAY) * sums[...] / counts
        mean = total(jnp.where(row_at == at, part, 0.0)) / model
        mine[first : first + 8, :] = jnp.broadcast_to(mean, (8, 128))

    sums_sent, sums_got = r.sums_sent, r.sums_got

    def hop(at, source, target, peer):
        return remote(source, target, sums_sent.at[at], sums_got.at[at], peer)

    plane = x * 2 + core
    mates = [core_peer, x_peer, device(z, 1 - x, 1 - core)]
    across = [(lax.rem(z + step, 4) * 4 + plane, 1 - tp) for step in range(4)]

    def sum_hops(first, value, acc, far, shared):
        plane_copies = [hop(first + at, acc.at[plane], acc.at[plane], mates[at]) for at in range(3)]
        part = acc.at[4 + z]
        z_copies = [hop(first + 3 + at, part, part, z_peers[at]) for at in range(3)]
        z_copies += [hop(first + 6 + at, part.at[shared:], far.at[z], across[at]) for at in range(4)]

        def begin():
            acc[plane] = value[...]
            for copy in plane_copies:
                copy.start()

        def middle():
            for copy in plane_copies:
                copy.wait()
            acc[4 + z] = (acc[0] + acc[1]) + (acc[2] + acc[3])
            for copy in z_copies:
                copy.start()

        def end():
            for copy in z_copies:
                copy.wait()
            value[...] = (acc[4] + acc[5]) + (acc[6] + acc[7])
            value[shared:] = value[shared:] + ((far[0] + far[1]) + (far[2] + far[3]))

        return begin, middle, end

    def cols_new(old, sums, count):
        return DECAY * old + (1.0 - DECAY) * (sums / count + EPS_FACTOR)

    def part_hops(first, low_row, high_row, low_far, high_far):
        return sum_hops(
            first,
            mine.at[low_row:high_row],
            r.acc.at[:, low_row:high_row],
            r.far.at[:, low_far:high_far],
            high_row - low_row - (high_far - low_far),
        )

    shared_rows = gain_tiles + 8
    early_hops = part_hops(0, 0, late, 0, shared_rows)
    late_hops = part_hops(20, late, late + tiles + 8, shared_rows, shared_rows + 8)
    pair_copy = hop(30, pair, r.pair_far, other_half())
    last_copy = hop(31, r.pair_last, r.pair_last_far, other_half())
    scales_out = r.scales
    sums = {}

    def early_begin():
        put_mean(4, pair, 2 * tiles + gain_tiles)
        pair_copy.start()
        early_hops[0]()

    def squares(ref, row_scale, first_row):
        def one(index, partial):
            columns = pl.ds(pl.multiple_of(index * span, span), span)
            col = vectors_new[pl.ds(first_row + lax.div(index, half // span), 1), pl.ds(
                pl.multiple_of(lax.rem(index, half // span) * span, span), span
            )]
            return partial + fold_square(ref[:, columns] * wide(row_scale, span) * lax.rsqrt(col))

        return total(
            lax.fori_loop(0, ref.shape[1] // span, one, jnp.zeros((ref.shape[0], 128), jnp.float32))
        )

    group_cols = {
        "step": (r.step_cols, 8),
        "select": (r.select_cols, 7),
        "decay": (r.decay_cols, 9),
        "conv": (r.conv_cols, 6),
    }

    def early_end():
        early_hops[2]()
        pair_copy.wait()
        lanes_new = held_lanes + (1.0 - DECAY) * (pair[...] + r.pair_far[...]) / counts
        r.lanes_new[...] = lanes_new
        flat = row_at * 128 + lane_at
        base = 2 * tiles + gain_tiles
        means = mine[base : base + 8, :]
        for low_edge, high_edge in groups.values():
            member = (flat >= low_edge) & (flat < high_edge)
            mean = total(jnp.where(member, lanes_new, 0.0)) / (high_edge - low_edge)
            means = jnp.where(member, mean, means)
        scale = lax.rsqrt(lanes_new / means)
        for at in (0, 1, 2, 4):
            scales_out[at] = lanes_to_rows(scale[at : at + 1, :])
        vectors_new[4:5, :] = cols_new(r.in_cols[1:2, :], take(mine, 0, tiles), model)
        vectors_new[5:6, :] = cols_new(line(r.out_cols), take(mine, tiles, tiles), model)
        sums["out"] = squares(r.out_grad, scales_out[4], 5)
        small_scale = jnp.concatenate([scales_out[0], scales_out[1], scales_out[2]], axis=0)
        for name, (low_edge, high_edge) in groups.items():
            old_cols, new_row = line(group_cols[name][0]), group_cols[name][1]
            partial = jnp.zeros((high_edge - low_edge, 128), jnp.float32)
            for at in range(0, small.shape[1], span):
                columns = slice(at, at + span)
                value = small[low_edge:high_edge, columns]
                col = cols_new(
                    old_cols[:, columns],
                    jnp.sum(value * value, axis=0, keepdims=True),
                    high_edge - low_edge,
                )
                vectors_new[new_row : new_row + 1, columns] = col
                row_scale = small_scale[low_edge:high_edge]
                partial = partial + fold_square(value * wide(row_scale, span) * lax.rsqrt(col))
            sums[name] = total(partial)
        for at in range(3):
            value = small[308 + at : 309 + at, :]
            old = line((r.bias_moment, r.step_moment, r.skip_moment)[at])
            moment = DECAY * old + (1.0 - DECAY) * (value * value + EPS_FACTOR)
            vectors_new[24 + at : 25 + at, :] = moment
            vectors_new[18 + at : 19 + at, :] = value
            update = value * lax.rsqrt(moment)
            vectors_new[21 + at : 22 + at, :] = update
            sums[at] = jnp.sum(update * update, axis=1, keepdims=True)
        gain_grad = take(mine, 2 * tiles, gain_tiles)
        moment = DECAY * line(r.norm_moment) + (1.0 - DECAY) * (gain_grad * gain_grad + EPS_FACTOR)
        update = gain_grad * lax.rsqrt(moment)
        root = jnp.sqrt(jnp.mean(update * update, axis=1, keepdims=True))
        vectors_new[0:1, :] = gain_grad
        vectors_new[1:2, :] = line(r.norm_gain) - RATES[0] / jnp.maximum(1.0, root / CLIP) * update
        vectors_new[2:3, :] = moment
        vectors_new[10:18, :] = jnp.zeros((8, half), jnp.float32)
        vectors_new[27:32, :] = jnp.zeros((5, half), jnp.float32)

    pair[...] = jnp.zeros(pair.shape, jnp.float32)
    r.pair_last[...] = jnp.zeros(pair.shape, jnp.float32)
    extra_core.start()
    extra_steps = {1: extra_stage_x, 3: extra_stage_z, 5: extra_stage_last, 7: extra_back_x, 9: extra_back_core}
    extra_steps.update({2: out_stage, 10: residual_stage, 11: small_stage})
    extra_steps.update({12: early_begin, 13: early_hops[1], 14: early_end})
    for step in range(max(main.chunks + LAGS[3] - main.at, 15)):
        main.advance()
        in_stage(main.at - 1 - LAGS[3])
        if step < kept_chunks:
            hidden_stage(step)
        if step in extra_steps:
            extra_steps[step]()
        if step == 11:
            for copy in stores:
                copy.start()

    r.pair_last[3:4, :] = rows_to_lanes(row_sums[...])
    last_copy.start()
    put_mean(3, r.pair_last, late + tiles)
    for action in late_hops:
        action()
    last_copy.wait()
    sums_in = (r.pair_last[...] + r.pair_last_far[...]) / counts
    lanes_new = jnp.where(row_at == 3, held_lanes + (1.0 - DECAY) * sums_in, r.lanes_new[...])
    r.lanes_new[...] = lanes_new
    in_mean = mine[late + tiles : late + tiles + 1, :]
    in_scale = lanes_to_rows(lax.rsqrt(lanes_new[3:4, :] / in_mean))
    vectors_new[3:4, :] = cols_new(r.in_cols[0:1, :], take(mine, late, tiles), model)
    in_sum = squares(r.in_grad, in_scale, 3)
    totals = r.totals
    for at, value in enumerate([in_sum, *sums.values()]):
        totals[at : at + 1, :] = jnp.broadcast_to(value, (1, 128))
    totals[9:16, :] = jnp.zeros((7, 128), jnp.float32)
    for action in sum_hops(10, totals, r.totals_acc, r.totals_far, 0):
        action()

    def rate(at, count, step_rate, copies):
        root = jnp.sqrt(totals[at : at + 1, :] / (copies * count))
        return step_rate / jnp.maximum(1.0, root / CLIP)

    in_rate = rate(0, 2.0 * channels * model, RATES[1], 1)
    out_rate = rate(1, 1.0 * channels * model, RATES[2], 1)

    scales_out[3] = in_scale * in_rate
    scales_out[4] = scales_out[4] * out_rate
    small_scale = jnp.concatenate([scales_out[0], scales_out[1], scales_out[2]], axis=0)
    small_rates = {"step": RATES[6], "select": RATES[5], "decay": RATES[8], "conv": RATES[3]}
    at_total = {"step": 2, "select": 3, "decay": 4, "conv": 5}
    row_number = lax.broadcasted_iota(jnp.int32, small_scale.shape, 0)
    for name, (low_edge, high_edge) in groups.items():
        step_rate = rate(
            at_total[name], 1.0 * (high_edge - low_edge) * channels, small_rates[name], 16
        )
        member = (row_number >= low_edge) & (row_number < high_edge)
        small_scale = jnp.where(member, small_scale * step_rate, small_scale)
    for at in range(3):
        scales_out[at] = small_scale[at * 128 : (at + 1) * 128, :]
    for at, step_rate in enumerate((RATES[4], RATES[7], RATES[9])):
        step_rate = rate(6 + at, 1.0 * channels, step_rate, 16)
        vectors_new[21 + at : 22 + at, :] = (
            line((r.conv_bias, r.step_bias, r.skip_gain)[at])
            - wide(step_rate, half) * vectors_new[21 + at : 22 + at, :]
        )

    for copy in [extra_core, extra_x] + extra_z + back_z + [back_x, back_core]:
        copy.wait_send()


class RenewIn(NamedTuple):
    value_grad: object
    gate_grad: object
    out_grad: object
    input_grad: object
    block_out: object
    small: object
    scales: object
    lanes_new: object
    vectors_new: object
    in_weight: object
    out_weight: object
    step_weight: object
    select_weight: object
    decay_log: object
    conv_weight: object


def renew_kernel(*refs):
    r, out = gathered(refs, RenewIn)
    cols, small, scales = r.vectors_new, r.small, r.scales
    span = small.shape[1]

    def write(*values):
        for value in values:
            ref = out.pop(0)
            ref[...] = value.astype(ref.dtype).reshape(ref.shape)

    def line(at):
        return cols[at : at + 1, :]

    def rows(low_edge, high_edge):
        flat = [r.lanes_new[at : at + 1, :] for at in range(5)]
        return jnp.concatenate(flat, axis=1)[:, low_edge:high_edge]

    def matrix(grad, weight, scale, col):
        new = weight - grad * wide(scale, span) * lax.rsqrt(line(col))
        write(grad, new, new)

    write(r.block_out[...], r.input_grad[...], line(0), line(1), line(1), line(2))
    in_refs = [out.pop(0) for _ in range(3)]
    for part, grad_ref in enumerate((r.value_grad, r.gate_grad)):
        grad = grad_ref[...]
        new = r.in_weight[:, part, :] - grad * wide(scales[3], span) * lax.rsqrt(line(3 + part))
        for ref, value in zip(in_refs, (grad, new, new)):
            ref[:, part, :] = value.astype(ref.dtype)
    write(rows(384, 512), cols[3:5, :])
    matrix(r.out_grad[...], r.out_weight[...], scales[4], 5)
    write(rows(512, 640), line(5))
    small_scale = jnp.concatenate([scales[0], scales[1], scales[2]], axis=0)
    matrix(small[304:308, :], r.conv_weight[...], small_scale[304:308], 6)
    write(rows(304, 308), line(6))
    write(line(18), line(21), line(21), line(24))
    matrix(small[128:288, :], r.select_weight[...], small_scale[128:288], 7)
    write(rows(128, 288), line(7))
    matrix(small[0:128, :], r.step_weight[...], small_scale[0:128], 8)
    write(rows(0, 128), line(8), line(19), line(22), line(22), line(25))
    matrix(small[288:304, :], r.decay_log[...], small_scale[288:304], 9)
    write(rows(288, 304), line(9))
    write(line(20), line(23), line(23), line(26))


def renew(given):
    f32, low = jnp.float32, jnp.bfloat16
    inner = given.out_grad.shape[1]
    shape = jax.ShapeDtypeStruct

    def three(ref):
        return [shape(ref.shape, f32), shape(ref.shape, f32), shape(ref.shape, low)]

    def vector(count):
        return shape((count,), f32)

    def trio(count):
        return [vector(count), vector(count), shape((count,), low)]

    model = given.block_out.shape[1]
    share = given.out_grad.shape[0]
    outs = (
        [shape(given.block_out.shape, f32), shape(given.input_grad.shape, f32)]
        + trio(model)
        + [vector(model)]
        + three(given.in_weight)
        + [vector(share), shape((2, inner), f32)]
        + three(given.out_weight)
        + [vector(share), vector(inner)]
        + three(given.conv_weight)
        + [vector(given.conv_weight.shape[0]), vector(inner)]
        + trio(inner)
        + [vector(inner)]
        + three(given.select_weight)
        + [vector(given.select_weight.shape[0]), vector(inner)]
        + three(given.step_weight)
        + [vector(given.step_weight.shape[0]), vector(inner)]
        + trio(inner)
        + [vector(inner)]
        + three(given.decay_log)
        + [vector(given.decay_log.shape[0]), vector(inner)]
        + trio(inner)
        + [vector(inner)]
    )
    span = inner // RENEW_TILES

    def by_tile(ref, first=0):
        *front, last = ref.shape
        if not front and last != inner:
            return pl.BlockSpec((last,), lambda i: (0,))
        zeros = (0,) * len(front)
        return pl.BlockSpec((*front, span), lambda i: zeros + (first + i,))

    def whole(ref):
        zeros = (0,) * len(ref.shape)
        return pl.BlockSpec(ref.shape, lambda i: zeros)

    specs = RenewIn(*[by_tile(ref) for ref in given])
    specs = specs._replace(
        gate_grad=by_tile(given.gate_grad, RENEW_TILES),
        scales=whole(given.scales),
        lanes_new=whole(given.lanes_new),
    )
    return tuple(
        pl.pallas_call(
            renew_kernel,
            grid=(RENEW_TILES,),
            in_specs=list(specs),
            out_specs=[by_tile(ref) for ref in outs],
            out_shape=outs,
            compiler_params=pltpu.CompilerParams(vmem_limit_bytes=FINISH_LIMIT),
        )(*given)
    )


class ForwardIn(NamedTuple):
    in_weight: object
    out_weight: object
    block: object
    cot: object
    norm_gain: object
    conv_weight: object
    conv_bias: object
    step_bias: object
    skip_gain: object
    masks: object
    select_weight: object
    step_weight: object
    decay_log: object


class ForwardOut(NamedTuple):
    hidden_t: object
    cot_t: object
    piece: object
    conv_in: object
    rim: object
    conv_pre: object
    conv_out: object
    select_out: object
    step_pre: object
    step_size: object
    held: object
    drive: object
    enter: object
    leave: object
    start: object
    gated: object
    d_mixed: object
    d_gate: object
    branch: object
    skip_grad: object
    weights: object


class ForwardLazy(NamedTuple):
    in_weight: object
    masks: object
    select_weight: object
    cot: object
    out_weight: object
    step_weight: object
    decay_log: object


class ForwardEarly(NamedTuple):
    hidden_t: object
    cot_t: object
    conv_in: object
    conv_pre: object
    conv_out: object
    step_pre: object
    step_size: object
    held: object
    drive: object
    enter: object
    leave: object
    start: object


class ForwardWork(NamedTuple):
    hidden: object
    full: object
    ext: object
    gate: object
    scanned: object
    state_piece: object
    come: object
    back: object
    select_far: object
    z_sent: object
    z_got: object
    x_sent: object
    x_got: object
    core_sems: object
    kept: object
    rim_sems: object
    chain_sems: object
    pair_sems: object


def forward_block_kernel(*refs):
    r, left = gathered(refs, ForwardIn, ForwardOut, ForwardWork)
    lazy, early = len(ForwardLazy._fields), len(ForwardEarly._fields)
    loads = mirrored(r, ForwardLazy, left[:lazy], left[lazy], False)
    stores = mirrored(r, ForwardEarly, left[lazy + 1 :], left[lazy + 1 + early], True)
    for copy in loads:
        copy.start()
    z, x, core = position()
    place, tp = lax.axis_index("seq"), lax.axis_index("tp")
    full, hidden = r.full, r.hidden

    def line(ref):
        return ref[...].reshape(1, -1)

    chunks, width = full.shape[0], full.shape[5]
    third = chunks // 3
    low = jnp.bfloat16
    z_peers = [device(lax.rem(z + step, 4), x, core) for step in (1, 2, 3)]
    x_peer, core_peer = device(z, 1 - x, core), device(z, x, 1 - core)
    seq_peers = [(lax.rem(place + step, 16), tp) for step in range(1, 16)]
    greet(seq_peers + [other_half()])

    def slot(chunk, level):
        if chunk in X_FIRST:
            return full.at[chunk, level, :, core]
        return full.at[chunk, level, x, core]

    def up(chunk, hop):
        ref = slot(chunk, z - hop)
        peer = device(z + 1, x, core)
        return remote(ref, ref, r.z_sent.at[chunk, hop], r.z_got.at[chunk, hop], peer)

    def down(chunk, hop):
        ref = slot(chunk, z + hop)
        peer = device(z - 1, x, core)
        return remote(ref, ref, r.z_sent.at[chunk, 3 + hop], r.z_got.at[chunk, 3 + hop], peer)

    def from_below(chunk, hop):
        ref = slot(chunk, z - hop)
        peer = device(z - 1, x, core)
        return remote(ref, ref, r.z_sent.at[chunk, hop - 1], r.z_got.at[chunk, hop - 1], peer)

    def from_above(chunk, hop):
        ref = slot(chunk, z + hop)
        peer = device(z + 1, x, core)
        return remote(ref, ref, r.z_sent.at[chunk, 2 + hop], r.z_got.at[chunk, 2 + hop], peer)

    def along_x(chunk, level):
        ref = full.at[chunk, level, x, core]
        return remote(ref, ref, r.x_sent.at[chunk, level], r.x_got.at[chunk, level], x_peer)

    def along_core(chunk):
        ref = full.at[chunk, :, :, core]
        return remote(ref, ref, r.core_sems.at[0, chunk], r.core_sems.at[1, chunk], core_peer)

    def keep(chunk):
        return pltpu.make_async_copy(full.at[chunk], r.weights.at[chunk], r.kept.at[chunk])

    def columns(at):
        return slice(at * width, (at + 1) * width)

    def when(condition, action):
        pl.when(condition)(action)

    def z_start(chunk):
        when(z < 3, lambda: up(chunk, 0).start())
        when(z > 0, lambda: down(chunk, 0).start())

    def z_hop(chunk, hop):
        def below():
            from_below(chunk, hop).wait_recv()
            if hop < 3:
                when(z < 3, lambda: up(chunk, hop).start())
            if chunk not in X_FIRST:
                along_x(chunk, z - hop).start()

        def above():
            from_above(chunk, hop).wait_recv()
            if hop < 3:
                when(z > 0, lambda: down(chunk, hop).start())
            if chunk not in X_FIRST:
                along_x(chunk, z + hop).start()

        when(z >= hop, below)
        when(z + hop < 4, above)

    def own_columns(chunk):
        if chunk < 2 * third:
            return r.in_weight[:, chunk // third, columns(chunk % third)]
        return r.out_weight[:, columns(chunk - 2 * third)]

    def ready(step):
        return 0 <= step < chunks

    def pump(step):
        for first in [step + 1] if step else range(2):
            if ready(first):
                full[first, z, x, core] = own_columns(first).astype(low)
                along_x(first, z).start()
                if first not in X_FIRST:
                    z_start(first)
        for hop in range(4):
            chunk = step - 1 - hop
            if not ready(chunk):
                continue
            late = 1 if chunk in X_FIRST else 0
            if late and hop == 0:
                along_x(chunk, z).wait_recv()
                z_start(chunk)
            elif hop + 1 - late < 4 and hop + 1 - late > 0:
                z_hop(chunk, hop + 1 - late)
            if hop == 3:
                if late == 0:
                    wait_all([along_x(chunk, level) for level in range(4)])
                along_core(chunk).start()
        if ready(step - 5):
            along_core(step - 5).wait_recv()
            if step - 5 < 2 * third:
                keep(step - 5).start()

    def weights(chunk):
        return full[chunk].reshape(hidden.shape[1], width)

    def dot(left, right):
        return jnp.dot(left, right, preferred_element_type=jnp.float32)

    def dot_last(left, right):
        return lax.dot_general(
            left, right, (((1,), (1,)), ((), ())), preferred_element_type=jnp.float32
        )

    half_rows = r.block.shape[0]
    mine = pl.ds(pl.multiple_of(tp * half_rows, half_rows), half_rows)
    residual = r.block[...].astype(jnp.float32)
    inv_rms = lax.rsqrt(jnp.mean(residual * residual, axis=1, keepdims=True) + EPS_NORM)
    hidden[mine] = (residual * inv_rms * line(r.norm_gain)).astype(low)
    pair_sems = r.pair_sems
    swap = remote(hidden.at[mine], hidden.at[mine], pair_sems.at[0], pair_sems.at[1], other_half())
    swap.start()
    loads.in_weight.wait()

    rows = hidden.shape[0]
    conv_in, conv_pre, conv_out, rim, ext = (
        r.conv_in,
        r.conv_pre,
        r.conv_out,
        r.rim,
        r.ext,
    )

    def rim_copy(tile):
        return remote(
            conv_in.at[rows - 16 :, columns(tile)],
            rim.at[:, columns(tile)],
            r.rim_sems.at[0, tile],
            r.rim_sems.at[1, tile],
            seq_peers[0],
        )

    def value_tile(tile):
        conv_in[:, columns(tile)] = dot(hidden[...], weights(tile)).astype(low)
        rim_copy(tile).start()

    masks = r.masks
    select_out = r.select_out

    def conv_tile(tile):
        rim_copy(tile).wait_recv()
        ext[0:8, :] = rim[8:16, columns(tile)].astype(jnp.float32)
        ext[8:, :] = conv_in[:, columns(tile)].astype(jnp.float32)
        conv_weight = r.conv_weight
        total = line(r.conv_bias)[:, columns(tile)] + conv_weight[0:1, columns(tile)] * ext[8:, :]
        for lag in range(1, 4):
            total = total + conv_weight[lag : lag + 1, columns(tile)] * (
                ext[8 - lag : 8 - lag + rows, :] * wide(masks[lag - 1], width)
            )
        conv_pre[:, columns(tile)] = total
        out = (total * jax.nn.sigmoid(total)).astype(low)
        conv_out[:, columns(tile)] = out
        select_low = r.select_weight[:, columns(tile)].astype(low)
        spare = jnp.zeros((select_out.shape[1] - select_low.shape[0], width), low)
        part = dot_last(out, jnp.concatenate([select_low, spare], axis=0))
        select_out[...] = part if tile == 0 else select_out[...] + part

    select_swap = remote(
        select_out, r.select_far, pair_sems.at[2], pair_sems.at[3], other_half()
    )
    enter, leave = r.enter, r.leave
    states = r.decay_log.shape[0]
    step_rank = r.step_weight.shape[0]
    held, drive = r.held, r.drive

    def select_stage():
        select_swap.wait()
        select_out[...] = select_out[...] + r.select_far[...]
        turned = select_out[:, step_rank : step_rank + 128].T
        for at in range(rows):
            enter[at] = jnp.broadcast_to(turned[:states, at : at + 1], (states, 128))
            leave[at] = jnp.broadcast_to(turned[states : 2 * states, at : at + 1], (states, 128))

    def step_tile(tile):
        here = columns(tile)
        step_low = r.step_weight[:, here].astype(low)
        pre = dot(select_out[:, :step_rank].astype(low), step_low) + line(r.step_bias)[:, here]
        size = jnp.maximum(pre, 0.0) + jnp.log1p(jnp.exp(-jnp.abs(pre)))
        r.step_pre[:, here] = pre
        r.step_size[:, here] = size
        held[:, here] = jnp.where(wide(masks[0], width) > 0.0, size, RESET)
        drive[:, here] = size * conv_out[:, here].astype(jnp.float32)

    piece = r.state_piece

    def rate_of(here):
        return -jnp.exp(r.decay_log[:, here]) * LOG2E

    def state_tile(tile):
        here = columns(tile)
        rate = rate_of(here)

        def block(index, state):
            base = pl.multiple_of(index * 8, 8)
            for offset in range(8):
                at = base + offset
                kept = jnp.exp2(rate * held[pl.ds(at, 1), here])
                state = kept * state + wide(enter[at], width) * drive[pl.ds(at, 1), here]
            return state

        piece[0:states, here] = lax.fori_loop(
            0, rows // 8, block, jnp.zeros((states, width), jnp.float32)
        )
        total = jnp.sum(held[:, here], axis=0, keepdims=True)
        piece[states:, here] = jnp.broadcast_to(total, (8, width))

    chain_out, chain_home, chain_middle, chain_end = chain_parts(
        False, piece, lambda: rate_of(own_lanes(place)), r.start, r.come, r.back, r.chain_sems
    )
    scanned, start = r.scanned, r.start

    def scan_tile(tile):
        here = columns(tile)
        rate = rate_of(here)

        def block(index, state):
            base = pl.multiple_of(index * 8, 8)
            for offset in range(8):
                at = base + offset
                kept = jnp.exp2(rate * held[pl.ds(at, 1), here])
                state = kept * state + wide(enter[at], width) * drive[pl.ds(at, 1), here]
                scanned[pl.ds(at, 1), here] = jnp.sum(
                    wide(leave[at], width) * state, axis=0, keepdims=True
                )
            return state

        lax.fori_loop(0, rows // 8, block, start[:, here])

    gate = r.gate

    def gate_tile(tile):
        gate[:, columns(tile)] = dot(hidden[...], weights(third + tile))

    def out_tile(tile):
        here = columns(tile)
        out_weight = weights(2 * third + tile)
        value = conv_out[:, here].astype(jnp.float32)
        mixed = scanned[:, here] + line(r.skip_gain)[:, here] * value
        pre = gate[:, here]
        sigmoid = jax.nn.sigmoid(pre)
        act = pre * sigmoid
        gated = (mixed * act).astype(low)
        r.gated[:, here] = gated
        d_gated = dot(r.cot[...], out_weight)
        d_mixed = d_gated * act
        r.d_mixed[:, here] = d_mixed
        slope = sigmoid * (1.0 + pre * (1.0 - sigmoid))
        r.d_gate[:, here] = (d_gated * mixed * slope).astype(low)
        r.skip_grad[:, here] = jnp.sum(d_mixed * value, axis=0, keepdims=True)
        part = dot_last(gated, out_weight)
        r.branch[...] = part if tile == 0 else r.branch[...] + part

    def adjoint_tile(tile):
        here = columns(tile)
        rate = rate_of(here)

        def block(index, state):
            base = pl.multiple_of((rows // 8 - 1 - index) * 8, 8)
            for offset in range(7, -1, -1):
                at = base + offset
                kept = jnp.exp2(rate * held[pl.ds(at, 1), here])
                state = kept * (state + wide(leave[at], width) * r.d_mixed[pl.ds(at, 1), here])
            return state

        r.piece[0:states, here] = lax.fori_loop(
            0, rows // 8, block, jnp.zeros((states, width), jnp.float32)
        )
        total = jnp.sum(held[:, here], axis=0, keepdims=True)
        r.piece[states:, here] = jnp.broadcast_to(total, (8, width))

    def turn(source, target):
        for at in range(target.shape[0]):
            value = source[:, at * 128 : (at + 1) * 128].astype(jnp.float32)
            target[at % 2 * 8 + at // 2 % 2 * 4 + at // 4] = value.T.astype(low)

    for step in range(third + 5):
        pump(step)
        if step == 2:
            swap.wait()
            for copy in loads[1:]:
                copy.wait()
        if step >= 5:
            value_tile(step - 5)
        if step >= 6:
            conv_tile(step - 6)
    conv_tile(third - 1)
    select_swap.start()
    pump(third + 5)
    gate_tile(0)
    select_stage()
    for tile in range(third):
        step_tile(tile)
    pump(third + 6)
    gate_tile(1)
    for tile in range(third):
        state_tile(tile)
    chain_out()
    turn(r.cot, r.cot_t)
    chain_middle()
    turn(hidden, r.hidden_t)
    pump(third + 7)
    gate_tile(2)
    chain_home()
    for tile in range(third):
        scan_tile(tile)
    pump(third + 8)
    gate_tile(3)
    for copy in stores:
        copy.start()
    for tile in range(third):
        pump(2 * third + 5 + tile)
        out_tile(tile)
        adjoint_tile(tile)
    chain_end()
    for chunk in range(chunks):
        for hop in range(3):
            when((z < 3) & (z >= hop), up(chunk, hop).wait_send)
            when((z > 0) & (z + hop < 4), down(chunk, hop).wait_send)
        for level in range(4):
            if chunk not in X_FIRST:
                along_x(chunk, level).wait_send()
        if chunk in X_FIRST:
            along_x(chunk, z).wait_send()
        along_core(chunk).wait_send()
        if chunk < 2 * third:
            keep(chunk).wait()
    for tile in range(third):
        rim_copy(tile).wait_send()
    for copy in stores:
        copy.wait()


def own_lanes(at):
    return pl.ds(pl.multiple_of(at * 128, 128), 128)


def chain_parts(backward, piece, rate_own, out, come, back, sems):
    place = lax.axis_index("seq")
    peers = [(lax.rem(place + step, 16), lax.axis_index("tp")) for step in range(1, 16)]
    states = out.shape[0]

    def away(at):
        return remote(
            piece.at[:, own_lanes(peers[at][0])],
            come.at[place],
            sems.at[0, at],
            sems.at[1, at],
            peers[at],
        )

    def home(at):
        return remote(
            back.at[peers[at][0]],
            out.at[:, own_lanes(place)],
            sems.at[2, at],
            sems.at[3, at],
            peers[at],
        )

    def begin():
        for at in range(15):
            away(at).start()
        come[place] = piece[:, own_lanes(place)]

    def middle():
        rate = rate_own()
        for at in range(15):
            away(at).wait_recv()

        def join(index, state):
            at = 15 - index if backward else index
            back[at] = state
            part = come[at]
            return jnp.exp2(rate * part[states : states + 1]) * state + part[:states]

        lax.fori_loop(0, 16, join, jnp.zeros((states, 128), jnp.float32))
        for at in range(15):
            home(at).start()
        out[:, own_lanes(place)] = back[place]

    def arrive():
        for at in range(15):
            home(at).wait_recv()

    def end():
        for at in range(15):
            away(at).wait_send()
            home(at).wait_send()

    return begin, arrive, middle, end


def forward_block(ident, given):
    half_rows, model = given.block.shape
    rows = 2 * half_rows
    share, inner = given.out_weight.shape
    total = 3 * inner
    states = given.decay_log.shape[0]
    f32, low = jnp.float32, jnp.bfloat16
    vmem = pl.BlockSpec(memory_space=pltpu.VMEM)
    dma = pltpu.SemaphoreType.DMA
    width = 512
    chunks = total // width
    select_rows = 256

    def like(columns, dtype):
        return jax.ShapeDtypeStruct((rows, columns), dtype)

    lanes = jax.ShapeDtypeStruct((rows, states, 128), f32)
    shapes = ForwardOut(*[
        jax.ShapeDtypeStruct((16, share, rows), low),
        jax.ShapeDtypeStruct((16, share, rows), low),
        jax.ShapeDtypeStruct((states + 8, inner), f32),
        like(inner, low),
        jax.ShapeDtypeStruct((16, inner), low),
        like(inner, f32),
        like(inner, low),
        like(select_rows, f32),
        like(inner, f32),
        like(inner, f32),
        like(inner, f32),
        like(inner, f32),
        lanes,
        lanes,
        jax.ShapeDtypeStruct((states, inner), f32),
        like(inner, low),
        like(inner, f32),
        like(inner, low),
        like(model, f32),
        jax.ShapeDtypeStruct((1, inner), f32),
        jax.ShapeDtypeStruct((chunks * 2 // 3, 4, 2, 2, share, width), low),
    ])
    specs = ForwardOut(*placed(ForwardOut, ForwardEarly))._replace(
        weights=pl.BlockSpec(memory_space=pltpu.HBM)
    )
    outs = pl.pallas_call(
        forward_block_kernel,
        in_specs=placed(ForwardIn, ForwardLazy),
        out_specs=list(specs),
        out_shape=list(shapes),
        scratch_shapes=[
            pltpu.VMEM((rows, model), low),
            pltpu.VMEM((chunks, 4, 2, 2, share, width), low),
            pltpu.VMEM((rows + 8, width), f32),
            pltpu.VMEM((rows, inner), f32),
            pltpu.VMEM((rows, inner), f32),
            pltpu.VMEM((states + 8, inner), f32),
            pltpu.VMEM((16, states + 8, 128), f32),
            pltpu.VMEM((16, states, 128), f32),
            pltpu.VMEM((rows, select_rows), f32),
            dma((chunks, 6)),
            dma((chunks, 6)),
            dma((chunks, 4)),
            dma((chunks, 4)),
            dma((2, chunks)),
            dma((chunks,)),
            dma((2, chunks // 3)),
            dma((4, 15)),
            dma((4,)),
        ]
        + mirrors(ForwardLazy, given)
        + mirrors(ForwardEarly, shapes),
        compiler_params=pltpu.CompilerParams(
            collective_id=ident, has_side_effects=True, vmem_limit_bytes=FINISH_LIMIT
        ),
    )(*given)
    out = ForwardOut(*outs)
    return out._replace(weights=out.weights.reshape(-1, model, width))


def backward_part(r, main, loads):
    z, x, core = position()
    place, tp = lax.axis_index("seq"), lax.axis_index("tp")
    low = jnp.bfloat16
    seq_peers = [(lax.rem(place + step, 16), tp) for step in range(1, 16)]
    rows, inner = r.held.shape
    states = r.decay_log.shape[0]
    width = 512
    tiles = inner // width
    pair_sems = r.pair_sems

    def columns(at):
        return slice(at * width, (at + 1) * width)

    def dot(left, right):
        return jnp.dot(left, right, preferred_element_type=jnp.float32)

    def dot_last(left, right):
        return lax.dot_general(
            left, right, (((1,), (1,)), ((), ())), preferred_element_type=jnp.float32
        )

    def line(ref):
        return ref[...].reshape(1, -1)

    half_rows = r.block.shape[0]
    own_half = pl.ds(pl.multiple_of(tp * half_rows, half_rows), half_rows)
    far_half = pl.ds(pl.multiple_of((1 - tp) * half_rows, half_rows), half_rows)
    branch_swap = remote(
        r.branch_send, r.branch_far, pair_sems.at[0], pair_sems.at[1], other_half()
    )

    held, drive, grad = r.held, r.drive, r.d_mixed
    enter, leave, piece = r.enter, r.leave, r.piece

    def rate_of(here):
        return -jnp.exp(r.decay_log[:, here])

    chain_out, chain_home, chain_middle, chain_end = chain_parts(
        True,
        piece,
        lambda: rate_of(own_lanes(place)) * LOG2E,
        r.follow,
        r.come,
        r.back,
        r.chain_sems,
    )
    kept_all, state_all = r.kept, r.state
    drive_grad, d_step_pre = r.drive_grad, r.d_step_pre
    enter_grad, leave_grad = r.enter_grad, r.leave_grad

    def again_tile(tile):
        here = columns(tile)
        rate = rate_of(here) * LOG2E

        def block(index, state):
            base = pl.multiple_of(index * 8, 8)
            for offset in range(8):
                at = base + offset
                kept = jnp.exp2(rate * held[pl.ds(at, 1), here])
                kept_all[at] = kept
                state = kept * state + wide(enter[at], width) * drive[pl.ds(at, 1), here]
                state_all[at + 1] = state
            return state

        start = r.start[:, here]
        state_all[0] = start
        lax.fori_loop(0, rows // 8, block, start)

    def reverse_tile(tile):
        here = columns(tile)
        rate = rate_of(here)

        def block(index, carry):
            follow, decay = carry
            base = pl.multiple_of((rows // 8 - 1 - index) * 8, 8)
            for offset in range(7, -1, -1):
                at = base + offset
                now = grad[pl.ds(at, 1), here]
                adjoint = wide(leave[at], width) * now + follow
                drive_grad[pl.ds(at, 1), here] = jnp.sum(
                    adjoint * wide(enter[at], width), axis=0, keepdims=True
                )
                enters = fold_lanes(adjoint * drive[pl.ds(at, 1), here])
                leaves = fold_lanes(state_all[at + 1] * now)
                if tile == 0:
                    enter_grad[at], leave_grad[at] = enters, leaves
                else:
                    enter_grad[at] += enters
                    leave_grad[at] += leaves
                follow = kept_all[at] * adjoint
                part = follow * state_all[at]
                r.ext[pl.ds(at, 1), :] = jnp.sum(part * rate, axis=0, keepdims=True)
                decay = decay + part * held[pl.ds(at, 1), here]
            return follow, decay

        follow = r.follow[:, here]
        _, decay = lax.fori_loop(0, rows // 8, block, (follow, jnp.zeros_like(follow)))
        r.decay_grad[:, here] = decay * rate
        d_step = (
            drive_grad[:, here] * r.conv_out[:, here].astype(jnp.float32) + r.ext[0:rows, :]
        )
        d_step_pre[:, here] = (d_step * jax.nn.sigmoid(r.step_pre[:, here])).astype(low)

    step_rank = r.step_weight.shape[0]
    select_grad = r.select_grad
    extra = r.extra

    def turned(value):
        return value.astype(jnp.float32).T.astype(low)

    def store_extra(first, tile, value):
        for at in range(width // 128):
            owner = tile * (width // 128) + at
            extra[owner // 2, owner % 2, first : first + value.shape[0], :] = value[
                :, at * 128 : (at + 1) * 128
            ].astype(low)

    def select_start():
        step_in = turned(r.select_out[:, :step_rank])
        total = jnp.zeros((rows, step_rank), jnp.float32)
        for tile in range(tiles):
            here = columns(tile)
            total = total + dot_last(d_step_pre[:, here], r.step_weight[:, here].astype(low))
            store_extra(0, tile, dot(step_in, d_step_pre[:, here]))
        select_grad[:, :step_rank] = total
        row_at = lax.broadcasted_iota(jnp.int32, (8, states, 128), 1)
        lane_at = lax.broadcasted_iota(jnp.int32, (8, states, 128), 2)

        def block(index, _):
            base = pl.multiple_of(index * 8, 8)
            here = pl.ds(base, 8)
            enters = jnp.sum(enter_grad[here], axis=2, keepdims=True)
            leaves = jnp.sum(leave_grad[here], axis=2, keepdims=True)
            spread = jnp.where(lane_at == row_at, enters, 0.0)
            spread = jnp.where(lane_at == row_at + states, leaves, spread)
            select_grad[here, step_rank:] = jnp.sum(spread, axis=1)
            return 0

        lax.fori_loop(0, rows // 8, block, 0)
        select_swap.start()

    select_swap = remote(
        select_grad, r.select_far, pair_sems.at[2], pair_sems.at[3], other_half()
    )
    conv_grad, rim_next, ext = r.conv_grad, r.rim_next, r.ext

    def rim_copy(tile):
        return remote(
            conv_grad.at[0:8, columns(tile)],
            rim_next.at[:, columns(tile)],
            r.rim_sems.at[0, tile],
            r.rim_sems.at[1, tile],
            seq_peers[14],
        )

    select_count = r.select_weight.shape[0]

    def select_end():
        select_swap.wait()
        total = (select_grad[...] + r.select_far[...]).astype(low)
        select_low = total[:, :256]
        first, second = turned(select_low[:, :128]), turned(select_low[:, 128:])
        for tile in range(tiles):
            here = columns(tile)
            conv_out = r.conv_out[:, here]
            store_extra(step_rank, tile, dot(first, conv_out))
            store_extra(step_rank + 128, tile, dot(second[: select_count - 128], conv_out))
            weight = r.select_weight[:, here].astype(low)
            spare = jnp.zeros((256 - select_count, width), low)
            d_conv = (
                drive_grad[:, here] * r.step_size[:, here]
                + grad[:, here] * line(r.skip_gain)[:, here]
                + dot(select_low, jnp.concatenate([weight, spare], axis=0))
            )
            pre = r.conv_pre[:, here]
            sigmoid = jax.nn.sigmoid(pre)
            conv_grad[:, here] = d_conv * (sigmoid * (1.0 + pre * (1.0 - sigmoid)))
            rim_copy(tile).start()
            if tile == 1:
                main.advance()

    masks = r.masks

    def conv_tile(tile):
        here = columns(tile)
        value = conv_grad[:, here]
        weight = r.conv_weight
        lines = []
        ext[0:8, :] = r.rim[8:16, here].astype(jnp.float32)
        ext[8:, :] = r.conv_in[:, here].astype(jnp.float32)
        for lag in range(4):
            shifted = ext[8 - lag : 8 - lag + rows, :]
            if lag > 0:
                shifted = shifted * wide(masks[lag - 1], width)
            lines.append(jnp.sum(value * shifted, axis=0, keepdims=True))
        lines.append(jnp.sum(value, axis=0, keepdims=True))
        lines.append(
            jnp.sum(d_step_pre[:, here].astype(jnp.float32), axis=0, keepdims=True)
        )
        lines.append(r.skip_grad[:, here])
        lines.append(jnp.zeros((9, width), jnp.float32))
        first = step_rank + select_count
        store_extra(first, tile, r.decay_grad[:, here])
        store_extra(first + states, tile, jnp.concatenate(lines, axis=0))
        rim_copy(tile).wait_recv()
        ext[0:rows, :] = value
        ext[rows:, :] = rim_next[:, here]
        total = weight[0:1, here] * value
        for lag in range(1, 4):
            total = total + weight[lag : lag + 1, here] * (
                ext[lag : lag + rows, :] * wide(masks[2 + lag], width)
            )
        r.d_value[:, here] = total.astype(low)

    for copy in loads[:3]:
        copy.wait()
    main.advance()
    chain_out()
    main.advance()
    for copy in loads[3:]:
        copy.wait()
    r.branch_send[...] = r.branch[far_half, :].astype(low)
    branch_swap.start()
    chain_middle()
    again_tile(0)
    main.advance(1)
    chain_home()
    for tile in range(tiles):
        if tile > 0:
            again_tile(tile)
        reverse_tile(tile)
        main.advance()
    select_start()
    main.advance()
    branch_swap.wait()
    r.block_out[...] = (
        r.block[...].astype(jnp.float32)
        + r.branch[own_half, :]
        + r.branch_far[...].astype(jnp.float32)
    )
    select_end()
    main.advance()
    for tile in range(tiles):
        conv_tile(tile)
        if tile % 2:
            main.advance()

    def end():
        chain_end()
        for tile in range(tiles):
            rim_copy(tile).wait_send()

    return end


def rest_kernel(channels, model, *refs):
    r, left = gathered(refs, RestIn, RestOut, RestWork)
    lazy, early = len(RestLazy._fields), len(RestEarly._fields)
    loads = mirrored(r, RestLazy, left, left[lazy], False)
    left = left[lazy + 1 :]
    stores = mirrored(r, RestEarly, left, left[early], True)
    for copy in loads:
        copy.start()
    reducer_refs = left[early + 1 :]
    z, x, core = position()
    place, tp = lax.axis_index("seq"), lax.axis_index("tp")
    seq_peers = [(lax.rem(place + step, 16), tp) for step in range(1, 16)]
    across = [(lax.rem(z + step, 4) * 4 + x * 2 + core, 1 - tp) for step in range(4)]
    greet(seq_peers + across)
    inner = r.out_grad.shape[1]
    starts = range(0, inner, SHARE_WIDTH)
    main = Reducer(
        [(r.cot_t, r.gated, at, r.out_grad, at) for at in starts]
        + [(r.hidden_t, r.d_gate, at, r.in_grad, inner + at) for at in starts]
        + [(r.hidden_t, r.d_value, at, r.in_grad, at) for at in starts],
        reducer_refs,
    )
    end = backward_part(r, main, loads)
    finish_part(channels, model, r, main, stores)
    end()
    main.drain()
    for copy in stores:
        copy.wait()


class RestIn(NamedTuple):
    hidden_t: object
    cot_t: object
    gated: object
    d_gate: object
    piece: object
    d_mixed: object
    held: object
    drive: object
    enter: object
    leave: object
    start: object
    conv_out: object
    step_pre: object
    step_size: object
    conv_pre: object
    conv_in: object
    rim: object
    select_out: object
    branch: object
    block: object
    skip_grad: object
    masks: object
    conv_weight: object
    skip_gain: object
    select_weight: object
    step_weight: object
    decay_log: object
    weights: object
    cot: object
    step_rows: object
    select_rows: object
    decay_rows: object
    conv_rows: object
    in_rows: object
    out_rows: object
    norm_gain: object
    norm_moment: object
    in_cols: object
    out_cols: object
    step_cols: object
    select_cols: object
    decay_cols: object
    conv_cols: object
    bias_moment: object
    step_moment: object
    skip_moment: object
    conv_bias: object
    step_bias: object


class RestOut(NamedTuple):
    out_grad: object
    block_out: object
    in_grad: object
    input_grad: object
    small: object
    scales: object
    lanes_new: object
    vectors_new: object


class RestLazy(NamedTuple):
    cot_t: object
    gated: object
    piece: object
    branch: object
    held: object
    drive: object
    enter: object
    start: object
    leave: object
    d_mixed: object
    conv_out: object
    step_pre: object
    step_weight: object
    select_weight: object
    step_size: object
    conv_pre: object
    conv_in: object
    hidden_t: object
    d_gate: object
    masks: object


class RestEarly(NamedTuple):
    out_grad: object
    block_out: object
    input_grad: object
    small: object


class RestWork(NamedTuple):
    d_value: object
    extra: object
    come: object
    back: object
    follow: object
    kept: object
    state: object
    drive_grad: object
    d_step_pre: object
    decay_grad: object
    enter_grad: object
    leave_grad: object
    select_grad: object
    select_far: object
    conv_grad: object
    rim_next: object
    ext: object
    branch_send: object
    branch_far: object
    chain_sems: object
    pair_sems: object
    rim_sems: object
    come_core: object
    send_x: object
    come_x: object
    send_z: object
    come_z: object
    full: object
    mine: object
    acc: object
    far: object
    row_sums: object
    pair: object
    pair_far: object
    pair_last: object
    pair_last_far: object
    lanes: object
    totals: object
    totals_acc: object
    totals_far: object
    come_half: object
    d_hidden: object
    fetched: object
    fetched_sems: object
    extra_sent: object
    extra_got: object
    sums_sent: object
    sums_got: object
    half_sems: object


def rest_block(ident, channels, given):
    rows, inner = given.held.shape
    half_rows, model = given.block.shape
    states = given.decay_log.shape[0]
    small_rows = given.step_weight.shape[0] + given.select_weight.shape[0] + states + 16
    columns = 2 * inner
    f32, low = jnp.float32, jnp.bfloat16
    dma = pltpu.SemaphoreType.DMA
    share = model // 16
    seq_rows = columns // 128 + inner // 128 + model // 128 + 16
    kept_chunks, _, kept_width = given.weights.shape
    block = (small_rows, 128)
    shape, space = jax.ShapeDtypeStruct, pltpu.VMEM
    vmem = pl.BlockSpec(memory_space=pltpu.VMEM)
    specs = RestIn(*placed(RestIn, RestLazy))._replace(
        weights=pl.BlockSpec(memory_space=pltpu.HBM)
    )
    shapes = RestOut(
        shape((share, inner), f32),
        shape((half_rows, model), f32),
        shape((share, columns), f32),
        shape((half_rows, model), f32),
        shape((small_rows, inner), f32),
        shape((5, 128, 128), f32),
        shape((8, 128), f32),
        shape((32, inner), f32),
    )
    outs = pl.pallas_call(
        functools.partial(rest_kernel, channels, model),
        in_specs=list(specs),
        out_specs=placed(RestOut, RestEarly),
        out_shape=list(shapes),
        scratch_shapes=[
            space((rows, inner), low),
            space((8, 2, small_rows, 128), low),
            space((16, states + 8, 128), f32),
            space((16, states, 128), f32),
            space((states, inner), f32),
            space((rows, states, 512), f32),
            space((rows + 1, states, 512), f32),
            space((rows, inner), f32),
            space((rows, inner), low),
            space((states, inner), f32),
            space((rows, states, 128), f32),
            space((rows, states, 128), f32),
            space((rows, 256), f32),
            space((rows, 256), f32),
            space((rows, inner), f32),
            space((8, inner), f32),
            space((rows + 8, 512), f32),
            space((half_rows, model), low),
            space((half_rows, model), low),
            dma((4, 15)),
            dma((4,)),
            dma((2, inner // 512)),
            space((8,) + block, low),
            space((4,) + block, low),
            space((4,) + block, low),
            space((3,) + block, low),
            space((3,) + block, low),
            space((4, 2, 2) + block, low),
            space((seq_rows, 128), f32),
            space((8, seq_rows, 128), f32),
            space((4, model // 128 + 16, 128), f32),
            space((share, 128), f32),
            space((8, 128), f32),
            space((8, 128), f32),
            space((8, 128), f32),
            space((8, 128), f32),
            space((8, 128), f32),
            space((16, 128), f32),
            space((8, 16, 128), f32),
            space((4, 16, 128), f32),
            space((half_rows, model), f32),
            space((2 * half_rows, model), f32),
            space((2, model, kept_width), low),
            dma((kept_chunks,)),
            dma((10,)),
            dma((10,)),
            dma((32,)),
            dma((32,)),
            dma((2,)),
        ]
        + mirrors(RestLazy, given)
        + mirrors(RestEarly, shapes)
        + reducer_scratch(inner + columns, share, SHARE_WIDTH),
        compiler_params=pltpu.CompilerParams(
            collective_id=ident, has_side_effects=True, vmem_limit_bytes=FINISH_LIMIT
        ),
    )(*given)
    return RestOut(*outs)


def on_device(
    block_in,
    cotangent,
    segment_ids,
    norm_gain,
    in_weight,
    out_weight,
    conv_weight,
    conv_bias,
    select_weight,
    step_weight,
    step_bias,
    decay_log,
    skip_gain,
    norm_moment,
    in_rows,
    in_cols,
    out_rows,
    out_cols,
    conv_rows,
    conv_cols,
    bias_moment,
    select_rows,
    select_cols,
    step_rows,
    step_cols,
    step_moment,
    decay_rows,
    decay_cols,
    skip_moment,
):
    tp_count = lax.axis_size("tp")
    seq_index = lax.axis_index("seq")
    tp_index = lax.axis_index("tp")
    seq_first = (seq_index == 0).astype(jnp.float32)
    tp_first = (tp_index == 0).astype(jnp.float32)
    half_rows, model_dim = block_in.shape
    row_count = cotangent.shape[0]
    inner_dim = in_weight.shape[2]
    channels = inner_dim * tp_count
    conv_taps = conv_weight.shape[0]
    states = decay_log.shape[0]
    step_rank = step_weight.shape[0]
    row_share = in_weight.shape[0]
    id_padded = jnp.concatenate(
        [
            jnp.full((conv_taps - 1,), -1, jnp.int32),
            segment_ids,
            jnp.full((conv_taps - 1,), -2, jnp.int32),
        ]
    )
    window = lax.dynamic_slice_in_dim(
        id_padded, seq_index * row_count, row_count + 2 * (conv_taps - 1)
    )
    local_ids = window[conv_taps - 1 : conv_taps - 1 + row_count]
    keep_mask = (local_ids == window[conv_taps - 2 : conv_taps - 2 + row_count]).astype(jnp.float32)
    residual = block_in.astype(jnp.float32)
    mean_sq = jnp.mean(residual * residual, axis=1, keepdims=True)
    inv_rms = lax.rsqrt(mean_sq + EPS_NORM)
    normed = residual * inv_rms
    low_type = jnp.bfloat16
    projected, hidden, in_full = project(
        (normed * norm_gain[None, :]).astype(low_type),
        in_weight.astype(low_type).reshape(row_share, 2 * inner_dim),
        0,
    )
    out_low, projected = lax.optimization_barrier((out_weight.astype(low_type), projected))
    out_full = lax.all_gather(out_low, "seq", axis=0, tiled=True)
    conv_in = projected[:, :inner_dim].astype(jnp.bfloat16)
    gate_pre = projected[:, inner_dim:]
    rim_rows = passed_along(conv_in[row_count - (conv_taps - 1) :], "seq", 1)
    ext_rows = jnp.concatenate([rim_rows, conv_in], axis=0).astype(jnp.float32)
    same_docs = []
    conv_pre = jnp.zeros_like(gate_pre) + conv_bias[None, :]
    for shift_lag in range(conv_taps):
        first_row = conv_taps - 1 - shift_lag
        same_doc = (window[first_row : first_row + row_count] == local_ids).astype(jnp.float32)[
            :, None
        ]
        same_docs.append(same_doc)
        conv_pre = (
            conv_pre
            + conv_weight[shift_lag][None, :]
            * ext_rows[first_row : first_row + row_count]
            * same_doc
        )
    conv_out = jax.nn.silu(conv_pre).astype(jnp.bfloat16)
    conv_value = conv_out.astype(jnp.float32)
    select_low = select_weight.astype(jnp.bfloat16)
    select_out = pair_sum(
        jnp.einsum("te,ke->tk", conv_out, select_low, preferred_element_type=jnp.float32), 1
    )
    step_in = select_out[:, :step_rank].astype(jnp.bfloat16)
    state_in = select_out[:, step_rank : step_rank + states]
    state_out = select_out[:, step_rank + states :]
    step_low = step_weight.astype(jnp.bfloat16)
    step_pre = jnp.dot(step_in, step_low, preferred_element_type=jnp.float32) + step_bias[None, :]
    step_size = jax.nn.softplus(step_pre)
    decay_rate = -jnp.exp(decay_log)
    drive = step_size * conv_value
    held_step = jnp.where(keep_mask[:, None] > 0.0, step_size, RESET)
    enter = jnp.broadcast_to(state_in[:, :, None], (row_count, states, 128))
    leave = jnp.broadcast_to(state_out[:, :, None], (row_count, states, 128))
    nothing = jnp.zeros((8, 128), jnp.float32)
    start, _ = chain(
        piece_state(held_step, drive, enter, decay_rate, False), decay_rate, nothing, False, 2
    )
    scanned = scan_forward(held_step, drive, enter, leave, decay_rate, start)
    mixed = scanned + skip_gain[None, :] * conv_value
    gate_act = jax.nn.silu(gate_pre)
    gated = (mixed * gate_act).astype(jnp.bfloat16)
    branch = jnp.einsum("te,de->td", gated, out_full, preferred_element_type=jnp.float32)
    own_rows, far_rows = tp_index * half_rows, (1 - tp_index) * half_rows
    d_gated = jnp.einsum("td,de->te", cotangent, out_full, preferred_element_type=jnp.float32)
    d_out_w = jnp.einsum("td,te->de", cotangent, gated, preferred_element_type=jnp.float32)
    out_half = lax.psum_scatter(
        d_out_w.astype(low_type), "seq", scatter_dimension=0, tiled=True
    )
    d_mixed = d_gated * gate_act
    d_gate = (d_gated * mixed * silu_slope(gate_pre)).astype(jnp.bfloat16)
    skip_grad = jnp.sum(d_mixed * conv_value, axis=0)
    follow, branch_far = chain(
        piece_state(held_step, d_mixed, leave, decay_rate, True),
        decay_rate,
        lax.dynamic_slice_in_dim(branch, far_rows, half_rows, 0).astype(low_type),
        True,
        3,
    )
    block_out = (
        residual
        + lax.dynamic_slice_in_dim(branch, own_rows, half_rows, 0)
        + branch_far.astype(jnp.float32)
    )
    drive_grad, step_grad, decay_grad, enter_grad, leave_grad = scan_backward(
        held_step, drive, d_mixed, enter, leave, decay_rate, start, follow
    )
    enter_grad = jnp.sum(enter_grad, axis=2)
    leave_grad = jnp.sum(leave_grad, axis=2)
    d_step = drive_grad * conv_value + step_grad
    d_step_pre = (d_step * jax.nn.sigmoid(step_pre)).astype(jnp.bfloat16)
    step_bias_grad = jnp.sum(d_step_pre.astype(jnp.float32), axis=0)
    step_w_grad = jnp.einsum("tr,te->re", step_in, d_step_pre, preferred_element_type=jnp.float32)
    d_step_in = jnp.einsum("te,re->tr", d_step_pre, step_low, preferred_element_type=jnp.float32)
    select_grads = jnp.concatenate(
        [d_step_in, enter_grad, leave_grad],
        axis=1,
    )
    d_select = pair_sum(select_grads, 4).astype(jnp.bfloat16)
    select_w_grad = jnp.einsum("tk,te->ke", d_select, conv_out, preferred_element_type=jnp.float32)
    d_conv = (
        drive_grad * step_size
        + d_mixed * skip_gain[None, :]
        + jnp.einsum("tk,ke->te", d_select, select_low, preferred_element_type=jnp.float32)
    )
    d_conv_pre = d_conv * silu_slope(conv_pre)
    rim_next = passed_along(d_conv_pre[: conv_taps - 1], "seq", -1)
    ext_grads = jnp.concatenate([d_conv_pre, rim_next], axis=0)
    ids_after = window[conv_taps - 1 :]
    d_conv_in = jnp.zeros_like(d_conv_pre)
    conv_w_rows = []
    for shift_lag in range(conv_taps):
        first_row = conv_taps - 1 - shift_lag
        later_same = (ids_after[shift_lag : shift_lag + row_count] == local_ids).astype(
            jnp.float32
        )[:, None]
        d_conv_in = (
            d_conv_in
            + conv_weight[shift_lag][None, :]
            * ext_grads[shift_lag : shift_lag + row_count]
            * later_same
        )
        conv_w_rows.append(
            jnp.sum(
                d_conv_pre * ext_rows[first_row : first_row + row_count] * same_docs[shift_lag],
                axis=0,
            )
        )
    conv_w_grad = jnp.stack(conv_w_rows, axis=0)
    conv_b_grad = jnp.sum(d_conv_pre, axis=0)
    d_projected = jnp.concatenate([d_conv_in.astype(jnp.bfloat16), d_gate], axis=1)
    d_hidden = jnp.einsum(
        "tkn,kdn->td",
        d_projected.reshape(row_count, in_full.shape[0], -1),
        in_full,
        preferred_element_type=jnp.float32,
    )
    vector_grads = jnp.stack([conv_b_grad, step_bias_grad, skip_grad], axis=0)
    small_grads = jnp.concatenate(
        [step_w_grad, select_w_grad, decay_grad, conv_w_grad, vector_grads], axis=0
    )
    out_grad = out_half.astype(jnp.float32)
    in_grad = lax.psum_scatter(
        jnp.einsum("td,tn->dn", hidden, d_projected, preferred_element_type=jnp.float32),
        "seq",
        scatter_dimension=0,
        tiled=True,
    )
    small_full = lax.psum(small_grads, "seq")
    d_hidden = lax.psum_scatter(d_hidden, "tp", scatter_dimension=0, tiled=True)
    in_grad = in_grad.reshape(in_weight.shape)
    gain_part = jnp.sum(d_hidden * normed, axis=0)
    scaled = d_hidden * norm_gain[None, :]
    cot_half = lax.dynamic_slice_in_dim(cotangent, own_rows, half_rows, 0).astype(
        jnp.float32
    )
    input_grad = cot_half + inv_rms * (
        scaled - normed * jnp.mean(scaled * normed, axis=1, keepdims=True)
    )
    edges = [step_rank, select_weight.shape[0], states, conv_taps, 3]
    edges = [sum(edges[:at]) for at in range(len(edges) + 1)]
    step_local, select_local, decay_local, conv_local, vector_local = [
        small_full[low:high] for low, high in zip(edges, edges[1:])
    ]
    in_square = in_grad * in_grad
    out_square = out_grad * out_grad
    in_row_part = jnp.sum(in_square, axis=(1, 2))
    out_row_part = jnp.sum(out_square, axis=1)
    small_row_part = jnp.sum(small_full * small_full, axis=1)
    in_total = jnp.sum(DECAY * in_rows + (1.0 - DECAY) * EPS_FACTOR) * tp_first + (
        1.0 - DECAY
    ) * jnp.sum(in_row_part) / (2 * channels)
    out_total = jnp.sum(DECAY * out_rows + (1.0 - DECAY) * EPS_FACTOR) * tp_first + (
        1.0 - DECAY
    ) * jnp.sum(out_row_part) / channels
    seq_part = jnp.concatenate(
        [jnp.sum(in_square, axis=0).reshape(-1, 128), jnp.sum(out_square, axis=0).reshape(-1, 128)]
    )
    shared_part = jnp.concatenate(
        [
            gain_part.reshape(-1, 128),
            jnp.broadcast_to(in_total, (8, 128)),
            jnp.broadcast_to(out_total, (8, 128)),
        ]
    )
    row_parts = jnp.concatenate([in_row_part, out_row_part, small_row_part])
    row_parts = jnp.pad(row_parts, (0, -row_parts.shape[0] % 1024)).reshape(-1, 128)
    col_sums, shared_sums, row_sums = sum_over(seq_part, shared_part, row_parts)
    col_sums = col_sums.reshape(-1)
    in_col_sums = col_sums[: 2 * inner_dim].reshape(2, inner_dim)
    out_col_sums = col_sums[2 * inner_dim :]
    gain_grad = shared_sums[: model_dim // 128].reshape(-1)
    in_mean = shared_sums[model_dim // 128, 0] / model_dim
    out_mean = shared_sums[model_dim // 128 + 8, 0] / model_dim
    row_sums = row_sums.reshape(-1)
    in_row_sums = row_sums[:row_share]
    out_row_sums = row_sums[row_share : 2 * row_share]
    small_row_sums = row_sums[2 * row_share :]
    in_rows_new = DECAY * in_rows + (1.0 - DECAY) * (in_row_sums / (2 * channels) + EPS_FACTOR)
    in_cols_new = DECAY * in_cols + (1.0 - DECAY) * (in_col_sums / model_dim + EPS_FACTOR)
    out_rows_new = DECAY * out_rows + (1.0 - DECAY) * (out_row_sums / channels + EPS_FACTOR)
    out_cols_new = DECAY * out_cols + (1.0 - DECAY) * (out_col_sums / model_dim + EPS_FACTOR)
    step_rows_new, step_cols_new, stepw_update = factor_update(
        step_local, small_row_sums[edges[0] : edges[1]], step_rows, step_cols, channels
    )
    select_rows_new, select_cols_new, select_update = factor_update(
        select_local, small_row_sums[edges[1] : edges[2]], select_rows, select_cols, channels
    )
    decay_rows_new, decay_cols_new, decay_update = factor_update(
        decay_local, small_row_sums[edges[2] : edges[3]], decay_rows, decay_cols, channels
    )
    conv_rows_new, conv_cols_new, conv_update = factor_update(
        conv_local, small_row_sums[edges[3] : edges[4]], conv_rows, conv_cols, channels
    )
    bias_moment_new, convb_update = moment_update(vector_local[0], bias_moment)
    step_moment_new, stepb_update = moment_update(vector_local[1], step_moment)
    skip_moment_new, skip_update = moment_update(vector_local[2], skip_moment)
    gain_moment_new, gain_update = moment_update(gain_grad, norm_moment)
    in_update = in_grad * lax.rsqrt(in_rows_new[:, None, None] * in_cols_new[None] / in_mean)
    out_update = out_grad * lax.rsqrt(out_rows_new[:, None] * out_cols_new[None, :] / out_mean)
    squares = jnp.stack(
        [
            sum_squares(in_update),
            sum_squares(out_update),
            seq_first * sum_squares(conv_update),
            seq_first * sum_squares(select_update),
            seq_first * sum_squares(stepw_update),
            seq_first * sum_squares(decay_update),
            seq_first * sum_squares(convb_update),
            seq_first * sum_squares(stepb_update),
            seq_first * sum_squares(skip_update),
        ]
    )
    _, clip_totals, _ = sum_over(
        nothing, jnp.broadcast_to(jnp.pad(squares, (0, 7))[:, None], (16, 128)), nothing
    )
    clip_totals = clip_totals[:, 0]
    gain_new = apply_step(norm_gain, gain_update, sum_squares(gain_update), model_dim, RATES[0])
    in_new = apply_step(in_weight, in_update, clip_totals[0], model_dim * 2 * channels, RATES[1])
    out_new = apply_step(out_weight, out_update, clip_totals[1], model_dim * channels, RATES[2])
    convw_new = apply_step(conv_weight, conv_update, clip_totals[2], conv_taps * channels, RATES[3])
    convb_new = apply_step(conv_bias, convb_update, clip_totals[6], channels, RATES[4])
    select_new = apply_step(
        select_weight, select_update, clip_totals[3], select_weight.shape[0] * channels, RATES[5]
    )
    stepw_new = apply_step(
        step_weight, stepw_update, clip_totals[4], step_rank * channels, RATES[6]
    )
    stepb_new = apply_step(step_bias, stepb_update, clip_totals[7], channels, RATES[7])
    decay_new = apply_step(decay_log, decay_update, clip_totals[5], states * channels, RATES[8])
    skip_new = apply_step(skip_gain, skip_update, clip_totals[8], channels, RATES[9])
    return (
        block_out,
        input_grad,
        gain_grad,
        gain_new,
        gain_new.astype(low_type),
        gain_moment_new,
        in_grad,
        in_new,
        in_new.astype(low_type),
        in_rows_new,
        in_cols_new,
        out_grad,
        out_new,
        out_new.astype(low_type),
        out_rows_new,
        out_cols_new,
        conv_local,
        convw_new,
        convw_new.astype(low_type),
        conv_rows_new,
        conv_cols_new,
        vector_local[0],
        convb_new,
        convb_new.astype(low_type),
        bias_moment_new,
        select_local,
        select_new,
        select_new.astype(low_type),
        select_rows_new,
        select_cols_new,
        step_local,
        stepw_new,
        stepw_new.astype(low_type),
        step_rows_new,
        step_cols_new,
        vector_local[1],
        stepb_new,
        stepb_new.astype(low_type),
        step_moment_new,
        decay_local,
        decay_new,
        decay_new.astype(low_type),
        decay_rows_new,
        decay_cols_new,
        vector_local[2],
        skip_new,
        skip_new.astype(low_type),
        skip_moment_new,
    )


def on_block_device(
    block_in,
    cotangent,
    segment_ids,
    norm_gain,
    in_weight,
    out_weight,
    conv_weight,
    conv_bias,
    select_weight,
    step_weight,
    step_bias,
    decay_log,
    skip_gain,
    norm_moment,
    in_rows,
    in_cols,
    out_rows,
    out_cols,
    conv_rows,
    conv_cols,
    bias_moment,
    select_rows,
    select_cols,
    step_rows,
    step_cols,
    step_moment,
    decay_rows,
    decay_cols,
    skip_moment,
):
    tp_count = lax.axis_size("tp")
    seq_index = lax.axis_index("seq")
    tp_index = lax.axis_index("tp")
    half_rows, model_dim = block_in.shape
    row_count = cotangent.shape[0]
    inner_dim = in_weight.shape[2]
    channels = inner_dim * tp_count
    conv_taps = conv_weight.shape[0]
    states = decay_log.shape[0]
    step_rank = step_weight.shape[0]
    row_share = in_weight.shape[0]
    low_type = jnp.bfloat16
    id_padded = jnp.concatenate(
        [
            jnp.full((conv_taps - 1,), -1, jnp.int32),
            segment_ids,
            jnp.full((conv_taps - 1,), -2, jnp.int32),
        ]
    )
    window = lax.dynamic_slice_in_dim(
        id_padded, seq_index * row_count, row_count + 2 * (conv_taps - 1)
    )
    local_ids = window[conv_taps - 1 : conv_taps - 1 + row_count]
    same_docs = [
        (window[conv_taps - 1 - lag : conv_taps - 1 - lag + row_count] == local_ids).astype(
            jnp.float32
        )[:, None]
        for lag in range(conv_taps)
    ]
    ids_after = window[conv_taps - 1 :]
    same_after = [
        (ids_after[lag : lag + row_count] == local_ids).astype(jnp.float32)[:, None]
        for lag in range(1, conv_taps)
    ]
    masks = jnp.broadcast_to(
        jnp.stack(same_docs[1:] + same_after), (2 * (conv_taps - 1), row_count, 128)
    )
    f = forward_block(
        0,
        ForwardIn(
        in_weight=in_weight,
        out_weight=out_weight,
        block=block_in,
        cot=cotangent,
        norm_gain=norm_gain,
        conv_weight=conv_weight,
        conv_bias=conv_bias,
        step_bias=step_bias,
        skip_gain=skip_gain,
        masks=masks,
        select_weight=select_weight,
        step_weight=step_weight,
        decay_log=decay_log,
        ),
    )
    rest = rest_block(
        1,
        channels,
        RestIn(
            block=block_in,
            cot=cotangent,
            step_rows=step_rows,
            select_rows=select_rows,
            decay_rows=decay_rows,
            conv_rows=conv_rows,
            in_rows=in_rows,
            out_rows=out_rows,
            masks=masks,
            conv_weight=conv_weight,
            select_weight=select_weight,
            step_weight=step_weight,
            decay_log=decay_log,
            norm_gain=norm_gain,
            norm_moment=norm_moment,
            in_cols=in_cols,
            out_cols=out_cols,
            step_cols=step_cols,
            select_cols=select_cols,
            decay_cols=decay_cols,
            conv_cols=conv_cols,
            bias_moment=bias_moment,
            step_moment=step_moment,
            skip_moment=skip_moment,
            conv_bias=conv_bias,
            step_bias=step_bias,
            skip_gain=skip_gain,
            **shared(f, RestIn),
        ),
    )
    return renew(
        RenewIn(
            value_grad=rest.in_grad,
            gate_grad=rest.in_grad,
            in_weight=in_weight,
            out_weight=out_weight,
            step_weight=step_weight,
            select_weight=select_weight,
            decay_log=decay_log,
            conv_weight=conv_weight,
            **shared(rest, RenewIn),
        )
    )


def solution(mesh):
    on_slice = mesh.shape["seq"] == 16 and mesh.shape["tp"] == 2
    return jax.shard_map(
        on_block_device if on_slice else on_device,
        mesh=mesh,
        in_specs=(
            P(("seq", "tp"), None),
            P("seq", None),
            P(),
            P(),
            P("seq", None, "tp"),
            P("seq", "tp"),
            P(None, "tp"),
            P("tp"),
            P(None, "tp"),
            P(None, "tp"),
            P("tp"),
            P(None, "tp"),
            P("tp"),
            P(),
            P("seq"),
            P(None, "tp"),
            P("seq"),
            P("tp"),
            P(),
            P("tp"),
            P("tp"),
            P(),
            P("tp"),
            P(),
            P("tp"),
            P("tp"),
            P(),
            P("tp"),
            P("tp"),
        ),
        out_specs=(
            P(("seq", "tp"), None),
            P(("seq", "tp"), None),
            P(),
            P(),
            P(),
            P(),
            P("seq", None, "tp"),
            P("seq", None, "tp"),
            P("seq", None, "tp"),
            P("seq"),
            P(None, "tp"),
            P("seq", "tp"),
            P("seq", "tp"),
            P("seq", "tp"),
            P("seq"),
            P("tp"),
            P(None, "tp"),
            P(None, "tp"),
            P(None, "tp"),
            P(),
            P("tp"),
            P("tp"),
            P("tp"),
            P("tp"),
            P("tp"),
            P(None, "tp"),
            P(None, "tp"),
            P(None, "tp"),
            P(),
            P("tp"),
            P(None, "tp"),
            P(None, "tp"),
            P(None, "tp"),
            P(),
            P("tp"),
            P("tp"),
            P("tp"),
            P("tp"),
            P("tp"),
            P(None, "tp"),
            P(None, "tp"),
            P(None, "tp"),
            P(),
            P("tp"),
            P("tp"),
            P("tp"),
            P("tp"),
            P("tp"),
        ),
        check_vma=False,
    )
```
